32 devices in a mesh: fsdp: 16 (over z, y, x), tensor: 2 (over core).
Axes of the slice: x: 2, y: 2, z: 4, core: 2. Of those that a mesh axis runs over, the one named last changes fastest.
Arguments:
- tokens: bfloat16 [16384, 768], P(('fsdp', 'tensor'))
- cotangent: bfloat16 [16384, 768], P(('fsdp', 'tensor')), may hold values from -6 to 6
- prefix_len: int32 [16], P('fsdp'), may hold values from 102 to 512
- expert_ids: int32 [16384, 1], P('fsdp'), may hold values from 0 to 3
- norm_gains: bfloat16 [2, 768], P(None, 'fsdp'), may hold values from 0.5 to 1.5
- qkv_weight: bfloat16 [3, 768, 768], P(None, 'fsdp', 'tensor'), may hold values from -0.21875 to 0.21875
- out_weight: bfloat16 [768, 768], P('fsdp', 'tensor'), may hold values from -1.75 to 1.75
- router_weight: bfloat16 [4, 768], P(None, 'fsdp'), may hold values from -0.15625 to 0.15625
- up_weight: bfloat16 [4, 768, 3072], P(None, 'fsdp', 'tensor'), may hold values from -0.21875 to 0.21875
- down_weight: bfloat16 [4, 768, 3072], P(None, 'fsdp', 'tensor'), may hold values from -0.21875 to 0.21875
Outputs:
- block_out: bfloat16 [16384, 768], P(('fsdp', 'tensor'))
- tokens_grad: float32 [16384, 768], P(('fsdp', 'tensor'))
- gains_grad: float32 [2, 768], P(None, 'fsdp')
- qkv_grad: float32 [3, 768, 768], P(None, 'fsdp', 'tensor')
- out_grad: float32 [768, 768], P('fsdp', 'tensor')
- router_grad: float32 [4, 768], P(None, 'fsdp')
- up_grad: float32 [4, 768, 3072], P(None, 'fsdp', 'tensor')
- down_grad: float32 [4, 768, 3072], P(None, 'fsdp', 'tensor')
- balance_loss: float32 [], replicated
The draws below stay inside these ranges and needn't reach their ends.
All inputs are finite; a program needn't handle non-finite values.
Results may differ from the reference program's by a relative error of at most 0.011.
Values may be sent and summed in bfloat16 or wider, within the bound.
A program may use at most 256 MiB of HBM per device.

```python
import math
import jax
import jax.numpy as jnp
from jax import lax

D = 768
HEADS = 12
HEAD = 64
FF = 3072
EXPERTS = 4
SEQ = 1024
SEQ_DEV = 1
WIDTH = 768
TOK_GROUP = 1024
CAP = 256
SEQS = 16
TOKENS = 16384


def draw_tokens(key, part):
    noise_key = jax.random.fold_in(key, 11)
    common_key = jax.random.fold_in(key, 12)
    group_count = TOKENS // TOK_GROUP
    group_of = lax.broadcasted_iota(jnp.int32, (TOKENS, 1), 0) // TOK_GROUP
    fraction = group_of.astype(jnp.float32) / float(max(group_count - 1, 1))
    common = jnp.clip(jax.random.normal(common_key, (1, D), jnp.float32), -3.0, 3.0)
    noise = jnp.clip(jax.random.normal(noise_key, (TOKENS, D), jnp.float32), -4.0, 4.0)
    weight_of = 0.3 + 0.7 * fraction
    return (noise + weight_of * common).astype(jnp.bfloat16)


def draw_expert_ids(key, part):
    pick_key = jax.random.fold_in(key, 21)
    group_count = TOKENS // TOK_GROUP
    group_of = lax.broadcasted_iota(jnp.int32, (TOKENS,), 0) // TOK_GROUP
    rising = 12 * group_of // max(group_count - 1, 1)
    expert_row = jnp.arange(EXPERTS, dtype=jnp.int32)[None, :]
    weights = 4 + jnp.where(expert_row == 0, rising[:, None], 0) + jnp.where(expert_row == EXPERTS - 1, 12 - rising[:, None], 0)
    total = 4 * EXPERTS + 12
    drawn = jax.random.randint(pick_key, (TOKENS, 1), 0, total, dtype=jnp.int32)
    bounds = jnp.cumsum(weights, axis=1).astype(jnp.int32)
    chosen = jnp.sum((drawn >= bounds).astype(jnp.int32), axis=1)
    return jnp.minimum(chosen, EXPERTS - 1).astype(jnp.int32)[:, None]


def place_ends(values, rng, least, largest):
    index_at = [jax.random.randint(jax.random.fold_in(rng, axis), (), 0, length) for axis, length in enumerate(values.shape)]
    widest = values.shape.index(max(values.shape))
    neighbour = index_at[:widest] + [(index_at[widest] + 1) % values.shape[widest]] + index_at[widest + 1:]
    return values.at[tuple(index_at)].set(least).at[tuple(neighbour)].set(largest)


def levels(rng, extent, split, low, top_value):
    level = 1.0
    for position, shards_of in split:
        draws = jax.random.uniform(jax.random.fold_in(jax.random.fold_in(rng, 6), position), (shards_of,), jnp.float32, low / len(split), top_value / len(split))
        level = level * jnp.repeat(jnp.exp(draws), extent[position] // shards_of).reshape((-1,) + (1,) * (len(extent) - 1 - position))
    return level


def bell_draw(stream_key, dims, scale, bound, shards=(), kind=jnp.bfloat16):
    values = scale * jax.random.normal(stream_key, dims, jnp.float32)
    if shards:
        values = values * levels(stream_key, dims, shards, -0.22, 0.18)
    return jnp.clip(values, -bound, bound).astype(kind)


def setup_inputs(seed: int = 0) -> dict:
    seeds = jax.random.split(jax.random.key(seed), 11)
    tokens = draw_tokens(jax.random.fold_in(seeds[10], 71), 0)
    cotangent = bell_draw(seeds[1], (TOKENS, D), 1.0, 6.0, ((0, 32),))
    prefix_len = place_ends(jax.random.randint(seeds[2], (SEQS,), SEQ // 10, SEQ // 2 + 1), jax.random.fold_in(seeds[2], 1), SEQ // 10, (SEQ // 2 + 1) - 1).astype(jnp.int32)
    expert_ids = draw_expert_ids(jax.random.fold_in(seeds[10], 71), 0)
    norm_gains = jnp.clip(1.0 + 0.1 * jax.random.normal(seeds[4], (2, D), jnp.float32), 0.5, 1.5).astype(jnp.bfloat16)
    qkv_weight = bell_draw(seeds[5], (3, D, WIDTH), D ** -0.5, 0.21875, ((1, 16), (2, 2)))
    out_weight = bell_draw(seeds[6], (D, WIDTH), HEADS ** -0.5, 1.75, ((0, 16), (1, 2)))
    router_weight = bell_draw(seeds[7], (EXPERTS, D), (2 * D) ** -0.5, 0.15625, ((1, 16),))
    up_weight = bell_draw(seeds[8], (EXPERTS, D, FF), D ** -0.5, 0.21875, ((1, 16), (2, 2)))
    down_weight = bell_draw(seeds[9], (EXPERTS, D, FF), (FF // 4) ** -0.5, 0.21875, ((1, 16), (2, 2)))
    return {"tokens": tokens, "cotangent": cotangent, "prefix_len": prefix_len, "expert_ids": expert_ids, "norm_gains": norm_gains, "qkv_weight": qkv_weight, "out_weight": out_weight, "router_weight": router_weight, "up_weight": up_weight, "down_weight": down_weight}


highest = lax.Precision.HIGHEST
norm_eps = 1e-05
balance_weight = 0.01
masked_score = -1e+30

@jax.custom_vjp
def low(v):
    return lax.optimization_barrier(v.astype(jnp.bfloat16)).astype(jnp.float32)

@jax.custom_vjp
def low_back(v):
    return v

def low_keep(v):
    return (low(v), None)

def low_pass(kept, grad):
    return (grad,)

def back_keep(v):
    return (v, None)

def back_low(kept, grad):
    return (low(grad),)
low.defvjp(low_keep, low_pass)
low_back.defvjp(back_keep, back_low)

def softmax_rows(scores):
    row_max = lax.optimization_barrier(jnp.max(scores, axis=-1, keepdims=True))
    shifted = jnp.exp(scores - row_max)
    return shifted / lax.optimization_barrier(jnp.sum(shifted, axis=-1, keepdims=True))

def slot_index(group_ids):
    onehot = (group_ids[:, None] == jnp.arange(EXPERTS, dtype=jnp.int32)[None, :]).astype(jnp.int32)
    running = jnp.cumsum(onehot, axis=0).astype(jnp.int32)
    placed = lax.optimization_barrier(jnp.sum(running * onehot, axis=1)).astype(jnp.int32) - 1
    return jnp.where(placed < CAP, group_ids * CAP + placed, EXPERTS * CAP).astype(jnp.int32)

def layer_group(group_tokens, group_prefix, group_ids, norm_gains, qkv_weight, out_weight, router_weight, up_weight, down_weight, route_share):
    score_scale = 1.0 / math.sqrt(HEAD)
    factor_one = lax.rsqrt(lax.optimization_barrier(jnp.mean(group_tokens * group_tokens, axis=-1, keepdims=True)) + norm_eps)
    normed = low(group_tokens * factor_one * norm_gains[0])
    project = jnp.einsum('td,sdw->tsw', normed, qkv_weight, precision=highest)
    project = low(low_back(project))
    shaped = project.reshape(SEQ_DEV, SEQ, 3, HEADS, HEAD)
    query_all = shaped[:, :, 0]
    key_all = shaped[:, :, 1]
    value_all = shaped[:, :, 2]
    scores = low_back(jnp.einsum('bqhd,bkhd->bhqk', query_all, key_all, precision=highest) * score_scale)
    positions = jnp.arange(SEQ, dtype=jnp.int32)
    allowed = (positions[None, None, :] <= positions[None, :, None]) | (positions[None, None, :] < group_prefix[:, None, None])
    scores = jnp.where(allowed[:, None], scores, masked_score)
    att_prob = low(softmax_rows(scores))
    attended = jnp.einsum('bhqk,bkhd->bqhd', att_prob, value_all, precision=highest).reshape(TOK_GROUP, WIDTH)
    attended = low(low_back(attended))
    branch = low_back(jnp.dot(attended, out_weight.T, precision=highest))
    hidden = group_tokens + branch
    factor_two = lax.rsqrt(lax.optimization_barrier(jnp.mean(hidden * hidden, axis=-1, keepdims=True)) + norm_eps)
    moe_input = low(hidden * factor_two * norm_gains[1])
    logits = jnp.dot(moe_input, router_weight.T, precision=highest)
    onehot = (group_ids[:, None] == jnp.arange(EXPERTS, dtype=jnp.int32)[None, :]).astype(jnp.float32)
    gate_value = jax.nn.sigmoid(lax.optimization_barrier(jnp.sum(logits * onehot, axis=-1)))
    router_prob = softmax_rows(logits)
    slot_rows = slot_index(group_ids)
    dispatched = jnp.zeros((EXPERTS * CAP, D), jnp.float32).at[slot_rows].set(moe_input, mode='drop').reshape(EXPERTS, CAP, D)
    before = low_back(jnp.einsum('ecd,edf->ecf', dispatched, up_weight, precision=highest))
    activated = low(jax.nn.gelu(before, approximate=False))
    expert_out = jnp.einsum('ecf,edf->ecd', activated, down_weight, precision=highest).reshape(EXPERTS * CAP, D)
    combined = jnp.concatenate([expert_out, jnp.zeros((1, D), jnp.float32)], axis=0)[slot_rows]
    combined = low_back(combined)
    block_out = hidden + gate_value[:, None] * combined
    loss_part = EXPERTS * jnp.sum(route_share * lax.optimization_barrier(jnp.sum(router_prob, axis=0))) / TOKENS
    return (block_out, loss_part)

def reference(tokens, cotangent, prefix_len, expert_ids, norm_gains, qkv_weight, out_weight, router_weight, up_weight, down_weight):
    groups = TOKENS // TOK_GROUP
    all_ids = expert_ids[:, 0].astype(jnp.int32)
    counts = lax.optimization_barrier(jnp.sum((all_ids[:, None] == jnp.arange(EXPERTS, dtype=jnp.int32)[None, :]).astype(jnp.float32), axis=0))
    route_share = counts / TOKENS
    token_blocks = tokens.astype(jnp.float32).reshape(groups, TOK_GROUP, D)
    id_blocks = all_ids.reshape(groups, TOK_GROUP)
    prefix_blocks = prefix_len.astype(jnp.int32).reshape(groups, SEQ_DEV)
    checked = jax.checkpoint(layer_group)

    def whole_layer(blocks, gains, qkv, outw, router, upw, downw):

        def group_step(loss_total, inputs):
            block_tokens, block_prefix, block_ids = inputs
            block_out, loss_part = checked(block_tokens, block_prefix, block_ids, gains, qkv, outw, router, upw, downw, route_share)
            return (loss_total + loss_part, block_out)
        loss_total, outputs = lax.scan(group_step, jnp.float32(0.0), (blocks, prefix_blocks, id_blocks))
        return (outputs, loss_total)
    primal, pullback = jax.vjp(whole_layer, token_blocks, norm_gains.astype(jnp.float32), qkv_weight.astype(jnp.float32), out_weight.astype(jnp.float32), router_weight.astype(jnp.float32), up_weight.astype(jnp.float32), down_weight.astype(jnp.float32))
    outputs, balance_loss = primal
    pulled = pullback((cotangent.astype(jnp.float32).reshape(groups, TOK_GROUP, D), jnp.float32(balance_weight)))
    block_out = outputs.reshape(TOKENS, D).astype(jnp.bfloat16)
    tokens_grad = pulled[0].reshape(TOKENS, D)
    return (block_out, tokens_grad, pulled[1], pulled[2], pulled[3], pulled[4], pulled[5], pulled[6], balance_loss)
```

```python
import math

import jax
import jax.numpy as jnp
from jax import lax
from jax.sharding import PartitionSpec as P

HEAD = 64
EXPERTS = 4
SEQ = 1024
CAP = 256


highest = lax.Precision.HIGHEST
norm_eps = 1e-05
balance_weight = 0.01
masked_score = -1e30


def softmax_rows(scores):
    row_max = jnp.max(scores, axis=-1, keepdims=True)
    shifted = jnp.exp(scores - row_max)
    return shifted / jnp.sum(shifted, axis=-1, keepdims=True)


def slot_index(group_ids):
    onehot = (group_ids[:, None] == jnp.arange(EXPERTS, dtype=jnp.int32)[None, :]).astype(jnp.int32)
    rows = group_ids.shape[0]
    earlier = lax.broadcasted_iota(jnp.int32, (rows, rows), 1) <= lax.broadcasted_iota(
        jnp.int32, (rows, rows), 0
    )
    running = jnp.dot(
        earlier.astype(jnp.bfloat16),
        onehot.astype(jnp.bfloat16),
        preferred_element_type=jnp.float32,
    ).astype(jnp.int32)
    placed = jnp.sum(running * onehot, axis=1) - 1
    return jnp.where(placed < CAP, group_ids * CAP + placed, EXPERTS * CAP)


def rms_factor(values):
    return lax.rsqrt(jnp.mean(values * values, axis=-1, keepdims=True) + norm_eps)


def norm_back(grad_out, inputs, factor, gain):
    scaled = grad_out * gain
    row_inner = jnp.mean(scaled * inputs, axis=-1, keepdims=True)
    grad_in = factor * (scaled - inputs * factor * factor * row_inner)
    grad_gain = jnp.sum(grad_out * inputs * factor, axis=0)
    return (grad_in, grad_gain)


def gelu_slope(values):
    cumulative = 0.5 * (1.0 + lax.erf(values / math.sqrt(2.0)))
    density = jnp.exp(-0.5 * values * values) / math.sqrt(2.0 * math.pi)
    return cumulative + values * density


def block_scores(query_block, key_seq, offset, prefix, score_scale):
    scores = (
        jnp.einsum("qhd,khd->hqk", query_block, key_seq, preferred_element_type=jnp.float32)
        * score_scale
    )
    shape_pair = (query_block.shape[0], key_seq.shape[0])
    row_pos = offset + lax.broadcasted_iota(jnp.int32, shape_pair, 0)
    col_pos = lax.broadcasted_iota(jnp.int32, shape_pair, 1)
    allowed = (col_pos <= row_pos) | (col_pos < prefix)
    return jnp.where(allowed[None], scores, masked_score)


def attend(project, prefix_len, score_scale):
    group_rows = project.shape[0]
    full_width = project.shape[2]
    heads_here = full_width // HEAD
    block_rows = min(512, SEQ)
    shaped = project.reshape(group_rows, 3, heads_here, HEAD)
    query_all = shaped[:, 0]
    key_all = shaped[:, 1]
    value_all = shaped[:, 2]

    def one_block(number):
        row_start = number * block_rows
        seq_number = row_start // SEQ
        seq_start = seq_number * SEQ
        query_block = lax.dynamic_slice_in_dim(query_all, row_start, block_rows, 0)
        scores = block_scores(
            query_block, key_all, row_start - seq_start, prefix_len[seq_number], score_scale
        )
        row_max = jnp.max(scores, axis=-1, keepdims=True)
        shifted = jnp.exp(scores - row_max)
        row_total = jnp.sum(shifted, axis=-1, keepdims=True)
        prob_low = (shifted / row_total).astype(jnp.bfloat16)
        result = jnp.einsum("hqk,khd->qhd", prob_low, value_all, preferred_element_type=jnp.float32)
        return (
            result.reshape(block_rows, full_width).astype(jnp.bfloat16),
            (row_max + jnp.log(row_total))[..., 0],
        )

    outputs, log_total = lax.map(one_block, jnp.arange(group_rows // block_rows, dtype=jnp.int32))
    return (outputs.reshape(group_rows, full_width), log_total)


def attend_back(project, grad_att, log_total, prefix_len, score_scale):
    group_rows = project.shape[0]
    full_width = project.shape[2]
    heads_here = full_width // HEAD
    block_rows = min(512, SEQ)
    shaped = project.reshape(group_rows, 3, heads_here, HEAD)
    query_all = shaped[:, 0]
    key_all = shaped[:, 1]
    value_all = shaped[:, 2]
    grad_shaped = grad_att.reshape(group_rows, heads_here, HEAD)

    def one_block(carried, number):
        grad_keys, grad_values = carried
        row_start = number * block_rows
        seq_number = row_start // SEQ
        seq_start = seq_number * SEQ
        query_block = lax.dynamic_slice_in_dim(query_all, row_start, block_rows, 0)
        grad_block = lax.dynamic_slice_in_dim(grad_shaped, row_start, block_rows, 0)
        scores = block_scores(
            query_block, key_all, row_start - seq_start, prefix_len[seq_number], score_scale
        )
        prob_block = jnp.exp(scores - log_total[number][..., None])
        prob_low = prob_block.astype(jnp.bfloat16)
        grad_prob = jnp.einsum(
            "qhd,khd->hqk", grad_block, value_all, preferred_element_type=jnp.float32
        )
        value_part = jnp.einsum(
            "hqk,qhd->khd", prob_low, grad_block, preferred_element_type=jnp.float32
        )
        row_inner = jnp.sum(prob_block * grad_prob, axis=-1, keepdims=True)
        grad_scores = (prob_block * (grad_prob - row_inner)).astype(jnp.bfloat16)
        query_grad = (
            jnp.einsum("hqk,khd->qhd", grad_scores, key_all, preferred_element_type=jnp.float32)
            * score_scale
        )
        key_part = (
            jnp.einsum("hqk,qhd->khd", grad_scores, query_block, preferred_element_type=jnp.float32)
            * score_scale
        )
        old_keys = grad_keys
        grad_keys = old_keys + key_part
        old_values = grad_values
        grad_values = old_values + value_part
        return ((grad_keys, grad_values), query_grad)

    zero_rows = jnp.zeros((group_rows, heads_here, HEAD), jnp.float32)
    final, grad_query = lax.scan(
        one_block, (zero_rows, zero_rows), jnp.arange(group_rows // block_rows, dtype=jnp.int32)
    )
    grad_keys, grad_values = final
    stacked = jnp.stack(
        [
            grad_query.reshape(group_rows, full_width),
            grad_keys.reshape(group_rows, full_width),
            grad_values.reshape(group_rows, full_width),
        ],
        axis=1,
    )
    return stacked.astype(jnp.bfloat16)


def low_scatter(grad):
    return lax.psum_scatter(
        grad.astype(jnp.bfloat16), "fsdp", scatter_dimension=1, tiled=True
    ).astype(jnp.float32)


def per_device(
    tokens,
    cotangent,
    prefix_len,
    expert_ids,
    norm_gains,
    qkv_weight,
    out_weight,
    router_weight,
    up_weight,
    down_weight,
):
    tensor_size = lax.axis_size("tensor")
    fsdp_size = lax.axis_size("fsdp")
    own_rows = tokens.shape[0]
    group_rows = own_rows * tensor_size
    all_tokens = group_rows * fsdp_size
    own_start = lax.axis_index("tensor") * own_rows
    score_scale = 1.0 / math.sqrt(HEAD)
    gains_full, qkv_full, out_stack = (
        lax.all_gather(norm_gains, "fsdp", axis=1, tiled=True),
        lax.all_gather(qkv_weight, "fsdp", axis=1, tiled=True),
        lax.all_gather(out_weight[None], "fsdp", axis=1, tiled=True),
    )
    out_full = out_stack[0]
    router_full, up_full, down_full = (
        lax.all_gather(router_weight, "fsdp", axis=1, tiled=True),
        lax.all_gather(up_weight, "fsdp", axis=1, tiled=True),
        lax.all_gather(down_weight, "fsdp", axis=1, tiled=True),
    )
    inputs = lax.all_gather(tokens, "tensor", axis=0, tiled=True)
    input_float = inputs.astype(jnp.float32)
    factor_one = rms_factor(input_float)
    gain_one = gains_full[0].astype(jnp.float32)
    normed_one = (input_float * factor_one * gain_one).astype(jnp.bfloat16)
    project = jnp.einsum(
        "td,sdw->tsw", normed_one, qkv_full, preferred_element_type=jnp.float32
    ).astype(jnp.bfloat16)
    attended, log_total = attend(project, prefix_len, score_scale)
    branch = lax.psum_scatter(
        lax.dot_general(
            attended, out_full, (((1,), (1,)), ((), ())), preferred_element_type=jnp.float32
        ),
        "tensor",
        scatter_dimension=0,
        tiled=True,
    )
    hidden_own = tokens.astype(jnp.float32) + branch
    hidden_group = lax.all_gather(hidden_own, "tensor", axis=0, tiled=True)
    factor_two = rms_factor(hidden_group)
    gain_two = gains_full[1].astype(jnp.float32)
    moe_input = (hidden_group * factor_two * gain_two).astype(jnp.bfloat16)
    logits = lax.dot_general(
        moe_input, router_full, (((1,), (1,)), ((), ())), preferred_element_type=jnp.float32
    )
    group_ids = expert_ids[:, 0]
    onehot = (group_ids[:, None] == jnp.arange(EXPERTS, dtype=jnp.int32)[None, :]).astype(
        jnp.float32
    )
    gate_value = jax.nn.sigmoid(jnp.sum(logits * onehot, axis=-1))
    router_prob = softmax_rows(logits)
    counts, prob_sums = lax.psum((jnp.sum(onehot, axis=0), jnp.sum(router_prob, axis=0)), "fsdp")
    route_share = counts / all_tokens
    balance_loss = EXPERTS * jnp.sum(route_share * prob_sums) / all_tokens
    slot_rows = slot_index(group_ids)
    model_width = moe_input.shape[1]
    dispatched = (
        jnp.zeros((EXPERTS * CAP, model_width), jnp.bfloat16)
        .at[slot_rows]
        .set(moe_input, mode="drop")
        .reshape(EXPERTS, CAP, model_width)
    )
    before = jnp.einsum("ecd,edf->ecf", dispatched, up_full, preferred_element_type=jnp.float32)
    activated = jax.nn.gelu(before, approximate=False).astype(jnp.bfloat16)
    expert_out = jnp.einsum(
        "ecf,edf->ecd", activated, down_full, preferred_element_type=jnp.float32
    ).reshape(EXPERTS * CAP, model_width)
    combined_part = jnp.concatenate([expert_out, jnp.zeros((1, model_width), jnp.float32)], axis=0)[
        slot_rows
    ]
    combined = lax.psum_scatter(combined_part, "tensor", scatter_dimension=0, tiled=True)
    gate_own = lax.dynamic_slice_in_dim(gate_value, own_start, own_rows, 0)
    block_out = (hidden_own + gate_own[:, None] * combined).astype(jnp.bfloat16)
    gains_back, qkv_back, out_again, router_back, up_back, down_back = (
        lax.all_gather(norm_gains, "fsdp", axis=1, tiled=True),
        lax.all_gather(qkv_weight, "fsdp", axis=1, tiled=True),
        lax.all_gather(out_weight[None], "fsdp", axis=1, tiled=True),
        lax.all_gather(router_weight, "fsdp", axis=1, tiled=True),
        lax.all_gather(up_weight, "fsdp", axis=1, tiled=True),
        lax.all_gather(down_weight, "fsdp", axis=1, tiled=True),
    )
    out_back = out_again[0]
    cot_group = lax.all_gather(cotangent, "tensor", axis=0, tiled=True).astype(jnp.float32)
    grad_combined = (gate_value[:, None] * cot_group).astype(jnp.bfloat16)
    gate_grad_own = jnp.sum(cotangent.astype(jnp.float32) * combined, axis=-1)
    gate_grad_placed = lax.dynamic_update_slice_in_dim(
        jnp.zeros((group_rows,), jnp.float32), gate_grad_own, own_start, 0
    )
    grad_slots = (
        jnp.zeros((EXPERTS * CAP, model_width), jnp.bfloat16)
        .at[slot_rows]
        .set(grad_combined, mode="drop")
        .reshape(EXPERTS, CAP, model_width)
    )
    grad_activated = jnp.einsum(
        "ecd,edf->ecf", grad_slots, down_back, preferred_element_type=jnp.float32
    )
    down_grad = jnp.einsum(
        "ecd,ecf->edf", grad_slots, activated, preferred_element_type=jnp.float32
    )
    grad_before = (grad_activated * gelu_slope(before)).astype(jnp.bfloat16)
    up_grad = jnp.einsum(
        "ecd,ecf->edf", dispatched, grad_before, preferred_element_type=jnp.float32
    )
    grad_dispatched = jnp.einsum(
        "ecf,edf->ecd", grad_before, up_back, preferred_element_type=jnp.float32
    ).reshape(EXPERTS * CAP, model_width)
    grad_input_part = jnp.concatenate(
        [grad_dispatched, jnp.zeros((1, model_width), jnp.float32)], axis=0
    )[slot_rows]
    grad_moe, gate_grad = lax.psum((grad_input_part, gate_grad_placed), "tensor")
    gate_slope = gate_value * (1.0 - gate_value)
    mixed_share = jnp.sum(router_prob * route_share[None, :], axis=-1, keepdims=True)
    logit_grad = onehot * (gate_grad * gate_slope)[
        :, None
    ] + balance_weight * EXPERTS / all_tokens * router_prob * (route_share[None, :] - mixed_share)
    grad_norm_two = grad_moe + jnp.dot(
        logit_grad, router_back.astype(jnp.float32), precision=highest
    )
    router_grad = jnp.dot(logit_grad.T, moe_input.astype(jnp.float32), precision=highest)
    grad_hidden, gain_two_grad = norm_back(
        grad_norm_two, hidden_group, factor_two, gains_back[1].astype(jnp.float32)
    )
    grad_hidden = grad_hidden + cot_group
    grad_branch = grad_hidden.astype(jnp.bfloat16)
    grad_att = jnp.dot(grad_branch, out_back, preferred_element_type=jnp.float32).astype(
        jnp.bfloat16
    )
    out_grad = lax.dot_general(
        grad_branch, attended, (((0,), (0,)), ((), ())), preferred_element_type=jnp.float32
    )
    grad_project = attend_back(project, grad_att, log_total, prefix_len, score_scale)
    qkv_grad = jnp.einsum(
        "td,tsw->sdw", normed_one, grad_project, preferred_element_type=jnp.float32
    )
    grad_normed_part = jnp.einsum(
        "tsw,sdw->td", grad_project, qkv_back, preferred_element_type=jnp.float32
    )
    grad_normed = lax.psum(grad_normed_part, "tensor")
    grad_tokens, gain_one_grad = norm_back(
        grad_normed, input_float, factor_one, gains_back[0].astype(jnp.float32)
    )
    grad_tokens = grad_tokens + grad_hidden
    tokens_grad = lax.dynamic_slice_in_dim(grad_tokens, own_start, own_rows, 0)
    gains_own, qkv_own, out_own, router_own, up_own, down_own = (
        lax.psum_scatter(
            jnp.stack([gain_one_grad, gain_two_grad], axis=0),
            "fsdp",
            scatter_dimension=1,
            tiled=True,
        ),
        low_scatter(qkv_grad),
        low_scatter(out_grad[None]),
        lax.psum_scatter(router_grad, "fsdp", scatter_dimension=1, tiled=True),
        low_scatter(up_grad),
        low_scatter(down_grad),
    )
    return (
        block_out,
        tokens_grad,
        gains_own,
        qkv_own,
        out_own[0],
        router_own,
        up_own,
        down_own,
        balance_loss,
    )


def solution(mesh):
    placed = (
        P(("fsdp", "tensor"), None),
        P(("fsdp", "tensor"), None),
        P("fsdp"),
        P("fsdp", None),
        P(None, "fsdp"),
        P(None, "fsdp", "tensor"),
        P("fsdp", "tensor"),
        P(None, "fsdp"),
        P(None, "fsdp", "tensor"),
        P(None, "fsdp", "tensor"),
    )
    return jax.shard_map(
        per_device,
        mesh=mesh,
        in_specs=placed,
        out_specs=(
            P(("fsdp", "tensor"), None),
            P(("fsdp", "tensor"), None),
            P(None, "fsdp"),
            P(None, "fsdp", "tensor"),
            P("fsdp", "tensor"),
            P(None, "fsdp"),
            P(None, "fsdp", "tensor"),
            P(None, "fsdp", "tensor"),
            P(),
        ),
        check_vma=False,
    )
```

```python
import math
import types

import jax
import jax.numpy as jnp
from jax import lax
from jax.experimental import pallas as pl
from jax.experimental.pallas import tpu as pltpu
from jax.sharding import PartitionSpec as P

MESH = pl.DeviceIdType.MESH
BF = jnp.bfloat16
F32 = jnp.float32
ROWS = 1024
WIDE = 768
HALF = 384
HID = 1536
norm_eps = 1e-05
balance_weight = 0.01
masked_score = -1e30


def mm(a, b, ca=1, cb=0):
    return lax.dot_general(a, b, (((ca,), (cb,)), ((), ())), preferred_element_type=F32)


def iota(shape, axis):
    return lax.broadcasted_iota(jnp.int32, shape, axis)


def blocks(count, size, body):
    def step(i, carry):
        body(pl.ds(pl.multiple_of(i * size, size), size))
        return carry

    lax.fori_loop(0, count // size, step, 0)


class Place:
    def __init__(self):
        f, t = lax.axis_index("fsdp"), lax.axis_index("tensor")
        self.f, self.t, self.o = f, t, 1 - t
        self.z, self.c = lax.div(f, 4), lax.rem(f, 4)
        c = self.c
        self.cx = c + 1 - 2 * lax.rem(c, 2)
        self.cy = c + 2 - 4 * lax.div(c, 2)
        self.cd = 3 - c
        base = 4 * self.z
        self.X = {"fsdp": base + self.cx, "tensor": t}
        self.Y = {"fsdp": base + self.cy, "tensor": t}
        self.DIAG = {"fsdp": base + self.cd, "tensor": t}
        self.PAIR = {"fsdp": f, "tensor": 1 - t}

    def zto(self, k):
        return lax.rem(self.z + k, 4)

    def zfrom(self, k):
        return lax.rem(self.z + 4 - k, 4)

    def Z(self, k):
        return {"fsdp": 4 * self.zto(k) + self.c, "tensor": self.t}


class Wire:
    def __init__(self, send, recv):
        self.send, self.recv, self.n, self.open = send, recv, 0, []

    def ids(self, n):
        self.n += n
        return self.n - n

    def copy(self, i, src, dst, dev):
        return pltpu.make_async_remote_copy(
            src_ref=src,
            dst_ref=dst,
            send_sem=self.send.at[i],
            recv_sem=self.recv.at[i],
            device_id=dev,
            device_id_type=MESH,
        )

    def go(self, i, src, dst, dev):
        c = self.copy(i, src, dst, dev)
        c.start()
        self.open.append(c)
        return c

    def flush(self):
        for c in self.open:
            c.wait_send()
        self.open = []


def enter(pc):
    barrier = pltpu.get_barrier_semaphore()
    for dev in (pc.PAIR, pc.X, pc.Y, pc.DIAG, pc.Z(1), pc.Z(2), pc.Z(3)):
        pl.semaphore_signal(barrier, inc=1, device_id=dev, device_id_type=MESH)
    pl.semaphore_wait(barrier, 7)


def visible(krow0, kn, qcol0, qn, prefix):
    kpos = krow0 + iota((kn, qn), 0)
    qpos = qcol0 + iota((kn, qn), 1)
    ok = kpos <= qpos
    if krow0 < 512 and qcol0 < 512:
        ok = ok | (kpos < prefix)
    return ok


SEEN = (
    ((0, 512, True),),
    ((0, 512, True),),
    ((0, 512, False), (512, 256, True)),
    ((0, 512, False), (512, 256, False), (768, 256, True)),
)


def phase_a(R, pc, w):
    f, t, z, c = pc.f, pc.t, pc.z, pc.c
    idr = R.idr[...]
    ohr = (iota((16, ROWS), 0) - 8 == idr).astype(F32)
    cnt = jnp.sum(ohr, axis=1, keepdims=True)
    hi = jnp.floor(cnt * (1.0 / 256.0))
    lane16 = iota((16, 128), 1)
    R.SM[f] = jnp.where(
        lane16 == 48,
        cnt - 256.0 * hi,
        jnp.where(lane16 == 49, hi, R.small[...].astype(F32)),
    ).astype(BF)
    R.WA[z, c] = R.watt[...]
    enter(pc)
    own = pl.ds(pl.multiple_of(t * 512, 512), 512)
    i_tok, i_cot, i_wo, i_att = w.ids(1), w.ids(1), w.ids(1), w.ids(1)
    i_z, i_sz = w.ids(4), w.ids(4)
    i_x, i_y, i_fx, i_fy, i_sx, i_sy, i_sf = (w.ids(4) for _ in range(7))
    i_mu, i_md = w.ids(4), w.ids(4)
    i_m = [w.ids(4) for _ in range(6)]
    i_cz, i_dz, i_cp, i_dp = w.ids(4), w.ids(4), w.ids(1), w.ids(1)

    za = [w.go(i_z + k, R.watt, R.WA.at[z, c], pc.Z(k)) for k in (1, 2, 3)]
    zs = [w.go(i_sz + k, R.SM.at[f], R.SM.at[f], pc.Z(k)) for k in (1, 2, 3)]
    cot_x = w.go(i_cot, R.cot, R.CT.at[own], pc.PAIR)
    tok_x = w.go(i_tok, R.tok, R.TK.at[own], pc.PAIR)

    def spread(k):
        zz = pc.zfrom(k)
        g = 4 * zz + c
        a = w.go(i_x + k, R.WA.at[zz, c], R.WA.at[zz, c], pc.X)
        b = w.go(i_y + k, R.WA.at[zz, c], R.WA.at[zz, c], pc.Y)
        d = w.go(i_sx + k, R.SM.at[g], R.SM.at[g], pc.X)
        e = w.go(i_sy + k, R.SM.at[g], R.SM.at[g], pc.Y)
        return a, b, d, e

    def forward(k, got):
        zz = pc.zfrom(k)
        a, b, d, e = got
        a.wait_recv()
        x = w.go(
            i_fx + k,
            R.WA.at[zz, pc.cx, pl.ds(0, 2)],
            R.WA.at[zz, pc.cx, pl.ds(0, 2)],
            pc.Y,
        )
        d.wait_recv()
        g = 4 * zz + pc.cx
        s = w.go(i_sf + k, R.SM.at[g], R.SM.at[g], pc.Y)
        b.wait_recv()
        y = w.go(
            i_fy + k,
            R.WA.at[zz, pc.cy, pl.ds(2, 2)],
            R.WA.at[zz, pc.cy, pl.ds(2, 2)],
            pc.X,
        )
        e.wait_recv()
        return x, y, s

    got = {0: spread(0)}
    local = [
        pltpu.make_async_copy(R.tok, R.TK.at[own], R.ls.at[0]),
        pltpu.make_async_copy(R.cot, R.CT.at[own], R.ls.at[1]),
        pltpu.make_async_copy(R.up.at[z], R.UE.at[z, c], R.ls.at[2]),
        pltpu.make_async_copy(R.down.at[z], R.DE.at[z, c], R.ls.at[3]),
    ]
    for m in local:
        m.start()
    before_or_at = (iota((ROWS, ROWS), 0) <= iota((ROWS, ROWS), 1)).astype(F32).astype(BF)
    running = mm(ohr.astype(BF), before_or_at)
    placed = jnp.sum(running * ohr, axis=0, keepdims=True) - 1.0
    key = jnp.where(placed < 256.0, idr.astype(F32) * 256.0 + placed, -1.0)
    R.KC[...] = jnp.broadcast_to(key, (128, ROWS)).T
    R.PR[...] = jnp.broadcast_to(idr.astype(F32), (128, ROWS)).T
    r = iota((512, ROWS), 0)
    want = lax.div(r, 128) * 256 + lax.rem(r, 128) + 128 * t
    R.DM[...] = (key.astype(jnp.int32) == want).astype(F32).astype(BF)

    za[0].wait_recv()
    zs[0].wait_recv()
    got[1] = spread(1)
    for m in local:
        m.wait()
    cot_x.wait_recv()

    def cot_rows(e, carry):
        R.CS[e] = mm(R.DM[pl.ds(pl.multiple_of(e * 128, 128), 128)], R.CT[...]).astype(BF)
        return carry

    lax.fori_loop(0, 4, cot_rows, 0)
    R.CR[z, t] = R.CS[z]
    za[1].wait_recv()
    zs[1].wait_recv()
    got[2] = spread(2)
    za[2].wait_recv()
    zs[2].wait_recv()
    got[3] = spread(3)
    mu = [w.go(i_mu + k, R.up.at[pc.zto(k)], R.UE.at[z, c], pc.Z(k)) for k in (1, 2, 3)]
    md = [w.go(i_md + k, R.down.at[pc.zto(k)], R.DE.at[z, c], pc.Z(k)) for k in (1, 2, 3)]
    cz = [w.go(i_cz + k, R.CS.at[pc.zto(k)], R.CR.at[z, t], pc.Z(k)) for k in (1, 2, 3)]
    ends = [forward(k, got[k]) for k in range(4)]

    tok_x.wait_recv()

    def factors(rows):
        x = R.TK[rows].astype(F32)
        R.F1[rows] = lax.rsqrt(jnp.mean(x * x, axis=1, keepdims=True) + norm_eps)

    blocks(ROWS, 128, factors)
    for x, y, s in ends:
        s.wait_recv()
    parts = [R.SM[g].astype(F32)[:, 0:48] for g in range(16)]
    vecs = jnp.concatenate(parts, axis=1)
    R.VEC[...] = vecs
    R.RW[...] = jnp.concatenate([vecs, jnp.zeros((112, WIDE), F32)], axis=0).T.astype(BF)
    total = jnp.zeros((16, 128), F32)
    for g in range(16):
        total = total + R.SM[g].astype(F32)
    counts = jnp.sum(
        jnp.where(lane16 == 48, total, jnp.where(lane16 == 49, 256.0 * total, 0.0)),
        axis=1,
        keepdims=True,
    )
    share = jnp.sum(
        jnp.where(iota((16, 128), 0) - 8 == lane16 - 2, counts, 0.0), axis=0, keepdims=True
    ) * (1.0 / (16 * ROWS))
    R.SHARE[...] = jnp.broadcast_to(share, (8, 128))

    def norm_one(rows):
        x = R.TK[rows].astype(F32)
        R.NM[rows] = (x * R.F1[rows] * R.VEC[0:1]).astype(BF)

    blocks(ROWS, 128, norm_one)
    for x, y, s in ends:
        x.wait_recv()
        y.wait_recv()
    wo = w.go(i_wo, R.WA.at[:, :, 3], R.WO, pc.PAIR)

    def moe_spread(k):
        zz = pc.zfrom(k)
        u, d = R.UE.at[zz, c], R.DE.at[zz, c]
        return [
            w.copy(i_m[0] + k, u, u, pc.X),
            w.copy(i_m[1] + k, d, d, pc.Y),
            w.copy(i_m[2] + k, u, u, pc.Y),
            w.copy(i_m[3] + k, d, d, pc.X),
        ]

    def moe_forward(k):
        zz = pc.zfrom(k)
        u, d = R.UE.at[zz, pc.cx], R.DE.at[zz, pc.cy]
        return [
            w.copy(i_m[4] + k, u, u, pc.Y),
            w.copy(i_m[5] + k, d, d, pc.X),
        ]

    for m in moe_spread(0):
        m.start()

    def project(rows):
        x = R.NM[rows]
        for s, ref in enumerate((R.QS, R.KS, R.VS)):
            y = mm(x, R.WA[:, :, s].reshape(WIDE, HALF))
            if s == 0:
                y = y.astype(BF).astype(F32) * 0.125
            for p in range(3):
                ref[p, rows] = y[:, 128 * p : 128 * p + 128].astype(BF)

    blocks(ROWS, 256, project)
    prefix = R.pre[0]

    def pair_of_heads(p, carry):
        value_t = R.VS[p].astype(F32).T.astype(BF)
        even = iota((256, 128), 1) < 64
        for qb in range(4):
            cols = pl.ds(qb * 256, 256)
            outs = []
            for i in range(2):
                q = R.QS[p, cols]
                q = jnp.where(even if i == 0 else ~even, q.astype(F32), 0.0).astype(BF)
                pieces = []
                for k0, kn, masked in SEEN[qb]:
                    s = mm(R.KS[p, pl.ds(k0, kn)], q, 1, 1)
                    if masked:
                        s = jnp.where(visible(k0, kn, qb * 256, 256, prefix), s, masked_score)
                    pieces.append(s)
                top = pieces[0].max(axis=0, keepdims=True)
                for s in pieces[1:]:
                    top = jnp.maximum(top, s.max(axis=0, keepdims=True))
                total_e = jnp.zeros((1, 256), F32)
                out = jnp.zeros((128, 256), F32)
                for (k0, kn, _), s in zip(SEEN[qb], pieces):
                    e = jnp.exp(s - top)
                    total_e = total_e + e.sum(axis=0, keepdims=True)
                    out = out + mm(value_t[:, k0 : k0 + kn], e.astype(BF))
                R.LT[p, i : i + 1, cols] = top + jnp.log(total_e)
                outs.append(out / total_e)
            both = jnp.where(iota((128, 256), 0) < 64, outs[0], outs[1])
            R.ATO[cols, pl.ds(pl.multiple_of(p * 128, 128), 128)] = both.T.astype(BF)

        @pl.when(p < 3)
        def _():
            k = p + 1
            for ref, i0 in ((R.UE, i_mu), (R.DE, i_md)):
                w.copy(i0 + k, ref.at[z, c], ref.at[z, c], pc.Z(k)).wait_recv()
            for m in moe_spread(k):
                m.start()

        a = moe_spread(p)
        a[0].wait_recv()
        a[1].wait_recv()
        for m in moe_forward(p):
            m.start()
        return carry

    lax.fori_loop(0, 3, pair_of_heads, 0)
    att = w.go(i_att, R.ATO, R.ATX, pc.PAIR)
    a = moe_spread(3)
    a[0].wait_recv()
    a[1].wait_recv()
    for m in moe_forward(3):
        m.start()
    for m in cz:
        m.wait_recv()
    cp = w.go(i_cp, R.CR.at[:, t], R.CR.at[:, t], pc.PAIR)
    wo.wait_recv()
    att.wait_recv()
    lane = iota((256, 128), 1)
    real = (lane >= 2) & (lane < 6)
    R.PS[...] = jnp.zeros((8, 128), F32)

    def out_block(rows):
        b = mm(R.ATO[rows], R.WA[:, :, 3].reshape(WIDE, HALF), 1, 1)
        b = b + mm(R.ATX[rows], R.WO[...].reshape(WIDE, HALF), 1, 1)
        h = R.TK[rows].astype(F32) + b
        R.HIDN[rows] = h
        f2 = lax.rsqrt(jnp.mean(h * h, axis=1, keepdims=True) + norm_eps)
        R.F2[rows] = f2
        moe = (h * f2 * R.VEC[1:2]).astype(BF)
        R.MOE[rows] = moe
        logits = mm(moe, R.RW[...])
        mine = jnp.where((lane - 2).astype(F32) == R.PR[rows], logits, 0.0)
        picked = jnp.sum(jnp.where(real, mine, 0.0), axis=1, keepdims=True)
        R.GV[rows] = jax.nn.sigmoid(picked)
        lg = jnp.where(real, logits, masked_score)
        e = jnp.exp(lg - jnp.max(lg, axis=1, keepdims=True))
        e = jnp.where(real, e, 0.0)
        pr = e / jnp.sum(e, axis=1, keepdims=True)
        R.PR[rows] = pr
        R.PS[0:1] = R.PS[0:1] + jnp.sum(pr, axis=0, keepdims=True)

    blocks(ROWS, 256, out_block)

    def moe_rows(e, carry):
        R.CS[e] = mm(R.DM[pl.ds(pl.multiple_of(e * 128, 128), 128)], R.MOE[...]).astype(BF)
        return carry

    w.flush()
    lax.fori_loop(0, 4, moe_rows, 0)
    R.DR[z, t] = R.CS[z]
    dz = [w.go(i_dz + k, R.CS.at[pc.zto(k)], R.DR.at[z, t], pc.Z(k)) for k in (1, 2, 3)]
    for k in range(4):
        a = moe_spread(k)
        b = moe_forward(k)
        a[2].wait_recv()
        a[3].wait_recv()
        b[0].wait_recv()
        b[1].wait_recv()
        for m in a + b:
            m.wait_send()
    for m in dz:
        m.wait_recv()
    dp = w.go(i_dp, R.DR.at[:, t], R.DR.at[:, t], pc.PAIR)
    cp.wait_recv()
    dp.wait_recv()
    w.flush()


def gelu_parts(v):
    cdf = 0.5 * (1.0 + lax.erf(v * (1.0 / math.sqrt(2.0))))
    slope = cdf + v * (jnp.exp(-0.5 * v * v) * (1.0 / math.sqrt(2.0 * math.pi)))
    return v * cdf, slope


def phase_b(R, pc, w):
    f, t, z, c, o = pc.f, pc.t, pc.z, pc.c, pc.o
    i_xe, i_xg = w.ids(1), w.ids(1)
    i_rg, i_re, i_rgp, i_rep = w.ids(4), w.ids(4), w.ids(1), w.ids(1)
    i_u1, i_u2, i_d1, i_d2 = w.ids(2), w.ids(1), w.ids(2), w.ids(1)
    DR, CR = R.DR.reshape(ROWS, WIDE), R.CR.reshape(ROWS, WIDE)
    EO, GM = R.EO.reshape(ROWS, WIDE), R.GM.reshape(ROWS, WIDE)
    lane = iota((256, 128), 1)

    def gates(rows):
        logits = mm(DR[rows], R.RW[...])
        gate = jax.nn.sigmoid(
            jnp.sum(jnp.where(lane == 2 + z, logits, 0.0), axis=1, keepdims=True)
        )
        R.GATE[rows] = gate
        R.GC[rows] = (gate * CR[rows].astype(F32)).astype(BF)
        EO[rows] = jnp.zeros((256, WIDE), F32)
        GM[rows] = jnp.zeros((256, WIDE), F32)

    blocks(ROWS, 256, gates)

    def hidden_units(cols):
        up = R.UE[:, :, :, cols].reshape(WIDE, 512)
        down = R.DE[:, :, :, cols].reshape(WIDE, 512)

        def tokens_block(rows):
            act, slope = gelu_parts(mm(DR[rows], up))
            act = act.astype(BF)
            gb = (mm(R.GC[rows], down) * slope).astype(BF)
            R.ACT[rows] = act
            R.GB[rows] = gb
            EO[rows] += mm(act, down, 1, 1)
            GM[rows] += mm(gb, up, 1, 1)

        blocks(ROWS, 256, tokens_block)
        R.UE[:, :, :, cols] = mm(DR[...], R.GB[...], 0, 0).astype(BF).reshape(4, 4, 48, 512)
        R.DE[:, :, :, cols] = mm(R.GC[...], R.ACT[...], 0, 0).astype(BF).reshape(4, 4, 48, 512)

    blocks(HID, 512, hidden_units)

    def partials(e, carry):
        R.CS[e] = R.GM[e, o].astype(BF)
        R.ES[e] = R.EO[e, o].astype(BF)
        return carry

    lax.fori_loop(0, 4, partials, 0)
    xg = w.go(i_xg, R.CS, R.XG, pc.PAIR)
    xe = w.go(i_xe, R.ES, R.XE, pc.PAIR)
    R.moe_sums = [
        w.go(i_u1, R.UE.at[:, pc.cx], R.RU.at[0], pc.X),
        w.go(i_u1 + 1, R.UE.at[:, pc.cd], R.RU.at[1], pc.X),
        w.go(i_d1, R.DE.at[:, pc.cy], R.RD.at[0], pc.Y),
        w.go(i_d1 + 1, R.DE.at[:, pc.cd], R.RD.at[1], pc.Y),
    ]
    R.i_u2, R.i_d2 = i_u2, i_d2
    xg.wait()
    xe.wait()
    w.open = [m for m in w.open if m is not xg and m is not xe]
    row = jnp.sum(
        jnp.where(iota((16, WIDE), 0) == 2 + z, R.VEC[...], 0.0), axis=0, keepdims=True
    )
    R.RGR[...] = jnp.zeros((16, WIDE), F32)

    def finish(e, carry):
        eo = R.EO[e, t] + R.XE[e].astype(F32)
        gate = R.GATE.reshape(4, 2, 128, 1)[e, t]
        gate_grad = jnp.sum(R.CR[e, t].astype(F32) * eo, axis=1, keepdims=True)
        gs = gate_grad * gate * (1.0 - gate)
        R.RGR[0:1] += jnp.sum(gs * R.DR[e, t].astype(F32), axis=0, keepdims=True)
        R.CS[e] = (R.GM[e, t] + R.XG[e].astype(F32) + gs * row).astype(BF)
        R.ES[e] = eo.astype(BF)
        return carry

    lax.fori_loop(0, 4, finish, 0)
    R.RGR[...] = jnp.where(iota((16, WIDE), 0) == 2 + z, R.RGR[0:1], 0.0)
    rg = [w.go(i_rg + k, R.CS.at[pc.zto(k)], R.RG.at[z, t], pc.Z(k)) for k in (1, 2, 3)]
    re = [w.go(i_re + k, R.ES.at[pc.zto(k)], R.RE.at[z, t], pc.Z(k)) for k in (1, 2, 3)]
    R.RG[z, t] = R.CS[z]
    R.RE[z, t] = R.ES[z]
    for m in rg:
        m.wait_recv()
    w.go(i_rgp, R.RG.at[:, t], R.RG.at[:, t], pc.PAIR).wait_recv()
    R.expert_rows = (re, i_rep)


def combine(key, rows, got):
    n = key.shape[0]
    keys = jnp.concatenate([key] * 8, axis=1)
    pick = (keys == iota((n, ROWS), 1).astype(F32)).astype(F32).astype(BF)
    return mm(pick, got)


def phase_c(R, pc, w):
    f, t, z, c, o = pc.f, pc.t, pc.z, pc.c, pc.o
    i_uz, i_dz = w.ids(4), w.ids(4)
    i_a1, i_a2, i_b1, i_b2, i_az = w.ids(2), w.ids(1), w.ids(2), w.ids(1), w.ids(4)
    i_n = w.ids(1)
    i_sp, i_sc, i_sz = w.ids(1), w.ids(4), w.ids(4)
    own = pl.ds(pl.multiple_of(t * 512, 512), 512)
    other = pl.ds(pl.multiple_of(o * 512, 512), 512)
    GH, GN = R.GM.reshape(ROWS, WIDE), R.EO.reshape(ROWS, WIDE)
    RG, RE = R.RG.reshape(ROWS, WIDE), R.RE.reshape(ROWS, WIDE)
    GBR = R.GC
    share = R.SHARE[0:1]
    vec = R.VEC[...]
    head = iota((24, HALF), 0)
    head = jnp.where(lax.rem(head, 8) < 2, 2 * lax.div(head, 8) + lax.rem(head, 8), -1)
    pick_head = (head == lax.div(iota((24, HALF), 1), 64)).astype(F32).astype(BF)
    R.SB[...] = jnp.zeros((16, WIDE), F32)

    def residual(i, carry):
        rows = pl.ds(pl.multiple_of(i * 256, 256), 256)
        gm = combine(R.KC[rows], rows, RG[...])
        pr = R.PR[rows]
        mixed = jnp.sum(pr * share, axis=1, keepdims=True)
        aux = (balance_weight * 4.0 / (16 * ROWS)) * pr * (share - mixed)
        aux = aux[:, 0:16]
        gm = gm + mm(aux.astype(BF), vec.astype(BF))
        mine = jnp.where(lax.div(i, 2) == t, 1.0, 0.0)
        R.SB[...] += mine * mm(aux.astype(BF), R.MOE[rows], 0, 0)
        h, f2 = R.HIDN[rows], R.F2[rows]
        g = gm * vec[1:2]
        inner = jnp.mean(g * h, axis=1, keepdims=True)
        gh = R.CT[rows].astype(F32) + f2 * (g - h * (f2 * f2 * inner))
        R.G2[0:1] += mine * jnp.sum(gm * h * f2, axis=0, keepdims=True)
        GH[rows] = gh
        low = gh.astype(BF)
        GBR[rows] = low
        ga = mm(low, R.WA[:, :, 3].reshape(WIDE, HALF)).astype(BF)
        for p in range(3):
            R.GAP[p, rows] = ga[:, 128 * p : 128 * p + 128]
        prod = ga.astype(F32) * R.ATO[rows].astype(F32)
        top = prod.astype(BF)
        rest = (prod - top.astype(F32)).astype(BF)
        dd = mm(pick_head, top, 1, 1) + mm(pick_head, rest, 1, 1)
        for p in range(3):
            R.DD[p, :, rows] = dd[8 * p : 8 * p + 8]
        return carry

    R.G2[...] = jnp.zeros((8, WIDE), F32)
    lax.fori_loop(0, 4, residual, 0)
    part = jnp.where(iota((16, WIDE), 0) == 1, R.G2[0:1], 0.0)
    sums6 = jnp.concatenate([0.5 * R.PS[0:1], jnp.zeros((1, WIDE - 128), F32)], axis=1)
    keep = (iota((16, WIDE), 0) >= 2) & (iota((16, WIDE), 0) < 6)
    R.SB[...] = (
        jnp.where(keep, R.SB[...] + R.RGR[...], 0.0)
        + part
        + jnp.where(iota((16, WIDE), 0) == 6, sums6, 0.0)
    )
    R.AG[:, :, 3] = mm(GBR[...], R.ATO[...], 0, 0).astype(BF).reshape(4, 4, 48, HALF)
    prefix = R.pre[0]

    def pair_of_heads(p, carry):
        key_t = R.KS[p].astype(F32).T.astype(BF)
        R.DK[...] = jnp.zeros((ROWS, 128), F32)
        R.DV[...] = jnp.zeros((ROWS, 128), F32)
        even = iota((256, 128), 1) < 64
        for qb in range(4):
            cols = pl.ds(qb * 256, 256)
            outs = []
            for i in range(2):
                side = even if i == 0 else ~even
                q = jnp.where(side, R.QS[p, cols].astype(F32), 0.0).astype(BF)
                do = jnp.where(side, R.GAP[p, cols].astype(F32), 0.0).astype(BF)
                lt, dd = R.LT[p, i : i + 1, cols], R.DD[p, i : i + 1, cols]
                dq = jnp.zeros((128, 256), F32)
                for kb in range(max(2, qb + 1)):
                    keys = pl.ds(kb * 256, 256)
                    s = mm(R.KS[p, keys], q, 1, 1)
                    if kb == qb or qb < 2:
                        ok = visible(kb * 256, 256, qb * 256, 256, prefix)
                        s = jnp.where(ok, s, masked_score)
                    prob = jnp.exp(s - lt)
                    ds = prob * (mm(R.VS[p, keys], do, 1, 1) - dd)
                    ds = ds.astype(BF)
                    R.DV[keys] += mm(prob.astype(BF), do)
                    R.DK[keys] += mm(ds, q)
                    dq = dq + mm(key_t[:, kb * 256 : kb * 256 + 256], ds)
                outs.append(dq)
            both = jnp.where(iota((128, 256), 0) < 64, outs[0], outs[1])
            R.QS[p, cols] = (both * 0.125).T.astype(BF)
        R.KS[p] = R.DK[...].astype(BF)
        R.VS[p] = R.DV[...].astype(BF)
        mu, md = R.UE.at[:, c], R.DE.at[:, c]

        @pl.when(p == 0)
        def _():
            for m in R.moe_sums:
                m.wait_recv()
            for zz in range(4):
                R.UE[zz, c] = R.UE[zz, c] + R.RU[0, zz]
                R.UE[zz, pc.cy] = R.UE[zz, pc.cy] + R.RU[1, zz]
                R.DE[zz, c] = R.DE[zz, c] + R.RD[0, zz]
                R.DE[zz, pc.cx] = R.DE[zz, pc.cx] + R.RD[1, zz]
            w.copy(R.i_u2, R.UE.at[:, pc.cy], R.RU2, pc.Y).start()
            w.copy(R.i_d2, R.DE.at[:, pc.cx], R.RD2, pc.X).start()

        @pl.when(p == 1)
        def _():
            w.copy(R.i_u2, R.UE.at[:, pc.cy], R.RU2, pc.Y).wait()
            w.copy(R.i_d2, R.DE.at[:, pc.cx], R.RD2, pc.X).wait()
            for zz in range(4):
                R.UE[zz, c] = R.UE[zz, c] + R.RU2[zz]
                R.DE[zz, c] = R.DE[zz, c] + R.RD2[zz]
            for k in (1, 2, 3):
                w.copy(i_uz + k, R.UE.at[pc.zto(k), c], R.ZU.at[z], pc.Z(k)).start()
                w.copy(i_dz + k, R.DE.at[pc.zto(k), c], R.ZD.at[z], pc.Z(k)).start()

        return carry

    lax.fori_loop(0, 3, pair_of_heads, 0)
    GP = (R.QS, R.KS, R.VS)

    def grads(ref, rows):
        return jnp.concatenate([ref[p, rows] for p in range(3)], axis=1)

    def normed_grad(rows):
        acc = jnp.zeros((256, WIDE), F32)
        for s in range(3):
            acc = acc + mm(grads(GP[s], rows), R.WA[:, :, s].reshape(WIDE, HALF), 1, 1)
        GN[rows] = acc

    blocks(ROWS, 256, normed_grad)
    w.flush()
    XS, XN, BO = (r.reshape(512, WIDE) for r in (R.CS, R.XG, R.ES))
    XS[...] = GN[other].astype(BF)
    xn = w.go(i_n, XS, XN, pc.PAIR)
    every = pl.ds(0, ROWS)
    for s in range(3):
        R.AG[:, :, s] = mm(R.NM[...], grads(GP[s], every), 0, 0).astype(BF).reshape(4, 4, 48, HALF)
    a_half, b_half = pl.ds(0, 2), pl.ds(2, 2)
    a1 = [
        w.go(i_a1, R.AG.at[:, pc.cx, a_half], R.RA.at[0], pc.X),
        w.go(i_a1 + 1, R.AG.at[:, pc.cd, a_half], R.RA.at[1], pc.X),
    ]
    b1 = [
        w.go(i_b1, R.AG.at[:, pc.cy, b_half], R.RB.at[0], pc.Y),
        w.go(i_b1 + 1, R.AG.at[:, pc.cd, b_half], R.RB.at[1], pc.Y),
    ]
    xn.wait_recv()
    R.G2[...] = jnp.zeros((8, WIDE), F32)

    def input_grad(i, carry):
        rows = pl.ds(pl.multiple_of(i * 128, 128), 128)
        full = pl.ds(pl.multiple_of(t * 512 + i * 128, 128), 128)
        gn = GN[full] + XN[rows].astype(F32)
        x, f1 = R.TK[full].astype(F32), R.F1[full]
        g = gn * R.VEC[0:1]
        inner = jnp.mean(g * x, axis=1, keepdims=True)
        GH[full] = GH[full] + f1 * (g - x * (f1 * f1 * inner))
        R.G2[0:1] += jnp.sum(gn * x * f1, axis=0, keepdims=True)
        return carry

    lax.fori_loop(0, 4, input_grad, 0)
    out_t = pltpu.make_async_copy(GH.at[own], R.tokens_grad, R.ls.at[0])
    out_t.start()
    R.SB[0:1] = R.G2[0:1]
    sp = w.go(i_sp, R.SB, R.SP, pc.PAIR)
    for m in a1 + b1:
        m.wait_recv()
    for zz in range(4):
        R.AG[zz, c, a_half] = R.AG[zz, c, a_half] + R.RA[0, zz]
        R.AG[zz, pc.cy, a_half] = R.AG[zz, pc.cy, a_half] + R.RA[1, zz]
        R.AG[zz, c, b_half] = R.AG[zz, c, b_half] + R.RB[0, zz]
        R.AG[zz, pc.cx, b_half] = R.AG[zz, pc.cx, b_half] + R.RB[1, zz]
    a2 = w.go(i_a2, R.AG.at[:, pc.cy, a_half], R.RA2, pc.Y)
    b2 = w.go(i_b2, R.AG.at[:, pc.cx, b_half], R.RB2, pc.X)
    sp.wait_recv()
    me = R.SB[...] + R.SP[...]
    R.SC[c] = me
    sc = [
        w.go(i_sc, R.SC.at[c], R.SC.at[c], pc.X),
        w.go(i_sc + 1, R.SC.at[c], R.SC.at[c], pc.Y),
        w.go(i_sc + 2, R.SC.at[c], R.SC.at[c], pc.DIAG),
    ]
    re, i_rep = R.expert_rows
    for m in re:
        m.wait_recv()
    w.go(i_rep, R.RE.at[:, t], R.RE.at[:, t], pc.PAIR).wait_recv()

    def block_rows(i, carry):
        rows = pl.ds(pl.multiple_of(i * 256, 256), 256)
        full = pl.ds(pl.multiple_of(t * 512 + i * 256, 256), 256)
        eo = combine(R.KC[full], full, RE[...])
        BO[rows] = (R.HIDN[full] + R.GV[full] * eo).astype(BF)
        return carry

    lax.fori_loop(0, 2, block_rows, 0)
    out_b = pltpu.make_async_copy(BO, R.block_out, R.ls.at[1])
    out_b.start()
    a2.wait_recv()
    b2.wait_recv()
    for zz in range(4):
        R.AG[zz, c, a_half] = R.AG[zz, c, a_half] + R.RA2[zz]
        R.AG[zz, c, b_half] = R.AG[zz, c, b_half] + R.RB2[zz]
    az = [w.go(i_az + k, R.AG.at[pc.zto(k), c], R.ZA.at[z], pc.Z(k)) for k in (1, 2, 3)]
    for m in sc:
        m.wait_recv()
    R.SZ[z] = R.SC[0] + R.SC[1] + R.SC[2] + R.SC[3]
    sz = [w.go(i_sz + k, R.SZ.at[z], R.SZ.at[z], pc.Z(k)) for k in (1, 2, 3)]
    R.ZU[z] = R.UE[z, c]
    R.ZD[z] = R.DE[z, c]
    for k in (1, 2, 3):
        w.copy(i_uz + k, R.UE.at[pc.zto(k), c], R.ZU.at[z], pc.Z(k)).wait()
        w.copy(i_dz + k, R.DE.at[pc.zto(k), c], R.ZD.at[z], pc.Z(k)).wait()
    R.up_grad[...] = R.ZU[...].astype(F32)
    R.down_grad[...] = R.ZD[...].astype(F32)
    for m in sz:
        m.wait_recv()
    total = R.SZ[0] + R.SZ[1] + R.SZ[2] + R.SZ[3]
    probs = total[6:7, 0:128]
    R.balance[...] = (4.0 / (16 * ROWS)) * jnp.sum(share * probs, axis=1, keepdims=True)
    column = (iota((WIDE, 128), 0) == 48 * f + iota((WIDE, 128), 1)).astype(F32).astype(BF)
    mine = jnp.zeros((16, 128), F32)
    for _ in range(3):
        top = total.astype(BF)
        mine = mine + mm(top, column)
        total = total - top.astype(F32)
    R.gains_grad[...] = mine[0:2, 0:48]
    R.router_grad[...] = mine[2:6, 0:48]
    R.ZA[z] = R.AG[z, c]
    for m in az:
        m.wait_recv()
    summed = R.ZA[0].astype(F32)
    for zz in range(1, 4):
        summed = summed + R.ZA[zz].astype(F32)
    R.qkv_grad[...] = summed[0:3]
    R.out_grad[...] = summed[3]
    out_t.wait()
    out_b.wait()
    w.flush()


OUTS = {
    "block_out": ((512, WIDE), BF),
    "tokens_grad": ((512, WIDE), F32),
    "gains_grad": ((2, 48), F32),
    "qkv_grad": ((3, 48, HALF), F32),
    "out_grad": ((48, HALF), F32),
    "router_grad": ((4, 48), F32),
    "up_grad": ((4, 48, HID), F32),
    "down_grad": ((4, 48, HID), F32),
    "balance": ((1, 1), F32),
}
SCRATCH = {
    "TK": ((ROWS, WIDE), BF),
    "CT": ((ROWS, WIDE), BF),
    "WA": ((4, 4, 4, 48, HALF), BF),
    "WO": ((4, 4, 48, HALF), BF),
    "UE": ((4, 4, 48, HID), BF),
    "DE": ((4, 4, 48, HID), BF),
    "KC": ((ROWS, 128), F32),
    "CR": ((4, 2, 128, WIDE), BF),
    "DR": ((4, 2, 128, WIDE), BF),
    "F1": ((ROWS, 1), F32),
    "F2": ((ROWS, 1), F32),
    "VEC": ((16, WIDE), F32),
    "RW": ((WIDE, 128), BF),
    "SHARE": ((8, 128), F32),
    "NM": ((ROWS, WIDE), BF),
    "QS": ((3, ROWS, 128), BF),
    "KS": ((3, ROWS, 128), BF),
    "VS": ((3, ROWS, 128), BF),
    "LT": ((3, 8, ROWS), F32),
    "ATO": ((ROWS, HALF), BF),
    "ATX": ((ROWS, HALF), BF),
    "HIDN": ((ROWS, WIDE), F32),
    "MOE": ((ROWS, WIDE), BF),
    "GV": ((ROWS, 1), F32),
    "PR": ((ROWS, 128), F32),
    "PS": ((8, 128), F32),
    "SM": ((16, 16, 128), BF),
    "DM": ((512, ROWS), BF),
    "CS": ((4, 128, WIDE), BF),
    "ES": ((4, 128, WIDE), BF),
    "GATE": ((ROWS, 1), F32),
    "GC": ((ROWS, WIDE), BF),
    "EO": ((4, 2, 128, WIDE), F32),
    "GM": ((4, 2, 128, WIDE), F32),
    "ACT": ((ROWS, 512), BF),
    "GB": ((ROWS, 512), BF),
    "XE": ((4, 128, WIDE), BF),
    "XG": ((4, 128, WIDE), BF),
    "RG": ((4, 2, 128, WIDE), BF),
    "RE": ((4, 2, 128, WIDE), BF),
    "RGR": ((16, WIDE), F32),
    "RU": ((2, 4, 48, HID), BF),
    "RD": ((2, 4, 48, HID), BF),
    "RU2": ((4, 48, HID), BF),
    "RD2": ((4, 48, HID), BF),
    "ZU": ((4, 48, HID), BF),
    "ZD": ((4, 48, HID), BF),
    "GAP": ((3, ROWS, 128), BF),
    "DD": ((3, 8, ROWS), F32),
    "DK": ((ROWS, 128), F32),
    "DV": ((ROWS, 128), F32),
    "AG": ((4, 4, 4, 48, HALF), BF),
    "RA": ((2, 4, 2, 48, HALF), BF),
    "RB": ((2, 4, 2, 48, HALF), BF),
    "RA2": ((4, 2, 48, HALF), BF),
    "RB2": ((4, 2, 48, HALF), BF),
    "ZA": ((4, 4, 48, HALF), BF),
    "G2": ((8, WIDE), F32),
    "SB": ((16, WIDE), F32),
    "SP": ((16, WIDE), F32),
    "SC": ((4, 16, WIDE), F32),
    "SZ": ((4, 16, WIDE), F32),
}
INS = ("tok", "cot", "pre", "idr", "watt", "small", "up", "down")
IN_HBM = ("tok", "cot", "up", "down")
OUT_HBM = ("block_out", "tokens_grad")
SEMAPHORES = 160


def fused(args):
    names = INS + tuple(OUTS) + tuple(SCRATCH) + ("ss", "rs", "ls")

    def body(*refs):
        R = types.SimpleNamespace(**dict(zip(names, refs)))
        pc = Place()
        w = Wire(R.ss, R.rs)
        phase_a(R, pc, w)
        phase_b(R, pc, w)
        phase_c(R, pc, w)

    vm = pl.BlockSpec(memory_space=pltpu.VMEM)
    hbm = pl.BlockSpec(memory_space=pl.ANY)
    sm = pl.BlockSpec(memory_space=pltpu.SMEM)
    dma = pltpu.SemaphoreType.DMA
    return pl.pallas_call(
        body,
        out_shape=[jax.ShapeDtypeStruct(s, d) for s, d in OUTS.values()],
        in_specs=[sm if n == "pre" else hbm if n in IN_HBM else vm for n in INS],
        out_specs=[hbm if n in OUT_HBM else vm for n in OUTS],
        scratch_shapes=[pltpu.VMEM(s, d) for s, d in SCRATCH.values()]
        + [dma((SEMAPHORES,)), dma((SEMAPHORES,)), dma((4,))],
        compiler_params=pltpu.CompilerParams(
            collective_id=1, has_side_effects=True, vmem_limit_bytes=63 << 20
        ),
        name="block",
    )(*args)


def prepare(
    tokens, cotangent, prefix_len, expert_ids, norm_gains, qkv_weight, out_weight, router_weight, up_weight, down_weight
):
    watt = jnp.concatenate([qkv_weight, out_weight[None]], axis=0)
    small = jnp.pad(jnp.concatenate([norm_gains, router_weight], axis=0), ((0, 10), (0, 80)))
    return (tokens, cotangent, prefix_len, expert_ids.reshape(1, ROWS), watt, small, up_weight, down_weight)


def fast_device(*args):
    outs = fused(prepare(*args))
    return tuple(outs[:8]) + (outs[8].reshape(()),)


HEAD = 64
EXPERTS = 4
SEQ = 1024
CAP = 256


highest = lax.Precision.HIGHEST


def softmax_rows(scores):
    row_max = jnp.max(scores, axis=-1, keepdims=True)
    shifted = jnp.exp(scores - row_max)
    return shifted / jnp.sum(shifted, axis=-1, keepdims=True)


def slot_index(group_ids):
    onehot = (group_ids[:, None] == jnp.arange(EXPERTS, dtype=jnp.int32)[None, :]).astype(jnp.int32)
    rows = group_ids.shape[0]
    earlier = lax.broadcasted_iota(jnp.int32, (rows, rows), 1) <= lax.broadcasted_iota(
        jnp.int32, (rows, rows), 0
    )
    running = jnp.dot(
        earlier.astype(jnp.bfloat16),
        onehot.astype(jnp.bfloat16),
        preferred_element_type=jnp.float32,
    ).astype(jnp.int32)
    placed = jnp.sum(running * onehot, axis=1) - 1
    return jnp.where(placed < CAP, group_ids * CAP + placed, EXPERTS * CAP)


def rms_factor(values):
    return lax.rsqrt(jnp.mean(values * values, axis=-1, keepdims=True) + norm_eps)


def norm_back(grad_out, inputs, factor, gain):
    scaled = grad_out * gain
    row_inner = jnp.mean(scaled * inputs, axis=-1, keepdims=True)
    grad_in = factor * (scaled - inputs * factor * factor * row_inner)
    grad_gain = jnp.sum(grad_out * inputs * factor, axis=0)
    return (grad_in, grad_gain)


def gelu_slope(values):
    cumulative = 0.5 * (1.0 + lax.erf(values / math.sqrt(2.0)))
    density = jnp.exp(-0.5 * values * values) / math.sqrt(2.0 * math.pi)
    return cumulative + values * density


def block_scores(query_block, key_seq, offset, prefix, score_scale):
    scores = (
        jnp.einsum("qhd,khd->hqk", query_block, key_seq, preferred_element_type=jnp.float32)
        * score_scale
    )
    shape_pair = (query_block.shape[0], key_seq.shape[0])
    row_pos = offset + lax.broadcasted_iota(jnp.int32, shape_pair, 0)
    col_pos = lax.broadcasted_iota(jnp.int32, shape_pair, 1)
    allowed = (col_pos <= row_pos) | (col_pos < prefix)
    return jnp.where(allowed[None], scores, masked_score)


def attend(project, prefix_len, score_scale):
    group_rows = project.shape[0]
    full_width = project.shape[2]
    heads_here = full_width // HEAD
    block_rows = min(512, SEQ)
    shaped = project.reshape(group_rows, 3, heads_here, HEAD)
    query_all = shaped[:, 0]
    key_all = shaped[:, 1]
    value_all = shaped[:, 2]

    def one_block(number):
        row_start = number * block_rows
        seq_number = row_start // SEQ
        seq_start = seq_number * SEQ
        query_block = lax.dynamic_slice_in_dim(query_all, row_start, block_rows, 0)
        scores = block_scores(
            query_block, key_all, row_start - seq_start, prefix_len[seq_number], score_scale
        )
        row_max = jnp.max(scores, axis=-1, keepdims=True)
        shifted = jnp.exp(scores - row_max)
        row_total = jnp.sum(shifted, axis=-1, keepdims=True)
        prob_low = (shifted / row_total).astype(jnp.bfloat16)
        result = jnp.einsum("hqk,khd->qhd", prob_low, value_all, preferred_element_type=jnp.float32)
        return (
            result.reshape(block_rows, full_width).astype(jnp.bfloat16),
            (row_max + jnp.log(row_total))[..., 0],
        )

    outputs, log_total = lax.map(one_block, jnp.arange(group_rows // block_rows, dtype=jnp.int32))
    return (outputs.reshape(group_rows, full_width), log_total)


def attend_back(project, grad_att, log_total, prefix_len, score_scale):
    group_rows = project.shape[0]
    full_width = project.shape[2]
    heads_here = full_width // HEAD
    block_rows = min(512, SEQ)
    shaped = project.reshape(group_rows, 3, heads_here, HEAD)
    query_all = shaped[:, 0]
    key_all = shaped[:, 1]
    value_all = shaped[:, 2]
    grad_shaped = grad_att.reshape(group_rows, heads_here, HEAD)

    def one_block(carried, number):
        grad_keys, grad_values = carried
        row_start = number * block_rows
        seq_number = row_start // SEQ
        seq_start = seq_number * SEQ
        query_block = lax.dynamic_slice_in_dim(query_all, row_start, block_rows, 0)
        grad_block = lax.dynamic_slice_in_dim(grad_shaped, row_start, block_rows, 0)
        scores = block_scores(
            query_block, key_all, row_start - seq_start, prefix_len[seq_number], score_scale
        )
        prob_block = jnp.exp(scores - log_total[number][..., None])
        prob_low = prob_block.astype(jnp.bfloat16)
        grad_prob = jnp.einsum(
            "qhd,khd->hqk", grad_block, value_all, preferred_element_type=jnp.float32
        )
        value_part = jnp.einsum(
            "hqk,qhd->khd", prob_low, grad_block, preferred_element_type=jnp.float32
        )
        row_inner = jnp.sum(prob_block * grad_prob, axis=-1, keepdims=True)
        grad_scores = (prob_block * (grad_prob - row_inner)).astype(jnp.bfloat16)
        query_grad = (
            jnp.einsum("hqk,khd->qhd", grad_scores, key_all, preferred_element_type=jnp.float32)
            * score_scale
        )
        key_part = (
            jnp.einsum("hqk,qhd->khd", grad_scores, query_block, preferred_element_type=jnp.float32)
            * score_scale
        )
        old_keys = grad_keys
        grad_keys = old_keys + key_part
        old_values = grad_values
        grad_values = old_values + value_part
        return ((grad_keys, grad_values), query_grad)

    zero_rows = jnp.zeros((group_rows, heads_here, HEAD), jnp.float32)
    final, grad_query = lax.scan(
        one_block, (zero_rows, zero_rows), jnp.arange(group_rows // block_rows, dtype=jnp.int32)
    )
    grad_keys, grad_values = final
    stacked = jnp.stack(
        [
            grad_query.reshape(group_rows, full_width),
            grad_keys.reshape(group_rows, full_width),
            grad_values.reshape(group_rows, full_width),
        ],
        axis=1,
    )
    return stacked.astype(jnp.bfloat16)


def low_scatter(grad):
    return lax.psum_scatter(
        grad.astype(jnp.bfloat16), "fsdp", scatter_dimension=1, tiled=True
    ).astype(jnp.float32)


def per_device(
    tokens,
    cotangent,
    prefix_len,
    expert_ids,
    norm_gains,
    qkv_weight,
    out_weight,
    router_weight,
    up_weight,
    down_weight,
):
    tensor_size = lax.axis_size("tensor")
    fsdp_size = lax.axis_size("fsdp")
    own_rows = tokens.shape[0]
    group_rows = own_rows * tensor_size
    all_tokens = group_rows * fsdp_size
    own_start = lax.axis_index("tensor") * own_rows
    score_scale = 1.0 / math.sqrt(HEAD)
    gains_full, qkv_full, out_stack = (
        lax.all_gather(norm_gains, "fsdp", axis=1, tiled=True),
        lax.all_gather(qkv_weight, "fsdp", axis=1, tiled=True),
        lax.all_gather(out_weight[None], "fsdp", axis=1, tiled=True),
    )
    out_full = out_stack[0]
    router_full, up_full, down_full = (
        lax.all_gather(router_weight, "fsdp", axis=1, tiled=True),
        lax.all_gather(up_weight, "fsdp", axis=1, tiled=True),
        lax.all_gather(down_weight, "fsdp", axis=1, tiled=True),
    )
    inputs = lax.all_gather(tokens, "tensor", axis=0, tiled=True)
    input_float = inputs.astype(jnp.float32)
    factor_one = rms_factor(input_float)
    gain_one = gains_full[0].astype(jnp.float32)
    normed_one = (input_float * factor_one * gain_one).astype(jnp.bfloat16)
    project = jnp.einsum(
        "td,sdw->tsw", normed_one, qkv_full, preferred_element_type=jnp.float32
    ).astype(jnp.bfloat16)
    attended, log_total = attend(project, prefix_len, score_scale)
    branch = lax.psum_scatter(
        lax.dot_general(
            attended, out_full, (((1,), (1,)), ((), ())), preferred_element_type=jnp.float32
        ),
        "tensor",
        scatter_dimension=0,
        tiled=True,
    )
    hidden_own = tokens.astype(jnp.float32) + branch
    hidden_group = lax.all_gather(hidden_own, "tensor", axis=0, tiled=True)
    factor_two = rms_factor(hidden_group)
    gain_two = gains_full[1].astype(jnp.float32)
    moe_input = (hidden_group * factor_two * gain_two).astype(jnp.bfloat16)
    logits = lax.dot_general(
        moe_input, router_full, (((1,), (1,)), ((), ())), preferred_element_type=jnp.float32
    )
    group_ids = expert_ids[:, 0]
    onehot = (group_ids[:, None] == jnp.arange(EXPERTS, dtype=jnp.int32)[None, :]).astype(
        jnp.float32
    )
    gate_value = jax.nn.sigmoid(jnp.sum(logits * onehot, axis=-1))
    router_prob = softmax_rows(logits)
    counts, prob_sums = lax.psum((jnp.sum(onehot, axis=0), jnp.sum(router_prob, axis=0)), "fsdp")
    route_share = counts / all_tokens
    balance_loss = EXPERTS * jnp.sum(route_share * prob_sums) / all_tokens
    slot_rows = slot_index(group_ids)
    model_width = moe_input.shape[1]
    dispatched = (
        jnp.zeros((EXPERTS * CAP, model_width), jnp.bfloat16)
        .at[slot_rows]
        .set(moe_input, mode="drop")
        .reshape(EXPERTS, CAP, model_width)
    )
    before = jnp.einsum("ecd,edf->ecf", dispatched, up_full, preferred_element_type=jnp.float32)
    activated = jax.nn.gelu(before, approximate=False).astype(jnp.bfloat16)
    expert_out = jnp.einsum(
        "ecf,edf->ecd", activated, down_full, preferred_element_type=jnp.float32
    ).reshape(EXPERTS * CAP, model_width)
    combined_part = jnp.concatenate([expert_out, jnp.zeros((1, model_width), jnp.float32)], axis=0)[
        slot_rows
    ]
    combined = lax.psum_scatter(combined_part, "tensor", scatter_dimension=0, tiled=True)
    gate_own = lax.dynamic_slice_in_dim(gate_value, own_start, own_rows, 0)
    block_out = (hidden_own + gate_own[:, None] * combined).astype(jnp.bfloat16)
    gains_back, qkv_back, out_again, router_back, up_back, down_back = (
        lax.all_gather(norm_gains, "fsdp", axis=1, tiled=True),
        lax.all_gather(qkv_weight, "fsdp", axis=1, tiled=True),
        lax.all_gather(out_weight[None], "fsdp", axis=1, tiled=True),
        lax.all_gather(router_weight, "fsdp", axis=1, tiled=True),
        lax.all_gather(up_weight, "fsdp", axis=1, tiled=True),
        lax.all_gather(down_weight, "fsdp", axis=1, tiled=True),
    )
    out_back = out_again[0]
    cot_group = lax.all_gather(cotangent, "tensor", axis=0, tiled=True).astype(jnp.float32)
    grad_combined = (gate_value[:, None] * cot_group).astype(jnp.bfloat16)
    gate_grad_own = jnp.sum(cotangent.astype(jnp.float32) * combined, axis=-1)
    gate_grad_placed = lax.dynamic_update_slice_in_dim(
        jnp.zeros((group_rows,), jnp.float32), gate_grad_own, own_start, 0
    )
    grad_slots = (
        jnp.zeros((EXPERTS * CAP, model_width), jnp.bfloat16)
        .at[slot_rows]
        .set(grad_combined, mode="drop")
        .reshape(EXPERTS, CAP, model_width)
    )
    grad_activated = jnp.einsum(
        "ecd,edf->ecf", grad_slots, down_back, preferred_element_type=jnp.float32
    )
    down_grad = jnp.einsum(
        "ecd,ecf->edf", grad_slots, activated, preferred_element_type=jnp.float32
    )
    grad_before = (grad_activated * gelu_slope(before)).astype(jnp.bfloat16)
    up_grad = jnp.einsum(
        "ecd,ecf->edf", dispatched, grad_before, preferred_element_type=jnp.float32
    )
    grad_dispatched = jnp.einsum(
        "ecf,edf->ecd", grad_before, up_back, preferred_element_type=jnp.float32
    ).reshape(EXPERTS * CAP, model_width)
    grad_input_part = jnp.concatenate(
        [grad_dispatched, jnp.zeros((1, model_width), jnp.float32)], axis=0
    )[slot_rows]
    grad_moe, gate_grad = lax.psum((grad_input_part, gate_grad_placed), "tensor")
    gate_slope = gate_value * (1.0 - gate_value)
    mixed_share = jnp.sum(router_prob * route_share[None, :], axis=-1, keepdims=True)
    logit_grad = onehot * (gate_grad * gate_slope)[
        :, None
    ] + balance_weight * EXPERTS / all_tokens * router_prob * (route_share[None, :] - mixed_share)
    grad_norm_two = grad_moe + jnp.dot(
        logit_grad, router_back.astype(jnp.float32), precision=highest
    )
    router_grad = jnp.dot(logit_grad.T, moe_input.astype(jnp.float32), precision=highest)
    grad_hidden, gain_two_grad = norm_back(
        grad_norm_two, hidden_group, factor_two, gains_back[1].astype(jnp.float32)
    )
    grad_hidden = grad_hidden + cot_group
    grad_branch = grad_hidden.astype(jnp.bfloat16)
    grad_att = jnp.dot(grad_branch, out_back, preferred_element_type=jnp.float32).astype(
        jnp.bfloat16
    )
    out_grad = lax.dot_general(
        grad_branch, attended, (((0,), (0,)), ((), ())), preferred_element_type=jnp.float32
    )
    grad_project = attend_back(project, grad_att, log_total, prefix_len, score_scale)
    qkv_grad = jnp.einsum(
        "td,tsw->sdw", normed_one, grad_project, preferred_element_type=jnp.float32
    )
    grad_normed_part = jnp.einsum(
        "tsw,sdw->td", grad_project, qkv_back, preferred_element_type=jnp.float32
    )
    grad_normed = lax.psum(grad_normed_part, "tensor")
    grad_tokens, gain_one_grad = norm_back(
        grad_normed, input_float, factor_one, gains_back[0].astype(jnp.float32)
    )
    grad_tokens = grad_tokens + grad_hidden
    tokens_grad = lax.dynamic_slice_in_dim(grad_tokens, own_start, own_rows, 0)
    gains_own, qkv_own, out_own, router_own, up_own, down_own = (
        lax.psum_scatter(
            jnp.stack([gain_one_grad, gain_two_grad], axis=0),
            "fsdp",
            scatter_dimension=1,
            tiled=True,
        ),
        low_scatter(qkv_grad),
        low_scatter(out_grad[None]),
        lax.psum_scatter(router_grad, "fsdp", scatter_dimension=1, tiled=True),
        low_scatter(up_grad),
        low_scatter(down_grad),
    )
    return (
        block_out,
        tokens_grad,
        gains_own,
        qkv_own,
        out_own[0],
        router_own,
        up_own,
        down_own,
        balance_loss,
    )


def solution(mesh):
    placed = (
        P(("fsdp", "tensor"), None),
        P(("fsdp", "tensor"), None),
        P("fsdp"),
        P("fsdp", None),
        P(None, "fsdp"),
        P(None, "fsdp", "tensor"),
        P("fsdp", "tensor"),
        P(None, "fsdp"),
        P(None, "fsdp", "tensor"),
        P(None, "fsdp", "tensor"),
    )
    fits = mesh.shape["fsdp"] == 16 and mesh.shape["tensor"] == 2
    return jax.shard_map(
        fast_device if fits else per_device,
        mesh=mesh,
        in_specs=placed,
        out_specs=(
            P(("fsdp", "tensor"), None),
            P(("fsdp", "tensor"), None),
            P(None, "fsdp"),
            P(None, "fsdp", "tensor"),
            P("fsdp", "tensor"),
            P(None, "fsdp"),
            P(None, "fsdp", "tensor"),
            P(None, "fsdp", "tensor"),
            P(),
        ),
        check_vma=False,
    )
```

```python
import math
import types

import jax
import jax.numpy as jnp
from jax import lax
from jax.experimental import pallas as pl
from jax.experimental.pallas import tpu as pltpu
from jax.sharding import PartitionSpec as P

MESH = pl.DeviceIdType.MESH
BF = jnp.bfloat16
F32 = jnp.float32
ROWS = 1024
WIDE = 768
HALF = 384
HID = 1536
norm_eps = 1e-05
balance_weight = 0.01
masked_score = -1e30


def mm(a, b, ca=1, cb=0):
    return lax.dot_general(a, b, (((ca,), (cb,)), ((), ())), preferred_element_type=F32)


def iota(shape, axis):
    return lax.broadcasted_iota(jnp.int32, shape, axis)


def blocks(count, size, body):
    def step(i, carry):
        body(pl.ds(pl.multiple_of(i * size, size), size))
        return carry

    lax.fori_loop(0, count // size, step, 0)


class Place:
    def __init__(self):
        f, t = lax.axis_index("fsdp"), lax.axis_index("tensor")
        self.f, self.t, self.o = f, t, 1 - t
        self.z, self.c = lax.div(f, 4), lax.rem(f, 4)
        c = self.c
        self.cx = c + 1 - 2 * lax.rem(c, 2)
        self.cy = c + 2 - 4 * lax.div(c, 2)
        self.cd = 3 - c
        base = 4 * self.z
        self.X = {"fsdp": base + self.cx, "tensor": t}
        self.Y = {"fsdp": base + self.cy, "tensor": t}
        self.DIAG = {"fsdp": base + self.cd, "tensor": t}
        self.PAIR = {"fsdp": f, "tensor": 1 - t}

    def zto(self, k):
        return lax.rem(self.z + k, 4)

    def zfrom(self, k):
        return lax.rem(self.z + 4 - k, 4)

    def Z(self, k):
        return {"fsdp": 4 * self.zto(k) + self.c, "tensor": self.t}


class Wire:
    def __init__(self, send, recv):
        self.send, self.recv, self.n, self.open = send, recv, 0, []

    def ids(self, n):
        self.n += n
        return self.n - n

    def copy(self, i, src, dst, dev):
        return pltpu.make_async_remote_copy(
            src_ref=src,
            dst_ref=dst,
            send_sem=self.send.at[i],
            recv_sem=self.recv.at[i],
            device_id=dev,
            device_id_type=MESH,
        )

    def go(self, i, src, dst, dev):
        c = self.copy(i, src, dst, dev)
        c.start()
        self.open.append(c)
        return c

    def flush(self):
        for c in self.open:
            c.wait_send()
        self.open = []


def enter(pc):
    barrier = pltpu.get_barrier_semaphore()
    for dev in (pc.PAIR, pc.X, pc.Y, pc.DIAG, pc.Z(1), pc.Z(2), pc.Z(3)):
        pl.semaphore_signal(barrier, inc=1, device_id=dev, device_id_type=MESH)
    pl.semaphore_wait(barrier, 7)


def visible(krow0, kn, qcol0, qn, prefix):
    kpos = krow0 + iota((kn, qn), 0)
    qpos = qcol0 + iota((kn, qn), 1)
    ok = kpos <= qpos
    if krow0 < 512 and qcol0 < 512:
        ok = ok | (kpos < prefix)
    return ok


SEEN = (
    ((0, 512, True),),
    ((0, 512, True),),
    ((0, 512, False), (512, 256, True)),
    ((0, 512, False), (512, 256, False), (768, 256, True)),
)


def phase_a(R, pc, w):
    f, t, z, c = pc.f, pc.t, pc.z, pc.c
    idr = R.idr[...]
    ohr = (iota((16, ROWS), 0) - 8 == idr).astype(F32)
    cnt = jnp.sum(ohr, axis=1, keepdims=True)
    hi = jnp.floor(cnt * (1.0 / 256.0))
    lane16 = iota((16, 128), 1)
    six = jnp.concatenate(
        [R.gains[...].astype(F32), R.router[...].astype(F32), jnp.zeros((10, 48), F32)], axis=0
    )
    small = jnp.concatenate([six, jnp.zeros((16, 80), F32)], axis=1)
    R.SM[f] = jnp.where(
        lane16 == 48,
        cnt - 256.0 * hi,
        jnp.where(lane16 == 49, hi, small),
    ).astype(BF)
    R.WA[z, c, pl.ds(0, 3)] = R.qkv[...]
    R.WA[z, c, 3] = R.out[...]
    enter(pc)
    own = pl.ds(pl.multiple_of(t * 512, 512), 512)
    i_tok, i_cot, i_wo, i_att = w.ids(1), w.ids(1), w.ids(1), w.ids(1)
    i_z, i_sz = w.ids(4), w.ids(4)
    i_x, i_y, i_fx, i_fy, i_sx, i_sy, i_sf = (w.ids(4) for _ in range(7))
    i_mu, i_md = w.ids(4), w.ids(4)
    i_m = [w.ids(4) for _ in range(6)]
    i_cz, i_dz, i_cp, i_dp = w.ids(4), w.ids(4), w.ids(1), w.ids(1)

    zs = [w.go(i_sz + k, R.SM.at[f], R.SM.at[f], pc.Z(k)) for k in (1, 2, 3)]
    za = [w.go(i_z + k, R.WA.at[z, c], R.WA.at[z, c], pc.Z(k)) for k in (1, 2, 3)]
    cot_x = w.go(i_cot, R.cot, R.CT.at[own], pc.PAIR)
    tok_x = w.go(i_tok, R.tok, R.TK.at[own], pc.PAIR)

    def spread(k):
        zz = pc.zfrom(k)
        g = 4 * zz + c
        d = w.go(i_sx + k, R.SM.at[g], R.SM.at[g], pc.X)
        e = w.go(i_sy + k, R.SM.at[g], R.SM.at[g], pc.Y)
        a = w.go(i_x + k, R.WA.at[zz, c], R.WA.at[zz, c], pc.X)
        b = w.go(i_y + k, R.WA.at[zz, c], R.WA.at[zz, c], pc.Y)
        return a, b, d, e

    def forward(k, got):
        zz = pc.zfrom(k)
        a, b, d, e = got
        d.wait_recv()
        g = 4 * zz + pc.cx
        s = w.go(i_sf + k, R.SM.at[g], R.SM.at[g], pc.Y)
        a.wait_recv()
        x = w.go(
            i_fx + k,
            R.WA.at[zz, pc.cx, pl.ds(0, 2)],
            R.WA.at[zz, pc.cx, pl.ds(0, 2)],
            pc.Y,
        )
        b.wait_recv()
        y = w.go(
            i_fy + k,
            R.WA.at[zz, pc.cy, pl.ds(2, 2)],
            R.WA.at[zz, pc.cy, pl.ds(2, 2)],
            pc.X,
        )
        e.wait_recv()
        return x, y, s

    got = {0: spread(0)}
    local = [
        pltpu.make_async_copy(R.tok, R.TK.at[own], R.ls.at[0]),
        pltpu.make_async_copy(R.cot, R.CT.at[own], R.ls.at[1]),
        pltpu.make_async_copy(R.up.at[z], R.UE.at[z, c], R.ls.at[2]),
        pltpu.make_async_copy(R.down.at[z], R.DE.at[z, c], R.ls.at[3]),
    ]
    for m in local:
        m.start()
    before_or_at = (iota((ROWS, ROWS), 0) <= iota((ROWS, ROWS), 1)).astype(F32).astype(BF)
    running = mm(ohr.astype(BF), before_or_at)
    placed = jnp.sum(running * ohr, axis=0, keepdims=True) - 1.0
    key = jnp.where(placed < 256.0, idr.astype(F32) * 256.0 + placed, -1.0)
    R.KC[...] = jnp.broadcast_to(key, (128, ROWS)).T
    R.PR[...] = jnp.broadcast_to(idr.astype(F32), (128, ROWS)).T
    r = iota((512, ROWS), 0)
    want = lax.div(r, 128) * 256 + lax.rem(r, 128) + 128 * t
    R.DM[...] = (key.astype(jnp.int32) == want).astype(F32).astype(BF)

    za[0].wait_recv()
    zs[0].wait_recv()
    got[1] = spread(1)
    for m in local:
        m.wait()
    cot_x.wait_recv()

    def cot_rows(e, carry):
        R.CS[e] = mm(R.DM[pl.ds(pl.multiple_of(e * 128, 128), 128)], R.CT[...]).astype(BF)
        return carry

    lax.fori_loop(0, 4, cot_rows, 0)
    R.CR[z, t] = R.CS[z]
    za[1].wait_recv()
    zs[1].wait_recv()
    got[2] = spread(2)
    za[2].wait_recv()
    zs[2].wait_recv()
    got[3] = spread(3)
    mu = [w.go(i_mu + k, R.up.at[pc.zto(k)], R.UE.at[z, c], pc.Z(k)) for k in (1, 2, 3)]
    md = [w.go(i_md + k, R.down.at[pc.zto(k)], R.DE.at[z, c], pc.Z(k)) for k in (1, 2, 3)]
    cz = [w.go(i_cz + k, R.CS.at[pc.zto(k)], R.CR.at[z, t], pc.Z(k)) for k in (1, 2, 3)]
    ends = [forward(k, got[k]) for k in range(4)]

    tok_x.wait_recv()

    def factors(rows):
        x = R.TK[rows].astype(F32)
        R.F1[rows] = lax.rsqrt(jnp.mean(x * x, axis=1, keepdims=True) + norm_eps)

    blocks(ROWS, 128, factors)
    for x, y, s in ends:
        s.wait_recv()
    parts = [R.SM[g].astype(F32)[:, 0:48] for g in range(16)]
    vecs = jnp.concatenate(parts, axis=1)
    R.VEC[...] = vecs
    R.RW[...] = jnp.concatenate([vecs, jnp.zeros((112, WIDE), F32)], axis=0).T.astype(BF)
    total = jnp.zeros((16, 128), F32)
    for g in range(16):
        total = total + R.SM[g].astype(F32)
    counts = jnp.sum(
        jnp.where(lane16 == 48, total, jnp.where(lane16 == 49, 256.0 * total, 0.0)),
        axis=1,
        keepdims=True,
    )
    share = jnp.sum(
        jnp.where(iota((16, 128), 0) - 8 == lane16 - 2, counts, 0.0), axis=0, keepdims=True
    ) * (1.0 / (16 * ROWS))
    R.SHARE[...] = jnp.broadcast_to(share, (8, 128))

    def norm_one(rows):
        x = R.TK[rows].astype(F32)
        R.NM[rows] = (x * R.F1[rows] * R.VEC[0:1]).astype(BF)

    blocks(ROWS, 128, norm_one)
    for x, y, s in ends:
        x.wait_recv()
        y.wait_recv()
    wo = w.go(i_wo, R.WA.at[:, :, 3], R.WO, pc.PAIR)

    def moe_spread(k):
        zz = pc.zfrom(k)
        u, d = R.UE.at[zz, c], R.DE.at[zz, c]
        return [
            w.copy(i_m[0] + k, u, u, pc.X),
            w.copy(i_m[1] + k, d, d, pc.Y),
            w.copy(i_m[2] + k, u, u, pc.Y),
            w.copy(i_m[3] + k, d, d, pc.X),
        ]

    def moe_forward(k):
        zz = pc.zfrom(k)
        u, d = R.UE.at[zz, pc.cx], R.DE.at[zz, pc.cy]
        return [
            w.copy(i_m[4] + k, u, u, pc.Y),
            w.copy(i_m[5] + k, d, d, pc.X),
        ]

    for m in moe_spread(0):
        m.start()

    def project(rows):
        x = R.NM[rows]
        for s, ref in enumerate((R.QS, R.KS, R.VS)):
            y = mm(x, R.WA[:, :, s].reshape(WIDE, HALF))
            if s == 0:
                y = y.astype(BF).astype(F32) * 0.125
            for p in range(3):
                ref[p, rows] = y[:, 128 * p : 128 * p + 128].astype(BF)

    blocks(ROWS, 256, project)
    prefix = R.pre[0]

    def pair_of_heads(p, carry):
        value_t = R.VS[p].astype(F32).T.astype(BF)
        even = iota((256, 128), 1) < 64
        for qb in range(4):
            cols = pl.ds(qb * 256, 256)
            outs = []
            for i in range(2):
                q = R.QS[p, cols]
                q = jnp.where(even if i == 0 else ~even, q.astype(F32), 0.0).astype(BF)
                pieces = []
                for k0, kn, masked in SEEN[qb]:
                    s = mm(R.KS[p, pl.ds(k0, kn)], q, 1, 1)
                    if masked:
                        s = jnp.where(visible(k0, kn, qb * 256, 256, prefix), s, masked_score)
                    pieces.append(s)
                top = pieces[0].max(axis=0, keepdims=True)
                for s in pieces[1:]:
                    top = jnp.maximum(top, s.max(axis=0, keepdims=True))
                total_e = jnp.zeros((1, 256), F32)
                out = jnp.zeros((128, 256), F32)
                for (k0, kn, _), s in zip(SEEN[qb], pieces):
                    e = jnp.exp(s - top)
                    total_e = total_e + e.sum(axis=0, keepdims=True)
                    out = out + mm(value_t[:, k0 : k0 + kn], e.astype(BF))
                R.LT[p, i : i + 1, cols] = top + jnp.log(total_e)
                outs.append(out / total_e)
            both = jnp.where(iota((128, 256), 0) < 64, outs[0], outs[1])
            R.ATO[cols, pl.ds(pl.multiple_of(p * 128, 128), 128)] = both.T.astype(BF)

        @pl.when(p < 3)
        def _():
            k = p + 1
            for ref, i0 in ((R.UE, i_mu), (R.DE, i_md)):
                w.copy(i0 + k, ref.at[z, c], ref.at[z, c], pc.Z(k)).wait_recv()
            for m in moe_spread(k):
                m.start()

        a = moe_spread(p)
        a[0].wait_recv()
        a[1].wait_recv()
        for m in moe_forward(p):
            m.start()
        return carry

    lax.fori_loop(0, 3, pair_of_heads, 0)
    att = w.go(i_att, R.ATO, R.ATX, pc.PAIR)
    wo.wait_recv()
    att.wait_recv()
    lane = iota((256, 128), 1)
    real = (lane >= 2) & (lane < 6)
    R.PS[...] = jnp.zeros((8, 128), F32)

    def out_block(rows):
        b = mm(R.ATO[rows], R.WA[:, :, 3].reshape(WIDE, HALF), 1, 1)
        b = b + mm(R.ATX[rows], R.WO[...].reshape(WIDE, HALF), 1, 1)
        h = R.TK[rows].astype(F32) + b
        R.HIDN[rows] = h
        f2 = lax.rsqrt(jnp.mean(h * h, axis=1, keepdims=True) + norm_eps)
        R.F2[rows] = f2
        moe = (h * f2 * R.VEC[1:2]).astype(BF)
        R.MOE[rows] = moe
        logits = mm(moe, R.RW[...])
        mine = jnp.where((lane - 2).astype(F32) == R.PR[rows], logits, 0.0)
        picked = jnp.sum(jnp.where(real, mine, 0.0), axis=1, keepdims=True)
        R.GV[rows] = jax.nn.sigmoid(picked)
        lg = jnp.where(real, logits, masked_score)
        e = jnp.exp(lg - jnp.max(lg, axis=1, keepdims=True))
        e = jnp.where(real, e, 0.0)
        pr = e / jnp.sum(e, axis=1, keepdims=True)
        R.PR[rows] = pr
        R.PS[0:1] = R.PS[0:1] + jnp.sum(pr, axis=0, keepdims=True)

    blocks(ROWS, 256, out_block)

    def moe_rows(e, carry):
        R.CS[e] = mm(R.DM[pl.ds(pl.multiple_of(e * 128, 128), 128)], R.MOE[...]).astype(BF)
        return carry

    w.flush()
    lax.fori_loop(0, 4, moe_rows, 0)
    R.DR[z, t] = R.CS[z]
    dz = [w.go(i_dz + k, R.CS.at[pc.zto(k)], R.DR.at[z, t], pc.Z(k)) for k in (1, 2, 3)]
    a = moe_spread(3)
    a[0].wait_recv()
    a[1].wait_recv()
    for m in moe_forward(3):
        m.start()
    for m in cz:
        m.wait_recv()
    cp = w.go(i_cp, R.CR.at[:, t], R.CR.at[:, t], pc.PAIR)
    for k in range(4):
        a = moe_spread(k)
        b = moe_forward(k)
        a[2].wait_recv()
        a[3].wait_recv()
        b[0].wait_recv()
        b[1].wait_recv()
        for m in a + b:
            m.wait_send()
    for m in dz:
        m.wait_recv()
    dp = w.go(i_dp, R.DR.at[:, t], R.DR.at[:, t], pc.PAIR)
    cp.wait_recv()
    dp.wait_recv()
    w.flush()


def gelu_parts(v):
    cdf = 0.5 * (1.0 + lax.erf(v * (1.0 / math.sqrt(2.0))))
    slope = cdf + v * (jnp.exp(-0.5 * v * v) * (1.0 / math.sqrt(2.0 * math.pi)))
    return v * cdf, slope


class ExpertSums:
    def __init__(self, R, pc, w):
        self.R, self.pc, self.w = R, pc, w
        self.i1, self.i2, self.i3 = w.ids(8), w.ids(4), w.ids(16)

    def step_one(self, g):
        R, pc, w = self.R, self.pc, self.w
        cols, i = pl.ds(768 * g, 768), self.i1 + 4 * g
        return [
            w.copy(i, R.UE.at[:, pc.cx, :, cols], R.RU.at[0, :, :, cols], pc.X),
            w.copy(i + 1, R.UE.at[:, pc.cd, :, cols], R.RU.at[1, :, :, cols], pc.X),
            w.copy(i + 2, R.DE.at[:, pc.cy, :, cols], R.RD.at[0, :, :, cols], pc.Y),
            w.copy(i + 3, R.DE.at[:, pc.cd, :, cols], R.RD.at[1, :, :, cols], pc.Y),
        ]

    def step_two(self, g):
        R, pc, w = self.R, self.pc, self.w
        cols, i = pl.ds(768 * g, 768), self.i2 + 2 * g
        return [
            w.copy(i, R.UE.at[:, pc.cy, :, cols], R.RU2.at[:, :, cols], pc.Y),
            w.copy(i + 1, R.DE.at[:, pc.cx, :, cols], R.RD2.at[:, :, cols], pc.X),
        ]

    def step_three(self, g):
        R, pc, w = self.R, self.pc, self.w
        cols, i, out = pl.ds(768 * g, 768), self.i3 + 8 * g, []
        for k in (1, 2, 3):
            to, z = pc.zto(k), pc.z
            out.append(w.copy(i + k, R.UE.at[to, pc.c, :, cols], R.ZU.at[z, :, cols], pc.Z(k)))
            out.append(w.copy(i + 4 + k, R.DE.at[to, pc.c, :, cols], R.ZD.at[z, :, cols], pc.Z(k)))
        return out

    def one(self, g):
        for m in self.step_one(g):
            m.start()

    def two(self, g):
        R, pc, cols = self.R, self.pc, pl.ds(768 * g, 768)
        for m in self.step_one(g):
            m.wait()

        def add(zz, carry):
            R.UE[zz, pc.cy, :, cols] = R.UE[zz, pc.cy, :, cols] + R.RU[1, zz, :, cols]
            R.DE[zz, pc.cx, :, cols] = R.DE[zz, pc.cx, :, cols] + R.RD[1, zz, :, cols]
            R.UE[zz, pc.c, :, cols] = R.UE[zz, pc.c, :, cols] + R.RU[0, zz, :, cols]
            R.DE[zz, pc.c, :, cols] = R.DE[zz, pc.c, :, cols] + R.RD[0, zz, :, cols]
            return carry

        lax.fori_loop(0, 4, add, 0)
        for m in self.step_two(g):
            m.start()

    def three(self, g):
        R, pc, cols = self.R, self.pc, pl.ds(768 * g, 768)
        for m in self.step_two(g):
            m.wait()

        def add(zz, carry):
            R.UE[zz, pc.c, :, cols] = R.UE[zz, pc.c, :, cols] + R.RU2[zz, :, cols]
            R.DE[zz, pc.c, :, cols] = R.DE[zz, pc.c, :, cols] + R.RD2[zz, :, cols]
            return carry

        lax.fori_loop(0, 4, add, 0)
        for m in self.step_three(g):
            m.start()

    def last(self):
        R, pc = self.R, self.pc
        R.ZU[pc.z] = R.UE[pc.z, pc.c]
        R.ZD[pc.z] = R.DE[pc.z, pc.c]
        for g in (0, 1):
            for m in self.step_three(g):
                m.wait()
        R.up_grad[...] = R.ZU[...].astype(F32)
        R.down_grad[...] = R.ZD[...].astype(F32)


class AttentionSums:
    def __init__(self, R, pc, w):
        self.R, self.pc, self.w = R, pc, w
        self.i1, self.i2, self.i3 = w.ids(16), w.ids(8), w.ids(16)
        self.low, self.high = pl.ds(0, 2), pl.ds(2, 2)

    def step_one(self, n):
        R, pc, w, i = self.R, self.pc, self.w, self.i1 + 4 * n
        return [
            w.copy(i, R.AG.at[n, self.low, pc.cx], R.RA.at[n, 0], pc.X),
            w.copy(i + 1, R.AG.at[n, self.low, pc.cd], R.RA.at[n, 1], pc.X),
            w.copy(i + 2, R.AG.at[n, self.high, pc.cy], R.RB.at[n, 0], pc.Y),
            w.copy(i + 3, R.AG.at[n, self.high, pc.cd], R.RB.at[n, 1], pc.Y),
        ]

    def step_two(self, n):
        R, pc, w, i = self.R, self.pc, self.w, self.i2 + 2 * n
        return [
            w.copy(i, R.AG.at[n, self.low, pc.cy], R.RA2.at[n], pc.Y),
            w.copy(i + 1, R.AG.at[n, self.high, pc.cx], R.RB2.at[n], pc.X),
        ]

    def step_three(self, n):
        R, pc, w, i = self.R, self.pc, self.w, self.i3 + 4 * n
        return [
            w.copy(i + k, R.AG.at[n, pc.zto(k), pc.c], R.ZA.at[n, pc.z], pc.Z(k))
            for k in (1, 2, 3)
        ]

    def one(self, n):
        for m in self.step_one(n):
            m.start()

    def two(self, n):
        R, pc = self.R, self.pc
        for m in self.step_one(n):
            m.wait()
        for j in range(2):
            R.AG[n, j, pc.cy] = R.AG[n, j, pc.cy] + R.RA[n, 1, j]
            R.AG[n, 2 + j, pc.cx] = R.AG[n, 2 + j, pc.cx] + R.RB[n, 1, j]
            R.AG[n, j, pc.c] = R.AG[n, j, pc.c] + R.RA[n, 0, j]
            R.AG[n, 2 + j, pc.c] = R.AG[n, 2 + j, pc.c] + R.RB[n, 0, j]
        for m in self.step_two(n):
            m.start()

    def three(self, n):
        R, pc = self.R, self.pc
        for m in self.step_two(n):
            m.wait()
        for j in range(2):
            R.AG[n, j, pc.c] = R.AG[n, j, pc.c] + R.RA2[n, j]
            R.AG[n, 2 + j, pc.c] = R.AG[n, 2 + j, pc.c] + R.RB2[n, j]
        for m in self.step_three(n):
            m.start()

    def last(self, n):
        R, pc = self.R, self.pc
        R.ZA[n, pc.z] = R.AG[n, pc.z, pc.c]
        for m in self.step_three(n):
            m.wait()
        total = R.ZA[n, 0].astype(F32)
        for zz in range(1, 4):
            total = total + R.ZA[n, zz].astype(F32)
        for j in range(3):
            block = total[48 * j : 48 * j + 48]
            if n == 0:
                R.out_grad[:, 128 * j : 128 * j + 128] = block
            else:
                R.qkv_grad[j, :, 128 * (n - 1) : 128 * n] = block


def phase_b(R, pc, w):
    f, t, z, c, o = pc.f, pc.t, pc.z, pc.c, pc.o
    i_xe, i_xg = w.ids(1), w.ids(1)
    i_rg, i_re, i_rgp, i_rep = w.ids(4), w.ids(4), w.ids(1), w.ids(1)
    DR, CR = R.DR.reshape(ROWS, WIDE), R.CR.reshape(ROWS, WIDE)
    EO, GM = R.EO.reshape(ROWS, WIDE), R.GM.reshape(ROWS, WIDE)
    lane = iota((256, 128), 1)

    def gates(rows):
        logits = mm(DR[rows], R.RW[...])
        gate = jax.nn.sigmoid(
            jnp.sum(jnp.where(lane == 2 + z, logits, 0.0), axis=1, keepdims=True)
        )
        R.GATE[rows] = gate
        R.GC[rows] = (gate * CR[rows].astype(F32)).astype(BF)
        EO[rows] = jnp.zeros((256, WIDE), F32)
        GM[rows] = jnp.zeros((256, WIDE), F32)

    blocks(ROWS, 256, gates)

    def hidden_units(cols):
        up = R.UE[:, :, :, cols].reshape(WIDE, 512)
        down = R.DE[:, :, :, cols].reshape(WIDE, 512)

        def tokens_block(rows):
            act, slope = gelu_parts(mm(DR[rows], up))
            act = act.astype(BF)
            gb = (mm(R.GC[rows], down) * slope).astype(BF)
            R.ACT[rows] = act
            R.GB[rows] = gb
            EO[rows] += mm(act, down, 1, 1)
            GM[rows] += mm(gb, up, 1, 1)

        blocks(ROWS, 256, tokens_block)
        R.UE[:, :, :, cols] = mm(DR[...], R.GB[...], 0, 0).astype(BF).reshape(4, 4, 48, 512)
        R.DE[:, :, :, cols] = mm(R.GC[...], R.ACT[...], 0, 0).astype(BF).reshape(4, 4, 48, 512)

    blocks(HID, 512, hidden_units)

    def partials(e, carry):
        R.CS[e] = R.GM[e, o].astype(BF)
        R.ES[e] = R.EO[e, o].astype(BF)
        return carry

    lax.fori_loop(0, 4, partials, 0)
    xg = w.go(i_xg, R.CS, R.XG, pc.PAIR)
    xe = w.go(i_xe, R.ES, R.XE, pc.PAIR)
    sums = ExpertSums(R, pc, w)
    sums.one(0)
    sums.one(1)
    xg.wait()
    xe.wait()
    w.open = [m for m in w.open if m is not xg and m is not xe]
    row = jnp.sum(
        jnp.where(iota((16, WIDE), 0) == 2 + z, R.VEC[...], 0.0), axis=0, keepdims=True
    )
    R.RGR[...] = jnp.zeros((16, WIDE), F32)

    def finish(e, carry):
        eo = R.EO[e, t] + R.XE[e].astype(F32)
        gate = R.GATE.reshape(4, 2, 128, 1)[e, t]
        gate_grad = jnp.sum(R.CR[e, t].astype(F32) * eo, axis=1, keepdims=True)
        gs = gate_grad * gate * (1.0 - gate)
        R.RGR[0:1] += jnp.sum(gs * R.DR[e, t].astype(F32), axis=0, keepdims=True)
        R.CS[e] = (R.GM[e, t] + R.XG[e].astype(F32) + gs * row).astype(BF)
        R.ES[e] = eo.astype(BF)
        return carry

    lax.fori_loop(0, 4, finish, 0)
    R.RGR[...] = jnp.where(iota((16, WIDE), 0) == 2 + z, R.RGR[0:1], 0.0)
    rg = [w.go(i_rg + k, R.CS.at[pc.zto(k)], R.RG.at[z, t], pc.Z(k)) for k in (1, 2, 3)]
    R.RG[z, t] = R.CS[z]
    R.RE[z, t] = R.ES[z]
    for m in rg:
        m.wait_recv()
    back = w.go(i_rgp, R.RG.at[:, t], R.RG.at[:, t], pc.PAIR)
    re = [w.go(i_re + k, R.ES.at[pc.zto(k)], R.RE.at[z, t], pc.Z(k)) for k in (1, 2, 3)]
    back.wait_recv()
    sums.two(0)
    return sums, re, i_rep


def combine(key, rows, got):
    n = key.shape[0]
    keys = jnp.concatenate([key] * 8, axis=1)
    pick = (keys == iota((n, ROWS), 1).astype(F32)).astype(F32).astype(BF)
    return mm(pick, got)


def phase_c(R, pc, w, sums, re, i_rep):
    f, t, z, c, o = pc.f, pc.t, pc.z, pc.c, pc.o
    att = AttentionSums(R, pc, w)
    i_n = w.ids(1)
    i_sp, i_sc, i_sz = w.ids(1), w.ids(4), w.ids(4)
    own = pl.ds(pl.multiple_of(t * 512, 512), 512)
    other = pl.ds(pl.multiple_of(o * 512, 512), 512)
    GH, GN = R.GM.reshape(ROWS, WIDE), R.EO.reshape(ROWS, WIDE)
    RG, RE = R.RG.reshape(ROWS, WIDE), R.RE.reshape(ROWS, WIDE)
    GBR = R.GC
    share = R.SHARE[0:1]
    vec = R.VEC[...]
    head = iota((24, HALF), 0)
    head = jnp.where(lax.rem(head, 8) < 2, 2 * lax.div(head, 8) + lax.rem(head, 8), -1)
    pick_head = (head == lax.div(iota((24, HALF), 1), 64)).astype(F32).astype(BF)
    R.SB[...] = jnp.zeros((16, WIDE), F32)

    def residual(i, carry):
        rows = pl.ds(pl.multiple_of(i * 256, 256), 256)
        gm = combine(R.KC[rows], rows, RG[...])
        pr = R.PR[rows]
        mixed = jnp.sum(pr * share, axis=1, keepdims=True)
        aux = (balance_weight * 4.0 / (16 * ROWS)) * pr * (share - mixed)
        aux = aux[:, 0:16]
        gm = gm + mm(aux.astype(BF), vec.astype(BF))
        mine = jnp.where(lax.div(i, 2) == t, 1.0, 0.0)
        R.SB[...] += mine * mm(aux.astype(BF), R.MOE[rows], 0, 0)
        h, f2 = R.HIDN[rows], R.F2[rows]
        g = gm * vec[1:2]
        inner = jnp.mean(g * h, axis=1, keepdims=True)
        gh = R.CT[rows].astype(F32) + f2 * (g - h * (f2 * f2 * inner))
        R.G2[0:1] += mine * jnp.sum(gm * h * f2, axis=0, keepdims=True)
        GH[rows] = gh
        low = gh.astype(BF)
        GBR[rows] = low
        ga = mm(low, R.WA[:, :, 3].reshape(WIDE, HALF)).astype(BF)
        for p in range(3):
            R.GAP[p, rows] = ga[:, 128 * p : 128 * p + 128]
        prod = ga.astype(F32) * R.ATO[rows].astype(F32)
        top = prod.astype(BF)
        rest = (prod - top.astype(F32)).astype(BF)
        dd = mm(pick_head, top, 1, 1) + mm(pick_head, rest, 1, 1)
        for p in range(3):
            R.DD[p, :, rows] = dd[8 * p : 8 * p + 8]
        return carry

    R.G2[...] = jnp.zeros((8, WIDE), F32)
    lax.fori_loop(0, 4, residual, 0)
    part = jnp.where(iota((16, WIDE), 0) == 1, R.G2[0:1], 0.0)
    sums6 = jnp.concatenate([0.5 * R.PS[0:1], jnp.zeros((1, WIDE - 128), F32)], axis=1)
    keep = (iota((16, WIDE), 0) >= 2) & (iota((16, WIDE), 0) < 6)
    R.SB[...] = (
        jnp.where(keep, R.SB[...] + R.RGR[...], 0.0)
        + part
        + jnp.where(iota((16, WIDE), 0) == 6, sums6, 0.0)
    )

    def place(n, grad):
        for j in range(3):
            block = grad[:, 128 * j : 128 * j + 128].astype(BF).reshape(4, 4, 48, 128)
            R.AG[n, :, :, pl.ds(48 * j, 48)] = block

    place(0, mm(GBR[...], R.ATO[...], 0, 0))
    sums.two(1)
    att.one(0)
    prefix = R.pre[0]

    def pair_of_heads(p, carry):
        key_t = R.KS[p].astype(F32).T.astype(BF)
        R.DK[...] = jnp.zeros((ROWS, 128), F32)
        R.DV[...] = jnp.zeros((ROWS, 128), F32)
        even = iota((256, 128), 1) < 64
        for qb in range(4):
            cols = pl.ds(qb * 256, 256)
            outs = []
            for i in range(2):
                side = even if i == 0 else ~even
                q = jnp.where(side, R.QS[p, cols].astype(F32), 0.0).astype(BF)
                do = jnp.where(side, R.GAP[p, cols].astype(F32), 0.0).astype(BF)
                lt, dd = R.LT[p, i : i + 1, cols], R.DD[p, i : i + 1, cols]
                dq = jnp.zeros((128, 256), F32)
                for kb in range(max(2, qb + 1)):
                    keys = pl.ds(kb * 256, 256)
                    s = mm(R.KS[p, keys], q, 1, 1)
                    if kb == qb or qb < 2:
                        ok = visible(kb * 256, 256, qb * 256, 256, prefix)
                        s = jnp.where(ok, s, masked_score)
                    prob = jnp.exp(s - lt)
                    ds = prob * (mm(R.VS[p, keys], do, 1, 1) - dd)
                    ds = ds.astype(BF)
                    R.DV[keys] += mm(prob.astype(BF), do)
                    R.DK[keys] += mm(ds, q)
                    dq = dq + mm(key_t[:, kb * 256 : kb * 256 + 256], ds)
                outs.append(dq)
            both = jnp.where(iota((128, 256), 0) < 64, outs[0], outs[1])
            R.QS[p, cols] = (both * 0.125).T.astype(BF)
        R.KS[p] = R.DK[...].astype(BF)
        R.VS[p] = R.DV[...].astype(BF)
        joined = jnp.concatenate([R.QS[p], R.KS[p], R.VS[p]], axis=1)
        place(p + 1, mm(R.NM[...], joined, 0, 0))
        att.one(p + 1)

        @pl.when(p == 0)
        def _():
            sums.three(0)

        @pl.when(p == 1)
        def _():
            sums.three(1)
            att.two(0)

        @pl.when(p == 2)
        def _():
            att.three(0)
            att.two(1)

        return carry

    lax.fori_loop(0, 3, pair_of_heads, 0)
    GP = (R.QS, R.KS, R.VS)

    def grads(ref, rows):
        return jnp.concatenate([ref[p, rows] for p in range(3)], axis=1)

    def normed_grad(rows):
        acc = jnp.zeros((256, WIDE), F32)
        for s in range(3):
            acc = acc + mm(grads(GP[s], rows), R.WA[:, :, s].reshape(WIDE, HALF), 1, 1)
        GN[rows] = acc

    blocks(ROWS, 256, normed_grad)
    w.flush()
    XS, XN, BO = (r.reshape(512, WIDE) for r in (R.CS, R.XG, R.ES))
    XS[...] = GN[other].astype(BF)
    xn = w.go(i_n, XS, XN, pc.PAIR)
    att.two(2)
    att.three(1)
    xn.wait_recv()
    R.G2[...] = jnp.zeros((8, WIDE), F32)

    def input_grad(i, carry):
        rows = pl.ds(pl.multiple_of(i * 128, 128), 128)
        full = pl.ds(pl.multiple_of(t * 512 + i * 128, 128), 128)
        gn = GN[full] + XN[rows].astype(F32)
        x, f1 = R.TK[full].astype(F32), R.F1[full]
        g = gn * R.VEC[0:1]
        inner = jnp.mean(g * x, axis=1, keepdims=True)
        GH[full] = GH[full] + f1 * (g - x * (f1 * f1 * inner))
        R.G2[0:1] += jnp.sum(gn * x * f1, axis=0, keepdims=True)
        return carry

    lax.fori_loop(0, 4, input_grad, 0)
    out_t = pltpu.make_async_copy(GH.at[own], R.tokens_grad, R.ls.at[0])
    out_t.start()
    R.SB[0:1] = R.G2[0:1]
    sp = w.go(i_sp, R.SB, R.SP, pc.PAIR)
    att.two(3)
    att.three(2)
    sp.wait_recv()
    me = R.SB[...] + R.SP[...]
    R.SC[c] = me
    sc = [
        w.go(i_sc, R.SC.at[c], R.SC.at[c], pc.X),
        w.go(i_sc + 1, R.SC.at[c], R.SC.at[c], pc.Y),
        w.go(i_sc + 2, R.SC.at[c], R.SC.at[c], pc.DIAG),
    ]
    for m in re:
        m.wait_recv()
    w.go(i_rep, R.RE.at[:, t], R.RE.at[:, t], pc.PAIR).wait_recv()

    def block_rows(i, carry):
        rows = pl.ds(pl.multiple_of(i * 256, 256), 256)
        full = pl.ds(pl.multiple_of(t * 512 + i * 256, 256), 256)
        eo = combine(R.KC[full], full, RE[...])
        BO[rows] = (R.HIDN[full] + R.GV[full] * eo).astype(BF)
        return carry

    lax.fori_loop(0, 2, block_rows, 0)
    out_b = pltpu.make_async_copy(BO, R.block_out, R.ls.at[1])
    out_b.start()
    att.three(3)
    for m in sc:
        m.wait_recv()
    R.SZ[z] = R.SC[0] + R.SC[1] + R.SC[2] + R.SC[3]
    sz = [w.go(i_sz + k, R.SZ.at[z], R.SZ.at[z], pc.Z(k)) for k in (1, 2, 3)]
    sums.last()
    for n in range(3):
        att.last(n)
    for m in sz:
        m.wait_recv()
    total = R.SZ[0] + R.SZ[1] + R.SZ[2] + R.SZ[3]
    probs = total[6:7, 0:128]
    R.balance[...] = (4.0 / (16 * ROWS)) * jnp.sum(share * probs, axis=1, keepdims=True)
    column = (iota((WIDE, 128), 0) == 48 * f + iota((WIDE, 128), 1)).astype(F32).astype(BF)
    mine = jnp.zeros((16, 128), F32)
    for _ in range(3):
        top = total.astype(BF)
        mine = mine + mm(top, column)
        total = total - top.astype(F32)
    R.gains_grad[...] = mine[0:2, 0:48]
    R.router_grad[...] = mine[2:6, 0:48]
    att.last(3)
    out_t.wait()
    out_b.wait()
    w.flush()


OUTS = {
    "block_out": ((512, WIDE), BF),
    "tokens_grad": ((512, WIDE), F32),
    "gains_grad": ((2, 48), F32),
    "qkv_grad": ((3, 48, HALF), F32),
    "out_grad": ((48, HALF), F32),
    "router_grad": ((4, 48), F32),
    "up_grad": ((4, 48, HID), F32),
    "down_grad": ((4, 48, HID), F32),
    "balance": ((1, 1), F32),
}
SCRATCH = {
    "TK": ((ROWS, WIDE), BF),
    "CT": ((ROWS, WIDE), BF),
    "WA": ((4, 4, 4, 48, HALF), BF),
    "WO": ((4, 4, 48, HALF), BF),
    "UE": ((4, 4, 48, HID), BF),
    "DE": ((4, 4, 48, HID), BF),
    "KC": ((ROWS, 128), F32),
    "CR": ((4, 2, 128, WIDE), BF),
    "DR": ((4, 2, 128, WIDE), BF),
    "F1": ((ROWS, 1), F32),
    "F2": ((ROWS, 1), F32),
    "VEC": ((16, WIDE), F32),
    "RW": ((WIDE, 128), BF),
    "SHARE": ((8, 128), F32),
    "NM": ((ROWS, WIDE), BF),
    "QS": ((3, ROWS, 128), BF),
    "KS": ((3, ROWS, 128), BF),
    "VS": ((3, ROWS, 128), BF),
    "LT": ((3, 8, ROWS), F32),
    "ATO": ((ROWS, HALF), BF),
    "ATX": ((ROWS, HALF), BF),
    "HIDN": ((ROWS, WIDE), F32),
    "MOE": ((ROWS, WIDE), BF),
    "GV": ((ROWS, 1), F32),
    "PR": ((ROWS, 128), F32),
    "PS": ((8, 128), F32),
    "SM": ((16, 16, 128), BF),
    "DM": ((512, ROWS), BF),
    "CS": ((4, 128, WIDE), BF),
    "ES": ((4, 128, WIDE), BF),
    "GATE": ((ROWS, 1), F32),
    "GC": ((ROWS, WIDE), BF),
    "EO": ((4, 2, 128, WIDE), F32),
    "GM": ((4, 2, 128, WIDE), F32),
    "ACT": ((ROWS, 512), BF),
    "GB": ((ROWS, 512), BF),
    "XE": ((4, 128, WIDE), BF),
    "XG": ((4, 128, WIDE), BF),
    "RG": ((4, 2, 128, WIDE), BF),
    "RE": ((4, 2, 128, WIDE), BF),
    "RGR": ((16, WIDE), F32),
    "RU": ((2, 4, 48, HID), BF),
    "RD": ((2, 4, 48, HID), BF),
    "RU2": ((4, 48, HID), BF),
    "RD2": ((4, 48, HID), BF),
    "ZU": ((4, 48, HID), BF),
    "ZD": ((4, 48, HID), BF),
    "GAP": ((3, ROWS, 128), BF),
    "DD": ((3, 8, ROWS), F32),
    "DK": ((ROWS, 128), F32),
    "DV": ((ROWS, 128), F32),
    "AG": ((4, 4, 4, 144, 128), BF),
    "RA": ((4, 2, 2, 144, 128), BF),
    "RB": ((4, 2, 2, 144, 128), BF),
    "RA2": ((4, 2, 144, 128), BF),
    "RB2": ((4, 2, 144, 128), BF),
    "ZA": ((4, 4, 144, 128), BF),
    "G2": ((8, WIDE), F32),
    "SB": ((16, WIDE), F32),
    "SP": ((16, WIDE), F32),
    "SC": ((4, 16, WIDE), F32),
    "SZ": ((4, 16, WIDE), F32),
}
INS = ("tok", "cot", "pre", "idr", "gains", "qkv", "out", "router", "up", "down")
IN_HBM = ("tok", "cot", "up", "down")
OUT_HBM = ("block_out", "tokens_grad")
SEMAPHORES = 192


def fused(args):
    names = INS + tuple(OUTS) + tuple(SCRATCH) + ("ss", "rs", "ls")

    def body(*refs):
        R = types.SimpleNamespace(**dict(zip(names, refs)))
        pc = Place()
        w = Wire(R.ss, R.rs)
        phase_a(R, pc, w)
        sums, re, i_rep = phase_b(R, pc, w)
        phase_c(R, pc, w, sums, re, i_rep)

    vm = pl.BlockSpec(memory_space=pltpu.VMEM)
    hbm = pl.BlockSpec(memory_space=pl.ANY)
    sm = pl.BlockSpec(memory_space=pltpu.SMEM)
    dma = pltpu.SemaphoreType.DMA
    return pl.pallas_call(
        body,
        out_shape=[jax.ShapeDtypeStruct(s, d) for s, d in OUTS.values()],
        in_specs=[sm if n == "pre" else hbm if n in IN_HBM else vm for n in INS],
        out_specs=[hbm if n in OUT_HBM else vm for n in OUTS],
        scratch_shapes=[pltpu.VMEM(s, d) for s, d in SCRATCH.values()]
        + [dma((SEMAPHORES,)), dma((SEMAPHORES,)), dma((4,))],
        compiler_params=pltpu.CompilerParams(
            collective_id=1, has_side_effects=True, vmem_limit_bytes=63 << 20
        ),
        name="block",
    )(*args)


def prepare(
    tokens, cotangent, prefix_len, expert_ids, norm_gains, qkv_weight, out_weight, router_weight, up_weight, down_weight
):
    ids = expert_ids.reshape(1, ROWS)
    return (tokens, cotangent, prefix_len, ids, norm_gains, qkv_weight, out_weight, router_weight, up_weight, down_weight)


def fast_device(*args):
    outs = fused(prepare(*args))
    return tuple(outs[:8]) + (outs[8].reshape(()),)


HEAD = 64
EXPERTS = 4
SEQ = 1024
CAP = 256


highest = lax.Precision.HIGHEST


def softmax_rows(scores):
    row_max = jnp.max(scores, axis=-1, keepdims=True)
    shifted = jnp.exp(scores - row_max)
    return shifted / jnp.sum(shifted, axis=-1, keepdims=True)


def slot_index(group_ids):
    onehot = (group_ids[:, None] == jnp.arange(EXPERTS, dtype=jnp.int32)[None, :]).astype(jnp.int32)
    rows = group_ids.shape[0]
    earlier = lax.broadcasted_iota(jnp.int32, (rows, rows), 1) <= lax.broadcasted_iota(
        jnp.int32, (rows, rows), 0
    )
    running = jnp.dot(
        earlier.astype(jnp.bfloat16),
        onehot.astype(jnp.bfloat16),
        preferred_element_type=jnp.float32,
    ).astype(jnp.int32)
    placed = jnp.sum(running * onehot, axis=1) - 1
    return jnp.where(placed < CAP, group_ids * CAP + placed, EXPERTS * CAP)


def rms_factor(values):
    return lax.rsqrt(jnp.mean(values * values, axis=-1, keepdims=True) + norm_eps)


def norm_back(grad_out, inputs, factor, gain):
    scaled = grad_out * gain
    row_inner = jnp.mean(scaled * inputs, axis=-1, keepdims=True)
    grad_in = factor * (scaled - inputs * factor * factor * row_inner)
    grad_gain = jnp.sum(grad_out * inputs * factor, axis=0)
    return (grad_in, grad_gain)


def gelu_slope(values):
    cumulative = 0.5 * (1.0 + lax.erf(values / math.sqrt(2.0)))
    density = jnp.exp(-0.5 * values * values) / math.sqrt(2.0 * math.pi)
    return cumulative + values * density


def block_scores(query_block, key_seq, offset, prefix, score_scale):
    scores = (
        jnp.einsum("qhd,khd->hqk", query_block, key_seq, preferred_element_type=jnp.float32)
        * score_scale
    )
    shape_pair = (query_block.shape[0], key_seq.shape[0])
    row_pos = offset + lax.broadcasted_iota(jnp.int32, shape_pair, 0)
    col_pos = lax.broadcasted_iota(jnp.int32, shape_pair, 1)
    allowed = (col_pos <= row_pos) | (col_pos < prefix)
    return jnp.where(allowed[None], scores, masked_score)


def attend(project, prefix_len, score_scale):
    group_rows = project.shape[0]
    full_width = project.shape[2]
    heads_here = full_width // HEAD
    block_rows = min(512, SEQ)
    shaped = project.reshape(group_rows, 3, heads_here, HEAD)
    query_all = shaped[:, 0]
    key_all = shaped[:, 1]
    value_all = shaped[:, 2]

    def one_block(number):
        row_start = number * block_rows
        seq_number = row_start // SEQ
        seq_start = seq_number * SEQ
        query_block = lax.dynamic_slice_in_dim(query_all, row_start, block_rows, 0)
        scores = block_scores(
            query_block, key_all, row_start - seq_start, prefix_len[seq_number], score_scale
        )
        row_max = jnp.max(scores, axis=-1, keepdims=True)
        shifted = jnp.exp(scores - row_max)
        row_total = jnp.sum(shifted, axis=-1, keepdims=True)
        prob_low = (shifted / row_total).astype(jnp.bfloat16)
        result = jnp.einsum("hqk,khd->qhd", prob_low, value_all, preferred_element_type=jnp.float32)
        return (
            result.reshape(block_rows, full_width).astype(jnp.bfloat16),
            (row_max + jnp.log(row_total))[..., 0],
        )

    outputs, log_total = lax.map(one_block, jnp.arange(group_rows // block_rows, dtype=jnp.int32))
    return (outputs.reshape(group_rows, full_width), log_total)


def attend_back(project, grad_att, log_total, prefix_len, score_scale):
    group_rows = project.shape[0]
    full_width = project.shape[2]
    heads_here = full_width // HEAD
    block_rows = min(512, SEQ)
    shaped = project.reshape(group_rows, 3, heads_here, HEAD)
    query_all = shaped[:, 0]
    key_all = shaped[:, 1]
    value_all = shaped[:, 2]
    grad_shaped = grad_att.reshape(group_rows, heads_here, HEAD)

    def one_block(carried, number):
        grad_keys, grad_values = carried
        row_start = number * block_rows
        seq_number = row_start // SEQ
        seq_start = seq_number * SEQ
        query_block = lax.dynamic_slice_in_dim(query_all, row_start, block_rows, 0)
        grad_block = lax.dynamic_slice_in_dim(grad_shaped, row_start, block_rows, 0)
        scores = block_scores(
            query_block, key_all, row_start - seq_start, prefix_len[seq_number], score_scale
        )
        prob_block = jnp.exp(scores - log_total[number][..., None])
        prob_low = prob_block.astype(jnp.bfloat16)
        grad_prob = jnp.einsum(
            "qhd,khd->hqk", grad_block, value_all, preferred_element_type=jnp.float32
        )
        value_part = jnp.einsum(
            "hqk,qhd->khd", prob_low, grad_block, preferred_element_type=jnp.float32
        )
        row_inner = jnp.sum(prob_block * grad_prob, axis=-1, keepdims=True)
        grad_scores = (prob_block * (grad_prob - row_inner)).astype(jnp.bfloat16)
        query_grad = (
            jnp.einsum("hqk,khd->qhd", grad_scores, key_all, preferred_element_type=jnp.float32)
            * score_scale
        )
        key_part = (
            jnp.einsum("hqk,qhd->khd", grad_scores, query_block, preferred_element_type=jnp.float32)
            * score_scale
        )
        old_keys = grad_keys
        grad_keys = old_keys + key_part
        old_values = grad_values
        grad_values = old_values + value_part
        return ((grad_keys, grad_values), query_grad)

    zero_rows = jnp.zeros((group_rows, heads_here, HEAD), jnp.float32)
    final, grad_query = lax.scan(
        one_block, (zero_rows, zero_rows), jnp.arange(group_rows // block_rows, dtype=jnp.int32)
    )
    grad_keys, grad_values = final
    stacked = jnp.stack(
        [
            grad_query.reshape(group_rows, full_width),
            grad_keys.reshape(group_rows, full_width),
            grad_values.reshape(group_rows, full_width),
        ],
        axis=1,
    )
    return stacked.astype(jnp.bfloat16)


def low_scatter(grad):
    return lax.psum_scatter(
        grad.astype(jnp.bfloat16), "fsdp", scatter_dimension=1, tiled=True
    ).astype(jnp.float32)


def per_device(
    tokens,
    cotangent,
    prefix_len,
    expert_ids,
    norm_gains,
    qkv_weight,
    out_weight,
    router_weight,
    up_weight,
    down_weight,
):
    tensor_size = lax.axis_size("tensor")
    fsdp_size = lax.axis_size("fsdp")
    own_rows = tokens.shape[0]
    group_rows = own_rows * tensor_size
    all_tokens = group_rows * fsdp_size
    own_start = lax.axis_index("tensor") * own_rows
    score_scale = 1.0 / math.sqrt(HEAD)
    gains_full, qkv_full, out_stack = (
        lax.all_gather(norm_gains, "fsdp", axis=1, tiled=True),
        lax.all_gather(qkv_weight, "fsdp", axis=1, tiled=True),
        lax.all_gather(out_weight[None], "fsdp", axis=1, tiled=True),
    )
    out_full = out_stack[0]
    router_full, up_full, down_full = (
        lax.all_gather(router_weight, "fsdp", axis=1, tiled=True),
        lax.all_gather(up_weight, "fsdp", axis=1, tiled=True),
        lax.all_gather(down_weight, "fsdp", axis=1, tiled=True),
    )
    inputs = lax.all_gather(tokens, "tensor", axis=0, tiled=True)
    input_float = inputs.astype(jnp.float32)
    factor_one = rms_factor(input_float)
    gain_one = gains_full[0].astype(jnp.float32)
    normed_one = (input_float * factor_one * gain_one).astype(jnp.bfloat16)
    project = jnp.einsum(
        "td,sdw->tsw", normed_one, qkv_full, preferred_element_type=jnp.float32
    ).astype(jnp.bfloat16)
    attended, log_total = attend(project, prefix_len, score_scale)
    branch = lax.psum_scatter(
        lax.dot_general(
            attended, out_full, (((1,), (1,)), ((), ())), preferred_element_type=jnp.float32
        ),
        "tensor",
        scatter_dimension=0,
        tiled=True,
    )
    hidden_own = tokens.astype(jnp.float32) + branch
    hidden_group = lax.all_gather(hidden_own, "tensor", axis=0, tiled=True)
    factor_two = rms_factor(hidden_group)
    gain_two = gains_full[1].astype(jnp.float32)
    moe_input = (hidden_group * factor_two * gain_two).astype(jnp.bfloat16)
    logits = lax.dot_general(
        moe_input, router_full, (((1,), (1,)), ((), ())), preferred_element_type=jnp.float32
    )
    group_ids = expert_ids[:, 0]
    onehot = (group_ids[:, None] == jnp.arange(EXPERTS, dtype=jnp.int32)[None, :]).astype(
        jnp.float32
    )
    gate_value = jax.nn.sigmoid(jnp.sum(logits * onehot, axis=-1))
    router_prob = softmax_rows(logits)
    counts, prob_sums = lax.psum((jnp.sum(onehot, axis=0), jnp.sum(router_prob, axis=0)), "fsdp")
    route_share = counts / all_tokens
    balance_loss = EXPERTS * jnp.sum(route_share * prob_sums) / all_tokens
    slot_rows = slot_index(group_ids)
    model_width = moe_input.shape[1]
    dispatched = (
        jnp.zeros((EXPERTS * CAP, model_width), jnp.bfloat16)
        .at[slot_rows]
        .set(moe_input, mode="drop")
        .reshape(EXPERTS, CAP, model_width)
    )
    before = jnp.einsum("ecd,edf->ecf", dispatched, up_full, preferred_element_type=jnp.float32)
    activated = jax.nn.gelu(before, approximate=False).astype(jnp.bfloat16)
    expert_out = jnp.einsum(
        "ecf,edf->ecd", activated, down_full, preferred_element_type=jnp.float32
    ).reshape(EXPERTS * CAP, model_width)
    combined_part = jnp.concatenate([expert_out, jnp.zeros((1, model_width), jnp.float32)], axis=0)[
        slot_rows
    ]
    combined = lax.psum_scatter(combined_part, "tensor", scatter_dimension=0, tiled=True)
    gate_own = lax.dynamic_slice_in_dim(gate_value, own_start, own_rows, 0)
    block_out = (hidden_own + gate_own[:, None] * combined).astype(jnp.bfloat16)
    gains_back, qkv_back, out_again, router_back, up_back, down_back = (
        lax.all_gather(norm_gains, "fsdp", axis=1, tiled=True),
        lax.all_gather(qkv_weight, "fsdp", axis=1, tiled=True),
        lax.all_gather(out_weight[None], "fsdp", axis=1, tiled=True),
        lax.all_gather(router_weight, "fsdp", axis=1, tiled=True),
        lax.all_gather(up_weight, "fsdp", axis=1, tiled=True),
        lax.all_gather(down_weight, "fsdp", axis=1, tiled=True),
    )
    out_back = out_again[0]
    cot_group = lax.all_gather(cotangent, "tensor", axis=0, tiled=True).astype(jnp.float32)
    grad_combined = (gate_value[:, None] * cot_group).astype(jnp.bfloat16)
    gate_grad_own = jnp.sum(cotangent.astype(jnp.float32) * combined, axis=-1)
    gate_grad_placed = lax.dynamic_update_slice_in_dim(
        jnp.zeros((group_rows,), jnp.float32), gate_grad_own, own_start, 0
    )
    grad_slots = (
        jnp.zeros((EXPERTS * CAP, model_width), jnp.bfloat16)
        .at[slot_rows]
        .set(grad_combined, mode="drop")
        .reshape(EXPERTS, CAP, model_width)
    )
    grad_activated = jnp.einsum(
        "ecd,edf->ecf", grad_slots, down_back, preferred_element_type=jnp.float32
    )
    down_grad = jnp.einsum(
        "ecd,ecf->edf", grad_slots, activated, preferred_element_type=jnp.float32
    )
    grad_before = (grad_activated * gelu_slope(before)).astype(jnp.bfloat16)
    up_grad = jnp.einsum(
        "ecd,ecf->edf", dispatched, grad_before, preferred_element_type=jnp.float32
    )
    grad_dispatched = jnp.einsum(
        "ecf,edf->ecd", grad_before, up_back, preferred_element_type=jnp.float32
    ).reshape(EXPERTS * CAP, model_width)
    grad_input_part = jnp.concatenate(
        [grad_dispatched, jnp.zeros((1, model_width), jnp.float32)], axis=0
    )[slot_rows]
    grad_moe, gate_grad = lax.psum((grad_input_part, gate_grad_placed), "tensor")
    gate_slope = gate_value * (1.0 - gate_value)
    mixed_share = jnp.sum(router_prob * route_share[None, :], axis=-1, keepdims=True)
    logit_grad = onehot * (gate_grad * gate_slope)[
        :, None
    ] + balance_weight * EXPERTS / all_tokens * router_prob * (route_share[None, :] - mixed_share)
    grad_norm_two = grad_moe + jnp.dot(
        logit_grad, router_back.astype(jnp.float32), precision=highest
    )
    router_grad = jnp.dot(logit_grad.T, moe_input.astype(jnp.float32), precision=highest)
    grad_hidden, gain_two_grad = norm_back(
        grad_norm_two, hidden_group, factor_two, gains_back[1].astype(jnp.float32)
    )
    grad_hidden = grad_hidden + cot_group
    grad_branch = grad_hidden.astype(jnp.bfloat16)
    grad_att = jnp.dot(grad_branch, out_back, preferred_element_type=jnp.float32).astype(
        jnp.bfloat16
    )
    out_grad = lax.dot_general(
        grad_branch, attended, (((0,), (0,)), ((), ())), preferred_element_type=jnp.float32
    )
    grad_project = attend_back(project, grad_att, log_total, prefix_len, score_scale)
    qkv_grad = jnp.einsum(
        "td,tsw->sdw", normed_one, grad_project, preferred_element_type=jnp.float32
    )
    grad_normed_part = jnp.einsum(
        "tsw,sdw->td", grad_project, qkv_back, preferred_element_type=jnp.float32
    )
    grad_normed = lax.psum(grad_normed_part, "tensor")
    grad_tokens, gain_one_grad = norm_back(
        grad_normed, input_float, factor_one, gains_back[0].astype(jnp.float32)
    )
    grad_tokens = grad_tokens + grad_hidden
    tokens_grad = lax.dynamic_slice_in_dim(grad_tokens, own_start, own_rows, 0)
    gains_own, qkv_own, out_own, router_own, up_own, down_own = (
        lax.psum_scatter(
            jnp.stack([gain_one_grad, gain_two_grad], axis=0),
            "fsdp",
            scatter_dimension=1,
            tiled=True,
        ),
        low_scatter(qkv_grad),
        low_scatter(out_grad[None]),
        lax.psum_scatter(router_grad, "fsdp", scatter_dimension=1, tiled=True),
        low_scatter(up_grad),
        low_scatter(down_grad),
    )
    return (
        block_out,
        tokens_grad,
        gains_own,
        qkv_own,
        out_own[0],
        router_own,
        up_own,
        down_own,
        balance_loss,
    )


def solution(mesh):
    placed = (
        P(("fsdp", "tensor"), None),
        P(("fsdp", "tensor"), None),
        P("fsdp"),
        P("fsdp", None),
        P(None, "fsdp"),
        P(None, "fsdp", "tensor"),
        P("fsdp", "tensor"),
        P(None, "fsdp"),
        P(None, "fsdp", "tensor"),
        P(None, "fsdp", "tensor"),
    )
    fits = mesh.shape["fsdp"] == 16 and mesh.shape["tensor"] == 2
    return jax.shard_map(
        fast_device if fits else per_device,
        mesh=mesh,
        in_specs=placed,
        out_specs=(
            P(("fsdp", "tensor"), None),
            P(("fsdp", "tensor"), None),
            P(None, "fsdp"),
            P(None, "fsdp", "tensor"),
            P("fsdp", "tensor"),
            P(None, "fsdp"),
            P(None, "fsdp", "tensor"),
            P(None, "fsdp", "tensor"),
            P(),
        ),
        check_vma=False,
    )
```

```python
import math
import types

import jax
import jax.numpy as jnp
from jax import lax
from jax.experimental import pallas as pl
from jax.experimental.pallas import tpu as pltpu
from jax.sharding import PartitionSpec as P

MESH = pl.DeviceIdType.MESH
BF = jnp.bfloat16
F32 = jnp.float32
ROWS = 1024
WIDE = 768
HALF = 384
HID = 1536
norm_eps = 1e-05
balance_weight = 0.01
masked_score = -1e30


def mm(a, b, ca=1, cb=0):
    return lax.dot_general(a, b, (((ca,), (cb,)), ((), ())), preferred_element_type=F32)


def iota(shape, axis):
    return lax.broadcasted_iota(jnp.int32, shape, axis)


def blocks(count, size, body):
    def step(i, carry):
        body(pl.ds(pl.multiple_of(i * size, size), size))
        return carry

    lax.fori_loop(0, count // size, step, 0)


class Place:
    def __init__(self):
        f, t = lax.axis_index("fsdp"), lax.axis_index("tensor")
        self.f, self.t, self.o = f, t, 1 - t
        self.z, self.c = lax.div(f, 4), lax.rem(f, 4)
        c = self.c
        self.cx = c + 1 - 2 * lax.rem(c, 2)
        self.cy = c + 2 - 4 * lax.div(c, 2)
        self.cd = 3 - c
        base = 4 * self.z
        self.X = {"fsdp": base + self.cx, "tensor": t}
        self.Y = {"fsdp": base + self.cy, "tensor": t}
        self.DIAG = {"fsdp": base + self.cd, "tensor": t}
        self.PAIR = {"fsdp": f, "tensor": 1 - t}

    def zto(self, k):
        return lax.rem(self.z + k, 4)

    def zfrom(self, k):
        return lax.rem(self.z + 4 - k, 4)

    def Z(self, k):
        return {"fsdp": 4 * self.zto(k) + self.c, "tensor": self.t}


class Wire:
    def __init__(self, send, recv):
        self.send, self.recv, self.n, self.open = send, recv, 0, []

    def ids(self, n):
        self.n += n
        return self.n - n

    def copy(self, i, src, dst, dev):
        return pltpu.make_async_remote_copy(
            src_ref=src,
            dst_ref=dst,
            send_sem=self.send.at[i],
            recv_sem=self.recv.at[i],
            device_id=dev,
            device_id_type=MESH,
        )

    def go(self, i, src, dst, dev):
        c = self.copy(i, src, dst, dev)
        c.start()
        self.open.append(c)
        return c

    def flush(self):
        for c in self.open:
            c.wait_send()
        self.open = []


def joined(ref, rows):
    return jnp.concatenate([ref[p, rows] for p in range(3)], axis=1)


def enter(pc):
    barrier = pltpu.get_barrier_semaphore()
    for dev in (pc.PAIR, pc.X, pc.Y, pc.DIAG, pc.Z(1), pc.Z(2), pc.Z(3)):
        pl.semaphore_signal(barrier, inc=1, device_id=dev, device_id_type=MESH)
    pl.semaphore_wait(barrier, 7)


def order(i):
    return i + lax.div(i, 2) * (5 - 2 * i)


def visible(krow0, kn, qcol0, qn, prefix):
    kpos = krow0 + iota((kn, qn), 0)
    qpos = qcol0 + iota((kn, qn), 1)
    ok = kpos <= qpos
    if krow0 < 512 and qcol0 < 512:
        ok = ok | (kpos < prefix)
    return ok


SEEN = (
    ((0, 512, True),),
    ((0, 512, True),),
    ((0, 512, False), (512, 256, True)),
    ((0, 512, False), (512, 256, False), (768, 256, True)),
)


def phase_a(R, pc, w):
    f, t, z, c = pc.f, pc.t, pc.z, pc.c
    idr = R.idr[...]
    ohr = (iota((16, ROWS), 0) - 8 == idr).astype(F32)
    cnt = jnp.sum(ohr, axis=1, keepdims=True)
    hi = jnp.floor(cnt * (1.0 / 256.0))
    lane16 = iota((16, 128), 1)
    six = jnp.concatenate(
        [R.gains[...].astype(F32), R.router[...].astype(F32), jnp.zeros((10, 48), F32)], axis=0
    )
    small = jnp.concatenate([six, jnp.zeros((16, 80), F32)], axis=1)
    R.SM[f] = jnp.where(
        lane16 == 48,
        cnt - 256.0 * hi,
        jnp.where(lane16 == 49, hi, small),
    ).astype(BF)
    R.WA[z, c, pl.ds(0, 3)] = R.qkv[...]
    R.WA[z, c, 3] = R.out[...]
    enter(pc)
    own = pl.ds(pl.multiple_of(t * 512, 512), 512)
    i_tok, i_cot, i_wo, i_att = w.ids(1), w.ids(1), w.ids(1), w.ids(3)
    i_z, i_sz = w.ids(4), w.ids(4)
    i_x, i_y, i_fx, i_fy, i_sx, i_sy, i_sf = (w.ids(4) for _ in range(7))
    i_mu, i_md = w.ids(4), w.ids(4)
    i_m = [w.ids(4) for _ in range(6)]
    i_cz, i_dz, i_cp, i_dp = w.ids(4), w.ids(4), w.ids(1), w.ids(4)

    zs = [w.go(i_sz + k, R.SM.at[f], R.SM.at[f], pc.Z(k)) for k in (1, 2, 3)]
    za = [w.go(i_z + k, R.WA.at[z, c], R.WA.at[z, c], pc.Z(k)) for k in (1, 2, 3)]
    cot_x = w.go(i_cot, R.cot, R.CT.at[own], pc.PAIR)
    tok_x = w.go(i_tok, R.tok, R.TK.at[own], pc.PAIR)

    def spread(k):
        zz = pc.zfrom(k)
        g = 4 * zz + c
        d = w.go(i_sx + k, R.SM.at[g], R.SM.at[g], pc.X)
        e = w.go(i_sy + k, R.SM.at[g], R.SM.at[g], pc.Y)
        a = w.go(i_x + k, R.WA.at[zz, c], R.WA.at[zz, c], pc.X)
        b = w.go(i_y + k, R.WA.at[zz, c], R.WA.at[zz, c], pc.Y)
        return a, b, d, e

    def forward(k, got):
        zz = pc.zfrom(k)
        a, b, d, e = got
        d.wait_recv()
        g = 4 * zz + pc.cx
        s = w.go(i_sf + k, R.SM.at[g], R.SM.at[g], pc.Y)
        a.wait_recv()
        x = w.go(
            i_fx + k,
            R.WA.at[zz, pc.cx, pl.ds(0, 2)],
            R.WA.at[zz, pc.cx, pl.ds(0, 2)],
            pc.Y,
        )
        b.wait_recv()
        y = w.go(
            i_fy + k,
            R.WA.at[zz, pc.cy, pl.ds(2, 2)],
            R.WA.at[zz, pc.cy, pl.ds(2, 2)],
            pc.X,
        )
        e.wait_recv()
        return x, y, s

    got = {0: spread(0)}
    local = [
        pltpu.make_async_copy(R.tok, R.TK.at[own], R.ls.at[0]),
        pltpu.make_async_copy(R.cot, R.CT.at[own], R.ls.at[1]),
        pltpu.make_async_copy(R.up.at[z], R.UE.at[z, c], R.ls.at[2]),
        pltpu.make_async_copy(R.down.at[z], R.DE.at[z, c], R.ls.at[3]),
    ]
    for m in local:
        m.start()
    before_or_at = (iota((ROWS, ROWS), 0) <= iota((ROWS, ROWS), 1)).astype(F32).astype(BF)
    running = mm(ohr.astype(BF), before_or_at)
    placed = jnp.sum(running * ohr, axis=0, keepdims=True) - 1.0
    key = jnp.where(placed < 256.0, idr.astype(F32) * 256.0 + placed, -1.0)
    R.KC[...] = jnp.broadcast_to(key, (128, ROWS)).T
    R.PR[...] = jnp.broadcast_to(idr.astype(F32), (128, ROWS)).T
    r = iota((512, ROWS), 0)
    want = lax.div(r, 128) * 256 + lax.rem(r, 128) + 128 * t
    R.DM[...] = (key.astype(jnp.int32) == want).astype(F32).astype(BF)

    za[0].wait_recv()
    zs[0].wait_recv()
    got[1] = spread(1)
    for m in local:
        m.wait()
    cot_x.wait_recv()

    def cot_rows(e, carry):
        R.PG[e] = mm(R.DM[pl.ds(pl.multiple_of(e * 128, 128), 128)], R.CT[...]).astype(BF)
        return carry

    lax.fori_loop(0, 4, cot_rows, 0)
    R.CR[z, t] = R.PG[z]
    za[1].wait_recv()
    zs[1].wait_recv()
    got[2] = spread(2)
    za[2].wait_recv()
    zs[2].wait_recv()
    got[3] = spread(3)
    mu = [w.go(i_mu + k, R.up.at[pc.zto(k)], R.UE.at[z, c], pc.Z(k)) for k in (1, 2, 3)]
    md = [w.go(i_md + k, R.down.at[pc.zto(k)], R.DE.at[z, c], pc.Z(k)) for k in (1, 2, 3)]
    cz = [w.go(i_cz + k, R.PG.at[pc.zto(k)], R.CR.at[z, t], pc.Z(k)) for k in (1, 2, 3)]
    ends = [forward(k, got[k]) for k in range(4)]

    tok_x.wait_recv()

    def factors(rows):
        x = R.TK[rows].astype(F32)
        R.STAT[rows, 0:1] = lax.rsqrt(jnp.mean(x * x, axis=1, keepdims=True) + norm_eps)

    blocks(ROWS, 128, factors)
    for x, y, s in ends:
        s.wait_recv()
    parts = [R.SM[g].astype(F32)[:, 0:48] for g in range(16)]
    vecs = jnp.concatenate(parts, axis=1)
    R.VEC[...] = vecs
    R.RW[...] = jnp.concatenate([vecs, jnp.zeros((112, WIDE), F32)], axis=0).T.astype(BF)
    total = jnp.zeros((16, 128), F32)
    for g in range(16):
        total = total + R.SM[g].astype(F32)
    counts = jnp.sum(
        jnp.where(lane16 == 48, total, jnp.where(lane16 == 49, 256.0 * total, 0.0)),
        axis=1,
        keepdims=True,
    )
    share = jnp.sum(
        jnp.where(iota((16, 128), 0) - 8 == lane16 - 2, counts, 0.0), axis=0, keepdims=True
    ) * (1.0 / (16 * ROWS))
    R.SHARE[...] = jnp.broadcast_to(share, (8, 128))

    def norm_one(rows):
        x = R.TK[rows].astype(F32)
        R.NM[rows] = (x * R.STAT[rows, 0:1] * R.VEC[0:1]).astype(BF)

    blocks(ROWS, 128, norm_one)
    for x, y, s in ends:
        x.wait_recv()
        y.wait_recv()
    wo = w.go(i_wo, R.WA.at[:, :, 3], R.WO, pc.PAIR)

    def moe_spread(k):
        zz = pc.zfrom(k)
        u, d = R.UE.at[zz, c], R.DE.at[zz, c]
        return [
            w.copy(i_m[0] + k, u, u, pc.X),
            w.copy(i_m[1] + k, d, d, pc.Y),
            w.copy(i_m[2] + k, u, u, pc.Y),
            w.copy(i_m[3] + k, d, d, pc.X),
        ]

    def moe_forward(k):
        zz = pc.zfrom(k)
        u, d = R.UE.at[zz, pc.cx], R.DE.at[zz, pc.cy]
        return [
            w.copy(i_m[4] + k, u, u, pc.Y),
            w.copy(i_m[5] + k, d, d, pc.X),
        ]

    for m in moe_spread(0):
        m.start()

    def project(rows):
        x = R.NM[rows]
        for s, ref in enumerate((R.QS, R.KS, R.VS)):
            y = mm(x, R.WA[:, :, s].reshape(WIDE, HALF))
            if s == 0:
                y = y.astype(BF).astype(F32) * 0.125
            for p in range(3):
                ref[p, rows] = y[:, 128 * p : 128 * p + 128].astype(BF)

    blocks(ROWS, 256, project)
    prefix = R.pre[0]

    def pair_of_heads(p, carry):
        value_t = R.VS[p].astype(F32).T.astype(BF)
        even = iota((256, 128), 1) < 64
        for qb in range(4):
            cols = pl.ds(qb * 256, 256)
            outs = []
            for i in range(2):
                q = R.QS[p, cols]
                q = jnp.where(even if i == 0 else ~even, q.astype(F32), 0.0).astype(BF)
                pieces = []
                for k0, kn, masked in SEEN[qb]:
                    s = mm(R.KS[p, pl.ds(k0, kn)], q, 1, 1)
                    if masked:
                        s = jnp.where(visible(k0, kn, qb * 256, 256, prefix), s, masked_score)
                    pieces.append(s)
                top = pieces[0].max(axis=0, keepdims=True)
                for s in pieces[1:]:
                    top = jnp.maximum(top, s.max(axis=0, keepdims=True))
                total_e = jnp.zeros((1, 256), F32)
                out = jnp.zeros((128, 256), F32)
                for (k0, kn, _), s in zip(SEEN[qb], pieces):
                    e = jnp.exp(s - top)
                    total_e = total_e + e.sum(axis=0, keepdims=True)
                    out = out + mm(value_t[:, k0 : k0 + kn], e.astype(BF))
                R.LT[p, i : i + 1, cols] = top + jnp.log(total_e)
                outs.append(out / total_e)
            both = jnp.where(iota((128, 256), 0) < 64, outs[0], outs[1])
            R.ATO[p, cols] = both.T.astype(BF)
        w.copy(i_att + p, R.ATO.at[p], R.ATX.at[p], pc.PAIR).start()

        @pl.when(p < 3)
        def _():
            k = p + 1
            for ref, i0 in ((R.UE, i_mu), (R.DE, i_md)):
                w.copy(i0 + k, ref.at[z, c], ref.at[z, c], pc.Z(k)).wait_recv()
            for m in moe_spread(k):
                m.start()

        a = moe_spread(p)
        a[0].wait_recv()
        a[1].wait_recv()
        for m in moe_forward(p):
            m.start()
        return carry

    lax.fori_loop(0, 3, pair_of_heads, 0)
    wo.wait_recv()
    for p in range(3):
        w.copy(i_att + p, R.ATO.at[p], R.ATX.at[p], pc.PAIR).wait()
    lane = iota((256, 128), 1)
    real = (lane >= 2) & (lane < 6)
    R.PS[...] = jnp.zeros((8, 128), F32)

    def out_block(rows):
        b = mm(joined(R.ATO, rows), R.WA[:, :, 3].reshape(WIDE, HALF), 1, 1)
        b = b + mm(joined(R.ATX, rows), R.WO[...].reshape(WIDE, HALF), 1, 1)
        h = R.TK[rows].astype(F32) + b
        R.HIDN[rows] = h
        f2 = lax.rsqrt(jnp.mean(h * h, axis=1, keepdims=True) + norm_eps)
        R.STAT[rows, 1:2] = f2
        moe = (h * f2 * R.VEC[1:2]).astype(BF)
        R.GC[rows] = moe
        logits = mm(moe, R.RW[...])
        mine = jnp.where((lane - 2).astype(F32) == R.PR[rows], logits, 0.0)
        picked = jnp.sum(jnp.where(real, mine, 0.0), axis=1, keepdims=True)
        R.STAT[rows, 2:3] = jax.nn.sigmoid(picked)
        lg = jnp.where(real, logits, masked_score)
        e = jnp.exp(lg - jnp.max(lg, axis=1, keepdims=True))
        e = jnp.where(real, e, 0.0)
        pr = e / jnp.sum(e, axis=1, keepdims=True)
        R.PR[rows] = pr
        R.PS[0:1] = R.PS[0:1] + jnp.sum(pr, axis=0, keepdims=True)

    blocks(ROWS, 256, out_block)

    def moe_rows(i, carry):
        k = order(lax.rem(i + 1, 4))
        e = pc.zto(k)
        R.CS[e] = mm(R.DM[pl.ds(pl.multiple_of(e * 128, 128), 128)], R.GC[...]).astype(BF)

        @pl.when(i < 3)
        def _():
            w.copy(i_dz + k, R.CS.at[e], R.DR.at[z, t], pc.Z(k)).start()

        return carry

    lax.fori_loop(0, 4, moe_rows, 0)
    R.DR[z, t] = R.CS[z]
    w.copy(i_dp, R.DR.at[z, t], R.DR.at[z, t], pc.PAIR).start()
    a = moe_spread(3)
    a[0].wait_recv()
    a[1].wait_recv()
    for m in moe_forward(3):
        m.start()
    for m in cz:
        m.wait_recv()
    cp = w.go(i_cp, R.CR.at[:, t], R.CR.at[:, t], pc.PAIR)
    for k in range(4):
        a = moe_spread(k)
        b = moe_forward(k)
        a[2].wait_recv()
        a[3].wait_recv()
        b[0].wait_recv()
        b[1].wait_recv()
        for m in a + b:
            m.wait_send()
    cp.wait_recv()
    w.flush()
    return i_dz, i_dp


def gelu_parts(v):
    cdf = 0.5 * (1.0 + lax.erf(v * (1.0 / math.sqrt(2.0))))
    slope = cdf + v * (jnp.exp(-0.5 * v * v) * (1.0 / math.sqrt(2.0 * math.pi)))
    return v * cdf, slope


class ExpertSums:
    def __init__(self, R, pc, w):
        self.R, self.pc, self.w = R, pc, w
        self.i1, self.i2, self.i3 = w.ids(8), w.ids(4), w.ids(16)

    def step_one(self, g):
        R, pc, w = self.R, self.pc, self.w
        cols, i = pl.ds(pl.multiple_of(768 * g, 128), 768), self.i1 + 4 * g
        return [
            w.copy(i, R.UE.at[:, pc.cx, :, cols], R.RU.at[0, :, :, cols], pc.X),
            w.copy(i + 1, R.UE.at[:, pc.cd, :, cols], R.RU.at[1, :, :, cols], pc.X),
            w.copy(i + 2, R.DE.at[:, pc.cy, :, cols], R.RD.at[0, :, :, cols], pc.Y),
            w.copy(i + 3, R.DE.at[:, pc.cd, :, cols], R.RD.at[1, :, :, cols], pc.Y),
        ]

    def step_two(self, g):
        R, pc, w = self.R, self.pc, self.w
        cols, i = pl.ds(768 * g, 768), self.i2 + 2 * g
        return [
            w.copy(i, R.UE.at[:, pc.cy, :, cols], R.RU2.at[:, :, cols], pc.Y),
            w.copy(i + 1, R.DE.at[:, pc.cx, :, cols], R.RD2.at[:, :, cols], pc.X),
        ]

    def step_three(self, g):
        R, pc, w = self.R, self.pc, self.w
        cols, i, out = pl.ds(768 * g, 768), self.i3 + 8 * g, []
        for k in (1, 2, 3):
            to, z = pc.zto(k), pc.z
            out.append(w.copy(i + k, R.UE.at[to, pc.c, :, cols], R.ZU.at[z, :, cols], pc.Z(k)))
            out.append(w.copy(i + 4 + k, R.DE.at[to, pc.c, :, cols], R.ZD.at[z, :, cols], pc.Z(k)))
        return out

    def two(self, g):
        R, pc, cols = self.R, self.pc, pl.ds(768 * g, 768)
        for m in self.step_one(g):
            m.wait()

        def add(zz, carry):
            R.UE[zz, pc.cy, :, cols] = R.UE[zz, pc.cy, :, cols] + R.RU[1, zz, :, cols]
            R.DE[zz, pc.cx, :, cols] = R.DE[zz, pc.cx, :, cols] + R.RD[1, zz, :, cols]
            R.UE[zz, pc.c, :, cols] = R.UE[zz, pc.c, :, cols] + R.RU[0, zz, :, cols]
            R.DE[zz, pc.c, :, cols] = R.DE[zz, pc.c, :, cols] + R.RD[0, zz, :, cols]
            return carry

        lax.fori_loop(0, 4, add, 0)
        for m in self.step_two(g):
            m.start()

    def three(self, g):
        R, pc, cols = self.R, self.pc, pl.ds(768 * g, 768)
        for m in self.step_two(g):
            m.wait()

        def add(zz, carry):
            R.UE[zz, pc.c, :, cols] = R.UE[zz, pc.c, :, cols] + R.RU2[zz, :, cols]
            R.DE[zz, pc.c, :, cols] = R.DE[zz, pc.c, :, cols] + R.RD2[zz, :, cols]
            return carry

        lax.fori_loop(0, 4, add, 0)
        for m in self.step_three(g):
            m.start()

    def last(self):
        R, pc = self.R, self.pc
        R.ZU[pc.z] = R.UE[pc.z, pc.c]
        R.ZD[pc.z] = R.DE[pc.z, pc.c]
        out = []
        for g in (0, 1):
            for m in self.step_three(g):
                m.wait()
            cols = pl.ds(768 * g, 768)
            for j, (got, to) in enumerate(((R.ZU, R.up_grad), (R.ZD, R.down_grad))):
                held = R.HIDN.at[pl.ds(192 * (2 * g + j), 192)].reshape(4, 48, 768)
                held[...] = got[:, :, cols].astype(F32)
                m = pltpu.make_async_copy(held, to.at[:, :, cols], R.ls.at[2 * g + j])
                m.start()
                out.append(m)
        return out


class AttentionSums:
    def __init__(self, R, pc, w):
        self.R, self.pc, self.w = R, pc, w
        self.i1, self.i2, self.i3 = w.ids(16), w.ids(8), w.ids(16)
        self.low, self.high = pl.ds(0, 2), pl.ds(2, 2)

    def step_one(self, n):
        R, pc, w, i = self.R, self.pc, self.w, self.i1 + 4 * n
        return [
            w.copy(i, R.AG.at[n, self.low, pc.cx], R.RA.at[n, 0], pc.X),
            w.copy(i + 1, R.AG.at[n, self.low, pc.cd], R.RA.at[n, 1], pc.X),
            w.copy(i + 2, R.AG.at[n, self.high, pc.cy], R.RB.at[n, 0], pc.Y),
            w.copy(i + 3, R.AG.at[n, self.high, pc.cd], R.RB.at[n, 1], pc.Y),
        ]

    def step_two(self, n):
        R, pc, w, i = self.R, self.pc, self.w, self.i2 + 2 * n
        return [
            w.copy(i, R.AG.at[n, self.low, pc.cy], R.RA2.at[n], pc.Y),
            w.copy(i + 1, R.AG.at[n, self.high, pc.cx], R.RB2.at[n], pc.X),
        ]

    def step_three(self, n):
        R, pc, w, i = self.R, self.pc, self.w, self.i3 + 4 * n
        return [
            w.copy(i + k, R.AG.at[n, pc.zto(k), pc.c], R.ZA.at[n, pc.z], pc.Z(k))
            for k in (1, 2, 3)
        ]

    def one(self, n):
        for m in self.step_one(n):
            m.start()

    def two(self, n):
        R, pc = self.R, self.pc
        for m in self.step_one(n):
            m.wait()
        for j in range(2):
            R.AG[n, j, pc.cy] = R.AG[n, j, pc.cy] + R.RA[n, 1, j]
            R.AG[n, 2 + j, pc.cx] = R.AG[n, 2 + j, pc.cx] + R.RB[n, 1, j]
            R.AG[n, j, pc.c] = R.AG[n, j, pc.c] + R.RA[n, 0, j]
            R.AG[n, 2 + j, pc.c] = R.AG[n, 2 + j, pc.c] + R.RB[n, 0, j]
        for m in self.step_two(n):
            m.start()

    def three(self, n):
        R, pc = self.R, self.pc
        for m in self.step_two(n):
            m.wait()
        for j in range(2):
            R.AG[n, j, pc.c] = R.AG[n, j, pc.c] + R.RA2[n, j]
            R.AG[n, 2 + j, pc.c] = R.AG[n, 2 + j, pc.c] + R.RB2[n, j]
        for m in self.step_three(n):
            m.start()

    def last(self, n):
        R, pc = self.R, self.pc
        R.ZA[n, pc.z] = R.AG[n, pc.z, pc.c]
        for m in self.step_three(n):
            m.wait()
        total = R.ZA[n, 0].astype(F32)
        for zz in range(1, 4):
            total = total + R.ZA[n, zz].astype(F32)
        for j in range(3):
            block = total[48 * j : 48 * j + 48]
            if n == 0:
                R.out_grad[:, 128 * j : 128 * j + 128] = block
            else:
                R.qkv_grad[j, :, 128 * (n - 1) : 128 * n] = block


def phase_b(R, pc, w, i_dz, i_dp):
    f, t, z, c, o = pc.f, pc.t, pc.z, pc.c, pc.o
    i_xe, i_xg = w.ids(4), w.ids(4)
    i_rg, i_re, i_rgp, i_rep = w.ids(4), w.ids(4), w.ids(1), w.ids(1)
    lane = iota((256, 128), 1)
    row = jnp.sum(
        jnp.where(iota((16, WIDE), 0) == 2 + z, R.VEC[...], 0.0), axis=0, keepdims=True
    )
    R.RGR[...] = jnp.zeros((16, WIDE), F32)

    def to_plane(s):
        return {"fsdp": 4 * s + c, "tensor": t}

    def rows_in(k):
        return w.copy(i_dz + k, R.CS.at[pc.zto(k)], R.DR.at[z, t], pc.Z(k))

    def rows_pair(k):
        s = pc.zfrom(k)
        return w.copy(i_dp + k, R.DR.at[s, t], R.DR.at[s, t], pc.PAIR)

    def pair_sums(k):
        s = pc.zfrom(k)
        return (
            w.copy(i_xg + k, R.PG.at[s], R.XG.at[s], pc.PAIR),
            w.copy(i_xe + k, R.PE.at[s], R.XE.at[s], pc.PAIR),
        )

    def home(k):
        s = pc.zfrom(k)
        return w.copy(i_rg + k, R.XG.at[s], R.RG.at[z, t], to_plane(s))

    def home_out(k):
        s = pc.zfrom(k)
        return w.copy(i_re + k, R.XE.at[s], R.RE.at[z, t], to_plane(s))

    def finish(k):
        s = pc.zfrom(k)
        for m in pair_sums(k):
            m.wait()
        eo = R.EOO[s] + R.XE[s].astype(F32)
        gate = R.STAT[pl.ds(pl.multiple_of(s * 256 + t * 128, 128), 128), 3:4]
        gate_grad = jnp.sum(R.CR[s, t].astype(F32) * eo, axis=1, keepdims=True)
        gs = gate_grad * gate * (1.0 - gate)
        R.RGR[0:1] += jnp.sum(gs * R.DR[s, t].astype(F32), axis=0, keepdims=True)
        R.XG[s] = (R.GMO[s] + R.XG[s].astype(F32) + gs * row).astype(BF)
        R.XE[s] = eo.astype(BF)

    def source(i, carry):
        k = order(i)
        s = pc.zfrom(k)
        rows = pl.ds(pl.multiple_of(s * 256, 256), 256)

        @pl.when(i > 0)
        def _():
            rows_in(k).wait()
            rows_pair(k).start()
            last = order(i - 1)
            finish(last)

            @pl.when(i > 1)
            def _():
                home(last).start()

        rows_pair(k).wait()
        x = R.DR[s].reshape(256, WIDE)
        logits = mm(x, R.RW[...])
        gate = jax.nn.sigmoid(
            jnp.sum(jnp.where(lane == 2 + z, logits, 0.0), axis=1, keepdims=True)
        )
        R.STAT[rows, 3:4] = gate
        R.GC[rows] = (gate * R.CR[s].reshape(256, WIDE).astype(F32)).astype(BF)
        R.EOB[...] = jnp.zeros((2, 128, WIDE), F32)
        R.GMB[...] = jnp.zeros((2, 128, WIDE), F32)

        def hidden_units(cols):
            up = R.UE[:, :, :, cols].reshape(WIDE, 512)
            down = R.DE[:, :, :, cols].reshape(WIDE, 512)
            act, slope = gelu_parts(mm(R.DR[s].reshape(256, WIDE), up))
            act = act.astype(BF)
            gb = (mm(R.GC[rows], down) * slope).astype(BF)
            R.ACT[rows, cols] = act
            R.GB[rows, cols] = gb
            R.EOB[...] += mm(act, down, 1, 1).reshape(2, 128, WIDE)
            R.GMB[...] += mm(gb, up, 1, 1).reshape(2, 128, WIDE)

        blocks(HID, 512, hidden_units)
        R.PG[s] = R.GMB[o].astype(BF)
        R.PE[s] = R.EOB[o].astype(BF)
        for m in pair_sums(k):
            m.start()
        R.GMO[s] = R.GMB[t]
        R.EOO[s] = R.EOB[t]
        return carry

    lax.fori_loop(0, 4, source, 0)
    finish(2)
    home(2).start()
    R.RG[z, t] = R.XG[z]
    R.RE[z, t] = R.XE[z]
    R.RGR[...] = jnp.where(iota((16, WIDE), 0) == 2 + z, R.RGR[0:1], 0.0)
    sums = ExpertSums(R, pc, w)
    DR = R.DR.reshape(ROWS, WIDE)

    def weight_grads(i, carry):
        cols = pl.ds(pl.multiple_of(i * 384, 128), 384)
        R.UE[:, :, :, cols] = mm(DR[...], R.GB[:, cols], 0, 0).astype(BF).reshape(4, 4, 48, 384)
        R.DE[:, :, :, cols] = mm(R.GC[...], R.ACT[:, cols], 0, 0).astype(BF).reshape(4, 4, 48, 384)

        @pl.when(lax.rem(i, 2) == 1)
        def _():
            for m in sums.step_one(lax.div(i, 2)):
                m.start()

        return carry

    lax.fori_loop(0, 4, weight_grads, 0)
    for k in (1, 3, 2):
        home(k).wait()
    back = w.go(i_rgp, R.RG.at[:, t], R.RG.at[:, t], pc.PAIR)
    for k in (1, 3, 2):
        home_out(k).start()
    back.wait_recv()
    sums.two(0)
    return sums, home_out, i_rep


def combine(key, rows, got):
    n = key.shape[0]
    keys = jnp.concatenate([key] * 8, axis=1)
    pick = (keys == iota((n, ROWS), 1).astype(F32)).astype(F32).astype(BF)
    return mm(pick, got)


def phase_c(R, pc, w, sums, home_out, i_rep):
    f, t, z, c, o = pc.f, pc.t, pc.z, pc.c, pc.o
    att = AttentionSums(R, pc, w)
    i_n = w.ids(1)
    i_sp, i_sc, i_sz = w.ids(1), w.ids(4), w.ids(4)
    own = pl.ds(pl.multiple_of(t * 512, 512), 512)
    GH, GN = R.GH, R.EOO.reshape(512, WIDE)
    RG, RE = R.RG.reshape(ROWS, WIDE), R.RE.reshape(ROWS, WIDE)
    GBR = R.GC
    share = R.SHARE[0:1]
    vec = R.VEC[...]
    head = iota((24, HALF), 0)
    head = jnp.where(lax.rem(head, 8) < 2, 2 * lax.div(head, 8) + lax.rem(head, 8), -1)
    pick_head = (head == lax.div(iota((24, HALF), 1), 64)).astype(F32).astype(BF)
    R.SB[...] = jnp.zeros((16, WIDE), F32)

    def residual(i, carry):
        rows = pl.ds(pl.multiple_of(i * 256, 256), 256)
        gm = combine(R.KC[rows], rows, RG[...])
        pr = R.PR[rows]
        mixed = jnp.sum(pr * share, axis=1, keepdims=True)
        aux = (balance_weight * 4.0 / (16 * ROWS)) * pr * (share - mixed)
        aux = aux[:, 0:16]
        gm = gm + mm(aux.astype(BF), vec.astype(BF))
        mine = jnp.where(lax.div(i, 2) == t, 1.0, 0.0)
        R.SB[...] += mine * mm(aux.astype(BF), (R.HIDN[rows] * R.STAT[rows, 1:2] * vec[1:2]).astype(BF), 0, 0)
        h, f2 = R.HIDN[rows], R.STAT[rows, 1:2]
        g = gm * vec[1:2]
        inner = jnp.mean(g * h, axis=1, keepdims=True)
        gh = R.CT[rows].astype(F32) + f2 * (g - h * (f2 * f2 * inner))
        R.G2[0:1] += mine * jnp.sum(gm * h * f2, axis=0, keepdims=True)
        GH[rows] = gh
        low = gh.astype(BF)
        GBR[rows] = low
        ga = mm(low, R.WA[:, :, 3].reshape(WIDE, HALF)).astype(BF)
        for p in range(3):
            R.ATX[p, rows] = ga[:, 128 * p : 128 * p + 128]
        prod = ga.astype(F32) * joined(R.ATO, rows).astype(F32)
        top = prod.astype(BF)
        rest = (prod - top.astype(F32)).astype(BF)
        dd = mm(pick_head, top, 1, 1) + mm(pick_head, rest, 1, 1)
        for p in range(3):
            R.DD[p, :, rows] = dd[8 * p : 8 * p + 8]
        return carry

    R.G2[...] = jnp.zeros((8, WIDE), F32)
    lax.fori_loop(0, 4, residual, 0)
    part = jnp.where(iota((16, WIDE), 0) == 1, R.G2[0:1], 0.0)
    sums6 = jnp.concatenate([0.5 * R.PS[0:1], jnp.zeros((1, WIDE - 128), F32)], axis=1)
    keep = (iota((16, WIDE), 0) >= 2) & (iota((16, WIDE), 0) < 6)
    R.SB[...] = (
        jnp.where(keep, R.SB[...] + R.RGR[...], 0.0)
        + part
        + jnp.where(iota((16, WIDE), 0) == 6, sums6, 0.0)
    )

    def place(n, grad):
        for j in range(3):
            block = grad[:, 128 * j : 128 * j + 128].astype(BF).reshape(4, 4, 48, 128)
            R.AG[n, :, :, pl.ds(48 * j, 48)] = block

    place(0, mm(GBR[...], joined(R.ATO, pl.ds(0, ROWS)), 0, 0))
    sums.two(1)
    att.one(0)
    prefix = R.pre[0]

    def pair_of_heads(p, carry):
        key_t = R.KS[p].astype(F32).T.astype(BF)
        R.DK[...] = jnp.zeros((ROWS, 128), F32)
        R.DV[...] = jnp.zeros((ROWS, 128), F32)
        even = iota((256, 128), 1) < 64
        for qb in range(4):
            cols = pl.ds(qb * 256, 256)
            outs = []
            for i in range(2):
                side = even if i == 0 else ~even
                q = jnp.where(side, R.QS[p, cols].astype(F32), 0.0).astype(BF)
                do = jnp.where(side, R.ATX[p, cols].astype(F32), 0.0).astype(BF)
                lt, dd = R.LT[p, i : i + 1, cols], R.DD[p, i : i + 1, cols]
                dq = jnp.zeros((128, 256), F32)
                for kb in range(max(2, qb + 1)):
                    keys = pl.ds(kb * 256, 256)
                    s = mm(R.KS[p, keys], q, 1, 1)
                    if kb == qb or qb < 2:
                        ok = visible(kb * 256, 256, qb * 256, 256, prefix)
                        s = jnp.where(ok, s, masked_score)
                    prob = jnp.exp(s - lt)
                    ds = prob * (mm(R.VS[p, keys], do, 1, 1) - dd)
                    ds = ds.astype(BF)
                    R.DV[keys] += mm(prob.astype(BF), do)
                    R.DK[keys] += mm(ds, q)
                    dq = dq + mm(key_t[:, kb * 256 : kb * 256 + 256], ds)
                outs.append(dq)
            both = jnp.where(iota((128, 256), 0) < 64, outs[0], outs[1])
            R.QS[p, cols] = (both * 0.125).T.astype(BF)
        R.KS[p] = R.DK[...].astype(BF)
        R.VS[p] = R.DV[...].astype(BF)
        three = jnp.concatenate([R.QS[p], R.KS[p], R.VS[p]], axis=1)
        place(p + 1, mm(R.NM[...], three, 0, 0))
        att.one(p + 1)

        @pl.when(p == 0)
        def _():
            sums.three(0)

        @pl.when(p == 1)
        def _():
            sums.three(1)
            att.two(0)

        @pl.when(p == 2)
        def _():
            att.three(0)
            att.two(1)

        return carry

    lax.fori_loop(0, 3, pair_of_heads, 0)
    GP = (R.QS, R.KS, R.VS)

    XS, XN, BO = (r.reshape(512, WIDE) for r in (R.CS, R.XG, R.PE))

    def normed_grad(i, carry):
        mine = pl.ds(pl.multiple_of(i * 256, 256), 256)

        def half(start):
            rows = pl.ds(pl.multiple_of(start * 512 + i * 256, 256), 256)
            acc = jnp.zeros((256, WIDE), F32)
            for s in range(3):
                acc = acc + mm(joined(GP[s], rows), R.WA[:, :, s].reshape(WIDE, HALF), 1, 1)
            return acc

        XS[mine] = half(o).astype(BF)
        GN[mine] = half(t)
        return carry

    w.flush()
    lax.fori_loop(0, 2, normed_grad, 0)
    xn = w.go(i_n, XS, XN, pc.PAIR)
    att.two(2)
    att.three(1)
    xn.wait_recv()
    R.G2[...] = jnp.zeros((8, WIDE), F32)

    def input_grad(i, carry):
        rows = pl.ds(pl.multiple_of(i * 128, 128), 128)
        full = pl.ds(pl.multiple_of(t * 512 + i * 128, 128), 128)
        gn = GN[rows] + XN[rows].astype(F32)
        x, f1 = R.TK[full].astype(F32), R.STAT[full, 0:1]
        g = gn * R.VEC[0:1]
        inner = jnp.mean(g * x, axis=1, keepdims=True)
        GH[full] = GH[full] + f1 * (g - x * (f1 * f1 * inner))
        R.G2[0:1] += jnp.sum(gn * x * f1, axis=0, keepdims=True)
        return carry

    lax.fori_loop(0, 4, input_grad, 0)
    out_t = pltpu.make_async_copy(GH.at[own], R.tokens_grad, R.ls.at[0])
    out_t.start()
    R.SB[0:1] = R.G2[0:1]
    sp = w.go(i_sp, R.SB, R.SP, pc.PAIR)
    att.two(3)
    att.three(2)
    sp.wait_recv()
    me = R.SB[...] + R.SP[...]
    R.SC[c] = me
    sc = [
        w.go(i_sc, R.SC.at[c], R.SC.at[c], pc.X),
        w.go(i_sc + 1, R.SC.at[c], R.SC.at[c], pc.Y),
        w.go(i_sc + 2, R.SC.at[c], R.SC.at[c], pc.DIAG),
    ]
    for k in (1, 2, 3):
        home_out(k).wait()
    w.go(i_rep, R.RE.at[:, t], R.RE.at[:, t], pc.PAIR).wait_recv()

    def block_rows(i, carry):
        rows = pl.ds(pl.multiple_of(i * 256, 256), 256)
        full = pl.ds(pl.multiple_of(t * 512 + i * 256, 256), 256)
        eo = combine(R.KC[full], full, RE[...])
        BO[rows] = (R.HIDN[full] + R.STAT[full, 2:3] * eo).astype(BF)
        return carry

    lax.fori_loop(0, 2, block_rows, 0)
    out_b = pltpu.make_async_copy(BO, R.block_out, R.ls.at[1])
    out_b.start()
    att.three(3)
    out_t.wait()
    out_b.wait()
    for m in sc:
        m.wait_recv()
    R.SZ[z] = R.SC[0] + R.SC[1] + R.SC[2] + R.SC[3]
    sz = [w.go(i_sz + k, R.SZ.at[z], R.SZ.at[z], pc.Z(k)) for k in (1, 2, 3)]
    written = sums.last()
    for n in range(3):
        att.last(n)
    for m in sz:
        m.wait_recv()
    total = R.SZ[0] + R.SZ[1] + R.SZ[2] + R.SZ[3]
    probs = total[6:7, 0:128]
    R.balance[...] = (4.0 / (16 * ROWS)) * jnp.sum(share * probs, axis=1, keepdims=True)
    column = (iota((WIDE, 128), 0) == 48 * f + iota((WIDE, 128), 1)).astype(F32).astype(BF)
    mine = jnp.zeros((16, 128), F32)
    for _ in range(3):
        top = total.astype(BF)
        mine = mine + mm(top, column)
        total = total - top.astype(F32)
    R.gains_grad[...] = mine[0:2, 0:48]
    R.router_grad[...] = mine[2:6, 0:48]
    att.last(3)
    for m in written:
        m.wait()
    w.flush()


OUTS = {
    "block_out": ((512, WIDE), BF),
    "tokens_grad": ((512, WIDE), F32),
    "gains_grad": ((2, 48), F32),
    "qkv_grad": ((3, 48, HALF), F32),
    "out_grad": ((48, HALF), F32),
    "router_grad": ((4, 48), F32),
    "up_grad": ((4, 48, HID), F32),
    "down_grad": ((4, 48, HID), F32),
    "balance": ((1, 1), F32),
}
SCRATCH = {
    "STAT": ((ROWS, 128), F32),
    "ATO": ((3, ROWS, 128), BF),
    "ATX": ((3, ROWS, 128), BF),
    "PG": ((4, 128, WIDE), BF),
    "PE": ((4, 128, WIDE), BF),
    "EOB": ((2, 128, WIDE), F32),
    "GMB": ((2, 128, WIDE), F32),
    "EOO": ((4, 128, WIDE), F32),
    "GMO": ((4, 128, WIDE), F32),
    "GH": ((ROWS, WIDE), F32),
    "ACT": ((ROWS, HID), BF),
    "GB": ((ROWS, HID), BF),
    "TK": ((ROWS, WIDE), BF),
    "CT": ((ROWS, WIDE), BF),
    "WA": ((4, 4, 4, 48, HALF), BF),
    "WO": ((4, 4, 48, HALF), BF),
    "UE": ((4, 4, 48, HID), BF),
    "DE": ((4, 4, 48, HID), BF),
    "KC": ((ROWS, 128), F32),
    "CR": ((4, 2, 128, WIDE), BF),
    "DR": ((4, 2, 128, WIDE), BF),
    "VEC": ((16, WIDE), F32),
    "RW": ((WIDE, 128), BF),
    "SHARE": ((8, 128), F32),
    "NM": ((ROWS, WIDE), BF),
    "QS": ((3, ROWS, 128), BF),
    "KS": ((3, ROWS, 128), BF),
    "VS": ((3, ROWS, 128), BF),
    "LT": ((3, 8, ROWS), F32),
    "HIDN": ((ROWS, WIDE), F32),
    "PR": ((ROWS, 128), F32),
    "PS": ((8, 128), F32),
    "SM": ((16, 16, 128), BF),
    "DM": ((512, ROWS), BF),
    "CS": ((4, 128, WIDE), BF),
    "GC": ((ROWS, WIDE), BF),
    "XE": ((4, 128, WIDE), BF),
    "XG": ((4, 128, WIDE), BF),
    "RG": ((4, 2, 128, WIDE), BF),
    "RE": ((4, 2, 128, WIDE), BF),
    "RGR": ((16, WIDE), F32),
    "RU": ((2, 4, 48, HID), BF),
    "RD": ((2, 4, 48, HID), BF),
    "RU2": ((4, 48, HID), BF),
    "RD2": ((4, 48, HID), BF),
    "ZU": ((4, 48, HID), BF),
    "ZD": ((4, 48, HID), BF),
    "DD": ((3, 8, ROWS), F32),
    "DK": ((ROWS, 128), F32),
    "DV": ((ROWS, 128), F32),
    "AG": ((4, 4, 4, 144, 128), BF),
    "RA": ((4, 2, 2, 144, 128), BF),
    "RB": ((4, 2, 2, 144, 128), BF),
    "RA2": ((4, 2, 144, 128), BF),
    "RB2": ((4, 2, 144, 128), BF),
    "ZA": ((4, 4, 144, 128), BF),
    "G2": ((8, WIDE), F32),
    "SB": ((16, WIDE), F32),
    "SP": ((16, WIDE), F32),
    "SC": ((4, 16, WIDE), F32),
    "SZ": ((4, 16, WIDE), F32),
}
INS = ("tok", "cot", "pre", "idr", "gains", "qkv", "out", "router", "up", "down")
IN_HBM = ("tok", "cot", "up", "down")
OUT_HBM = ("block_out", "tokens_grad", "up_grad", "down_grad")
SEMAPHORES = 208


def fused(args):
    names = INS + tuple(OUTS) + tuple(SCRATCH) + ("ss", "rs", "ls")

    def body(*refs):
        R = types.SimpleNamespace(**dict(zip(names, refs)))
        pc = Place()
        w = Wire(R.ss, R.rs)
        phase_c(R, pc, w, *phase_b(R, pc, w, *phase_a(R, pc, w)))

    vm = pl.BlockSpec(memory_space=pltpu.VMEM)
    hbm = pl.BlockSpec(memory_space=pl.ANY)
    sm = pl.BlockSpec(memory_space=pltpu.SMEM)
    dma = pltpu.SemaphoreType.DMA
    return pl.pallas_call(
        body,
        out_shape=[jax.ShapeDtypeStruct(s, d) for s, d in OUTS.values()],
        in_specs=[sm if n == "pre" else hbm if n in IN_HBM else vm for n in INS],
        out_specs=[hbm if n in OUT_HBM else vm for n in OUTS],
        scratch_shapes=[pltpu.VMEM(s, d) for s, d in SCRATCH.values()]
        + [dma((SEMAPHORES,)), dma((SEMAPHORES,)), dma((4,))],
        compiler_params=pltpu.CompilerParams(
            collective_id=1, has_side_effects=True, vmem_limit_bytes=63 << 20
        ),
        name="block",
    )(*args)


def prepare(
    tokens, cotangent, prefix_len, expert_ids, norm_gains, qkv_weight, out_weight, router_weight, up_weight, down_weight
):
    ids = expert_ids.reshape(1, ROWS)
    return (tokens, cotangent, prefix_len, ids, norm_gains, qkv_weight, out_weight, router_weight, up_weight, down_weight)


def fast_device(*args):
    outs = fused(prepare(*args))
    return tuple(outs[:8]) + (outs[8].reshape(()),)


HEAD = 64
EXPERTS = 4
SEQ = 1024
CAP = 256


highest = lax.Precision.HIGHEST


def softmax_rows(scores):
    row_max = jnp.max(scores, axis=-1, keepdims=True)
    shifted = jnp.exp(scores - row_max)
    return shifted / jnp.sum(shifted, axis=-1, keepdims=True)


def slot_index(group_ids):
    onehot = (group_ids[:, None] == jnp.arange(EXPERTS, dtype=jnp.int32)[None, :]).astype(jnp.int32)
    rows = group_ids.shape[0]
    earlier = lax.broadcasted_iota(jnp.int32, (rows, rows), 1) <= lax.broadcasted_iota(
        jnp.int32, (rows, rows), 0
    )
    running = jnp.dot(
        earlier.astype(jnp.bfloat16),
        onehot.astype(jnp.bfloat16),
        preferred_element_type=jnp.float32,
    ).astype(jnp.int32)
    placed = jnp.sum(running * onehot, axis=1) - 1
    return jnp.where(placed < CAP, group_ids * CAP + placed, EXPERTS * CAP)


def rms_factor(values):
    return lax.rsqrt(jnp.mean(values * values, axis=-1, keepdims=True) + norm_eps)


def norm_back(grad_out, inputs, factor, gain):
    scaled = grad_out * gain
    row_inner = jnp.mean(scaled * inputs, axis=-1, keepdims=True)
    grad_in = factor * (scaled - inputs * factor * factor * row_inner)
    grad_gain = jnp.sum(grad_out * inputs * factor, axis=0)
    return (grad_in, grad_gain)


def gelu_slope(values):
    cumulative = 0.5 * (1.0 + lax.erf(values / math.sqrt(2.0)))
    density = jnp.exp(-0.5 * values * values) / math.sqrt(2.0 * math.pi)
    return cumulative + values * density


def block_scores(query_block, key_seq, offset, prefix, score_scale):
    scores = (
        jnp.einsum("qhd,khd->hqk", query_block, key_seq, preferred_element_type=jnp.float32)
        * score_scale
    )
    shape_pair = (query_block.shape[0], key_seq.shape[0])
    row_pos = offset + lax.broadcasted_iota(jnp.int32, shape_pair, 0)
    col_pos = lax.broadcasted_iota(jnp.int32, shape_pair, 1)
    allowed = (col_pos <= row_pos) | (col_pos < prefix)
    return jnp.where(allowed[None], scores, masked_score)


def attend(project, prefix_len, score_scale):
    group_rows = project.shape[0]
    full_width = project.shape[2]
    heads_here = full_width // HEAD
    block_rows = min(512, SEQ)
    shaped = project.reshape(group_rows, 3, heads_here, HEAD)
    query_all = shaped[:, 0]
    key_all = shaped[:, 1]
    value_all = shaped[:, 2]

    def one_block(number):
        row_start = number * block_rows
        seq_number = row_start // SEQ
        seq_start = seq_number * SEQ
        query_block = lax.dynamic_slice_in_dim(query_all, row_start, block_rows, 0)
        scores = block_scores(
            query_block, key_all, row_start - seq_start, prefix_len[seq_number], score_scale
        )
        row_max = jnp.max(scores, axis=-1, keepdims=True)
        shifted = jnp.exp(scores - row_max)
        row_total = jnp.sum(shifted, axis=-1, keepdims=True)
        prob_low = (shifted / row_total).astype(jnp.bfloat16)
        result = jnp.einsum("hqk,khd->qhd", prob_low, value_all, preferred_element_type=jnp.float32)
        return (
            result.reshape(block_rows, full_width).astype(jnp.bfloat16),
            (row_max + jnp.log(row_total))[..., 0],
        )

    outputs, log_total = lax.map(one_block, jnp.arange(group_rows // block_rows, dtype=jnp.int32))
    return (outputs.reshape(group_rows, full_width), log_total)


def attend_back(project, grad_att, log_total, prefix_len, score_scale):
    group_rows = project.shape[0]
    full_width = project.shape[2]
    heads_here = full_width // HEAD
    block_rows = min(512, SEQ)
    shaped = project.reshape(group_rows, 3, heads_here, HEAD)
    query_all = shaped[:, 0]
    key_all = shaped[:, 1]
    value_all = shaped[:, 2]
    grad_shaped = grad_att.reshape(group_rows, heads_here, HEAD)

    def one_block(carried, number):
        grad_keys, grad_values = carried
        row_start = number * block_rows
        seq_number = row_start // SEQ
        seq_start = seq_number * SEQ
        query_block = lax.dynamic_slice_in_dim(query_all, row_start, block_rows, 0)
        grad_block = lax.dynamic_slice_in_dim(grad_shaped, row_start, block_rows, 0)
        scores = block_scores(
            query_block, key_all, row_start - seq_start, prefix_len[seq_number], score_scale
        )
        prob_block = jnp.exp(scores - log_total[number][..., None])
        prob_low = prob_block.astype(jnp.bfloat16)
        grad_prob = jnp.einsum(
            "qhd,khd->hqk", grad_block, value_all, preferred_element_type=jnp.float32
        )
        value_part = jnp.einsum(
            "hqk,qhd->khd", prob_low, grad_block, preferred_element_type=jnp.float32
        )
        row_inner = jnp.sum(prob_block * grad_prob, axis=-1, keepdims=True)
        grad_scores = (prob_block * (grad_prob - row_inner)).astype(jnp.bfloat16)
        query_grad = (
            jnp.einsum("hqk,khd->qhd", grad_scores, key_all, preferred_element_type=jnp.float32)
            * score_scale
        )
        key_part = (
            jnp.einsum("hqk,qhd->khd", grad_scores, query_block, preferred_element_type=jnp.float32)
            * score_scale
        )
        old_keys = grad_keys
        grad_keys = old_keys + key_part
        old_values = grad_values
        grad_values = old_values + value_part
        return ((grad_keys, grad_values), query_grad)

    zero_rows = jnp.zeros((group_rows, heads_here, HEAD), jnp.float32)
    final, grad_query = lax.scan(
        one_block, (zero_rows, zero_rows), jnp.arange(group_rows // block_rows, dtype=jnp.int32)
    )
    grad_keys, grad_values = final
    stacked = jnp.stack(
        [
            grad_query.reshape(group_rows, full_width),
            grad_keys.reshape(group_rows, full_width),
            grad_values.reshape(group_rows, full_width),
        ],
        axis=1,
    )
    return stacked.astype(jnp.bfloat16)


def low_scatter(grad):
    return lax.psum_scatter(
        grad.astype(jnp.bfloat16), "fsdp", scatter_dimension=1, tiled=True
    ).astype(jnp.float32)


def per_device(
    tokens,
    cotangent,
    prefix_len,
    expert_ids,
    norm_gains,
    qkv_weight,
    out_weight,
    router_weight,
    up_weight,
    down_weight,
):
    tensor_size = lax.axis_size("tensor")
    fsdp_size = lax.axis_size("fsdp")
    own_rows = tokens.shape[0]
    group_rows = own_rows * tensor_size
    all_tokens = group_rows * fsdp_size
    own_start = lax.axis_index("tensor") * own_rows
    score_scale = 1.0 / math.sqrt(HEAD)
    gains_full, qkv_full, out_stack = (
        lax.all_gather(norm_gains, "fsdp", axis=1, tiled=True),
        lax.all_gather(qkv_weight, "fsdp", axis=1, tiled=True),
        lax.all_gather(out_weight[None], "fsdp", axis=1, tiled=True),
    )
    out_full = out_stack[0]
    router_full, up_full, down_full = (
        lax.all_gather(router_weight, "fsdp", axis=1, tiled=True),
        lax.all_gather(up_weight, "fsdp", axis=1, tiled=True),
        lax.all_gather(down_weight, "fsdp", axis=1, tiled=True),
    )
    inputs = lax.all_gather(tokens, "tensor", axis=0, tiled=True)
    input_float = inputs.astype(jnp.float32)
    factor_one = rms_factor(input_float)
    gain_one = gains_full[0].astype(jnp.float32)
    normed_one = (input_float * factor_one * gain_one).astype(jnp.bfloat16)
    project = jnp.einsum(
        "td,sdw->tsw", normed_one, qkv_full, preferred_element_type=jnp.float32
    ).astype(jnp.bfloat16)
    attended, log_total = attend(project, prefix_len, score_scale)
    branch = lax.psum_scatter(
        lax.dot_general(
            attended, out_full, (((1,), (1,)), ((), ())), preferred_element_type=jnp.float32
        ),
        "tensor",
        scatter_dimension=0,
        tiled=True,
    )
    hidden_own = tokens.astype(jnp.float32) + branch
    hidden_group = lax.all_gather(hidden_own, "tensor", axis=0, tiled=True)
    factor_two = rms_factor(hidden_group)
    gain_two = gains_full[1].astype(jnp.float32)
    moe_input = (hidden_group * factor_two * gain_two).astype(jnp.bfloat16)
    logits = lax.dot_general(
        moe_input, router_full, (((1,), (1,)), ((), ())), preferred_element_type=jnp.float32
    )
    group_ids = expert_ids[:, 0]
    onehot = (group_ids[:, None] == jnp.arange(EXPERTS, dtype=jnp.int32)[None, :]).astype(
        jnp.float32
    )
    gate_value = jax.nn.sigmoid(jnp.sum(logits * onehot, axis=-1))
    router_prob = softmax_rows(logits)
    counts, prob_sums = lax.psum((jnp.sum(onehot, axis=0), jnp.sum(router_prob, axis=0)), "fsdp")
    route_share = counts / all_tokens
    balance_loss = EXPERTS * jnp.sum(route_share * prob_sums) / all_tokens
    slot_rows = slot_index(group_ids)
    model_width = moe_input.shape[1]
    dispatched = (
        jnp.zeros((EXPERTS * CAP, model_width), jnp.bfloat16)
        .at[slot_rows]
        .set(moe_input, mode="drop")
        .reshape(EXPERTS, CAP, model_width)
    )
    before = jnp.einsum("ecd,edf->ecf", dispatched, up_full, preferred_element_type=jnp.float32)
    activated = jax.nn.gelu(before, approximate=False).astype(jnp.bfloat16)
    expert_out = jnp.einsum(
        "ecf,edf->ecd", activated, down_full, preferred_element_type=jnp.float32
    ).reshape(EXPERTS * CAP, model_width)
    combined_part = jnp.concatenate([expert_out, jnp.zeros((1, model_width), jnp.float32)], axis=0)[
        slot_rows
    ]
    combined = lax.psum_scatter(combined_part, "tensor", scatter_dimension=0, tiled=True)
    gate_own = lax.dynamic_slice_in_dim(gate_value, own_start, own_rows, 0)
    block_out = (hidden_own + gate_own[:, None] * combined).astype(jnp.bfloat16)
    gains_back, qkv_back, out_again, router_back, up_back, down_back = (
        lax.all_gather(norm_gains, "fsdp", axis=1, tiled=True),
        lax.all_gather(qkv_weight, "fsdp", axis=1, tiled=True),
        lax.all_gather(out_weight[None], "fsdp", axis=1, tiled=True),
        lax.all_gather(router_weight, "fsdp", axis=1, tiled=True),
        lax.all_gather(up_weight, "fsdp", axis=1, tiled=True),
        lax.all_gather(down_weight, "fsdp", axis=1, tiled=True),
    )
    out_back = out_again[0]
    cot_group = lax.all_gather(cotangent, "tensor", axis=0, tiled=True).astype(jnp.float32)
    grad_combined = (gate_value[:, None] * cot_group).astype(jnp.bfloat16)
    gate_grad_own = jnp.sum(cotangent.astype(jnp.float32) * combined, axis=-1)
    gate_grad_placed = lax.dynamic_update_slice_in_dim(
        jnp.zeros((group_rows,), jnp.float32), gate_grad_own, own_start, 0
    )
    grad_slots = (
        jnp.zeros((EXPERTS * CAP, model_width), jnp.bfloat16)
        .at[slot_rows]
        .set(grad_combined, mode="drop")
        .reshape(EXPERTS, CAP, model_width)
    )
    grad_activated = jnp.einsum(
        "ecd,edf->ecf", grad_slots, down_back, preferred_element_type=jnp.float32
    )
    down_grad = jnp.einsum(
        "ecd,ecf->edf", grad_slots, activated, preferred_element_type=jnp.float32
    )
    grad_before = (grad_activated * gelu_slope(before)).astype(jnp.bfloat16)
    up_grad = jnp.einsum(
        "ecd,ecf->edf", dispatched, grad_before, preferred_element_type=jnp.float32
    )
    grad_dispatched = jnp.einsum(
        "ecf,edf->ecd", grad_before, up_back, preferred_element_type=jnp.float32
    ).reshape(EXPERTS * CAP, model_width)
    grad_input_part = jnp.concatenate(
        [grad_dispatched, jnp.zeros((1, model_width), jnp.float32)], axis=0
    )[slot_rows]
    grad_moe, gate_grad = lax.psum((grad_input_part, gate_grad_placed), "tensor")
    gate_slope = gate_value * (1.0 - gate_value)
    mixed_share = jnp.sum(router_prob * route_share[None, :], axis=-1, keepdims=True)
    logit_grad = onehot * (gate_grad * gate_slope)[
        :, None
    ] + balance_weight * EXPERTS / all_tokens * router_prob * (route_share[None, :] - mixed_share)
    grad_norm_two = grad_moe + jnp.dot(
        logit_grad, router_back.astype(jnp.float32), precision=highest
    )
    router_grad = jnp.dot(logit_grad.T, moe_input.astype(jnp.float32), precision=highest)
    grad_hidden, gain_two_grad = norm_back(
        grad_norm_two, hidden_group, factor_two, gains_back[1].astype(jnp.float32)
    )
    grad_hidden = grad_hidden + cot_group
    grad_branch = grad_hidden.astype(jnp.bfloat16)
    grad_att = jnp.dot(grad_branch, out_back, preferred_element_type=jnp.float32).astype(
        jnp.bfloat16
    )
    out_grad = lax.dot_general(
        grad_branch, attended, (((0,), (0,)), ((), ())), preferred_element_type=jnp.float32
    )
    grad_project = attend_back(project, grad_att, log_total, prefix_len, score_scale)
    qkv_grad = jnp.einsum(
        "td,tsw->sdw", normed_one, grad_project, preferred_element_type=jnp.float32
    )
    grad_normed_part = jnp.einsum(
        "tsw,sdw->td", grad_project, qkv_back, preferred_element_type=jnp.float32
    )
    grad_normed = lax.psum(grad_normed_part, "tensor")
    grad_tokens, gain_one_grad = norm_back(
        grad_normed, input_float, factor_one, gains_back[0].astype(jnp.float32)
    )
    grad_tokens = grad_tokens + grad_hidden
    tokens_grad = lax.dynamic_slice_in_dim(grad_tokens, own_start, own_rows, 0)
    gains_own, qkv_own, out_own, router_own, up_own, down_own = (
        lax.psum_scatter(
            jnp.stack([gain_one_grad, gain_two_grad], axis=0),
            "fsdp",
            scatter_dimension=1,
            tiled=True,
        ),
        low_scatter(qkv_grad),
        low_scatter(out_grad[None]),
        lax.psum_scatter(router_grad, "fsdp", scatter_dimension=1, tiled=True),
        low_scatter(up_grad),
        low_scatter(down_grad),
    )
    return (
        block_out,
        tokens_grad,
        gains_own,
        qkv_own,
        out_own[0],
        router_own,
        up_own,
        down_own,
        balance_loss,
    )


def solution(mesh):
    placed = (
        P(("fsdp", "tensor"), None),
        P(("fsdp", "tensor"), None),
        P("fsdp"),
        P("fsdp", None),
        P(None, "fsdp"),
        P(None, "fsdp", "tensor"),
        P("fsdp", "tensor"),
        P(None, "fsdp"),
        P(None, "fsdp", "tensor"),
        P(None, "fsdp", "tensor"),
    )
    fits = mesh.shape["fsdp"] == 16 and mesh.shape["tensor"] == 2
    return jax.shard_map(
        fast_device if fits else per_device,
        mesh=mesh,
        in_specs=placed,
        out_specs=(
            P(("fsdp", "tensor"), None),
            P(("fsdp", "tensor"), None),
            P(None, "fsdp"),
            P(None, "fsdp", "tensor"),
            P("fsdp", "tensor"),
            P(None, "fsdp"),
            P(None, "fsdp", "tensor"),
            P(None, "fsdp", "tensor"),
            P(),
        ),
        check_vma=False,
    )
```

```python
import math
import types

import jax
import jax.numpy as jnp
from jax import lax
from jax.experimental import pallas as pl
from jax.experimental.pallas import tpu as pltpu
from jax.sharding import PartitionSpec as P

MESH = pl.DeviceIdType.MESH
BF = jnp.bfloat16
F32 = jnp.float32
ROWS = 1024
WIDE = 768
HALF = 384
HID = 1536
norm_eps = 1e-05
balance_weight = 0.01
masked_score = -1e30


def mm(a, b, ca=1, cb=0):
    return lax.dot_general(a, b, (((ca,), (cb,)), ((), ())), preferred_element_type=F32)


def iota(shape, axis):
    return lax.broadcasted_iota(jnp.int32, shape, axis)


def blocks(count, size, body):
    def step(i, carry):
        body(pl.ds(pl.multiple_of(i * size, size), size))
        return carry

    lax.fori_loop(0, count // size, step, 0)


class Place:
    def __init__(self):
        f, t = lax.axis_index("fsdp"), lax.axis_index("tensor")
        self.f, self.t, self.o = f, t, 1 - t
        self.z, self.c = lax.div(f, 4), lax.rem(f, 4)
        c = self.c
        self.cx = c + 1 - 2 * lax.rem(c, 2)
        self.cy = c + 2 - 4 * lax.div(c, 2)
        self.cd = 3 - c
        base = 4 * self.z
        self.X = {"fsdp": base + self.cx, "tensor": t}
        self.Y = {"fsdp": base + self.cy, "tensor": t}
        self.DIAG = {"fsdp": base + self.cd, "tensor": t}
        self.PAIR = {"fsdp": f, "tensor": 1 - t}

    def zto(self, k):
        return lax.rem(self.z + k, 4)

    def zfrom(self, k):
        return lax.rem(self.z + 4 - k, 4)

    def Z(self, k):
        return {"fsdp": 4 * self.zto(k) + self.c, "tensor": self.t}


class Wire:
    def __init__(self, send, recv):
        self.send, self.recv, self.n, self.open = send, recv, 0, []

    def ids(self, n):
        self.n += n
        return self.n - n

    def copy(self, i, src, dst, dev):
        return pltpu.make_async_remote_copy(
            src_ref=src,
            dst_ref=dst,
            send_sem=self.send.at[i],
            recv_sem=self.recv.at[i],
            device_id=dev,
            device_id_type=MESH,
        )

    def go(self, i, src, dst, dev):
        c = self.copy(i, src, dst, dev)
        c.start()
        self.open.append(c)
        return c

    def flush(self):
        for c in self.open:
            c.wait_send()
        self.open = []


def joined(ref, rows):
    return jnp.concatenate([ref[p, rows] for p in range(3)], axis=1)


def enter(pc):
    barrier = pltpu.get_barrier_semaphore()
    for dev in (pc.PAIR, pc.X, pc.Y, pc.DIAG, pc.Z(1), pc.Z(2), pc.Z(3)):
        pl.semaphore_signal(barrier, inc=1, device_id=dev, device_id_type=MESH)
    pl.semaphore_wait(barrier, 7)


def order(i):
    return i + lax.div(i, 2) * (5 - 2 * i)


def visible(krow0, kn, qcol0, qn, prefix):
    kpos = krow0 + iota((kn, qn), 0)
    qpos = qcol0 + iota((kn, qn), 1)
    ok = kpos <= qpos
    if krow0 < 512 and qcol0 < 512:
        ok = ok | (kpos < prefix)
    return ok


SEEN = (
    ((0, 512, True),),
    ((0, 512, True),),
    ((0, 512, False), (512, 256, True)),
    ((0, 512, False), (512, 256, False), (768, 256, True)),
)


def hook(table, p, qb):
    for (pp, qq), step in table.items():
        if qq == qb:
            pl.when(p == pp)(step)


def both(*steps):
    def run():
        for step in steps:
            step()

    return run


def phase_a(R, pc, w):
    f, t, z, c = pc.f, pc.t, pc.z, pc.c
    idr = R.idr[...]
    ohr = (iota((16, ROWS), 0) - 8 == idr).astype(F32)
    cnt = jnp.sum(ohr, axis=1, keepdims=True)
    hi = jnp.floor(cnt * (1.0 / 256.0))
    lane16 = iota((16, 128), 1)
    six = jnp.concatenate(
        [R.gains[...].astype(F32), R.router[...].astype(F32), jnp.zeros((10, 48), F32)], axis=0
    )
    small = jnp.concatenate([six, jnp.zeros((16, 80), F32)], axis=1)
    R.SM[f] = jnp.where(
        lane16 == 48,
        cnt - 256.0 * hi,
        jnp.where(lane16 == 49, hi, small),
    ).astype(BF)
    R.WA[z, c, pl.ds(0, 3)] = R.qkv[...]
    R.WA[z, c, 3] = R.out[...]
    enter(pc)
    own = pl.ds(pl.multiple_of(t * 512, 512), 512)
    i_tok, i_cot, i_wo, i_att = w.ids(1), w.ids(1), w.ids(1), w.ids(3)
    i_z, i_sz = w.ids(4), w.ids(4)
    i_x, i_y, i_fx, i_fy, i_sx, i_sy, i_sf = (w.ids(4) for _ in range(7))
    i_mz = w.ids(24)
    i_m = [w.ids(3) for _ in range(6)]
    i_cz, i_dz, i_cp, i_dp = w.ids(4), w.ids(4), w.ids(4), w.ids(4)

    zs = [w.go(i_sz + k, R.SM.at[f], R.SM.at[f], pc.Z(k)) for k in (1, 2, 3)]
    za = [w.go(i_z + k, R.WA.at[z, c], R.WA.at[z, c], pc.Z(k)) for k in (1, 2, 3)]
    cot_x = w.go(i_cot, R.cot, R.CT.at[own], pc.PAIR)
    tok_x = w.go(i_tok, R.tok, R.TK.at[own], pc.PAIR)

    def spread(k):
        zz = pc.zfrom(k)
        g = 4 * zz + c
        d = w.go(i_sx + k, R.SM.at[g], R.SM.at[g], pc.X)
        e = w.go(i_sy + k, R.SM.at[g], R.SM.at[g], pc.Y)
        a = w.go(i_x + k, R.WA.at[zz, c], R.WA.at[zz, c], pc.X)
        b = w.go(i_y + k, R.WA.at[zz, c], R.WA.at[zz, c], pc.Y)
        return a, b, d, e

    def forward(k, got):
        zz = pc.zfrom(k)
        a, b, d, e = got
        d.wait_recv()
        g = 4 * zz + pc.cx
        s = w.go(i_sf + k, R.SM.at[g], R.SM.at[g], pc.Y)
        a.wait_recv()
        x = w.go(
            i_fx + k,
            R.WA.at[zz, pc.cx, pl.ds(0, 2)],
            R.WA.at[zz, pc.cx, pl.ds(0, 2)],
            pc.Y,
        )
        b.wait_recv()
        y = w.go(
            i_fy + k,
            R.WA.at[zz, pc.cy, pl.ds(2, 2)],
            R.WA.at[zz, pc.cy, pl.ds(2, 2)],
            pc.X,
        )
        e.wait_recv()
        return x, y, s

    got = {0: spread(0)}
    local = [
        pltpu.make_async_copy(R.tok, R.TK.at[own], R.ls.at[0]),
        pltpu.make_async_copy(R.cot, R.CT.at[own], R.ls.at[1]),
        pltpu.make_async_copy(R.up.at[z], R.UE.at[z, c], R.ls.at[2]),
        pltpu.make_async_copy(R.down.at[z], R.DE.at[z, c], R.ls.at[3]),
    ]
    for m in local:
        m.start()
    before_or_at = (iota((ROWS, ROWS), 0) <= iota((ROWS, ROWS), 1)).astype(F32).astype(BF)
    running = mm(ohr.astype(BF), before_or_at)
    placed = jnp.sum(running * ohr, axis=0, keepdims=True) - 1.0
    key = jnp.where(placed < 256.0, idr.astype(F32) * 256.0 + placed, -1.0)
    R.KC[...] = jnp.broadcast_to(key, (128, ROWS)).T
    R.PR[...] = jnp.broadcast_to(idr.astype(F32), (128, ROWS)).T
    r = iota((512, ROWS), 0)
    want = lax.div(r, 128) * 256 + lax.rem(r, 128) + 128 * t
    R.ACT[0:512, 0:ROWS] = (key.astype(jnp.int32) == want).astype(F32).astype(BF)

    za[0].wait_recv()
    zs[0].wait_recv()
    got[1] = spread(1)
    ends = [forward(0, got[0])]
    for m in local:
        m.wait()
    cot_x.wait_recv()

    def cot_rows(e, carry):
        R.CQ[e] = mm(R.ACT[pl.ds(pl.multiple_of(e * 128, 128), 128), pl.ds(0, ROWS)], R.CT[...]).astype(BF)
        return carry

    lax.fori_loop(0, 4, cot_rows, 0)
    R.CR[z, t] = R.CQ[z]
    w.copy(i_cp, R.CR.at[z, t], R.CR.at[z, t], pc.PAIR).start()
    za[1].wait_recv()
    zs[1].wait_recv()
    got[2] = spread(2)

    def chunk(j):
        return pl.ds(pl.multiple_of(j * 512, 128), 512)

    def from_plane(j):
        out = []
        for k in (1, 3, 2):
            to, cols, i = pc.zto(k), chunk(j), i_mz + 8 * j + k
            out.append(w.copy(i, R.up.at[to, :, cols], R.UE.at[z, c, :, cols], pc.Z(k)))
            out.append(w.copy(i + 4, R.down.at[to, :, cols], R.DE.at[z, c, :, cols], pc.Z(k)))
        return out

    def moe_spread(j):
        u, d = R.UE.at[:, c, :, chunk(j)], R.DE.at[:, c, :, chunk(j)]
        return [
            w.copy(i_m[0] + j, u, u, pc.X),
            w.copy(i_m[1] + j, d, d, pc.Y),
            w.copy(i_m[2] + j, u, u, pc.Y),
            w.copy(i_m[3] + j, d, d, pc.X),
        ]

    def moe_forward(j):
        u, d = R.UE.at[:, pc.cx, :, chunk(j)], R.DE.at[:, pc.cy, :, chunk(j)]
        return [w.copy(i_m[4] + j, u, u, pc.Y), w.copy(i_m[5] + j, d, d, pc.X)]

    def start_spread(j):
        for m in from_plane(j):
            m.wait()
        for m in moe_spread(j):
            m.start()

    def start_forward(j):
        a = moe_spread(j)
        a[0].wait()
        a[1].wait()
        for m in moe_forward(j):
            m.start()

    def weights_here(j):
        for m in moe_spread(j)[2:] + moe_forward(j):
            m.wait()

    def start_plane(j):
        for m in from_plane(j):
            m.start()

    def start_cot():
        for m in cz:
            m.start()

    start_plane(0)
    cz = [w.copy(i_cz + k, R.CQ.at[pc.zto(k)], R.CR.at[z, t], pc.Z(k)) for k in (1, 3, 2)]
    ends.append(forward(1, got[1]))
    za[2].wait_recv()
    zs[2].wait_recv()
    got[3] = spread(3)
    ends.append(forward(2, got[2]))
    ends.append(forward(3, got[3]))
    start_plane(1)
    agenda = {
        (0, 3): lambda: start_spread(1),
        (1, 1): lambda: start_forward(0),
        (2, 1): both(lambda: start_spread(2), start_cot),
        (2, 3): lambda: start_forward(1),
    }

    tok_x.wait_recv()

    def factors(rows):
        x = R.TK[rows].astype(F32)
        R.STAT[rows, 0:1] = lax.rsqrt(jnp.mean(x * x, axis=1, keepdims=True) + norm_eps)

    blocks(ROWS, 128, factors)
    for x, y, s in ends:
        s.wait_recv()
    parts = [R.SM[g].astype(F32)[:, 0:48] for g in range(16)]
    vecs = jnp.concatenate(parts, axis=1)
    R.VEC[...] = vecs
    R.RW[...] = jnp.concatenate([vecs, jnp.zeros((112, WIDE), F32)], axis=0).T.astype(BF)
    total = jnp.zeros((16, 128), F32)
    for g in range(16):
        total = total + R.SM[g].astype(F32)
    counts = jnp.sum(
        jnp.where(lane16 == 48, total, jnp.where(lane16 == 49, 256.0 * total, 0.0)),
        axis=1,
        keepdims=True,
    )
    share = jnp.sum(
        jnp.where(iota((16, 128), 0) - 8 == lane16 - 2, counts, 0.0), axis=0, keepdims=True
    ) * (1.0 / (16 * ROWS))
    R.SHARE[...] = jnp.broadcast_to(share, (8, 128))

    def norm_one(rows):
        x = R.TK[rows].astype(F32)
        R.NM[rows] = (x * R.STAT[rows, 0:1] * R.VEC[0:1]).astype(BF)

    blocks(ROWS, 128, norm_one)
    for x, y, s in ends:
        x.wait_recv()
        y.wait_recv()
    wo = w.go(i_wo, R.WA.at[:, :, 3], R.WO, pc.PAIR)

    start_spread(0)
    start_plane(2)

    def project(rows):
        x = R.NM[rows]
        for s, ref in enumerate((R.QS, R.KS, R.VS)):
            y = mm(x, R.WA[:, :, s].reshape(WIDE, HALF))
            if s == 0:
                y = y.astype(BF).astype(F32) * 0.125
            for p in range(3):
                ref[p, rows] = y[:, 128 * p : 128 * p + 128].astype(BF)

    blocks(ROWS, 256, project)
    prefix = R.pre[0]

    def pair_of_heads(p, carry):
        value_t = R.VS[p].astype(F32).T.astype(BF)
        even = iota((256, 128), 1) < 64
        for qb in range(4):
            cols = pl.ds(qb * 256, 256)
            outs = []
            for i in range(2):
                q = R.QS[p, cols]
                q = jnp.where(even if i == 0 else ~even, q.astype(F32), 0.0).astype(BF)
                pieces = []
                for k0, kn, masked in SEEN[qb]:
                    s = mm(R.KS[p, pl.ds(k0, kn)], q, 1, 1)
                    if masked:
                        s = jnp.where(visible(k0, kn, qb * 256, 256, prefix), s, masked_score)
                    pieces.append(s)
                top = pieces[0].max(axis=0, keepdims=True)
                for s in pieces[1:]:
                    top = jnp.maximum(top, s.max(axis=0, keepdims=True))
                total_e = jnp.zeros((1, 256), F32)
                out = jnp.zeros((128, 256), F32)
                for (k0, kn, _), s in zip(SEEN[qb], pieces):
                    e = jnp.exp(s - top)
                    total_e = total_e + e.sum(axis=0, keepdims=True)
                    out = out + mm(value_t[:, k0 : k0 + kn], e.astype(BF))
                R.LT[p, i : i + 1, cols] = top + jnp.log(total_e)
                outs.append(out / total_e)
            merged = jnp.where(iota((128, 256), 0) < 64, outs[0], outs[1])
            R.ATO[p, cols] = merged.T.astype(BF)
            if qb == 3:
                w.copy(i_att + p, R.ATO.at[p], R.ATX.at[p], pc.PAIR).start()
            hook(agenda, p, qb)
        return carry

    lax.fori_loop(0, 3, pair_of_heads, 0)
    wo.wait_recv()
    for p in range(3):
        w.copy(i_att + p, R.ATO.at[p], R.ATX.at[p], pc.PAIR).wait()
    lane = iota((256, 128), 1)
    real = (lane >= 2) & (lane < 6)
    R.PS[...] = jnp.zeros((8, 128), F32)

    def out_block(rows):
        b = mm(joined(R.ATO, rows), R.WA[:, :, 3].reshape(WIDE, HALF), 1, 1)
        b = b + mm(joined(R.ATX, rows), R.WO[...].reshape(WIDE, HALF), 1, 1)
        h = R.TK[rows].astype(F32) + b
        R.HIDN[rows] = h
        f2 = lax.rsqrt(jnp.mean(h * h, axis=1, keepdims=True) + norm_eps)
        R.STAT[rows, 1:2] = f2
        moe = (h * f2 * R.VEC[1:2]).astype(BF)
        R.GC[rows] = moe
        logits = mm(moe, R.RW[...])
        mine = jnp.where((lane - 2).astype(F32) == R.PR[rows], logits, 0.0)
        picked = jnp.sum(jnp.where(real, mine, 0.0), axis=1, keepdims=True)
        R.STAT[rows, 2:3] = jax.nn.sigmoid(picked)
        lg = jnp.where(real, logits, masked_score)
        e = jnp.exp(lg - jnp.max(lg, axis=1, keepdims=True))
        e = jnp.where(real, e, 0.0)
        pr = e / jnp.sum(e, axis=1, keepdims=True)
        R.PR[rows] = pr
        R.PS[0:1] = R.PS[0:1] + jnp.sum(pr, axis=0, keepdims=True)

    blocks(ROWS, 256, out_block)

    def moe_rows(i, carry):
        k = order(lax.rem(i + 1, 4))
        e = pc.zto(k)
        R.CS[e] = mm(R.ACT[pl.ds(pl.multiple_of(e * 128, 128), 128), pl.ds(0, ROWS)], R.GC[...]).astype(BF)

        @pl.when(i < 3)
        def _():
            w.copy(i_dz + k, R.CS.at[e], R.DR.at[z, t], pc.Z(k)).start()

        return carry

    lax.fori_loop(0, 4, moe_rows, 0)
    R.DR[z, t] = R.CS[z]
    w.copy(i_dp, R.DR.at[z, t], R.DR.at[z, t], pc.PAIR).start()
    start_forward(2)
    w.flush()
    return i_dz, i_dp, i_cz, i_cp, weights_here


def gelu_parts(v):
    cdf = 0.5 * (1.0 + lax.erf(v * (1.0 / math.sqrt(2.0))))
    slope = cdf + v * (jnp.exp(-0.5 * v * v) * (1.0 / math.sqrt(2.0 * math.pi)))
    return v * cdf, slope


class ExpertSums:
    def __init__(self, R, pc, w):
        self.R, self.pc, self.w = R, pc, w
        self.i1, self.i2, self.i3 = w.ids(16), w.ids(8), w.ids(32)

    def cols(self, g):
        return pl.ds(pl.multiple_of(384 * g, 128), 384)

    def step_one(self, g):
        R, pc, w = self.R, self.pc, self.w
        cols, i = self.cols(g), self.i1 + 4 * g
        return [
            w.copy(i, R.UE.at[:, pc.cx, :, cols], R.RU.at[0, :, :, cols], pc.X),
            w.copy(i + 1, R.UE.at[:, pc.cd, :, cols], R.RU.at[1, :, :, cols], pc.X),
            w.copy(i + 2, R.DE.at[:, pc.cy, :, cols], R.RD.at[0, :, :, cols], pc.Y),
            w.copy(i + 3, R.DE.at[:, pc.cd, :, cols], R.RD.at[1, :, :, cols], pc.Y),
        ]

    def step_two(self, g):
        R, pc, w = self.R, self.pc, self.w
        cols, i = self.cols(g), self.i2 + 2 * g
        return [
            w.copy(i, R.UE.at[:, pc.cy, :, cols], R.RU2.at[:, :, cols], pc.Y),
            w.copy(i + 1, R.DE.at[:, pc.cx, :, cols], R.RD2.at[:, :, cols], pc.X),
        ]

    def step_three(self, g):
        R, pc, w = self.R, self.pc, self.w
        cols, i, out = self.cols(g), self.i3 + 8 * g, []
        for k in (1, 2, 3):
            to, z = pc.zto(k), pc.z
            out.append(w.copy(i + k, R.UE.at[to, pc.c, :, cols], R.ZU.at[z, :, cols], pc.Z(k)))
            out.append(w.copy(i + 4 + k, R.DE.at[to, pc.c, :, cols], R.ZD.at[z, :, cols], pc.Z(k)))
        return out

    def one(self, g):
        for m in self.step_one(g):
            m.start()

    def two(self, g):
        R, pc, cols = self.R, self.pc, self.cols(g)
        for m in self.step_one(g):
            m.wait()

        def add(zz, carry):
            R.UE[zz, pc.cy, :, cols] = R.UE[zz, pc.cy, :, cols] + R.RU[1, zz, :, cols]
            R.DE[zz, pc.cx, :, cols] = R.DE[zz, pc.cx, :, cols] + R.RD[1, zz, :, cols]
            R.UE[zz, pc.c, :, cols] = R.UE[zz, pc.c, :, cols] + R.RU[0, zz, :, cols]
            R.DE[zz, pc.c, :, cols] = R.DE[zz, pc.c, :, cols] + R.RD[0, zz, :, cols]
            return carry

        lax.fori_loop(0, 4, add, 0)
        for m in self.step_two(g):
            m.start()

    def three(self, g):
        R, pc, cols = self.R, self.pc, self.cols(g)
        for m in self.step_two(g):
            m.wait()

        def add(zz, carry):
            R.UE[zz, pc.c, :, cols] = R.UE[zz, pc.c, :, cols] + R.RU2[zz, :, cols]
            R.DE[zz, pc.c, :, cols] = R.DE[zz, pc.c, :, cols] + R.RD2[zz, :, cols]
            return carry

        lax.fori_loop(0, 4, add, 0)
        for m in self.step_three(g):
            m.start()

    def last(self):
        R, pc = self.R, self.pc
        R.ZU[pc.z] = R.UE[pc.z, pc.c]
        R.ZD[pc.z] = R.DE[pc.z, pc.c]
        out = []
        for g in range(4):
            for m in self.step_three(g):
                m.wait()
        for g in (0, 1):
            cols = pl.ds(768 * g, 768)
            for j, (got, to) in enumerate(((R.ZU, R.up_grad), (R.ZD, R.down_grad))):
                held = R.HIDN.at[pl.ds(192 * (2 * g + j), 192)].reshape(4, 48, 768)
                held[...] = got[:, :, cols].astype(F32)
                m = pltpu.make_async_copy(held, to.at[:, :, cols], R.ls.at[2 * g + j])
                m.start()
                out.append(m)
        return out


class AttentionSums:
    def __init__(self, R, pc, w):
        self.R, self.pc, self.w = R, pc, w
        self.i1, self.i2, self.i3 = w.ids(16), w.ids(8), w.ids(16)
        self.low, self.high = pl.ds(0, 2), pl.ds(2, 2)

    def step_one(self, n):
        R, pc, w, i = self.R, self.pc, self.w, self.i1 + 4 * n
        return [
            w.copy(i, R.AG.at[n, self.low, pc.cx], R.RA.at[n, 0], pc.X),
            w.copy(i + 1, R.AG.at[n, self.low, pc.cd], R.RA.at[n, 1], pc.X),
            w.copy(i + 2, R.AG.at[n, self.high, pc.cy], R.RB.at[n, 0], pc.Y),
            w.copy(i + 3, R.AG.at[n, self.high, pc.cd], R.RB.at[n, 1], pc.Y),
        ]

    def step_two(self, n):
        R, pc, w, i = self.R, self.pc, self.w, self.i2 + 2 * n
        return [
            w.copy(i, R.AG.at[n, self.low, pc.cy], R.RA2.at[n], pc.Y),
            w.copy(i + 1, R.AG.at[n, self.high, pc.cx], R.RB2.at[n], pc.X),
        ]

    def step_three(self, n):
        R, pc, w, i = self.R, self.pc, self.w, self.i3 + 4 * n
        return [
            w.copy(i + k, R.AG.at[n, pc.zto(k), pc.c], R.ZA.at[n, pc.z], pc.Z(k))
            for k in (1, 2, 3)
        ]

    def one(self, n):
        for m in self.step_one(n):
            m.start()

    def two(self, n):
        R, pc = self.R, self.pc
        for m in self.step_one(n):
            m.wait()
        for j in range(2):
            R.AG[n, j, pc.cy] = R.AG[n, j, pc.cy] + R.RA[n, 1, j]
            R.AG[n, 2 + j, pc.cx] = R.AG[n, 2 + j, pc.cx] + R.RB[n, 1, j]
            R.AG[n, j, pc.c] = R.AG[n, j, pc.c] + R.RA[n, 0, j]
            R.AG[n, 2 + j, pc.c] = R.AG[n, 2 + j, pc.c] + R.RB[n, 0, j]
        for m in self.step_two(n):
            m.start()

    def three(self, n):
        R, pc = self.R, self.pc
        for m in self.step_two(n):
            m.wait()
        for j in range(2):
            R.AG[n, j, pc.c] = R.AG[n, j, pc.c] + R.RA2[n, j]
            R.AG[n, 2 + j, pc.c] = R.AG[n, 2 + j, pc.c] + R.RB2[n, j]
        for m in self.step_three(n):
            m.start()

    def last(self, n):
        R, pc = self.R, self.pc
        R.ZA[n, pc.z] = R.AG[n, pc.z, pc.c]
        for m in self.step_three(n):
            m.wait()
        total = R.ZA[n, 0].astype(F32)
        for zz in range(1, 4):
            total = total + R.ZA[n, zz].astype(F32)
        for j in range(3):
            block = total[48 * j : 48 * j + 48]
            if n == 0:
                R.out_grad[:, 128 * j : 128 * j + 128] = block
            else:
                R.qkv_grad[j, :, 128 * (n - 1) : 128 * n] = block


def phase_b(R, pc, w, i_dz, i_dp, i_cz, i_cp, weights_here):
    f, t, z, c, o = pc.f, pc.t, pc.z, pc.c, pc.o
    i_xe, i_xg = w.ids(4), w.ids(4)
    i_rg, i_re, i_rgp, i_rep = w.ids(4), w.ids(4), w.ids(1), w.ids(1)
    lane = iota((256, 128), 1)
    row = jnp.sum(
        jnp.where(iota((16, WIDE), 0) == 2 + z, R.VEC[...], 0.0), axis=0, keepdims=True
    )
    R.RGR[...] = jnp.zeros((16, WIDE), F32)

    def to_plane(s):
        return {"fsdp": 4 * s + c, "tensor": t}

    def rows_in(k):
        return w.copy(i_dz + k, R.CS.at[pc.zto(k)], R.DR.at[z, t], pc.Z(k))

    def cot_in(k):
        return w.copy(i_cz + k, R.CQ.at[pc.zto(k)], R.CR.at[z, t], pc.Z(k))

    def rows_pair(k):
        s = pc.zfrom(k)
        return (
            w.copy(i_dp + k, R.DR.at[s, t], R.DR.at[s, t], pc.PAIR),
            w.copy(i_cp + k, R.CR.at[s, t], R.CR.at[s, t], pc.PAIR),
        )

    def pair_sums(k):
        s = pc.zfrom(k)
        return (
            w.copy(i_xg + k, R.PG.at[s], R.XG.at[s], pc.PAIR),
            w.copy(i_xe + k, R.PE.at[s], R.XE.at[s], pc.PAIR),
        )

    def home(k):
        s = pc.zfrom(k)
        return w.copy(i_rg + k, R.XG.at[s], R.RG.at[z, t], to_plane(s))

    def home_out(k):
        s = pc.zfrom(k)
        return w.copy(i_re + k, R.XE.at[s], R.RE.at[z, t], to_plane(s))

    def finish(k):
        s = pc.zfrom(k)
        for m in pair_sums(k):
            m.wait()
        eo = R.EOO[s] + R.XE[s].astype(F32)
        gate = R.STAT[pl.ds(pl.multiple_of(s * 256 + t * 128, 128), 128), 3:4]
        gate_grad = jnp.sum(R.CR[s, t].astype(F32) * eo, axis=1, keepdims=True)
        gs = gate_grad * gate * (1.0 - gate)
        R.RGR[0:1] += jnp.sum(gs * R.DR[s, t].astype(F32), axis=0, keepdims=True)
        R.XG[s] = (R.GMO[s] + R.XG[s].astype(F32) + gs * row).astype(BF)
        R.XE[s] = eo.astype(BF)

    def source(i, carry):
        k = order(i)
        s = pc.zfrom(k)
        rows = pl.ds(pl.multiple_of(s * 256, 256), 256)

        for m in rows_pair(k):
            m.wait()
        x = R.DR[s].reshape(256, WIDE)
        logits = mm(x, R.RW[...])
        gate = jax.nn.sigmoid(
            jnp.sum(jnp.where(lane == 2 + z, logits, 0.0), axis=1, keepdims=True)
        )
        R.STAT[rows, 3:4] = gate
        R.GC[rows] = (gate * R.CR[s].reshape(256, WIDE).astype(F32)).astype(BF)

        def hidden_units(j, carry):
            @pl.when(i == 0)
            def _():
                weights_here(j)

            cols = pl.ds(pl.multiple_of(j * 512, 128), 512)
            up = R.UE[:, :, :, cols].reshape(WIDE, 512)
            down = R.DE[:, :, :, cols].reshape(WIDE, 512)
            act, slope = gelu_parts(mm(R.DR[s].reshape(256, WIDE), up))
            act = act.astype(BF)
            gb = (mm(R.GC[rows], down) * slope).astype(BF)
            R.ACT[rows, cols] = act
            R.GB[rows, cols] = gb
            return carry

        lax.fori_loop(0, 3, hidden_units, 0)
        @pl.when(i < 3)
        def _():
            after = order(i + 1)
            cot_in(after).wait()
            rows_pair(after)[1].start()
            rows_in(after).wait()
            rows_pair(after)[0].start()

        up, down = R.UE[...].reshape(WIDE, HID), R.DE[...].reshape(WIDE, HID)
        R.GMB[...] = mm(R.GB[rows], up, 1, 1).reshape(2, 128, WIDE)
        R.PG[s] = R.GMB[o].astype(BF)
        pair_sums(k)[0].start()
        R.GMO[s] = R.GMB[t]
        R.GMB[...] = mm(R.ACT[rows], down, 1, 1).reshape(2, 128, WIDE)
        R.PE[s] = R.GMB[o].astype(BF)
        pair_sums(k)[1].start()
        R.EOO[s] = R.GMB[t]

        @pl.when(i > 0)
        def _():
            last = order(i - 1)
            finish(last)

            @pl.when(i > 1)
            def _():
                home(last).start()

        return carry

    lax.fori_loop(0, 4, source, 0)
    finish(2)
    home(2).start()
    R.RG[z, t] = R.XG[z]
    R.RE[z, t] = R.XE[z]
    R.RGR[...] = jnp.where(iota((16, WIDE), 0) == 2 + z, R.RGR[0:1], 0.0)
    sums = ExpertSums(R, pc, w)
    DR = R.DR.reshape(ROWS, WIDE)

    def weight_grads(i, carry):
        cols = pl.ds(pl.multiple_of(i * 384, 128), 384)
        R.UE[:, :, :, cols] = mm(DR[...], R.GB[:, cols], 0, 0).astype(BF).reshape(4, 4, 48, 384)
        R.DE[:, :, :, cols] = mm(R.GC[...], R.ACT[:, cols], 0, 0).astype(BF).reshape(4, 4, 48, 384)


        @pl.when(i < 2)
        def _():
            for m in sums.step_one(i):
                m.start()

        return carry

    lax.fori_loop(0, 4, weight_grads, 0)
    share, vec = R.SHARE[0:1], R.VEC[...]
    R.SB[...] = jnp.zeros((16, WIDE), F32)

    def prepared(i, carry):
        rows = pl.ds(pl.multiple_of(i * 256, 256), 256)
        R.ACT[rows, pl.ds(0, ROWS)] = pick_rows(R.KC[rows])
        pr = R.PR[rows]
        mixed = jnp.sum(pr * share, axis=1, keepdims=True)
        aux = (balance_weight * 4.0 / (16 * ROWS)) * pr * (share - mixed)
        aux = aux[:, 0:16].astype(BF)
        R.GH[rows] = mm(aux, vec.astype(BF))
        mine = jnp.where(lax.div(i, 2) == t, 1.0, 0.0)
        moe = (R.HIDN[rows] * R.STAT[rows, 1:2] * vec[1:2]).astype(BF)
        R.SB[...] += mine * mm(aux, moe, 0, 0)
        return carry

    lax.fori_loop(0, 4, prepared, 0)
    sums.two(0)
    sums.one(2)
    for k in (1, 3, 2):
        home(k).wait()
    back = w.go(i_rgp, R.RG.at[:, t], R.RG.at[:, t], pc.PAIR)
    for k in (1, 3, 2):
        home_out(k).start()
    back.wait_recv()
    return sums, home_out, i_rep


def pick_rows(key):
    keys = jnp.concatenate([key] * 8, axis=1)
    return (keys == iota((key.shape[0], ROWS), 1).astype(F32)).astype(F32).astype(BF)


def phase_c(R, pc, w, sums, home_out, i_rep):
    f, t, z, c, o = pc.f, pc.t, pc.z, pc.c, pc.o
    att = AttentionSums(R, pc, w)
    i_n = w.ids(1)
    i_sp, i_sc, i_sz = w.ids(1), w.ids(4), w.ids(4)
    own = pl.ds(pl.multiple_of(t * 512, 512), 512)
    GH, GN = R.GH, R.EOO.reshape(512, WIDE)
    RG, RE = R.RG.reshape(ROWS, WIDE), R.RE.reshape(ROWS, WIDE)
    GBR = R.GC
    share = R.SHARE[0:1]
    vec = R.VEC[...]
    head = iota((24, HALF), 0)
    head = jnp.where(lax.rem(head, 8) < 2, 2 * lax.div(head, 8) + lax.rem(head, 8), -1)
    pick_head = (head == lax.div(iota((24, HALF), 1), 64)).astype(F32).astype(BF)

    def residual(i, carry):
        rows = pl.ds(pl.multiple_of(i * 256, 256), 256)
        gm = mm(R.ACT[rows, pl.ds(0, ROWS)], RG[...]) + R.GH[rows]
        mine = jnp.where(lax.div(i, 2) == t, 1.0, 0.0)
        h, f2 = R.HIDN[rows], R.STAT[rows, 1:2]
        g = gm * vec[1:2]
        inner = jnp.mean(g * h, axis=1, keepdims=True)
        gh = R.CT[rows].astype(F32) + f2 * (g - h * (f2 * f2 * inner))
        R.G2[0:1] += mine * jnp.sum(gm * h * f2, axis=0, keepdims=True)
        GH[rows] = gh
        low = gh.astype(BF)
        GBR[rows] = low
        ga = mm(low, R.WA[:, :, 3].reshape(WIDE, HALF)).astype(BF)
        for p in range(3):
            R.ATX[p, rows] = ga[:, 128 * p : 128 * p + 128]
        prod = ga.astype(F32) * joined(R.ATO, rows).astype(F32)
        top = prod.astype(BF)
        rest = (prod - top.astype(F32)).astype(BF)
        dd = mm(pick_head, top, 1, 1) + mm(pick_head, rest, 1, 1)
        for p in range(3):
            R.DD[p, :, rows] = dd[8 * p : 8 * p + 8]

        @pl.when(i == 2)
        def _():
            sums.two(1)
            sums.one(3)

        return carry

    R.G2[...] = jnp.zeros((8, WIDE), F32)
    lax.fori_loop(0, 4, residual, 0)
    part = jnp.where(iota((16, WIDE), 0) == 1, R.G2[0:1], 0.0)
    sums6 = jnp.concatenate([0.5 * R.PS[0:1], jnp.zeros((1, WIDE - 128), F32)], axis=1)
    keep = (iota((16, WIDE), 0) >= 2) & (iota((16, WIDE), 0) < 6)
    R.SB[...] = (
        jnp.where(keep, R.SB[...] + R.RGR[...], 0.0)
        + part
        + jnp.where(iota((16, WIDE), 0) == 6, sums6, 0.0)
    )

    def place(n, grad):
        for j in range(3):
            block = grad[:, 128 * j : 128 * j + 128].astype(BF).reshape(4, 4, 48, 128)
            R.AG[n, :, :, pl.ds(48 * j, 48)] = block

    place(0, mm(GBR[...], joined(R.ATO, pl.ds(0, ROWS)), 0, 0))

    def outputs_pair():
        return w.copy(i_rep, R.RE.at[:, t], R.RE.at[:, t], pc.PAIR)

    def outputs_home():
        for k in (1, 2, 3):
            home_out(k).wait()
        outputs_pair().start()


    agenda = {
        (0, 1): both(lambda: sums.two(2), lambda: sums.three(0)),
        (0, 3): lambda: sums.three(1),
        (1, 2): lambda: sums.two(3),
        (1, 3): lambda: att.one(0),
        (2, 0): lambda: sums.three(2),
        (2, 1): outputs_home,
        (2, 2): lambda: sums.three(3),
        (2, 3): lambda: att.two(0),
    }
    prefix = R.pre[0]

    def pair_of_heads(p, carry):
        key_t = R.KS[p].astype(F32).T.astype(BF)
        R.DK[...] = jnp.zeros((ROWS, 128), F32)
        R.DV[...] = jnp.zeros((ROWS, 128), F32)
        even = iota((256, 128), 1) < 64
        for qb in range(4):
            cols = pl.ds(qb * 256, 256)
            outs = []
            for i in range(2):
                side = even if i == 0 else ~even
                q = jnp.where(side, R.QS[p, cols].astype(F32), 0.0).astype(BF)
                do = jnp.where(side, R.ATX[p, cols].astype(F32), 0.0).astype(BF)
                lt, dd = R.LT[p, i : i + 1, cols], R.DD[p, i : i + 1, cols]
                dq = jnp.zeros((128, 256), F32)
                for kb in range(max(2, qb + 1)):
                    keys = pl.ds(kb * 256, 256)
                    s = mm(R.KS[p, keys], q, 1, 1)
                    if kb == qb or qb < 2:
                        ok = visible(kb * 256, 256, qb * 256, 256, prefix)
                        s = jnp.where(ok, s, masked_score)
                    prob = jnp.exp(s - lt)
                    ds = prob * (mm(R.VS[p, keys], do, 1, 1) - dd)
                    ds = ds.astype(BF)
                    R.DV[keys] += mm(prob.astype(BF), do)
                    R.DK[keys] += mm(ds, q)
                    dq = dq + mm(key_t[:, kb * 256 : kb * 256 + 256], ds)
                outs.append(dq)
            merged = jnp.where(iota((128, 256), 0) < 64, outs[0], outs[1])
            R.QS[p, cols] = (merged * 0.125).T.astype(BF)
            hook(agenda, p, qb)
        R.KS[p] = R.DK[...].astype(BF)
        R.VS[p] = R.DV[...].astype(BF)
        three = jnp.concatenate([R.QS[p], R.KS[p], R.VS[p]], axis=1)
        place(p + 1, mm(R.NM[...], three, 0, 0))

        @pl.when(p == 1)
        def _():
            att.one(1)

        @pl.when(p > 0)
        def _():
            att.one(p + 1)

        return carry

    lax.fori_loop(0, 3, pair_of_heads, 0)
    GP = (R.QS, R.KS, R.VS)

    XS, XN, BO = (r.reshape(512, WIDE) for r in (R.CS, R.XG, R.PE))

    R.G2[...] = jnp.zeros((8, WIDE), F32)

    def normed_grad(i, carry):
        mine = pl.ds(pl.multiple_of(i * 256, 256), 256)

        def half(start):
            rows = pl.ds(pl.multiple_of(start * 512 + i * 256, 256), 256)
            acc = jnp.zeros((256, WIDE), F32)
            for s in range(3):
                acc = acc + mm(joined(GP[s], rows), R.WA[:, :, s].reshape(WIDE, HALF), 1, 1)
            x = R.TK[rows].astype(F32) * R.STAT[rows, 0:1]
            R.G2[0:1] += jnp.sum(acc * x, axis=0, keepdims=True)
            return acc

        XS[mine] = half(o).astype(BF)
        GN[mine] = half(t)
        return carry

    w.flush()
    lax.fori_loop(0, 2, normed_grad, 0)
    xn = w.go(i_n, XS, XN, pc.PAIR)
    R.SB[0:1] = R.G2[0:1]
    sp = w.go(i_sp, R.SB, R.SP, pc.PAIR)
    att.two(1)
    att.three(0)
    outputs_pair().wait()

    def block_rows(i, carry):
        rows = pl.ds(pl.multiple_of(i * 256, 256), 256)
        full = pl.ds(pl.multiple_of(t * 512 + i * 256, 256), 256)
        eo = mm(R.ACT[full, pl.ds(0, ROWS)], RE[...])
        BO[rows] = (R.HIDN[full] + R.STAT[full, 2:3] * eo).astype(BF)
        return carry

    lax.fori_loop(0, 2, block_rows, 0)
    out_b = pltpu.make_async_copy(BO, R.block_out, R.ls.at[1])
    out_b.start()
    att.two(2)
    att.three(1)
    sp.wait_recv()
    R.SC[c] = R.SB[...] + R.SP[...]
    sc = [
        w.go(i_sc, R.SC.at[c], R.SC.at[c], pc.X),
        w.go(i_sc + 1, R.SC.at[c], R.SC.at[c], pc.Y),
        w.go(i_sc + 2, R.SC.at[c], R.SC.at[c], pc.DIAG),
    ]
    xn.wait_recv()

    def input_grad(i, carry):
        rows = pl.ds(pl.multiple_of(i * 128, 128), 128)
        full = pl.ds(pl.multiple_of(t * 512 + i * 128, 128), 128)
        gn = GN[rows] + XN[rows].astype(F32)
        x, f1 = R.TK[full].astype(F32), R.STAT[full, 0:1]
        g = gn * R.VEC[0:1]
        inner = jnp.mean(g * x, axis=1, keepdims=True)
        GH[full] = GH[full] + f1 * (g - x * (f1 * f1 * inner))
        return carry

    lax.fori_loop(0, 4, input_grad, 0)
    out_t = pltpu.make_async_copy(GH.at[own], R.tokens_grad, R.ls.at[0])
    out_t.start()
    att.two(3)
    att.three(2)
    for m in sc:
        m.wait_recv()
    R.SZ[z] = R.SC[0] + R.SC[1] + R.SC[2] + R.SC[3]
    sz = [w.go(i_sz + k, R.SZ.at[z], R.SZ.at[z], pc.Z(k)) for k in (1, 2, 3)]
    att.three(3)
    out_t.wait()
    out_b.wait()
    written = sums.last()
    for n in range(3):
        att.last(n)
    for m in sz:
        m.wait_recv()
    total = R.SZ[0] + R.SZ[1] + R.SZ[2] + R.SZ[3]
    probs = total[6:7, 0:128]
    R.balance[...] = (4.0 / (16 * ROWS)) * jnp.sum(share * probs, axis=1, keepdims=True)
    column = (iota((WIDE, 128), 0) == 48 * f + iota((WIDE, 128), 1)).astype(F32).astype(BF)
    mine = jnp.zeros((16, 128), F32)
    for _ in range(3):
        top = total.astype(BF)
        mine = mine + mm(top, column)
        total = total - top.astype(F32)
    R.gains_grad[...] = mine[0:2, 0:48]
    R.router_grad[...] = mine[2:6, 0:48]
    att.last(3)
    for m in written:
        m.wait()
    w.flush()


OUTS = {
    "block_out": ((512, WIDE), BF),
    "tokens_grad": ((512, WIDE), F32),
    "gains_grad": ((2, 48), F32),
    "qkv_grad": ((3, 48, HALF), F32),
    "out_grad": ((48, HALF), F32),
    "router_grad": ((4, 48), F32),
    "up_grad": ((4, 48, HID), F32),
    "down_grad": ((4, 48, HID), F32),
    "balance": ((1, 1), F32),
}
SCRATCH = {
    "STAT": ((ROWS, 128), F32),
    "ATO": ((3, ROWS, 128), BF),
    "ATX": ((3, ROWS, 128), BF),
    "PG": ((4, 128, WIDE), BF),
    "CQ": ((4, 128, WIDE), BF),
    "PE": ((4, 128, WIDE), BF),
    "GMB": ((2, 128, WIDE), F32),
    "EOO": ((4, 128, WIDE), F32),
    "GMO": ((4, 128, WIDE), F32),
    "GH": ((ROWS, WIDE), F32),
    "ACT": ((ROWS, HID), BF),
    "GB": ((ROWS, HID), BF),
    "TK": ((ROWS, WIDE), BF),
    "CT": ((ROWS, WIDE), BF),
    "WA": ((4, 4, 4, 48, HALF), BF),
    "WO": ((4, 4, 48, HALF), BF),
    "UE": ((4, 4, 48, HID), BF),
    "DE": ((4, 4, 48, HID), BF),
    "KC": ((ROWS, 128), F32),
    "CR": ((4, 2, 128, WIDE), BF),
    "DR": ((4, 2, 128, WIDE), BF),
    "VEC": ((16, WIDE), F32),
    "RW": ((WIDE, 128), BF),
    "SHARE": ((8, 128), F32),
    "NM": ((ROWS, WIDE), BF),
    "QS": ((3, ROWS, 128), BF),
    "KS": ((3, ROWS, 128), BF),
    "VS": ((3, ROWS, 128), BF),
    "LT": ((3, 8, ROWS), F32),
    "HIDN": ((ROWS, WIDE), F32),
    "PR": ((ROWS, 128), F32),
    "PS": ((8, 128), F32),
    "SM": ((16, 16, 128), BF),
    "CS": ((4, 128, WIDE), BF),
    "GC": ((ROWS, WIDE), BF),
    "XE": ((4, 128, WIDE), BF),
    "XG": ((4, 128, WIDE), BF),
    "RG": ((4, 2, 128, WIDE), BF),
    "RE": ((4, 2, 128, WIDE), BF),
    "RGR": ((16, WIDE), F32),
    "RU": ((2, 4, 48, HID), BF),
    "RD": ((2, 4, 48, HID), BF),
    "RU2": ((4, 48, HID), BF),
    "RD2": ((4, 48, HID), BF),
    "ZU": ((4, 48, HID), BF),
    "ZD": ((4, 48, HID), BF),
    "DD": ((3, 8, ROWS), F32),
    "DK": ((ROWS, 128), F32),
    "DV": ((ROWS, 128), F32),
    "AG": ((4, 4, 4, 144, 128), BF),
    "RA": ((4, 2, 2, 144, 128), BF),
    "RB": ((4, 2, 2, 144, 128), BF),
    "RA2": ((4, 2, 144, 128), BF),
    "RB2": ((4, 2, 144, 128), BF),
    "ZA": ((4, 4, 144, 128), BF),
    "G2": ((8, WIDE), F32),
    "SB": ((16, WIDE), F32),
    "SP": ((16, WIDE), F32),
    "SC": ((4, 16, WIDE), F32),
    "SZ": ((4, 16, WIDE), F32),
}
INS = ("tok", "cot", "pre", "idr", "gains", "qkv", "out", "router", "up", "down")
IN_HBM = ("tok", "cot", "up", "down")
OUT_HBM = ("block_out", "tokens_grad", "up_grad", "down_grad")
SEMAPHORES = 256


def fused(args):
    names = INS + tuple(OUTS) + tuple(SCRATCH) + ("ss", "rs", "ls")

    def body(*refs):
        R = types.SimpleNamespace(**dict(zip(names, refs)))
        pc = Place()
        w = Wire(R.ss, R.rs)
        phase_c(R, pc, w, *phase_b(R, pc, w, *phase_a(R, pc, w)))

    vm = pl.BlockSpec(memory_space=pltpu.VMEM)
    hbm = pl.BlockSpec(memory_space=pl.ANY)
    sm = pl.BlockSpec(memory_space=pltpu.SMEM)
    dma = pltpu.SemaphoreType.DMA
    return pl.pallas_call(
        body,
        out_shape=[jax.ShapeDtypeStruct(s, d) for s, d in OUTS.values()],
        in_specs=[sm if n == "pre" else hbm if n in IN_HBM else vm for n in INS],
        out_specs=[hbm if n in OUT_HBM else vm for n in OUTS],
        scratch_shapes=[pltpu.VMEM(s, d) for s, d in SCRATCH.values()]
        + [dma((SEMAPHORES,)), dma((SEMAPHORES,)), dma((4,))],
        compiler_params=pltpu.CompilerParams(
            collective_id=1, has_side_effects=True, vmem_limit_bytes=63 << 20
        ),
        name="block",
    )(*args)


def copy_out(arrays):
    n = len(arrays)

    def body(*refs):
        src, dst, held, sem = refs[:n], refs[n : 2 * n], refs[2 * n : 3 * n], refs[3 * n]
        come = [pltpu.make_async_copy(src[i], held[i], sem.at[0, i]) for i in range(n)]
        go = [pltpu.make_async_copy(held[i], dst[i], sem.at[1, i]) for i in range(n)]
        for m in come:
            m.start()
        for i in range(n):
            come[i].wait()
            go[i].start()
        for m in go:
            m.wait()

    hbm = pl.BlockSpec(memory_space=pl.ANY)
    return pl.pallas_call(
        body,
        out_shape=[jax.ShapeDtypeStruct(a.shape, a.dtype) for a in arrays],
        in_specs=[hbm] * n,
        out_specs=[hbm] * n,
        scratch_shapes=[pltpu.VMEM(a.shape, a.dtype) for a in arrays]
        + [pltpu.SemaphoreType.DMA((2, n))],
        name="outputs",
    )(*arrays)


def prepare(
    tokens, cotangent, prefix_len, expert_ids, norm_gains, qkv_weight, out_weight, router_weight, up_weight, down_weight
):
    ids = expert_ids.reshape(1, ROWS)
    return (tokens, cotangent, prefix_len, ids, norm_gains, qkv_weight, out_weight, router_weight, up_weight, down_weight)


def fast_device(*args):
    outs = copy_out(fused(prepare(*args)))
    return tuple(outs[:8]) + (outs[8].reshape(()),)


HEAD = 64
EXPERTS = 4
SEQ = 1024
CAP = 256


highest = lax.Precision.HIGHEST


def softmax_rows(scores):
    row_max = jnp.max(scores, axis=-1, keepdims=True)
    shifted = jnp.exp(scores - row_max)
    return shifted / jnp.sum(shifted, axis=-1, keepdims=True)


def slot_index(group_ids):
    onehot = (group_ids[:, None] == jnp.arange(EXPERTS, dtype=jnp.int32)[None, :]).astype(jnp.int32)
    rows = group_ids.shape[0]
    earlier = lax.broadcasted_iota(jnp.int32, (rows, rows), 1) <= lax.broadcasted_iota(
        jnp.int32, (rows, rows), 0
    )
    running = jnp.dot(
        earlier.astype(jnp.bfloat16),
        onehot.astype(jnp.bfloat16),
        preferred_element_type=jnp.float32,
    ).astype(jnp.int32)
    placed = jnp.sum(running * onehot, axis=1) - 1
    return jnp.where(placed < CAP, group_ids * CAP + placed, EXPERTS * CAP)


def rms_factor(values):
    return lax.rsqrt(jnp.mean(values * values, axis=-1, keepdims=True) + norm_eps)


def norm_back(grad_out, inputs, factor, gain):
    scaled = grad_out * gain
    row_inner = jnp.mean(scaled * inputs, axis=-1, keepdims=True)
    grad_in = factor * (scaled - inputs * factor * factor * row_inner)
    grad_gain = jnp.sum(grad_out * inputs * factor, axis=0)
    return (grad_in, grad_gain)


def gelu_slope(values):
    cumulative = 0.5 * (1.0 + lax.erf(values / math.sqrt(2.0)))
    density = jnp.exp(-0.5 * values * values) / math.sqrt(2.0 * math.pi)
    return cumulative + values * density


def block_scores(query_block, key_seq, offset, prefix, score_scale):
    scores = (
        jnp.einsum("qhd,khd->hqk", query_block, key_seq, preferred_element_type=jnp.float32)
        * score_scale
    )
    shape_pair = (query_block.shape[0], key_seq.shape[0])
    row_pos = offset + lax.broadcasted_iota(jnp.int32, shape_pair, 0)
    col_pos = lax.broadcasted_iota(jnp.int32, shape_pair, 1)
    allowed = (col_pos <= row_pos) | (col_pos < prefix)
    return jnp.where(allowed[None], scores, masked_score)


def attend(project, prefix_len, score_scale):
    group_rows = project.shape[0]
    full_width = project.shape[2]
    heads_here = full_width // HEAD
    block_rows = min(512, SEQ)
    shaped = project.reshape(group_rows, 3, heads_here, HEAD)
    query_all = shaped[:, 0]
    key_all = shaped[:, 1]
    value_all = shaped[:, 2]

    def one_block(number):
        row_start = number * block_rows
        seq_number = row_start // SEQ
        seq_start = seq_number * SEQ
        query_block = lax.dynamic_slice_in_dim(query_all, row_start, block_rows, 0)
        scores = block_scores(
            query_block, key_all, row_start - seq_start, prefix_len[seq_number], score_scale
        )
        row_max = jnp.max(scores, axis=-1, keepdims=True)
        shifted = jnp.exp(scores - row_max)
        row_total = jnp.sum(shifted, axis=-1, keepdims=True)
        prob_low = (shifted / row_total).astype(jnp.bfloat16)
        result = jnp.einsum("hqk,khd->qhd", prob_low, value_all, preferred_element_type=jnp.float32)
        return (
            result.reshape(block_rows, full_width).astype(jnp.bfloat16),
            (row_max + jnp.log(row_total))[..., 0],
        )

    outputs, log_total = lax.map(one_block, jnp.arange(group_rows // block_rows, dtype=jnp.int32))
    return (outputs.reshape(group_rows, full_width), log_total)


def attend_back(project, grad_att, log_total, prefix_len, score_scale):
    group_rows = project.shape[0]
    full_width = project.shape[2]
    heads_here = full_width // HEAD
    block_rows = min(512, SEQ)
    shaped = project.reshape(group_rows, 3, heads_here, HEAD)
    query_all = shaped[:, 0]
    key_all = shaped[:, 1]
    value_all = shaped[:, 2]
    grad_shaped = grad_att.reshape(group_rows, heads_here, HEAD)

    def one_block(carried, number):
        grad_keys, grad_values = carried
        row_start = number * block_rows
        seq_number = row_start // SEQ
        seq_start = seq_number * SEQ
        query_block = lax.dynamic_slice_in_dim(query_all, row_start, block_rows, 0)
        grad_block = lax.dynamic_slice_in_dim(grad_shaped, row_start, block_rows, 0)
        scores = block_scores(
            query_block, key_all, row_start - seq_start, prefix_len[seq_number], score_scale
        )
        prob_block = jnp.exp(scores - log_total[number][..., None])
        prob_low = prob_block.astype(jnp.bfloat16)
        grad_prob = jnp.einsum(
            "qhd,khd->hqk", grad_block, value_all, preferred_element_type=jnp.float32
        )
        value_part = jnp.einsum(
            "hqk,qhd->khd", prob_low, grad_block, preferred_element_type=jnp.float32
        )
        row_inner = jnp.sum(prob_block * grad_prob, axis=-1, keepdims=True)
        grad_scores = (prob_block * (grad_prob - row_inner)).astype(jnp.bfloat16)
        query_grad = (
            jnp.einsum("hqk,khd->qhd", grad_scores, key_all, preferred_element_type=jnp.float32)
            * score_scale
        )
        key_part = (
            jnp.einsum("hqk,qhd->khd", grad_scores, query_block, preferred_element_type=jnp.float32)
            * score_scale
        )
        old_keys = grad_keys
        grad_keys = old_keys + key_part
        old_values = grad_values
        grad_values = old_values + value_part
        return ((grad_keys, grad_values), query_grad)

    zero_rows = jnp.zeros((group_rows, heads_here, HEAD), jnp.float32)
    final, grad_query = lax.scan(
        one_block, (zero_rows, zero_rows), jnp.arange(group_rows // block_rows, dtype=jnp.int32)
    )
    grad_keys, grad_values = final
    stacked = jnp.stack(
        [
            grad_query.reshape(group_rows, full_width),
            grad_keys.reshape(group_rows, full_width),
            grad_values.reshape(group_rows, full_width),
        ],
        axis=1,
    )
    return stacked.astype(jnp.bfloat16)


def low_scatter(grad):
    return lax.psum_scatter(
        grad.astype(jnp.bfloat16), "fsdp", scatter_dimension=1, tiled=True
    ).astype(jnp.float32)


def per_device(
    tokens,
    cotangent,
    prefix_len,
    expert_ids,
    norm_gains,
    qkv_weight,
    out_weight,
    router_weight,
    up_weight,
    down_weight,
):
    tensor_size = lax.axis_size("tensor")
    fsdp_size = lax.axis_size("fsdp")
    own_rows = tokens.shape[0]
    group_rows = own_rows * tensor_size
    all_tokens = group_rows * fsdp_size
    own_start = lax.axis_index("tensor") * own_rows
    score_scale = 1.0 / math.sqrt(HEAD)
    gains_full, qkv_full, out_stack = (
        lax.all_gather(norm_gains, "fsdp", axis=1, tiled=True),
        lax.all_gather(qkv_weight, "fsdp", axis=1, tiled=True),
        lax.all_gather(out_weight[None], "fsdp", axis=1, tiled=True),
    )
    out_full = out_stack[0]
    router_full, up_full, down_full = (
        lax.all_gather(router_weight, "fsdp", axis=1, tiled=True),
        lax.all_gather(up_weight, "fsdp", axis=1, tiled=True),
        lax.all_gather(down_weight, "fsdp", axis=1, tiled=True),
    )
    inputs = lax.all_gather(tokens, "tensor", axis=0, tiled=True)
    input_float = inputs.astype(jnp.float32)
    factor_one = rms_factor(input_float)
    gain_one = gains_full[0].astype(jnp.float32)
    normed_one = (input_float * factor_one * gain_one).astype(jnp.bfloat16)
    project = jnp.einsum(
        "td,sdw->tsw", normed_one, qkv_full, preferred_element_type=jnp.float32
    ).astype(jnp.bfloat16)
    attended, log_total = attend(project, prefix_len, score_scale)
    branch = lax.psum_scatter(
        lax.dot_general(
            attended, out_full, (((1,), (1,)), ((), ())), preferred_element_type=jnp.float32
        ),
        "tensor",
        scatter_dimension=0,
        tiled=True,
    )
    hidden_own = tokens.astype(jnp.float32) + branch
    hidden_group = lax.all_gather(hidden_own, "tensor", axis=0, tiled=True)
    factor_two = rms_factor(hidden_group)
    gain_two = gains_full[1].astype(jnp.float32)
    moe_input = (hidden_group * factor_two * gain_two).astype(jnp.bfloat16)
    logits = lax.dot_general(
        moe_input, router_full, (((1,), (1,)), ((), ())), preferred_element_type=jnp.float32
    )
    group_ids = expert_ids[:, 0]
    onehot = (group_ids[:, None] == jnp.arange(EXPERTS, dtype=jnp.int32)[None, :]).astype(
        jnp.float32
    )
    gate_value = jax.nn.sigmoid(jnp.sum(logits * onehot, axis=-1))
    router_prob = softmax_rows(logits)
    counts, prob_sums = lax.psum((jnp.sum(onehot, axis=0), jnp.sum(router_prob, axis=0)), "fsdp")
    route_share = counts / all_tokens
    balance_loss = EXPERTS * jnp.sum(route_share * prob_sums) / all_tokens
    slot_rows = slot_index(group_ids)
    model_width = moe_input.shape[1]
    dispatched = (
        jnp.zeros((EXPERTS * CAP, model_width), jnp.bfloat16)
        .at[slot_rows]
        .set(moe_input, mode="drop")
        .reshape(EXPERTS, CAP, model_width)
    )
    before = jnp.einsum("ecd,edf->ecf", dispatched, up_full, preferred_element_type=jnp.float32)
    activated = jax.nn.gelu(before, approximate=False).astype(jnp.bfloat16)
    expert_out = jnp.einsum(
        "ecf,edf->ecd", activated, down_full, preferred_element_type=jnp.float32
    ).reshape(EXPERTS * CAP, model_width)
    combined_part = jnp.concatenate([expert_out, jnp.zeros((1, model_width), jnp.float32)], axis=0)[
        slot_rows
    ]
    combined = lax.psum_scatter(combined_part, "tensor", scatter_dimension=0, tiled=True)
    gate_own = lax.dynamic_slice_in_dim(gate_value, own_start, own_rows, 0)
    block_out = (hidden_own + gate_own[:, None] * combined).astype(jnp.bfloat16)
    gains_back, qkv_back, out_again, router_back, up_back, down_back = (
        lax.all_gather(norm_gains, "fsdp", axis=1, tiled=True),
        lax.all_gather(qkv_weight, "fsdp", axis=1, tiled=True),
        lax.all_gather(out_weight[None], "fsdp", axis=1, tiled=True),
        lax.all_gather(router_weight, "fsdp", axis=1, tiled=True),
        lax.all_gather(up_weight, "fsdp", axis=1, tiled=True),
        lax.all_gather(down_weight, "fsdp", axis=1, tiled=True),
    )
    out_back = out_again[0]
    cot_group = lax.all_gather(cotangent, "tensor", axis=0, tiled=True).astype(jnp.float32)
    grad_combined = (gate_value[:, None] * cot_group).astype(jnp.bfloat16)
    gate_grad_own = jnp.sum(cotangent.astype(jnp.float32) * combined, axis=-1)
    gate_grad_placed = lax.dynamic_update_slice_in_dim(
        jnp.zeros((group_rows,), jnp.float32), gate_grad_own, own_start, 0
    )
    grad_slots = (
        jnp.zeros((EXPERTS * CAP, model_width), jnp.bfloat16)
        .at[slot_rows]
        .set(grad_combined, mode="drop")
        .reshape(EXPERTS, CAP, model_width)
    )
    grad_activated = jnp.einsum(
        "ecd,edf->ecf", grad_slots, down_back, preferred_element_type=jnp.float32
    )
    down_grad = jnp.einsum(
        "ecd,ecf->edf", grad_slots, activated, preferred_element_type=jnp.float32
    )
    grad_before = (grad_activated * gelu_slope(before)).astype(jnp.bfloat16)
    up_grad = jnp.einsum(
        "ecd,ecf->edf", dispatched, grad_before, preferred_element_type=jnp.float32
    )
    grad_dispatched = jnp.einsum(
        "ecf,edf->ecd", grad_before, up_back, preferred_element_type=jnp.float32
    ).reshape(EXPERTS * CAP, model_width)
    grad_input_part = jnp.concatenate(
        [grad_dispatched, jnp.zeros((1, model_width), jnp.float32)], axis=0
    )[slot_rows]
    grad_moe, gate_grad = lax.psum((grad_input_part, gate_grad_placed), "tensor")
    gate_slope = gate_value * (1.0 - gate_value)
    mixed_share = jnp.sum(router_prob * route_share[None, :], axis=-1, keepdims=True)
    logit_grad = onehot * (gate_grad * gate_slope)[
        :, None
    ] + balance_weight * EXPERTS / all_tokens * router_prob * (route_share[None, :] - mixed_share)
    grad_norm_two = grad_moe + jnp.dot(
        logit_grad, router_back.astype(jnp.float32), precision=highest
    )
    router_grad = jnp.dot(logit_grad.T, moe_input.astype(jnp.float32), precision=highest)
    grad_hidden, gain_two_grad = norm_back(
        grad_norm_two, hidden_group, factor_two, gains_back[1].astype(jnp.float32)
    )
    grad_hidden = grad_hidden + cot_group
    grad_branch = grad_hidden.astype(jnp.bfloat16)
    grad_att = jnp.dot(grad_branch, out_back, preferred_element_type=jnp.float32).astype(
        jnp.bfloat16
    )
    out_grad = lax.dot_general(
        grad_branch, attended, (((0,), (0,)), ((), ())), preferred_element_type=jnp.float32
    )
    grad_project = attend_back(project, grad_att, log_total, prefix_len, score_scale)
    qkv_grad = jnp.einsum(
        "td,tsw->sdw", normed_one, grad_project, preferred_element_type=jnp.float32
    )
    grad_normed_part = jnp.einsum(
        "tsw,sdw->td", grad_project, qkv_back, preferred_element_type=jnp.float32
    )
    grad_normed = lax.psum(grad_normed_part, "tensor")
    grad_tokens, gain_one_grad = norm_back(
        grad_normed, input_float, factor_one, gains_back[0].astype(jnp.float32)
    )
    grad_tokens = grad_tokens + grad_hidden
    tokens_grad = lax.dynamic_slice_in_dim(grad_tokens, own_start, own_rows, 0)
    gains_own, qkv_own, out_own, router_own, up_own, down_own = (
        lax.psum_scatter(
            jnp.stack([gain_one_grad, gain_two_grad], axis=0),
            "fsdp",
            scatter_dimension=1,
            tiled=True,
        ),
        low_scatter(qkv_grad),
        low_scatter(out_grad[None]),
        lax.psum_scatter(router_grad, "fsdp", scatter_dimension=1, tiled=True),
        low_scatter(up_grad),
        low_scatter(down_grad),
    )
    return (
        block_out,
        tokens_grad,
        gains_own,
        qkv_own,
        out_own[0],
        router_own,
        up_own,
        down_own,
        balance_loss,
    )


def solution(mesh):
    placed = (
        P(("fsdp", "tensor"), None),
        P(("fsdp", "tensor"), None),
        P("fsdp"),
        P("fsdp", None),
        P(None, "fsdp"),
        P(None, "fsdp", "tensor"),
        P("fsdp", "tensor"),
        P(None, "fsdp"),
        P(None, "fsdp", "tensor"),
        P(None, "fsdp", "tensor"),
    )
    fits = mesh.shape["fsdp"] == 16 and mesh.shape["tensor"] == 2
    return jax.shard_map(
        fast_device if fits else per_device,
        mesh=mesh,
        in_specs=placed,
        out_specs=(
            P(("fsdp", "tensor"), None),
            P(("fsdp", "tensor"), None),
            P(None, "fsdp"),
            P(None, "fsdp", "tensor"),
            P("fsdp", "tensor"),
            P(None, "fsdp"),
            P(None, "fsdp", "tensor"),
            P(None, "fsdp", "tensor"),
            P(),
        ),
        check_vma=False,
    )
```

```python
import math
import types

import jax
import jax.numpy as jnp
from jax import lax
from jax.experimental import pallas as pl
from jax.experimental.pallas import tpu as pltpu
from jax.sharding import PartitionSpec as P

MESH = pl.DeviceIdType.MESH
BF = jnp.bfloat16
F32 = jnp.float32
ROWS = 1024
WIDE = 768
HALF = 384
HID = 1536
norm_eps = 1e-05
balance_weight = 0.01
masked_score = -1e30


def mm(a, b, ca=1, cb=0):
    return lax.dot_general(a, b, (((ca,), (cb,)), ((), ())), preferred_element_type=F32)


def iota(shape, axis):
    return lax.broadcasted_iota(jnp.int32, shape, axis)


def blocks(count, size, body):
    def step(i, carry):
        body(pl.ds(pl.multiple_of(i * size, size), size))
        return carry

    lax.fori_loop(0, count // size, step, 0)


class Place:
    def __init__(self):
        f, t = lax.axis_index("fsdp"), lax.axis_index("tensor")
        self.f, self.t, self.o = f, t, 1 - t
        self.z, self.c = lax.div(f, 4), lax.rem(f, 4)
        c = self.c
        self.cx = c + 1 - 2 * lax.rem(c, 2)
        self.cy = c + 2 - 4 * lax.div(c, 2)
        self.cd = 3 - c
        base = 4 * self.z
        self.X = {"fsdp": base + self.cx, "tensor": t}
        self.Y = {"fsdp": base + self.cy, "tensor": t}
        self.DIAG = {"fsdp": base + self.cd, "tensor": t}
        self.PAIR = {"fsdp": f, "tensor": 1 - t}

    def zto(self, k):
        return lax.rem(self.z + k, 4)

    def zfrom(self, k):
        return lax.rem(self.z + 4 - k, 4)

    def plane(self, z):
        return {"fsdp": 4 * z + self.c, "tensor": self.t}

    def Z(self, k):
        return {"fsdp": 4 * self.zto(k) + self.c, "tensor": self.t}


class Wire:
    def __init__(self, send, recv):
        self.send, self.recv, self.n, self.open = send, recv, 0, []

    def ids(self, n):
        self.n += n
        return self.n - n

    def copy(self, i, src, dst, dev):
        return pltpu.make_async_remote_copy(
            src_ref=src,
            dst_ref=dst,
            send_sem=self.send.at[i],
            recv_sem=self.recv.at[i],
            device_id=dev,
            device_id_type=MESH,
        )

    def go(self, i, src, dst, dev):
        c = self.copy(i, src, dst, dev)
        c.start()
        self.open.append(c)
        return c

    def flush(self):
        for c in self.open:
            c.wait_send()
        self.open = []


def joined(ref, rows):
    return jnp.concatenate([ref[p, rows] for p in range(3)], axis=1)


def enter(pc):
    barrier = pltpu.get_barrier_semaphore()
    for dev in (pc.PAIR, pc.X, pc.Y, pc.DIAG, pc.Z(1), pc.Z(2), pc.Z(3)):
        pl.semaphore_signal(barrier, inc=1, device_id=dev, device_id_type=MESH)
    pl.semaphore_wait(barrier, 7)


def order(i):
    return i + lax.div(i, 2) * (5 - 2 * i)


def visible(krow0, kn, qcol0, qn, prefix):
    kpos = krow0 + iota((kn, qn), 0)
    qpos = qcol0 + iota((kn, qn), 1)
    ok = kpos <= qpos
    if krow0 < 512 and qcol0 < 512:
        ok = ok | (kpos < prefix)
    return ok


SEEN = (
    ((0, 512, True),),
    ((0, 512, True),),
    ((0, 512, False), (512, 256, True)),
    ((0, 512, False), (512, 256, False), (768, 256, True)),
)


def hook(table, p, qb):
    for (pp, qq), step in table.items():
        if qq == qb:
            pl.when(p == pp)(step)


def both(*steps):
    def run():
        for step in steps:
            step()

    return run


def phase_a(R, pc, w):
    f, t, z, c = pc.f, pc.t, pc.z, pc.c
    idr = R.idr[...]
    ohr = (iota((16, ROWS), 0) - 8 == idr).astype(F32)
    cnt = jnp.sum(ohr, axis=1, keepdims=True)
    hi = jnp.floor(cnt * (1.0 / 256.0))
    lane16 = iota((16, 128), 1)
    six = jnp.concatenate(
        [R.gains[...].astype(F32), R.router[...].astype(F32), jnp.zeros((10, 48), F32)], axis=0
    )
    small = jnp.concatenate([six, jnp.zeros((16, 80), F32)], axis=1)
    R.SM[f] = jnp.where(
        lane16 == 48,
        cnt - 256.0 * hi,
        jnp.where(lane16 == 49, hi, small),
    ).astype(BF)
    R.WA[z, c, pl.ds(0, 3)] = R.qkv[...]
    R.WA[z, c, 3] = R.out[...]
    enter(pc)
    own = pl.ds(pl.multiple_of(t * 512, 512), 512)
    i_tok, i_cot, i_wo, i_att = w.ids(1), w.ids(1), w.ids(1), w.ids(3)
    i_up, i_dn, i_sz, i_s = w.ids(3) - 1, w.ids(3) - 1, w.ids(3) - 1, w.ids(3)
    i_x, i_y, i_fx, i_fy = (w.ids(4) for _ in range(4))
    i_mz = w.ids(18) - 1
    i_m = [w.ids(3) for _ in range(6)]
    i_cz, i_dz, i_cp, i_dp = w.ids(3) - 1, w.ids(3) - 1, w.ids(4), w.ids(4)

    SM = R.SM.reshape(4, 4, 16, 128)
    zs = [w.go(i_sz + k, SM.at[z, c], SM.at[z, c], pc.Z(k)) for k in (1, 2, 3)]

    def up(d):
        block = R.WA.at[z - d + 1, c]
        return w.copy(i_up + d, block, block, pc.plane(z + 1))

    def down(d):
        block = R.WA.at[z + d - 1, c]
        return w.copy(i_dn + d, block, block, pc.plane(z - 1))

    def spread(zz):
        block = R.WA.at[zz, c]
        return w.copy(i_x + zz, block, block, pc.X), w.copy(i_y + zz, block, block, pc.Y)

    def forward(zz):
        a = R.WA.at[zz, pc.cx, pl.ds(0, 2)]
        b = R.WA.at[zz, pc.cy, pl.ds(2, 2)]
        return w.copy(i_fx + zz, a, a, pc.Y), w.copy(i_fy + zz, b, b, pc.X)

    def start_all(copies):
        for m in copies:
            m.start()

    def pass_on(zz):
        for m in spread(zz):
            m.wait_recv()
        start_all(forward(zz))

    def stage(d):
        @pl.when(z >= d)
        def _():
            w.copy(i_up + d, R.WA.at[z, c], R.WA.at[z, c], pc.plane(z - 1)).wait_recv()
            start_all(spread(z - d))
            if d < 3:
                pl.when(z < 3)(lambda: up(d + 1).start())

        @pl.when(z + d <= 3)
        def _():
            w.copy(i_dn + d, R.WA.at[z, c], R.WA.at[z, c], pc.plane(z + 1)).wait_recv()
            start_all(spread(z + d))
            if d < 3:
                pl.when(z > 0)(lambda: down(d + 1).start())

    def pass_on_stage(d):
        pl.when(z >= d)(lambda: pass_on(z - d))
        pl.when(z + d <= 3)(lambda: pass_on(z + d))

    pl.when(z < 3)(lambda: up(1).start())
    pl.when(z > 0)(lambda: down(1).start())
    start_all(spread(z))
    cot_x = w.go(i_cot, R.cot, R.CT.at[own], pc.PAIR)
    tok_x = w.go(i_tok, R.tok, R.TK.at[own], pc.PAIR)
    local = [
        pltpu.make_async_copy(R.tok, R.TK.at[own], R.ls.at[0]),
        pltpu.make_async_copy(R.cot, R.CT.at[own], R.ls.at[1]),
        pltpu.make_async_copy(R.up.at[z], R.UE.at[z, c], R.ls.at[2]),
        pltpu.make_async_copy(R.down.at[z], R.DE.at[z, c], R.ls.at[3]),
    ]
    for m in local:
        m.start()
    before_or_at = (iota((ROWS, ROWS), 0) <= iota((ROWS, ROWS), 1)).astype(F32).astype(BF)
    running = mm(ohr.astype(BF), before_or_at)
    placed = jnp.sum(running * ohr, axis=0, keepdims=True) - 1.0
    key = jnp.where(placed < 256.0, idr.astype(F32) * 256.0 + placed, -1.0)
    R.KC[...] = jnp.broadcast_to(key, (128, ROWS)).T
    R.PR[...] = jnp.broadcast_to(idr.astype(F32), (128, ROWS)).T
    r = iota((512, ROWS), 0)
    want = lax.div(r, 128) * 256 + lax.rem(r, 128) + 128 * t
    R.ACT[0:512, 0:ROWS] = (key.astype(jnp.int32) == want).astype(F32).astype(BF)

    stage(1)
    pass_on(z)
    for m in local:
        m.wait()
    cot_x.wait_recv()

    def cot_rows(e, carry):
        R.CQ[e] = mm(R.ACT[pl.ds(pl.multiple_of(e * 128, 128), 128), pl.ds(0, ROWS)], R.CT[...]).astype(BF)
        return carry

    lax.fori_loop(0, 4, cot_rows, 0)
    R.CR[z, t] = R.CQ[z]
    w.copy(i_cp, R.CR.at[z, t], R.CR.at[z, t], pc.PAIR).start()
    stage(2)
    for m in zs:
        m.wait_recv()
    mine = SM.at[:, c]
    sx, sy = w.go(i_s, mine, mine, pc.X), w.go(i_s + 1, mine, mine, pc.Y)
    pass_on_stage(1)

    def chunk(j):
        return pl.ds(pl.multiple_of(j * 512, 128), 512)

    def from_plane(j):
        out = []
        for k in (1, 3, 2):
            to, cols, i = pc.zto(k), chunk(j), i_mz + 6 * j + k
            out.append(w.copy(i, R.up.at[to, :, cols], R.UE.at[z, c, :, cols], pc.Z(k)))
            out.append(w.copy(i + 3, R.down.at[to, :, cols], R.DE.at[z, c, :, cols], pc.Z(k)))
        return out

    def moe_spread(j):
        u, d = R.UE.at[:, c, :, chunk(j)], R.DE.at[:, c, :, chunk(j)]
        return [
            w.copy(i_m[0] + j, u, u, pc.X),
            w.copy(i_m[1] + j, d, d, pc.Y),
            w.copy(i_m[2] + j, u, u, pc.Y),
            w.copy(i_m[3] + j, d, d, pc.X),
        ]

    def moe_forward(j):
        u, d = R.UE.at[:, pc.cx, :, chunk(j)], R.DE.at[:, pc.cy, :, chunk(j)]
        return [w.copy(i_m[4] + j, u, u, pc.Y), w.copy(i_m[5] + j, d, d, pc.X)]

    def start_spread(j):
        for m in from_plane(j):
            m.wait()
        for m in moe_spread(j):
            m.start()

    def start_forward(j):
        a = moe_spread(j)
        a[0].wait()
        a[1].wait()
        for m in moe_forward(j):
            m.start()

    def weights_here(j):
        for m in moe_spread(j)[2:] + moe_forward(j):
            m.wait()

    def start_plane(j):
        for m in from_plane(j):
            m.start()

    def start_cot():
        for m in cz:
            m.start()

    cz = [w.copy(i_cz + k, R.CQ.at[pc.zto(k)], R.CR.at[z, t], pc.Z(k)) for k in (1, 3, 2)]
    stage(3)
    start_plane(0)
    sx.wait_recv()
    theirs = SM.at[:, pc.cx]
    sf = w.go(i_s + 2, theirs, theirs, pc.Y)
    pass_on_stage(2)
    pass_on_stage(3)
    start_plane(1)
    agenda = {
        (0, 3): lambda: start_spread(1),
        (1, 1): lambda: start_forward(0),
        (2, 1): both(lambda: start_spread(2), start_cot),
        (2, 3): lambda: start_forward(1),
    }

    tok_x.wait_recv()

    def factors(rows):
        x = R.TK[rows].astype(F32)
        R.STAT[rows, 0:1] = lax.rsqrt(jnp.mean(x * x, axis=1, keepdims=True) + norm_eps)

    blocks(ROWS, 128, factors)
    sy.wait_recv()
    sf.wait_recv()
    parts = [R.SM[g].astype(F32)[:, 0:48] for g in range(16)]
    vecs = jnp.concatenate(parts, axis=1)
    R.VEC[...] = vecs
    R.RW[...] = jnp.concatenate([vecs, jnp.zeros((112, WIDE), F32)], axis=0).T.astype(BF)
    total = jnp.zeros((16, 128), F32)
    for g in range(16):
        total = total + R.SM[g].astype(F32)
    counts = jnp.sum(
        jnp.where(lane16 == 48, total, jnp.where(lane16 == 49, 256.0 * total, 0.0)),
        axis=1,
        keepdims=True,
    )
    share = jnp.sum(
        jnp.where(iota((16, 128), 0) - 8 == lane16 - 2, counts, 0.0), axis=0, keepdims=True
    ) * (1.0 / (16 * ROWS))
    R.SHARE[...] = jnp.broadcast_to(share, (8, 128))

    def norm_one(rows):
        x = R.TK[rows].astype(F32)
        R.NM[rows] = (x * R.STAT[rows, 0:1] * R.VEC[0:1]).astype(BF)

    blocks(ROWS, 128, norm_one)
    for zz in range(4):
        for m in spread(zz):
            m.wait_send()
        for m in forward(zz):
            m.wait()
    for d in (1, 2, 3):
        pl.when((z < 3) & (z >= d - 1))(lambda: up(d).wait_send())
        pl.when((z > 0) & (z + d - 1 <= 3))(lambda: down(d).wait_send())
    wo = w.go(i_wo, R.WA.at[:, :, 3], R.WO, pc.PAIR)

    start_spread(0)
    start_plane(2)

    def project(rows):
        x = R.NM[rows]
        for s, ref in enumerate((R.QS, R.KS, R.VS)):
            y = mm(x, R.WA[:, :, s].reshape(WIDE, HALF))
            if s == 0:
                y = y.astype(BF).astype(F32) * 0.125
            for p in range(3):
                ref[p, rows] = y[:, 128 * p : 128 * p + 128].astype(BF)

    blocks(ROWS, 256, project)
    prefix = R.pre[0]

    def pair_of_heads(p, carry):
        value_t = R.VS[p].astype(F32).T.astype(BF)
        even = iota((256, 128), 1) < 64
        for qb in range(4):
            cols = pl.ds(qb * 256, 256)
            outs = []
            for i in range(2):
                q = R.QS[p, cols]
                q = jnp.where(even if i == 0 else ~even, q.astype(F32), 0.0).astype(BF)
                pieces = []
                for k0, kn, masked in SEEN[qb]:
                    s = mm(R.KS[p, pl.ds(k0, kn)], q, 1, 1)
                    if masked:
                        s = jnp.where(visible(k0, kn, qb * 256, 256, prefix), s, masked_score)
                    pieces.append(s)
                top = pieces[0].max(axis=0, keepdims=True)
                for s in pieces[1:]:
                    top = jnp.maximum(top, s.max(axis=0, keepdims=True))
                total_e = jnp.zeros((1, 256), F32)
                out = jnp.zeros((128, 256), F32)
                for (k0, kn, _), s in zip(SEEN[qb], pieces):
                    e = jnp.exp(s - top)
                    total_e = total_e + e.sum(axis=0, keepdims=True)
                    out = out + mm(value_t[:, k0 : k0 + kn], e.astype(BF))
                R.LT[p, i : i + 1, cols] = top + jnp.log(total_e)
                outs.append(out / total_e)
            merged = jnp.where(iota((128, 256), 0) < 64, outs[0], outs[1])
            R.ATO[p, cols] = merged.T.astype(BF)
            if qb == 3:
                w.copy(i_att + p, R.ATO.at[p], R.ATX.at[p], pc.PAIR).start()
            hook(agenda, p, qb)
        return carry

    lax.fori_loop(0, 3, pair_of_heads, 0)
    wo.wait_recv()
    for p in range(3):
        w.copy(i_att + p, R.ATO.at[p], R.ATX.at[p], pc.PAIR).wait()
    lane = iota((256, 128), 1)
    real = (lane >= 2) & (lane < 6)
    R.PS[...] = jnp.zeros((8, 128), F32)

    def out_block(rows):
        b = mm(joined(R.ATO, rows), R.WA[:, :, 3].reshape(WIDE, HALF), 1, 1)
        b = b + mm(joined(R.ATX, rows), R.WO[...].reshape(WIDE, HALF), 1, 1)
        h = R.TK[rows].astype(F32) + b
        R.HIDN[rows] = h
        f2 = lax.rsqrt(jnp.mean(h * h, axis=1, keepdims=True) + norm_eps)
        R.STAT[rows, 1:2] = f2
        moe = (h * f2 * R.VEC[1:2]).astype(BF)
        R.GC[rows] = moe
        logits = mm(moe, R.RW[...])
        mine = jnp.where((lane - 2).astype(F32) == R.PR[rows], logits, 0.0)
        picked = jnp.sum(jnp.where(real, mine, 0.0), axis=1, keepdims=True)
        R.STAT[rows, 2:3] = jax.nn.sigmoid(picked)
        lg = jnp.where(real, logits, masked_score)
        e = jnp.exp(lg - jnp.max(lg, axis=1, keepdims=True))
        e = jnp.where(real, e, 0.0)
        pr = e / jnp.sum(e, axis=1, keepdims=True)
        R.PR[rows] = pr
        R.PS[0:1] = R.PS[0:1] + jnp.sum(pr, axis=0, keepdims=True)

    blocks(ROWS, 256, out_block)

    def moe_rows(i, carry):
        k = order(lax.rem(i + 1, 4))
        e = pc.zto(k)
        R.CS[e] = mm(R.ACT[pl.ds(pl.multiple_of(e * 128, 128), 128), pl.ds(0, ROWS)], R.GC[...]).astype(BF)

        @pl.when(i < 3)
        def _():
            w.copy(i_dz + k, R.CS.at[e], R.DR.at[z, t], pc.Z(k)).start()

        return carry

    lax.fori_loop(0, 4, moe_rows, 0)
    R.DR[z, t] = R.CS[z]
    w.copy(i_dp, R.DR.at[z, t], R.DR.at[z, t], pc.PAIR).start()
    start_forward(2)
    w.flush()
    return i_dz, i_dp, i_cz, i_cp, weights_here


def gelu_parts(v):
    cdf = 0.5 * (1.0 + lax.erf(v * (1.0 / math.sqrt(2.0))))
    slope = cdf + v * (jnp.exp(-0.5 * v * v) * (1.0 / math.sqrt(2.0 * math.pi)))
    return v * cdf, slope


class ExpertSums:
    def __init__(self, R, pc, w):
        self.R, self.pc, self.w = R, pc, w
        self.i1, self.i2, self.i3 = w.ids(16), w.ids(8), w.ids(24) - 1

    def cols(self, g):
        return pl.ds(pl.multiple_of(384 * g, 128), 384)

    def step_one(self, g):
        R, pc, w = self.R, self.pc, self.w
        cols, i = self.cols(g), self.i1 + 4 * g
        return [
            w.copy(i, R.UE.at[:, pc.cx, :, cols], R.RU.at[0, :, :, cols], pc.X),
            w.copy(i + 1, R.UE.at[:, pc.cd, :, cols], R.RU.at[1, :, :, cols], pc.X),
            w.copy(i + 2, R.DE.at[:, pc.cy, :, cols], R.RD.at[0, :, :, cols], pc.Y),
            w.copy(i + 3, R.DE.at[:, pc.cd, :, cols], R.RD.at[1, :, :, cols], pc.Y),
        ]

    def step_two(self, g):
        R, pc, w = self.R, self.pc, self.w
        cols, i = self.cols(g), self.i2 + 2 * g
        return [
            w.copy(i, R.UE.at[:, pc.cy, :, cols], R.RU2.at[:, :, cols], pc.Y),
            w.copy(i + 1, R.DE.at[:, pc.cx, :, cols], R.RD2.at[:, :, cols], pc.X),
        ]

    def step_three(self, g):
        R, pc, w = self.R, self.pc, self.w
        cols, i, out = self.cols(g), self.i3 + 6 * g, []
        for k in (1, 2, 3):
            to, z = pc.zto(k), pc.z
            out.append(w.copy(i + k, R.UE.at[to, pc.c, :, cols], R.ZU.at[z, :, cols], pc.Z(k)))
            out.append(w.copy(i + 3 + k, R.DE.at[to, pc.c, :, cols], R.ZD.at[z, :, cols], pc.Z(k)))
        return out

    def one(self, g):
        for m in self.step_one(g):
            m.start()

    def two(self, g):
        R, pc, cols = self.R, self.pc, self.cols(g)
        for m in self.step_one(g):
            m.wait()

        def add(zz, carry):
            R.UE[zz, pc.cy, :, cols] = R.UE[zz, pc.cy, :, cols] + R.RU[1, zz, :, cols]
            R.DE[zz, pc.cx, :, cols] = R.DE[zz, pc.cx, :, cols] + R.RD[1, zz, :, cols]
            R.UE[zz, pc.c, :, cols] = R.UE[zz, pc.c, :, cols] + R.RU[0, zz, :, cols]
            R.DE[zz, pc.c, :, cols] = R.DE[zz, pc.c, :, cols] + R.RD[0, zz, :, cols]
            return carry

        lax.fori_loop(0, 4, add, 0)
        for m in self.step_two(g):
            m.start()

    def three(self, g):
        R, pc, cols = self.R, self.pc, self.cols(g)
        for m in self.step_two(g):
            m.wait()

        def add(zz, carry):
            R.UE[zz, pc.c, :, cols] = R.UE[zz, pc.c, :, cols] + R.RU2[zz, :, cols]
            R.DE[zz, pc.c, :, cols] = R.DE[zz, pc.c, :, cols] + R.RD2[zz, :, cols]
            return carry

        lax.fori_loop(0, 4, add, 0)
        for m in self.step_three(g):
            m.start()

    def last(self):
        R, pc = self.R, self.pc
        R.ZU[pc.z] = R.UE[pc.z, pc.c]
        R.ZD[pc.z] = R.DE[pc.z, pc.c]
        out = []
        for g in range(4):
            for m in self.step_three(g):
                m.wait()
        for g in (0, 1):
            cols = pl.ds(768 * g, 768)
            for j, (got, to) in enumerate(((R.ZU, R.up_grad), (R.ZD, R.down_grad))):
                held = R.HIDN.at[pl.ds(192 * (2 * g + j), 192)].reshape(4, 48, 768)
                held[...] = got[:, :, cols].astype(F32)
                m = pltpu.make_async_copy(held, to.at[:, :, cols], R.ls.at[2 * g + j])
                m.start()
                out.append(m)
        return out


class AttentionSums:
    def __init__(self, R, pc, w):
        self.R, self.pc, self.w = R, pc, w
        self.i1, self.i2, self.i3 = w.ids(16), w.ids(8), w.ids(12) - 1
        self.low, self.high = pl.ds(0, 2), pl.ds(2, 2)

    def step_one(self, n):
        R, pc, w, i = self.R, self.pc, self.w, self.i1 + 4 * n
        return [
            w.copy(i, R.AG.at[n, self.low, pc.cx], R.RA.at[n, 0], pc.X),
            w.copy(i + 1, R.AG.at[n, self.low, pc.cd], R.RA.at[n, 1], pc.X),
            w.copy(i + 2, R.AG.at[n, self.high, pc.cy], R.RB.at[n, 0], pc.Y),
            w.copy(i + 3, R.AG.at[n, self.high, pc.cd], R.RB.at[n, 1], pc.Y),
        ]

    def step_two(self, n):
        R, pc, w, i = self.R, self.pc, self.w, self.i2 + 2 * n
        return [
            w.copy(i, R.AG.at[n, self.low, pc.cy], R.RA2.at[n], pc.Y),
            w.copy(i + 1, R.AG.at[n, self.high, pc.cx], R.RB2.at[n], pc.X),
        ]

    def step_three(self, n):
        R, pc, w, i = self.R, self.pc, self.w, self.i3 + 3 * n
        return [
            w.copy(i + k, R.AG.at[n, pc.zto(k), pc.c], R.ZA.at[n, pc.z], pc.Z(k))
            for k in (1, 2, 3)
        ]

    def one(self, n):
        for m in self.step_one(n):
            m.start()

    def two(self, n):
        R, pc = self.R, self.pc
        for m in self.step_one(n):
            m.wait()
        for j in range(2):
            R.AG[n, j, pc.cy] = R.AG[n, j, pc.cy] + R.RA[n, 1, j]
            R.AG[n, 2 + j, pc.cx] = R.AG[n, 2 + j, pc.cx] + R.RB[n, 1, j]
            R.AG[n, j, pc.c] = R.AG[n, j, pc.c] + R.RA[n, 0, j]
            R.AG[n, 2 + j, pc.c] = R.AG[n, 2 + j, pc.c] + R.RB[n, 0, j]
        for m in self.step_two(n):
            m.start()

    def three(self, n):
        R, pc = self.R, self.pc
        for m in self.step_two(n):
            m.wait()
        for j in range(2):
            R.AG[n, j, pc.c] = R.AG[n, j, pc.c] + R.RA2[n, j]
            R.AG[n, 2 + j, pc.c] = R.AG[n, 2 + j, pc.c] + R.RB2[n, j]
        for m in self.step_three(n):
            m.start()

    def last(self, n):
        R, pc = self.R, self.pc
        R.ZA[n, pc.z] = R.AG[n, pc.z, pc.c]
        for m in self.step_three(n):
            m.wait()
        total = R.ZA[n, 0].astype(F32)
        for zz in range(1, 4):
            total = total + R.ZA[n, zz].astype(F32)
        for j in range(3):
            block = total[48 * j : 48 * j + 48]
            if n == 0:
                R.out_grad[:, 128 * j : 128 * j + 128] = block
            else:
                R.qkv_grad[j, :, 128 * (n - 1) : 128 * n] = block


def phase_b(R, pc, w, i_dz, i_dp, i_cz, i_cp, weights_here):
    f, t, z, c, o = pc.f, pc.t, pc.z, pc.c, pc.o
    i_xe, i_xg = w.ids(4), w.ids(4)
    i_rg, i_re, i_rgp, i_rep = w.ids(3) - 1, w.ids(3) - 1, w.ids(1), w.ids(1)
    lane = iota((256, 128), 1)
    row = jnp.sum(
        jnp.where(iota((16, WIDE), 0) == 2 + z, R.VEC[...], 0.0), axis=0, keepdims=True
    )
    R.RGR[...] = jnp.zeros((16, WIDE), F32)

    def to_plane(s):
        return {"fsdp": 4 * s + c, "tensor": t}

    def rows_in(k):
        return w.copy(i_dz + k, R.CS.at[pc.zto(k)], R.DR.at[z, t], pc.Z(k))

    def cot_in(k):
        return w.copy(i_cz + k, R.CQ.at[pc.zto(k)], R.CR.at[z, t], pc.Z(k))

    def rows_pair(k):
        s = pc.zfrom(k)
        return (
            w.copy(i_dp + k, R.DR.at[s, t], R.DR.at[s, t], pc.PAIR),
            w.copy(i_cp + k, R.CR.at[s, t], R.CR.at[s, t], pc.PAIR),
        )

    def pair_sums(k):
        s = pc.zfrom(k)
        return (
            w.copy(i_xg + k, R.PG.at[s], R.XG.at[s], pc.PAIR),
            w.copy(i_xe + k, R.PE.at[s], R.XE.at[s], pc.PAIR),
        )

    def home(k):
        s = pc.zfrom(k)
        return w.copy(i_rg + k, R.XG.at[s], R.RG.at[z, t], to_plane(s))

    def home_out(k):
        s = pc.zfrom(k)
        return w.copy(i_re + k, R.XE.at[s], R.RE.at[z, t], to_plane(s))

    def finish(k):
        s = pc.zfrom(k)
        for m in pair_sums(k):
            m.wait()
        eo = R.EOO[s] + R.XE[s].astype(F32)
        gate = R.STAT[pl.ds(pl.multiple_of(s * 256 + t * 128, 128), 128), 3:4]
        gate_grad = jnp.sum(R.CR[s, t].astype(F32) * eo, axis=1, keepdims=True)
        gs = gate_grad * gate * (1.0 - gate)
        R.RGR[0:1] += jnp.sum(gs * R.DR[s, t].astype(F32), axis=0, keepdims=True)
        R.XG[s] = (R.GMO[s] + R.XG[s].astype(F32) + gs * row).astype(BF)
        R.XE[s] = eo.astype(BF)

    def source(i, carry):
        k = order(i)
        s = pc.zfrom(k)
        rows = pl.ds(pl.multiple_of(s * 256, 256), 256)

        for m in rows_pair(k):
            m.wait()
        x = R.DR[s].reshape(256, WIDE)
        logits = mm(x, R.RW[...])
        gate = jax.nn.sigmoid(
            jnp.sum(jnp.where(lane == 2 + z, logits, 0.0), axis=1, keepdims=True)
        )
        R.STAT[rows, 3:4] = gate
        R.GC[rows] = (gate * R.CR[s].reshape(256, WIDE).astype(F32)).astype(BF)

        def hidden_units(j, carry):
            @pl.when(i == 0)
            def _():
                weights_here(j)

            cols = pl.ds(pl.multiple_of(j * 512, 128), 512)
            up = R.UE[:, :, :, cols].reshape(WIDE, 512)
            down = R.DE[:, :, :, cols].reshape(WIDE, 512)
            act, slope = gelu_parts(mm(R.DR[s].reshape(256, WIDE), up))
            act = act.astype(BF)
            gb = (mm(R.GC[rows], down) * slope).astype(BF)
            R.ACT[rows, cols] = act
            R.GB[rows, cols] = gb
            return carry

        lax.fori_loop(0, 3, hidden_units, 0)
        @pl.when(i < 3)
        def _():
            after = order(i + 1)
            cot_in(after).wait()
            rows_pair(after)[1].start()
            rows_in(after).wait()
            rows_pair(after)[0].start()

        up, down = R.UE[...].reshape(WIDE, HID), R.DE[...].reshape(WIDE, HID)
        R.GMB[...] = mm(R.GB[rows], up, 1, 1).reshape(2, 128, WIDE)
        R.PG[s] = R.GMB[o].astype(BF)
        pair_sums(k)[0].start()
        R.GMO[s] = R.GMB[t]
        R.GMB[...] = mm(R.ACT[rows], down, 1, 1).reshape(2, 128, WIDE)
        R.PE[s] = R.GMB[o].astype(BF)
        pair_sums(k)[1].start()
        R.EOO[s] = R.GMB[t]

        @pl.when(i > 0)
        def _():
            last = order(i - 1)
            finish(last)

            @pl.when(i > 1)
            def _():
                home(last).start()

        return carry

    lax.fori_loop(0, 4, source, 0)
    finish(2)
    home(2).start()
    R.RG[z, t] = R.XG[z]
    R.RE[z, t] = R.XE[z]
    R.RGR[...] = jnp.where(iota((16, WIDE), 0) == 2 + z, R.RGR[0:1], 0.0)
    sums = ExpertSums(R, pc, w)
    DR = R.DR.reshape(ROWS, WIDE)

    def weight_grads(i, carry):
        cols = pl.ds(pl.multiple_of(i * 384, 128), 384)
        R.UE[:, :, :, cols] = mm(DR[...], R.GB[:, cols], 0, 0).astype(BF).reshape(4, 4, 48, 384)
        R.DE[:, :, :, cols] = mm(R.GC[...], R.ACT[:, cols], 0, 0).astype(BF).reshape(4, 4, 48, 384)


        @pl.when(i < 2)
        def _():
            for m in sums.step_one(i):
                m.start()

        return carry

    lax.fori_loop(0, 4, weight_grads, 0)
    share, vec = R.SHARE[0:1], R.VEC[...]
    R.SB[...] = jnp.zeros((16, WIDE), F32)

    def prepared(i, carry):
        rows = pl.ds(pl.multiple_of(i * 256, 256), 256)
        R.ACT[rows, pl.ds(0, ROWS)] = pick_rows(R.KC[rows])
        pr = R.PR[rows]
        mixed = jnp.sum(pr * share, axis=1, keepdims=True)
        aux = (balance_weight * 4.0 / (16 * ROWS)) * pr * (share - mixed)
        aux = aux[:, 0:16].astype(BF)
        R.GH[rows] = mm(aux, vec.astype(BF))
        mine = jnp.where(lax.div(i, 2) == t, 1.0, 0.0)
        moe = (R.HIDN[rows] * R.STAT[rows, 1:2] * vec[1:2]).astype(BF)
        R.SB[...] += mine * mm(aux, moe, 0, 0)
        return carry

    lax.fori_loop(0, 4, prepared, 0)
    sums.two(0)
    sums.one(2)
    for k in (1, 3, 2):
        home(k).wait()
    back = w.go(i_rgp, R.RG.at[:, t], R.RG.at[:, t], pc.PAIR)
    for k in (1, 3, 2):
        home_out(k).start()
    back.wait_recv()
    return sums, home_out, i_rep


def pick_rows(key):
    keys = jnp.concatenate([key] * 8, axis=1)
    return (keys == iota((key.shape[0], ROWS), 1).astype(F32)).astype(F32).astype(BF)


def phase_c(R, pc, w, sums, home_out, i_rep):
    f, t, z, c, o = pc.f, pc.t, pc.z, pc.c, pc.o
    att = AttentionSums(R, pc, w)
    i_n = w.ids(1)
    i_sp, i_sc, i_sz = w.ids(1), w.ids(3), w.ids(3) - 1
    own = pl.ds(pl.multiple_of(t * 512, 512), 512)
    GH, GN = R.GH, R.EOO.reshape(512, WIDE)
    RG, RE = R.RG.reshape(ROWS, WIDE), R.RE.reshape(ROWS, WIDE)
    GBR = R.GC
    share = R.SHARE[0:1]
    vec = R.VEC[...]
    head = iota((24, HALF), 0)
    head = jnp.where(lax.rem(head, 8) < 2, 2 * lax.div(head, 8) + lax.rem(head, 8), -1)
    pick_head = (head == lax.div(iota((24, HALF), 1), 64)).astype(F32).astype(BF)

    def residual(i, carry):
        rows = pl.ds(pl.multiple_of(i * 256, 256), 256)
        gm = mm(R.ACT[rows, pl.ds(0, ROWS)], RG[...]) + R.GH[rows]
        mine = jnp.where(lax.div(i, 2) == t, 1.0, 0.0)
        h, f2 = R.HIDN[rows], R.STAT[rows, 1:2]
        g = gm * vec[1:2]
        inner = jnp.mean(g * h, axis=1, keepdims=True)
        gh = R.CT[rows].astype(F32) + f2 * (g - h * (f2 * f2 * inner))
        R.G2[0:1] += mine * jnp.sum(gm * h * f2, axis=0, keepdims=True)
        GH[rows] = gh
        low = gh.astype(BF)
        GBR[rows] = low
        ga = mm(low, R.WA[:, :, 3].reshape(WIDE, HALF)).astype(BF)
        for p in range(3):
            R.ATX[p, rows] = ga[:, 128 * p : 128 * p + 128]
        prod = ga.astype(F32) * joined(R.ATO, rows).astype(F32)
        top = prod.astype(BF)
        rest = (prod - top.astype(F32)).astype(BF)
        dd = mm(pick_head, top, 1, 1) + mm(pick_head, rest, 1, 1)
        for p in range(3):
            R.DD[p, :, rows] = dd[8 * p : 8 * p + 8]

        @pl.when(i == 2)
        def _():
            sums.two(1)
            sums.one(3)

        return carry

    R.G2[...] = jnp.zeros((8, WIDE), F32)
    lax.fori_loop(0, 4, residual, 0)
    part = jnp.where(iota((16, WIDE), 0) == 1, R.G2[0:1], 0.0)
    sums6 = jnp.concatenate([0.5 * R.PS[0:1], jnp.zeros((1, WIDE - 128), F32)], axis=1)
    keep = (iota((16, WIDE), 0) >= 2) & (iota((16, WIDE), 0) < 6)
    R.SB[...] = (
        jnp.where(keep, R.SB[...] + R.RGR[...], 0.0)
        + part
        + jnp.where(iota((16, WIDE), 0) == 6, sums6, 0.0)
    )

    def place(n, grad):
        for j in range(3):
            block = grad[:, 128 * j : 128 * j + 128].astype(BF).reshape(4, 4, 48, 128)
            R.AG[n, :, :, pl.ds(48 * j, 48)] = block

    place(0, mm(GBR[...], joined(R.ATO, pl.ds(0, ROWS)), 0, 0))

    def outputs_pair():
        return w.copy(i_rep, R.RE.at[:, t], R.RE.at[:, t], pc.PAIR)

    def outputs_home():
        for k in (1, 2, 3):
            home_out(k).wait()
        outputs_pair().start()


    agenda = {
        (0, 1): both(lambda: sums.two(2), lambda: sums.three(0)),
        (0, 3): lambda: sums.three(1),
        (1, 2): lambda: sums.two(3),
        (1, 3): lambda: att.one(0),
        (2, 0): lambda: sums.three(2),
        (2, 1): outputs_home,
        (2, 2): lambda: sums.three(3),
        (2, 3): lambda: att.two(0),
    }
    prefix = R.pre[0]

    def pair_of_heads(p, carry):
        key_t = R.KS[p].astype(F32).T.astype(BF)
        R.DK[...] = jnp.zeros((ROWS, 128), F32)
        R.DV[...] = jnp.zeros((ROWS, 128), F32)
        even = iota((256, 128), 1) < 64
        for qb in range(4):
            cols = pl.ds(qb * 256, 256)
            outs = []
            for i in range(2):
                side = even if i == 0 else ~even
                q = jnp.where(side, R.QS[p, cols].astype(F32), 0.0).astype(BF)
                do = jnp.where(side, R.ATX[p, cols].astype(F32), 0.0).astype(BF)
                lt, dd = R.LT[p, i : i + 1, cols], R.DD[p, i : i + 1, cols]
                dq = jnp.zeros((128, 256), F32)
                for kb in range(max(2, qb + 1)):
                    keys = pl.ds(kb * 256, 256)
                    s = mm(R.KS[p, keys], q, 1, 1)
                    if kb == qb or qb < 2:
                        ok = visible(kb * 256, 256, qb * 256, 256, prefix)
                        s = jnp.where(ok, s, masked_score)
                    prob = jnp.exp(s - lt)
                    ds = prob * (mm(R.VS[p, keys], do, 1, 1) - dd)
                    ds = ds.astype(BF)
                    R.DV[keys] += mm(prob.astype(BF), do)
                    R.DK[keys] += mm(ds, q)
                    dq = dq + mm(key_t[:, kb * 256 : kb * 256 + 256], ds)
                outs.append(dq)
            merged = jnp.where(iota((128, 256), 0) < 64, outs[0], outs[1])
            R.QS[p, cols] = (merged * 0.125).T.astype(BF)
            hook(agenda, p, qb)
        R.KS[p] = R.DK[...].astype(BF)
        R.VS[p] = R.DV[...].astype(BF)
        three = jnp.concatenate([R.QS[p], R.KS[p], R.VS[p]], axis=1)
        place(p + 1, mm(R.NM[...], three, 0, 0))

        @pl.when(p == 1)
        def _():
            att.one(1)

        @pl.when(p > 0)
        def _():
            att.one(p + 1)

        return carry

    lax.fori_loop(0, 3, pair_of_heads, 0)
    GP = (R.QS, R.KS, R.VS)

    XS, XN, BO = (r.reshape(512, WIDE) for r in (R.CS, R.XG, R.PE))

    R.G2[...] = jnp.zeros((8, WIDE), F32)

    def normed_grad(i, carry):
        mine = pl.ds(pl.multiple_of(i * 256, 256), 256)

        def half(start):
            rows = pl.ds(pl.multiple_of(start * 512 + i * 256, 256), 256)
            acc = jnp.zeros((256, WIDE), F32)
            for s in range(3):
                acc = acc + mm(joined(GP[s], rows), R.WA[:, :, s].reshape(WIDE, HALF), 1, 1)
            x = R.TK[rows].astype(F32) * R.STAT[rows, 0:1]
            R.G2[0:1] += jnp.sum(acc * x, axis=0, keepdims=True)
            return acc

        XS[mine] = half(o).astype(BF)
        GN[mine] = half(t)
        return carry

    w.flush()
    lax.fori_loop(0, 2, normed_grad, 0)
    xn = w.go(i_n, XS, XN, pc.PAIR)
    R.SB[0:1] = R.G2[0:1]
    sp = w.go(i_sp, R.SB, R.SP, pc.PAIR)
    att.two(1)
    att.three(0)
    outputs_pair().wait()

    def block_rows(i, carry):
        rows = pl.ds(pl.multiple_of(i * 256, 256), 256)
        full = pl.ds(pl.multiple_of(t * 512 + i * 256, 256), 256)
        eo = mm(R.ACT[full, pl.ds(0, ROWS)], RE[...])
        BO[rows] = (R.HIDN[full] + R.STAT[full, 2:3] * eo).astype(BF)
        return carry

    lax.fori_loop(0, 2, block_rows, 0)
    out_b = pltpu.make_async_copy(BO, R.block_out, R.ls.at[1])
    out_b.start()
    att.two(2)
    att.three(1)
    sp.wait_recv()
    R.SC[c] = R.SB[...] + R.SP[...]
    sc = [
        w.go(i_sc, R.SC.at[c], R.SC.at[c], pc.X),
        w.go(i_sc + 1, R.SC.at[c], R.SC.at[c], pc.Y),
        w.go(i_sc + 2, R.SC.at[c], R.SC.at[c], pc.DIAG),
    ]
    xn.wait_recv()

    def input_grad(i, carry):
        rows = pl.ds(pl.multiple_of(i * 128, 128), 128)
        full = pl.ds(pl.multiple_of(t * 512 + i * 128, 128), 128)
        gn = GN[rows] + XN[rows].astype(F32)
        x, f1 = R.TK[full].astype(F32), R.STAT[full, 0:1]
        g = gn * R.VEC[0:1]
        inner = jnp.mean(g * x, axis=1, keepdims=True)
        GH[full] = GH[full] + f1 * (g - x * (f1 * f1 * inner))
        return carry

    lax.fori_loop(0, 4, input_grad, 0)
    out_t = pltpu.make_async_copy(GH.at[own], R.tokens_grad, R.ls.at[0])
    out_t.start()
    att.two(3)
    att.three(2)
    for m in sc:
        m.wait_recv()
    R.SZ[z] = R.SC[0] + R.SC[1] + R.SC[2] + R.SC[3]
    sz = [w.go(i_sz + k, R.SZ.at[z], R.SZ.at[z], pc.Z(k)) for k in (1, 2, 3)]
    att.three(3)
    out_t.wait()
    out_b.wait()
    written = sums.last()
    for n in range(3):
        att.last(n)
    for m in sz:
        m.wait_recv()
    total = R.SZ[0] + R.SZ[1] + R.SZ[2] + R.SZ[3]
    probs = total[6:7, 0:128]
    R.balance[...] = (4.0 / (16 * ROWS)) * jnp.sum(share * probs, axis=1, keepdims=True)
    column = (iota((WIDE, 128), 0) == 48 * f + iota((WIDE, 128), 1)).astype(F32).astype(BF)
    mine = jnp.zeros((16, 128), F32)
    for _ in range(3):
        top = total.astype(BF)
        mine = mine + mm(top, column)
        total = total - top.astype(F32)
    R.gains_grad[...] = mine[0:2, 0:48]
    R.router_grad[...] = mine[2:6, 0:48]
    att.last(3)
    for m in written:
        m.wait()
    w.flush()


OUTS = {
    "block_out": ((512, WIDE), BF),
    "tokens_grad": ((512, WIDE), F32),
    "gains_grad": ((2, 48), F32),
    "qkv_grad": ((3, 48, HALF), F32),
    "out_grad": ((48, HALF), F32),
    "router_grad": ((4, 48), F32),
    "up_grad": ((4, 48, HID), F32),
    "down_grad": ((4, 48, HID), F32),
    "balance": ((1, 1), F32),
}
SCRATCH = {
    "STAT": ((ROWS, 128), F32),
    "ATO": ((3, ROWS, 128), BF),
    "ATX": ((3, ROWS, 128), BF),
    "PG": ((4, 128, WIDE), BF),
    "CQ": ((4, 128, WIDE), BF),
    "PE": ((4, 128, WIDE), BF),
    "GMB": ((2, 128, WIDE), F32),
    "EOO": ((4, 128, WIDE), F32),
    "GMO": ((4, 128, WIDE), F32),
    "GH": ((ROWS, WIDE), F32),
    "ACT": ((ROWS, HID), BF),
    "GB": ((ROWS, HID), BF),
    "TK": ((ROWS, WIDE), BF),
    "CT": ((ROWS, WIDE), BF),
    "WA": ((4, 4, 4, 48, HALF), BF),
    "WO": ((4, 4, 48, HALF), BF),
    "UE": ((4, 4, 48, HID), BF),
    "DE": ((4, 4, 48, HID), BF),
    "KC": ((ROWS, 128), F32),
    "CR": ((4, 2, 128, WIDE), BF),
    "DR": ((4, 2, 128, WIDE), BF),
    "VEC": ((16, WIDE), F32),
    "RW": ((WIDE, 128), BF),
    "SHARE": ((8, 128), F32),
    "NM": ((ROWS, WIDE), BF),
    "QS": ((3, ROWS, 128), BF),
    "KS": ((3, ROWS, 128), BF),
    "VS": ((3, ROWS, 128), BF),
    "LT": ((3, 8, ROWS), F32),
    "HIDN": ((ROWS, WIDE), F32),
    "PR": ((ROWS, 128), F32),
    "PS": ((8, 128), F32),
    "SM": ((16, 16, 128), BF),
    "CS": ((4, 128, WIDE), BF),
    "GC": ((ROWS, WIDE), BF),
    "XE": ((4, 128, WIDE), BF),
    "XG": ((4, 128, WIDE), BF),
    "RG": ((4, 2, 128, WIDE), BF),
    "RE": ((4, 2, 128, WIDE), BF),
    "RGR": ((16, WIDE), F32),
    "RU": ((2, 4, 48, HID), BF),
    "RD": ((2, 4, 48, HID), BF),
    "RU2": ((4, 48, HID), BF),
    "RD2": ((4, 48, HID), BF),
    "ZU": ((4, 48, HID), BF),
    "ZD": ((4, 48, HID), BF),
    "DD": ((3, 8, ROWS), F32),
    "DK": ((ROWS, 128), F32),
    "DV": ((ROWS, 128), F32),
    "AG": ((4, 4, 4, 144, 128), BF),
    "RA": ((4, 2, 2, 144, 128), BF),
    "RB": ((4, 2, 2, 144, 128), BF),
    "RA2": ((4, 2, 144, 128), BF),
    "RB2": ((4, 2, 144, 128), BF),
    "ZA": ((4, 4, 144, 128), BF),
    "G2": ((8, WIDE), F32),
    "SB": ((16, WIDE), F32),
    "SP": ((16, WIDE), F32),
    "SC": ((4, 16, WIDE), F32),
    "SZ": ((4, 16, WIDE), F32),
}
INS = ("tok", "cot", "pre", "idr", "gains", "qkv", "out", "router", "up", "down")
IN_HBM = ("tok", "cot", "up", "down")
OUT_HBM = ("block_out", "tokens_grad", "up_grad", "down_grad")
SEMAPHORES = 192


def fused(args):
    names = INS + tuple(OUTS) + tuple(SCRATCH) + ("ss", "rs", "ls")

    def body(*refs):
        R = types.SimpleNamespace(**dict(zip(names, refs)))
        pc = Place()
        w = Wire(R.ss, R.rs)
        phase_c(R, pc, w, *phase_b(R, pc, w, *phase_a(R, pc, w)))

    vm = pl.BlockSpec(memory_space=pltpu.VMEM)
    hbm = pl.BlockSpec(memory_space=pl.ANY)
    sm = pl.BlockSpec(memory_space=pltpu.SMEM)
    dma = pltpu.SemaphoreType.DMA
    return pl.pallas_call(
        body,
        out_shape=[jax.ShapeDtypeStruct(s, d) for s, d in OUTS.values()],
        in_specs=[sm if n == "pre" else hbm if n in IN_HBM else vm for n in INS],
        out_specs=[hbm if n in OUT_HBM else vm for n in OUTS],
        scratch_shapes=[pltpu.VMEM(s, d) for s, d in SCRATCH.values()]
        + [dma((SEMAPHORES,)), dma((SEMAPHORES,)), dma((4,))],
        compiler_params=pltpu.CompilerParams(
            collective_id=1, has_side_effects=True, vmem_limit_bytes=63 << 20
        ),
        name="block",
    )(*args)


def copy_out(arrays):
    n = len(arrays)

    def body(*refs):
        src, dst, held, sem = refs[:n], refs[n : 2 * n], refs[2 * n : 3 * n], refs[3 * n]
        come = [pltpu.make_async_copy(src[i], held[i], sem.at[0, i]) for i in range(n)]
        go = [pltpu.make_async_copy(held[i], dst[i], sem.at[1, i]) for i in range(n)]
        for m in come:
            m.start()
        for i in range(n):
            come[i].wait()
            go[i].start()
        for m in go:
            m.wait()

    hbm = pl.BlockSpec(memory_space=pl.ANY)
    return pl.pallas_call(
        body,
        out_shape=[jax.ShapeDtypeStruct(a.shape, a.dtype) for a in arrays],
        in_specs=[hbm] * n,
        out_specs=[hbm] * n,
        scratch_shapes=[pltpu.VMEM(a.shape, a.dtype) for a in arrays]
        + [pltpu.SemaphoreType.DMA((2, n))],
        name="outputs",
    )(*arrays)


def prepare(
    tokens, cotangent, prefix_len, expert_ids, norm_gains, qkv_weight, out_weight, router_weight, up_weight, down_weight
):
    ids = expert_ids.reshape(1, ROWS)
    return (tokens, cotangent, prefix_len, ids, norm_gains, qkv_weight, out_weight, router_weight, up_weight, down_weight)


def fast_device(*args):
    outs = copy_out(fused(prepare(*args)))
    return tuple(outs[:8]) + (outs[8].reshape(()),)


HEAD = 64
EXPERTS = 4
SEQ = 1024
CAP = 256


highest = lax.Precision.HIGHEST


def softmax_rows(scores):
    row_max = jnp.max(scores, axis=-1, keepdims=True)
    shifted = jnp.exp(scores - row_max)
    return shifted / jnp.sum(shifted, axis=-1, keepdims=True)


def slot_index(group_ids):
    onehot = (group_ids[:, None] == jnp.arange(EXPERTS, dtype=jnp.int32)[None, :]).astype(jnp.int32)
    rows = group_ids.shape[0]
    earlier = lax.broadcasted_iota(jnp.int32, (rows, rows), 1) <= lax.broadcasted_iota(
        jnp.int32, (rows, rows), 0
    )
    running = jnp.dot(
        earlier.astype(jnp.bfloat16),
        onehot.astype(jnp.bfloat16),
        preferred_element_type=jnp.float32,
    ).astype(jnp.int32)
    placed = jnp.sum(running * onehot, axis=1) - 1
    return jnp.where(placed < CAP, group_ids * CAP + placed, EXPERTS * CAP)


def rms_factor(values):
    return lax.rsqrt(jnp.mean(values * values, axis=-1, keepdims=True) + norm_eps)


def norm_back(grad_out, inputs, factor, gain):
    scaled = grad_out * gain
    row_inner = jnp.mean(scaled * inputs, axis=-1, keepdims=True)
    grad_in = factor * (scaled - inputs * factor * factor * row_inner)
    grad_gain = jnp.sum(grad_out * inputs * factor, axis=0)
    return (grad_in, grad_gain)


def gelu_slope(values):
    cumulative = 0.5 * (1.0 + lax.erf(values / math.sqrt(2.0)))
    density = jnp.exp(-0.5 * values * values) / math.sqrt(2.0 * math.pi)
    return cumulative + values * density


def block_scores(query_block, key_seq, offset, prefix, score_scale):
    scores = (
        jnp.einsum("qhd,khd->hqk", query_block, key_seq, preferred_element_type=jnp.float32)
        * score_scale
    )
    shape_pair = (query_block.shape[0], key_seq.shape[0])
    row_pos = offset + lax.broadcasted_iota(jnp.int32, shape_pair, 0)
    col_pos = lax.broadcasted_iota(jnp.int32, shape_pair, 1)
    allowed = (col_pos <= row_pos) | (col_pos < prefix)
    return jnp.where(allowed[None], scores, masked_score)


def attend(project, prefix_len, score_scale):
    group_rows = project.shape[0]
    full_width = project.shape[2]
    heads_here = full_width // HEAD
    block_rows = min(512, SEQ)
    shaped = project.reshape(group_rows, 3, heads_here, HEAD)
    query_all = shaped[:, 0]
    key_all = shaped[:, 1]
    value_all = shaped[:, 2]

    def one_block(number):
        row_start = number * block_rows
        seq_number = row_start // SEQ
        seq_start = seq_number * SEQ
        query_block = lax.dynamic_slice_in_dim(query_all, row_start, block_rows, 0)
        scores = block_scores(
            query_block, key_all, row_start - seq_start, prefix_len[seq_number], score_scale
        )
        row_max = jnp.max(scores, axis=-1, keepdims=True)
        shifted = jnp.exp(scores - row_max)
        row_total = jnp.sum(shifted, axis=-1, keepdims=True)
        prob_low = (shifted / row_total).astype(jnp.bfloat16)
        result = jnp.einsum("hqk,khd->qhd", prob_low, value_all, preferred_element_type=jnp.float32)
        return (
            result.reshape(block_rows, full_width).astype(jnp.bfloat16),
            (row_max + jnp.log(row_total))[..., 0],
        )

    outputs, log_total = lax.map(one_block, jnp.arange(group_rows // block_rows, dtype=jnp.int32))
    return (outputs.reshape(group_rows, full_width), log_total)


def attend_back(project, grad_att, log_total, prefix_len, score_scale):
    group_rows = project.shape[0]
    full_width = project.shape[2]
    heads_here = full_width // HEAD
    block_rows = min(512, SEQ)
    shaped = project.reshape(group_rows, 3, heads_here, HEAD)
    query_all = shaped[:, 0]
    key_all = shaped[:, 1]
    value_all = shaped[:, 2]
    grad_shaped = grad_att.reshape(group_rows, heads_here, HEAD)

    def one_block(carried, number):
        grad_keys, grad_values = carried
        row_start = number * block_rows
        seq_number = row_start // SEQ
        seq_start = seq_number * SEQ
        query_block = lax.dynamic_slice_in_dim(query_all, row_start, block_rows, 0)
        grad_block = lax.dynamic_slice_in_dim(grad_shaped, row_start, block_rows, 0)
        scores = block_scores(
            query_block, key_all, row_start - seq_start, prefix_len[seq_number], score_scale
        )
        prob_block = jnp.exp(scores - log_total[number][..., None])
        prob_low = prob_block.astype(jnp.bfloat16)
        grad_prob = jnp.einsum(
            "qhd,khd->hqk", grad_block, value_all, preferred_element_type=jnp.float32
        )
        value_part = jnp.einsum(
            "hqk,qhd->khd", prob_low, grad_block, preferred_element_type=jnp.float32
        )
        row_inner = jnp.sum(prob_block * grad_prob, axis=-1, keepdims=True)
        grad_scores = (prob_block * (grad_prob - row_inner)).astype(jnp.bfloat16)
        query_grad = (
            jnp.einsum("hqk,khd->qhd", grad_scores, key_all, preferred_element_type=jnp.float32)
            * score_scale
        )
        key_part = (
            jnp.einsum("hqk,qhd->khd", grad_scores, query_block, preferred_element_type=jnp.float32)
            * score_scale
        )
        old_keys = grad_keys
        grad_keys = old_keys + key_part
        old_values = grad_values
        grad_values = old_values + value_part
        return ((grad_keys, grad_values), query_grad)

    zero_rows = jnp.zeros((group_rows, heads_here, HEAD), jnp.float32)
    final, grad_query = lax.scan(
        one_block, (zero_rows, zero_rows), jnp.arange(group_rows // block_rows, dtype=jnp.int32)
    )
    grad_keys, grad_values = final
    stacked = jnp.stack(
        [
            grad_query.reshape(group_rows, full_width),
            grad_keys.reshape(group_rows, full_width),
            grad_values.reshape(group_rows, full_width),
        ],
        axis=1,
    )
    return stacked.astype(jnp.bfloat16)


def low_scatter(grad):
    return lax.psum_scatter(
        grad.astype(jnp.bfloat16), "fsdp", scatter_dimension=1, tiled=True
    ).astype(jnp.float32)


def per_device(
    tokens,
    cotangent,
    prefix_len,
    expert_ids,
    norm_gains,
    qkv_weight,
    out_weight,
    router_weight,
    up_weight,
    down_weight,
):
    tensor_size = lax.axis_size("tensor")
    fsdp_size = lax.axis_size("fsdp")
    own_rows = tokens.shape[0]
    group_rows = own_rows * tensor_size
    all_tokens = group_rows * fsdp_size
    own_start = lax.axis_index("tensor") * own_rows
    score_scale = 1.0 / math.sqrt(HEAD)
    gains_full, qkv_full, out_stack = (
        lax.all_gather(norm_gains, "fsdp", axis=1, tiled=True),
        lax.all_gather(qkv_weight, "fsdp", axis=1, tiled=True),
        lax.all_gather(out_weight[None], "fsdp", axis=1, tiled=True),
    )
    out_full = out_stack[0]
    router_full, up_full, down_full = (
        lax.all_gather(router_weight, "fsdp", axis=1, tiled=True),
        lax.all_gather(up_weight, "fsdp", axis=1, tiled=True),
        lax.all_gather(down_weight, "fsdp", axis=1, tiled=True),
    )
    inputs = lax.all_gather(tokens, "tensor", axis=0, tiled=True)
    input_float = inputs.astype(jnp.float32)
    factor_one = rms_factor(input_float)
    gain_one = gains_full[0].astype(jnp.float32)
    normed_one = (input_float * factor_one * gain_one).astype(jnp.bfloat16)
    project = jnp.einsum(
        "td,sdw->tsw", normed_one, qkv_full, preferred_element_type=jnp.float32
    ).astype(jnp.bfloat16)
    attended, log_total = attend(project, prefix_len, score_scale)
    branch = lax.psum_scatter(
        lax.dot_general(
            attended, out_full, (((1,), (1,)), ((), ())), preferred_element_type=jnp.float32
        ),
        "tensor",
        scatter_dimension=0,
        tiled=True,
    )
    hidden_own = tokens.astype(jnp.float32) + branch
    hidden_group = lax.all_gather(hidden_own, "tensor", axis=0, tiled=True)
    factor_two = rms_factor(hidden_group)
    gain_two = gains_full[1].astype(jnp.float32)
    moe_input = (hidden_group * factor_two * gain_two).astype(jnp.bfloat16)
    logits = lax.dot_general(
        moe_input, router_full, (((1,), (1,)), ((), ())), preferred_element_type=jnp.float32
    )
    group_ids = expert_ids[:, 0]
    onehot = (group_ids[:, None] == jnp.arange(EXPERTS, dtype=jnp.int32)[None, :]).astype(
        jnp.float32
    )
    gate_value = jax.nn.sigmoid(jnp.sum(logits * onehot, axis=-1))
    router_prob = softmax_rows(logits)
    counts, prob_sums = lax.psum((jnp.sum(onehot, axis=0), jnp.sum(router_prob, axis=0)), "fsdp")
    route_share = counts / all_tokens
    balance_loss = EXPERTS * jnp.sum(route_share * prob_sums) / all_tokens
    slot_rows = slot_index(group_ids)
    model_width = moe_input.shape[1]
    dispatched = (
        jnp.zeros((EXPERTS * CAP, model_width), jnp.bfloat16)
        .at[slot_rows]
        .set(moe_input, mode="drop")
        .reshape(EXPERTS, CAP, model_width)
    )
    before = jnp.einsum("ecd,edf->ecf", dispatched, up_full, preferred_element_type=jnp.float32)
    activated = jax.nn.gelu(before, approximate=False).astype(jnp.bfloat16)
    expert_out = jnp.einsum(
        "ecf,edf->ecd", activated, down_full, preferred_element_type=jnp.float32
    ).reshape(EXPERTS * CAP, model_width)
    combined_part = jnp.concatenate([expert_out, jnp.zeros((1, model_width), jnp.float32)], axis=0)[
        slot_rows
    ]
    combined = lax.psum_scatter(combined_part, "tensor", scatter_dimension=0, tiled=True)
    gate_own = lax.dynamic_slice_in_dim(gate_value, own_start, own_rows, 0)
    block_out = (hidden_own + gate_own[:, None] * combined).astype(jnp.bfloat16)
    gains_back, qkv_back, out_again, router_back, up_back, down_back = (
        lax.all_gather(norm_gains, "fsdp", axis=1, tiled=True),
        lax.all_gather(qkv_weight, "fsdp", axis=1, tiled=True),
        lax.all_gather(out_weight[None], "fsdp", axis=1, tiled=True),
        lax.all_gather(router_weight, "fsdp", axis=1, tiled=True),
        lax.all_gather(up_weight, "fsdp", axis=1, tiled=True),
        lax.all_gather(down_weight, "fsdp", axis=1, tiled=True),
    )
    out_back = out_again[0]
    cot_group = lax.all_gather(cotangent, "tensor", axis=0, tiled=True).astype(jnp.float32)
    grad_combined = (gate_value[:, None] * cot_group).astype(jnp.bfloat16)
    gate_grad_own = jnp.sum(cotangent.astype(jnp.float32) * combined, axis=-1)
    gate_grad_placed = lax.dynamic_update_slice_in_dim(
        jnp.zeros((group_rows,), jnp.float32), gate_grad_own, own_start, 0
    )
    grad_slots = (
        jnp.zeros((EXPERTS * CAP, model_width), jnp.bfloat16)
        .at[slot_rows]
        .set(grad_combined, mode="drop")
        .reshape(EXPERTS, CAP, model_width)
    )
    grad_activated = jnp.einsum(
        "ecd,edf->ecf", grad_slots, down_back, preferred_element_type=jnp.float32
    )
    down_grad = jnp.einsum(
        "ecd,ecf->edf", grad_slots, activated, preferred_element_type=jnp.float32
    )
    grad_before = (grad_activated * gelu_slope(before)).astype(jnp.bfloat16)
    up_grad = jnp.einsum(
        "ecd,ecf->edf", dispatched, grad_before, preferred_element_type=jnp.float32
    )
    grad_dispatched = jnp.einsum(
        "ecf,edf->ecd", grad_before, up_back, preferred_element_type=jnp.float32
    ).reshape(EXPERTS * CAP, model_width)
    grad_input_part = jnp.concatenate(
        [grad_dispatched, jnp.zeros((1, model_width), jnp.float32)], axis=0
    )[slot_rows]
    grad_moe, gate_grad = lax.psum((grad_input_part, gate_grad_placed), "tensor")
    gate_slope = gate_value * (1.0 - gate_value)
    mixed_share = jnp.sum(router_prob * route_share[None, :], axis=-1, keepdims=True)
    logit_grad = onehot * (gate_grad * gate_slope)[
        :, None
    ] + balance_weight * EXPERTS / all_tokens * router_prob * (route_share[None, :] - mixed_share)
    grad_norm_two = grad_moe + jnp.dot(
        logit_grad, router_back.astype(jnp.float32), precision=highest
    )
    router_grad = jnp.dot(logit_grad.T, moe_input.astype(jnp.float32), precision=highest)
    grad_hidden, gain_two_grad = norm_back(
        grad_norm_two, hidden_group, factor_two, gains_back[1].astype(jnp.float32)
    )
    grad_hidden = grad_hidden + cot_group
    grad_branch = grad_hidden.astype(jnp.bfloat16)
    grad_att = jnp.dot(grad_branch, out_back, preferred_element_type=jnp.float32).astype(
        jnp.bfloat16
    )
    out_grad = lax.dot_general(
        grad_branch, attended, (((0,), (0,)), ((), ())), preferred_element_type=jnp.float32
    )
    grad_project = attend_back(project, grad_att, log_total, prefix_len, score_scale)
    qkv_grad = jnp.einsum(
        "td,tsw->sdw", normed_one, grad_project, preferred_element_type=jnp.float32
    )
    grad_normed_part = jnp.einsum(
        "tsw,sdw->td", grad_project, qkv_back, preferred_element_type=jnp.float32
    )
    grad_normed = lax.psum(grad_normed_part, "tensor")
    grad_tokens, gain_one_grad = norm_back(
        grad_normed, input_float, factor_one, gains_back[0].astype(jnp.float32)
    )
    grad_tokens = grad_tokens + grad_hidden
    tokens_grad = lax.dynamic_slice_in_dim(grad_tokens, own_start, own_rows, 0)
    gains_own, qkv_own, out_own, router_own, up_own, down_own = (
        lax.psum_scatter(
            jnp.stack([gain_one_grad, gain_two_grad], axis=0),
            "fsdp",
            scatter_dimension=1,
            tiled=True,
        ),
        low_scatter(qkv_grad),
        low_scatter(out_grad[None]),
        lax.psum_scatter(router_grad, "fsdp", scatter_dimension=1, tiled=True),
        low_scatter(up_grad),
        low_scatter(down_grad),
    )
    return (
        block_out,
        tokens_grad,
        gains_own,
        qkv_own,
        out_own[0],
        router_own,
        up_own,
        down_own,
        balance_loss,
    )


def solution(mesh):
    placed = (
        P(("fsdp", "tensor"), None),
        P(("fsdp", "tensor"), None),
        P("fsdp"),
        P("fsdp", None),
        P(None, "fsdp"),
        P(None, "fsdp", "tensor"),
        P("fsdp", "tensor"),
        P(None, "fsdp"),
        P(None, "fsdp", "tensor"),
        P(None, "fsdp", "tensor"),
    )
    fits = mesh.shape["fsdp"] == 16 and mesh.shape["tensor"] == 2
    return jax.shard_map(
        fast_device if fits else per_device,
        mesh=mesh,
        in_specs=placed,
        out_specs=(
            P(("fsdp", "tensor"), None),
            P(("fsdp", "tensor"), None),
            P(None, "fsdp"),
            P(None, "fsdp", "tensor"),
            P("fsdp", "tensor"),
            P(None, "fsdp"),
            P(None, "fsdp", "tensor"),
            P(None, "fsdp", "tensor"),
            P(),
        ),
        check_vma=False,
    )
```

```python
import math
import types

import jax
import jax.numpy as jnp
from jax import lax
from jax.experimental import pallas as pl
from jax.experimental.pallas import tpu as pltpu
from jax.sharding import PartitionSpec as P

MESH = pl.DeviceIdType.MESH
BF = jnp.bfloat16
F32 = jnp.float32
ROWS = 1024
WIDE = 768
HALF = 384
HID = 1536
norm_eps = 1e-05
balance_weight = 0.01
masked_score = -1e30


def mm(a, b, ca=1, cb=0):
    return lax.dot_general(a, b, (((ca,), (cb,)), ((), ())), preferred_element_type=F32)


def iota(shape, axis):
    return lax.broadcasted_iota(jnp.int32, shape, axis)


def blocks(count, size, body):
    def step(i, carry):
        body(pl.ds(pl.multiple_of(i * size, size), size))
        return carry

    lax.fori_loop(0, count // size, step, 0)


class Place:
    def __init__(self):
        f, t = lax.axis_index("fsdp"), lax.axis_index("tensor")
        self.f, self.t, self.o = f, t, 1 - t
        self.z, self.c = lax.div(f, 4), lax.rem(f, 4)
        c = self.c
        self.cx = c + 1 - 2 * lax.rem(c, 2)
        self.cy = c + 2 - 4 * lax.div(c, 2)
        self.cd = 3 - c
        base = 4 * self.z
        self.X = {"fsdp": base + self.cx, "tensor": t}
        self.Y = {"fsdp": base + self.cy, "tensor": t}
        self.DIAG = {"fsdp": base + self.cd, "tensor": t}
        self.PAIR = {"fsdp": f, "tensor": 1 - t}

    def zto(self, k):
        return lax.rem(self.z + k, 4)

    def zfrom(self, k):
        return lax.rem(self.z + 4 - k, 4)

    def plane(self, z):
        return {"fsdp": 4 * z + self.c, "tensor": self.t}

    def Z(self, k):
        return {"fsdp": 4 * self.zto(k) + self.c, "tensor": self.t}


class Wire:
    def __init__(self, send, recv):
        self.send, self.recv, self.n, self.open = send, recv, 0, []

    def ids(self, n):
        self.n += n
        return self.n - n

    def copy(self, i, src, dst, dev):
        return pltpu.make_async_remote_copy(
            src_ref=src,
            dst_ref=dst,
            send_sem=self.send.at[i],
            recv_sem=self.recv.at[i],
            device_id=dev,
            device_id_type=MESH,
        )

    def go(self, i, src, dst, dev):
        c = self.copy(i, src, dst, dev)
        c.start()
        self.open.append(c)
        return c

    def flush(self):
        for c in self.open:
            c.wait_send()
        self.open = []


def joined(ref, rows):
    return jnp.concatenate([ref[p, rows] for p in range(3)], axis=1)


def enter(pc):
    barrier = pltpu.get_barrier_semaphore()
    for dev in (pc.PAIR, pc.X, pc.Y, pc.DIAG, pc.Z(1), pc.Z(2), pc.Z(3)):
        pl.semaphore_signal(barrier, inc=1, device_id=dev, device_id_type=MESH)
    pl.semaphore_wait(barrier, 7)


def order(i):
    return i + lax.div(i, 2) * (5 - 2 * i)


def visible(krow0, kn, qcol0, qn, prefix):
    kpos = krow0 + iota((kn, qn), 0)
    qpos = qcol0 + iota((kn, qn), 1)
    ok = kpos <= qpos
    if krow0 < 512 and qcol0 < 512:
        ok = ok | (kpos < prefix)
    return ok


SEEN = (
    ((0, 512, True),),
    ((0, 512, True),),
    ((0, 512, False), (512, 256, True)),
    ((0, 512, False), (512, 256, False), (768, 256, True)),
)


def hook(table, p, qb):
    for (pp, qq), step in table.items():
        if qq == qb:
            pl.when(p == pp)(step)


def both(*steps):
    def run():
        for step in steps:
            step()

    return run


def phase_a(R, pc, w):
    f, t, z, c = pc.f, pc.t, pc.z, pc.c
    idr = R.idr[...]
    ohr = (iota((16, ROWS), 0) - 8 == idr).astype(F32)
    cnt = jnp.sum(ohr, axis=1, keepdims=True)
    hi = jnp.floor(cnt * (1.0 / 256.0))
    lane16 = iota((16, 128), 1)
    six = jnp.concatenate(
        [R.gains[...].astype(F32), R.router[...].astype(F32), jnp.zeros((10, 48), F32)], axis=0
    )
    small = jnp.concatenate([six, jnp.zeros((16, 80), F32)], axis=1)
    R.SM[f] = jnp.where(
        lane16 == 48,
        cnt - 256.0 * hi,
        jnp.where(lane16 == 49, hi, small),
    ).astype(BF)
    R.WA[z, c, pl.ds(0, 3)] = R.qkv[...]
    R.WA[z, c, 3] = R.out[...]
    enter(pc)
    own = pl.ds(pl.multiple_of(t * 512, 512), 512)
    i_tok, i_cot, i_wo, i_att = w.ids(1), w.ids(1), w.ids(1), w.ids(3)
    i_up, i_dn, i_sz, i_s = w.ids(3) - 1, w.ids(3) - 1, w.ids(3) - 1, w.ids(3)
    i_x, i_y, i_fx, i_fy = (w.ids(4) for _ in range(4))
    i_mz = w.ids(18) - 1
    i_m = [w.ids(3) for _ in range(6)]
    i_cz, i_dz, i_cp, i_dp = w.ids(3) - 1, w.ids(3) - 1, w.ids(4), w.ids(4)

    SM = R.SM.reshape(4, 4, 16, 128)
    zs = [w.go(i_sz + k, SM.at[z, c], SM.at[z, c], pc.Z(k)) for k in (1, 2, 3)]

    def up(d):
        block = R.WA.at[z - d + 1, c]
        return w.copy(i_up + d, block, block, pc.plane(z + 1))

    def down(d):
        block = R.WA.at[z + d - 1, c]
        return w.copy(i_dn + d, block, block, pc.plane(z - 1))

    def spread(zz):
        block = R.WA.at[zz, c]
        return w.copy(i_x + zz, block, block, pc.X), w.copy(i_y + zz, block, block, pc.Y)

    def forward(zz):
        a = R.WA.at[zz, pc.cx, pl.ds(0, 2)]
        b = R.WA.at[zz, pc.cy, pl.ds(2, 2)]
        return w.copy(i_fx + zz, a, a, pc.Y), w.copy(i_fy + zz, b, b, pc.X)

    def start_all(copies):
        for m in copies:
            m.start()

    def pass_on(zz):
        for m in spread(zz):
            m.wait_recv()
        start_all(forward(zz))

    def stage(d):
        @pl.when(z >= d)
        def _():
            w.copy(i_up + d, R.WA.at[z, c], R.WA.at[z, c], pc.plane(z - 1)).wait_recv()
            start_all(spread(z - d))
            if d < 3:
                pl.when(z < 3)(lambda: up(d + 1).start())

        @pl.when(z + d <= 3)
        def _():
            w.copy(i_dn + d, R.WA.at[z, c], R.WA.at[z, c], pc.plane(z + 1)).wait_recv()
            start_all(spread(z + d))
            if d < 3:
                pl.when(z > 0)(lambda: down(d + 1).start())

    def pass_on_stage(d):
        pl.when(z >= d)(lambda: pass_on(z - d))
        pl.when(z + d <= 3)(lambda: pass_on(z + d))

    pl.when(z < 3)(lambda: up(1).start())
    pl.when(z > 0)(lambda: down(1).start())
    start_all(spread(z))
    cot_x = w.go(i_cot, R.cot, R.CT.at[own], pc.PAIR)
    tok_x = w.go(i_tok, R.tok, R.TK.at[own], pc.PAIR)
    local = [
        pltpu.make_async_copy(R.tok, R.TK.at[own], R.ls.at[0]),
        pltpu.make_async_copy(R.cot, R.CT.at[own], R.ls.at[1]),
        pltpu.make_async_copy(R.up.at[z], R.UE.at[z, c], R.ls.at[2]),
        pltpu.make_async_copy(R.down.at[z], R.DE.at[z, c], R.ls.at[3]),
    ]
    for m in local:
        m.start()
    before_or_at = (iota((ROWS, ROWS), 0) <= iota((ROWS, ROWS), 1)).astype(F32).astype(BF)
    running = mm(ohr.astype(BF), before_or_at)
    placed = jnp.sum(running * ohr, axis=0, keepdims=True) - 1.0
    key = jnp.where(placed < 256.0, idr.astype(F32) * 256.0 + placed, -1.0)
    R.KC[...] = jnp.broadcast_to(key, (128, ROWS)).T
    R.PR[...] = jnp.broadcast_to(idr.astype(F32), (128, ROWS)).T
    r = iota((512, ROWS), 0)
    want = lax.div(r, 128) * 256 + lax.rem(r, 128) + 128 * t
    R.ACT[0:512, 0:ROWS] = (key.astype(jnp.int32) == want).astype(F32).astype(BF)

    stage(1)
    pass_on(z)
    for m in local:
        m.wait()
    cot_x.wait_recv()

    def cot_rows(e, carry):
        R.CQ[e] = mm(R.ACT[pl.ds(pl.multiple_of(e * 128, 128), 128), pl.ds(0, ROWS)], R.CT[...]).astype(BF)
        return carry

    lax.fori_loop(0, 4, cot_rows, 0)
    R.CR[z, t] = R.CQ[z]
    w.copy(i_cp, R.CR.at[z, t], R.CR.at[z, t], pc.PAIR).start()
    stage(2)
    for m in zs:
        m.wait_recv()
    mine = SM.at[:, c]
    sx, sy = w.go(i_s, mine, mine, pc.X), w.go(i_s + 1, mine, mine, pc.Y)
    pass_on_stage(1)

    def chunk(j):
        return pl.ds(pl.multiple_of(j * 512, 128), 512)

    def from_plane(j):
        out = []
        for k in (1, 3, 2):
            to, cols, i = pc.zto(k), chunk(j), i_mz + 6 * j + k
            out.append(w.copy(i, R.up.at[to, :, cols], R.UE.at[z, c, :, cols], pc.Z(k)))
            out.append(w.copy(i + 3, R.down.at[to, :, cols], R.DE.at[z, c, :, cols], pc.Z(k)))
        return out

    def moe_spread(j):
        u, d = R.UE.at[:, c, :, chunk(j)], R.DE.at[:, c, :, chunk(j)]
        return [
            w.copy(i_m[0] + j, u, u, pc.X),
            w.copy(i_m[1] + j, d, d, pc.Y),
            w.copy(i_m[2] + j, u, u, pc.Y),
            w.copy(i_m[3] + j, d, d, pc.X),
        ]

    def moe_forward(j):
        u, d = R.UE.at[:, pc.cx, :, chunk(j)], R.DE.at[:, pc.cy, :, chunk(j)]
        return [w.copy(i_m[4] + j, u, u, pc.Y), w.copy(i_m[5] + j, d, d, pc.X)]

    def start_spread(j):
        for m in from_plane(j):
            m.wait()
        for m in moe_spread(j):
            m.start()

    def start_forward(j):
        a = moe_spread(j)
        a[0].wait()
        a[1].wait()
        for m in moe_forward(j):
            m.start()

    def weights_here(j):
        for m in moe_spread(j)[2:] + moe_forward(j):
            m.wait()

    def start_plane(j):
        for m in from_plane(j):
            m.start()

    def start_cot():
        for m in cz:
            m.start()

    cz = [w.copy(i_cz + k, R.CQ.at[pc.zto(k)], R.CR.at[z, t], pc.Z(k)) for k in (1, 3, 2)]
    start_plane(0)
    stage(3)
    sx.wait_recv()
    theirs = SM.at[:, pc.cx]
    sf = w.go(i_s + 2, theirs, theirs, pc.Y)
    pass_on_stage(2)
    pass_on_stage(3)
    start_plane(1)
    agenda = {
        (0, 3): lambda: start_spread(1),
        (1, 1): lambda: start_forward(0),
        (2, 1): both(lambda: start_spread(2), start_cot),
        (2, 3): lambda: start_forward(1),
    }

    tok_x.wait_recv()

    def factors(rows):
        x = R.TK[rows].astype(F32)
        R.STAT[rows, 0:1] = lax.rsqrt(jnp.mean(x * x, axis=1, keepdims=True) + norm_eps)

    blocks(ROWS, 128, factors)
    sy.wait_recv()
    sf.wait_recv()
    parts = [R.SM[g].astype(F32)[:, 0:48] for g in range(16)]
    vecs = jnp.concatenate(parts, axis=1)
    R.VEC[...] = vecs
    R.RW[...] = jnp.concatenate([vecs, jnp.zeros((112, WIDE), F32)], axis=0).T.astype(BF)
    total = jnp.zeros((16, 128), F32)
    for g in range(16):
        total = total + R.SM[g].astype(F32)
    counts = jnp.sum(
        jnp.where(lane16 == 48, total, jnp.where(lane16 == 49, 256.0 * total, 0.0)),
        axis=1,
        keepdims=True,
    )
    share = jnp.sum(
        jnp.where(iota((16, 128), 0) - 8 == lane16 - 2, counts, 0.0), axis=0, keepdims=True
    ) * (1.0 / (16 * ROWS))
    R.SHARE[...] = jnp.broadcast_to(share, (8, 128))

    def norm_one(rows):
        x = R.TK[rows].astype(F32)
        R.NM[rows] = (x * R.STAT[rows, 0:1] * R.VEC[0:1]).astype(BF)

    blocks(ROWS, 128, norm_one)
    for zz in range(4):
        for m in spread(zz):
            m.wait_send()
        for m in forward(zz):
            m.wait()
    for d in (1, 2, 3):
        pl.when((z < 3) & (z >= d - 1))(lambda: up(d).wait_send())
        pl.when((z > 0) & (z + d - 1 <= 3))(lambda: down(d).wait_send())
    wo = w.go(i_wo, R.WA.at[:, :, 3], R.WO, pc.PAIR)

    start_spread(0)
    start_plane(2)

    def project(rows):
        x = R.NM[rows]
        for s, ref in enumerate((R.QS, R.KS, R.VS)):
            y = mm(x, R.WA[:, :, s].reshape(WIDE, HALF))
            if s == 0:
                y = y.astype(BF).astype(F32) * 0.125
            for p in range(3):
                ref[p, rows] = y[:, 128 * p : 128 * p + 128].astype(BF)

    blocks(ROWS, 256, project)
    prefix = R.pre[0]

    def pair_of_heads(p, carry):
        value_t = R.VS[p].astype(F32).T.astype(BF)
        even = iota((256, 128), 1) < 64
        for qb in range(4):
            cols = pl.ds(qb * 256, 256)
            outs = []
            for i in range(2):
                q = R.QS[p, cols]
                q = jnp.where(even if i == 0 else ~even, q.astype(F32), 0.0).astype(BF)
                pieces = []
                for k0, kn, masked in SEEN[qb]:
                    s = mm(R.KS[p, pl.ds(k0, kn)], q, 1, 1)
                    if masked:
                        s = jnp.where(visible(k0, kn, qb * 256, 256, prefix), s, masked_score)
                    pieces.append(s)
                top = pieces[0].max(axis=0, keepdims=True)
                for s in pieces[1:]:
                    top = jnp.maximum(top, s.max(axis=0, keepdims=True))
                total_e = jnp.zeros((1, 256), F32)
                out = jnp.zeros((128, 256), F32)
                for (k0, kn, _), s in zip(SEEN[qb], pieces):
                    e = jnp.exp(s - top)
                    total_e = total_e + e.sum(axis=0, keepdims=True)
                    out = out + mm(value_t[:, k0 : k0 + kn], e.astype(BF))
                R.LT[p, i : i + 1, cols] = top + jnp.log(total_e)
                outs.append(out / total_e)
            merged = jnp.where(iota((128, 256), 0) < 64, outs[0], outs[1])
            R.ATO[p, cols] = merged.T.astype(BF)
            if qb == 3:
                w.copy(i_att + p, R.ATO.at[p], R.ATX.at[p], pc.PAIR).start()
            hook(agenda, p, qb)
        return carry

    lax.fori_loop(0, 3, pair_of_heads, 0)
    wo.wait_recv()
    for p in range(3):
        w.copy(i_att + p, R.ATO.at[p], R.ATX.at[p], pc.PAIR).wait()
    lane = iota((256, 128), 1)
    real = (lane >= 2) & (lane < 6)
    R.PS[...] = jnp.zeros((8, 128), F32)

    def out_block(rows):
        b = mm(joined(R.ATO, rows), R.WA[:, :, 3].reshape(WIDE, HALF), 1, 1)
        b = b + mm(joined(R.ATX, rows), R.WO[...].reshape(WIDE, HALF), 1, 1)
        h = R.TK[rows].astype(F32) + b
        R.HIDN[rows] = h
        f2 = lax.rsqrt(jnp.mean(h * h, axis=1, keepdims=True) + norm_eps)
        R.STAT[rows, 1:2] = f2
        moe = (h * f2 * R.VEC[1:2]).astype(BF)
        R.GC[rows] = moe
        logits = mm(moe, R.RW[...])
        mine = jnp.where((lane - 2).astype(F32) == R.PR[rows], logits, 0.0)
        picked = jnp.sum(jnp.where(real, mine, 0.0), axis=1, keepdims=True)
        R.STAT[rows, 2:3] = jax.nn.sigmoid(picked)
        lg = jnp.where(real, logits, masked_score)
        e = jnp.exp(lg - jnp.max(lg, axis=1, keepdims=True))
        e = jnp.where(real, e, 0.0)
        pr = e / jnp.sum(e, axis=1, keepdims=True)
        R.PR[rows] = pr
        R.PS[0:1] = R.PS[0:1] + jnp.sum(pr, axis=0, keepdims=True)

    blocks(ROWS, 256, out_block)

    def moe_rows(i, carry):
        k = order(lax.rem(i + 1, 4))
        e = pc.zto(k)
        R.CS[e] = mm(R.ACT[pl.ds(pl.multiple_of(e * 128, 128), 128), pl.ds(0, ROWS)], R.GC[...]).astype(BF)

        @pl.when(i < 3)
        def _():
            w.copy(i_dz + k, R.CS.at[e], R.DR.at[z, t], pc.Z(k)).start()

        return carry

    lax.fori_loop(0, 4, moe_rows, 0)
    R.DR[z, t] = R.CS[z]
    w.copy(i_dp, R.DR.at[z, t], R.DR.at[z, t], pc.PAIR).start()
    start_forward(2)
    w.flush()
    return i_dz, i_dp, i_cz, i_cp, weights_here


def gelu_parts(v):
    cdf = 0.5 * (1.0 + lax.erf(v * (1.0 / math.sqrt(2.0))))
    slope = cdf + v * (jnp.exp(-0.5 * v * v) * (1.0 / math.sqrt(2.0 * math.pi)))
    return v * cdf, slope


class ExpertSums:
    def __init__(self, R, pc, w):
        self.R, self.pc, self.w = R, pc, w
        self.i1, self.i2, self.i3 = w.ids(16), w.ids(8), w.ids(24) - 1

    def cols(self, g):
        return pl.ds(pl.multiple_of(384 * g, 128), 384)

    def step_one(self, g):
        R, pc, w = self.R, self.pc, self.w
        cols, i = self.cols(g), self.i1 + 4 * g
        return [
            w.copy(i, R.UE.at[:, pc.cx, :, cols], R.RU.at[0, :, :, cols], pc.X),
            w.copy(i + 1, R.UE.at[:, pc.cd, :, cols], R.RU.at[1, :, :, cols], pc.X),
            w.copy(i + 2, R.DE.at[:, pc.cy, :, cols], R.RD.at[0, :, :, cols], pc.Y),
            w.copy(i + 3, R.DE.at[:, pc.cd, :, cols], R.RD.at[1, :, :, cols], pc.Y),
        ]

    def step_two(self, g):
        R, pc, w = self.R, self.pc, self.w
        cols, i = self.cols(g), self.i2 + 2 * g
        return [
            w.copy(i, R.UE.at[:, pc.cy, :, cols], R.RU2.at[:, :, cols], pc.Y),
            w.copy(i + 1, R.DE.at[:, pc.cx, :, cols], R.RD2.at[:, :, cols], pc.X),
        ]

    def step_three(self, g):
        R, pc, w = self.R, self.pc, self.w
        cols, i, out = self.cols(g), self.i3 + 6 * g, []
        for k in (1, 2, 3):
            to, z = pc.zto(k), pc.z
            out.append(w.copy(i + k, R.UE.at[to, pc.c, :, cols], R.ZU.at[z, :, cols], pc.Z(k)))
            out.append(w.copy(i + 3 + k, R.DE.at[to, pc.c, :, cols], R.ZD.at[z, :, cols], pc.Z(k)))
        return out

    def one(self, g):
        for m in self.step_one(g):
            m.start()

    def two(self, g):
        R, pc, cols = self.R, self.pc, self.cols(g)
        for m in self.step_one(g):
            m.wait()

        def add(zz, carry):
            R.UE[zz, pc.cy, :, cols] = R.UE[zz, pc.cy, :, cols] + R.RU[1, zz, :, cols]
            R.DE[zz, pc.cx, :, cols] = R.DE[zz, pc.cx, :, cols] + R.RD[1, zz, :, cols]
            R.UE[zz, pc.c, :, cols] = R.UE[zz, pc.c, :, cols] + R.RU[0, zz, :, cols]
            R.DE[zz, pc.c, :, cols] = R.DE[zz, pc.c, :, cols] + R.RD[0, zz, :, cols]
            return carry

        lax.fori_loop(0, 4, add, 0)
        for m in self.step_two(g):
            m.start()

    def three(self, g):
        R, pc, cols = self.R, self.pc, self.cols(g)
        for m in self.step_two(g):
            m.wait()

        def add(zz, carry):
            R.UE[zz, pc.c, :, cols] = R.UE[zz, pc.c, :, cols] + R.RU2[zz, :, cols]
            R.DE[zz, pc.c, :, cols] = R.DE[zz, pc.c, :, cols] + R.RD2[zz, :, cols]
            return carry

        lax.fori_loop(0, 4, add, 0)
        for m in self.step_three(g):
            m.start()

    def last(self):
        R, pc = self.R, self.pc
        R.ZU[pc.z] = R.UE[pc.z, pc.c]
        R.ZD[pc.z] = R.DE[pc.z, pc.c]
        out = []
        for g in range(4):
            for m in self.step_three(g):
                m.wait()
        for g in (0, 1):
            cols = pl.ds(768 * g, 768)
            for j, (got, to) in enumerate(((R.ZU, R.up_grad), (R.ZD, R.down_grad))):
                held = R.HIDN.at[pl.ds(192 * (2 * g + j), 192)].reshape(4, 48, 768)
                held[...] = got[:, :, cols].astype(F32)
                m = pltpu.make_async_copy(held, to.at[:, :, cols], R.ls.at[2 * g + j])
                m.start()
                out.append(m)
        return out


class AttentionSums:
    def __init__(self, R, pc, w):
        self.R, self.pc, self.w = R, pc, w
        self.i1, self.i2, self.i3 = w.ids(16), w.ids(8), w.ids(12) - 1
        self.low, self.high = pl.ds(0, 2), pl.ds(2, 2)

    def step_one(self, n):
        R, pc, w, i = self.R, self.pc, self.w, self.i1 + 4 * n
        return [
            w.copy(i, R.AG.at[n, self.low, pc.cx], R.RA.at[n, 0], pc.X),
            w.copy(i + 1, R.AG.at[n, self.low, pc.cd], R.RA.at[n, 1], pc.X),
            w.copy(i + 2, R.AG.at[n, self.high, pc.cy], R.RB.at[n, 0], pc.Y),
            w.copy(i + 3, R.AG.at[n, self.high, pc.cd], R.RB.at[n, 1], pc.Y),
        ]

    def step_two(self, n):
        R, pc, w, i = self.R, self.pc, self.w, self.i2 + 2 * n
        return [
            w.copy(i, R.AG.at[n, self.low, pc.cy], R.RA2.at[n], pc.Y),
            w.copy(i + 1, R.AG.at[n, self.high, pc.cx], R.RB2.at[n], pc.X),
        ]

    def step_three(self, n):
        R, pc, w, i = self.R, self.pc, self.w, self.i3 + 3 * n
        return [
            w.copy(i + k, R.AG.at[n, pc.zto(k), pc.c], R.ZA.at[n, pc.z], pc.Z(k))
            for k in (1, 2, 3)
        ]

    def one(self, n):
        for m in self.step_one(n):
            m.start()

    def two(self, n):
        R, pc = self.R, self.pc
        for m in self.step_one(n):
            m.wait()
        for j in range(2):
            R.AG[n, j, pc.cy] = R.AG[n, j, pc.cy] + R.RA[n, 1, j]
            R.AG[n, 2 + j, pc.cx] = R.AG[n, 2 + j, pc.cx] + R.RB[n, 1, j]
            R.AG[n, j, pc.c] = R.AG[n, j, pc.c] + R.RA[n, 0, j]
            R.AG[n, 2 + j, pc.c] = R.AG[n, 2 + j, pc.c] + R.RB[n, 0, j]
        for m in self.step_two(n):
            m.start()

    def three(self, n):
        R, pc = self.R, self.pc
        for m in self.step_two(n):
            m.wait()
        for j in range(2):
            R.AG[n, j, pc.c] = R.AG[n, j, pc.c] + R.RA2[n, j]
            R.AG[n, 2 + j, pc.c] = R.AG[n, 2 + j, pc.c] + R.RB2[n, j]
        for m in self.step_three(n):
            m.start()

    def last(self, n):
        R, pc = self.R, self.pc
        R.ZA[n, pc.z] = R.AG[n, pc.z, pc.c]
        for m in self.step_three(n):
            m.wait()
        total = R.ZA[n, 0].astype(F32)
        for zz in range(1, 4):
            total = total + R.ZA[n, zz].astype(F32)
        for j in range(3):
            block = total[48 * j : 48 * j + 48]
            if n == 0:
                R.out_grad[:, 128 * j : 128 * j + 128] = block
            else:
                R.qkv_grad[j, :, 128 * (n - 1) : 128 * n] = block


def phase_b(R, pc, w, i_dz, i_dp, i_cz, i_cp, weights_here):
    f, t, z, c, o = pc.f, pc.t, pc.z, pc.c, pc.o
    i_xe, i_xg = w.ids(4), w.ids(4)
    i_rg, i_re, i_rgp, i_rep = w.ids(3) - 1, w.ids(3) - 1, w.ids(1), w.ids(1)
    lane = iota((256, 128), 1)
    row = jnp.sum(
        jnp.where(iota((16, WIDE), 0) == 2 + z, R.VEC[...], 0.0), axis=0, keepdims=True
    )
    R.RGR[...] = jnp.zeros((16, WIDE), F32)

    def to_plane(s):
        return {"fsdp": 4 * s + c, "tensor": t}

    def rows_in(k):
        return w.copy(i_dz + k, R.CS.at[pc.zto(k)], R.DR.at[z, t], pc.Z(k))

    def cot_in(k):
        return w.copy(i_cz + k, R.CQ.at[pc.zto(k)], R.CR.at[z, t], pc.Z(k))

    def rows_pair(k):
        s = pc.zfrom(k)
        return (
            w.copy(i_dp + k, R.DR.at[s, t], R.DR.at[s, t], pc.PAIR),
            w.copy(i_cp + k, R.CR.at[s, t], R.CR.at[s, t], pc.PAIR),
        )

    def pair_sums(k):
        s = pc.zfrom(k)
        return (
            w.copy(i_xg + k, R.PG.at[s], R.XG.at[s], pc.PAIR),
            w.copy(i_xe + k, R.PE.at[s], R.XE.at[s], pc.PAIR),
        )

    def home(k):
        s = pc.zfrom(k)
        return w.copy(i_rg + k, R.XG.at[s], R.RG.at[z, t], to_plane(s))

    def home_out(k):
        s = pc.zfrom(k)
        return w.copy(i_re + k, R.XE.at[s], R.RE.at[z, t], to_plane(s))

    def finish(k):
        s = pc.zfrom(k)
        for m in pair_sums(k):
            m.wait()
        eo = R.EOO[s] + R.XE[s].astype(F32)
        gate = R.STAT[pl.ds(pl.multiple_of(s * 256 + t * 128, 128), 128), 3:4]
        gate_grad = jnp.sum(R.CR[s, t].astype(F32) * eo, axis=1, keepdims=True)
        gs = gate_grad * gate * (1.0 - gate)
        R.RGR[0:1] += jnp.sum(gs * R.DR[s, t].astype(F32), axis=0, keepdims=True)
        R.XG[s] = (R.GMO[s] + R.XG[s].astype(F32) + gs * row).astype(BF)
        R.XE[s] = eo.astype(BF)

    def source(i, carry):
        k = order(i)
        s = pc.zfrom(k)
        rows = pl.ds(pl.multiple_of(s * 256, 256), 256)

        for m in rows_pair(k):
            m.wait()
        x = R.DR[s].reshape(256, WIDE)
        logits = mm(x, R.RW[...])
        gate = jax.nn.sigmoid(
            jnp.sum(jnp.where(lane == 2 + z, logits, 0.0), axis=1, keepdims=True)
        )
        R.STAT[rows, 3:4] = gate
        R.GC[rows] = (gate * R.CR[s].reshape(256, WIDE).astype(F32)).astype(BF)

        def hidden_units(j, carry):
            @pl.when(i == 0)
            def _():
                weights_here(j)

            cols = pl.ds(pl.multiple_of(j * 512, 128), 512)
            up = R.UE[:, :, :, cols].reshape(WIDE, 512)
            down = R.DE[:, :, :, cols].reshape(WIDE, 512)
            act, slope = gelu_parts(mm(R.DR[s].reshape(256, WIDE), up))
            act = act.astype(BF)
            gb = (mm(R.GC[rows], down) * slope).astype(BF)
            R.ACT[rows, cols] = act
            R.GB[rows, cols] = gb
            return carry

        lax.fori_loop(0, 3, hidden_units, 0)
        @pl.when(i < 3)
        def _():
            after = order(i + 1)
            cot_in(after).wait()
            rows_pair(after)[1].start()
            rows_in(after).wait()
            rows_pair(after)[0].start()

        up, down = R.UE[...].reshape(WIDE, HID), R.DE[...].reshape(WIDE, HID)
        R.GMB[...] = mm(R.GB[rows], up, 1, 1).reshape(2, 128, WIDE)
        R.PG[s] = R.GMB[o].astype(BF)
        pair_sums(k)[0].start()
        R.GMO[s] = R.GMB[t]
        R.GMB[...] = mm(R.ACT[rows], down, 1, 1).reshape(2, 128, WIDE)
        R.PE[s] = R.GMB[o].astype(BF)
        pair_sums(k)[1].start()
        R.EOO[s] = R.GMB[t]

        @pl.when(i > 0)
        def _():
            last = order(i - 1)
            finish(last)

            @pl.when(i > 1)
            def _():
                home(last).start()

        return carry

    lax.fori_loop(0, 4, source, 0)
    finish(2)
    home(2).start()
    R.RG[z, t] = R.XG[z]
    R.RE[z, t] = R.XE[z]
    R.RGR[...] = jnp.where(iota((16, WIDE), 0) == 2 + z, R.RGR[0:1], 0.0)
    sums = ExpertSums(R, pc, w)
    DR = R.DR.reshape(ROWS, WIDE)

    def weight_grads(i, carry):
        cols = pl.ds(pl.multiple_of(i * 384, 128), 384)
        R.UE[:, :, :, cols] = mm(DR[...], R.GB[:, cols], 0, 0).astype(BF).reshape(4, 4, 48, 384)
        R.DE[:, :, :, cols] = mm(R.GC[...], R.ACT[:, cols], 0, 0).astype(BF).reshape(4, 4, 48, 384)


        @pl.when(i < 2)
        def _():
            for m in sums.step_one(i):
                m.start()

        return carry

    lax.fori_loop(0, 4, weight_grads, 0)
    share, vec = R.SHARE[0:1], R.VEC[...]
    R.SB[...] = jnp.zeros((16, WIDE), F32)

    def prepared(i, carry):
        rows = pl.ds(pl.multiple_of(i * 256, 256), 256)
        R.ACT[rows, pl.ds(0, ROWS)] = pick_rows(R.KC[rows])
        pr = R.PR[rows]
        mixed = jnp.sum(pr * share, axis=1, keepdims=True)
        aux = (balance_weight * 4.0 / (16 * ROWS)) * pr * (share - mixed)
        aux = aux[:, 0:16].astype(BF)
        R.GH[rows] = mm(aux, vec.astype(BF))
        mine = jnp.where(lax.div(i, 2) == t, 1.0, 0.0)
        moe = (R.HIDN[rows] * R.STAT[rows, 1:2] * vec[1:2]).astype(BF)
        R.SB[...] += mine * mm(aux, moe, 0, 0)
        return carry

    lax.fori_loop(0, 4, prepared, 0)
    sums.two(0)
    sums.one(2)
    for k in (1, 3, 2):
        home(k).wait()
    back = w.go(i_rgp, R.RG.at[:, t], R.RG.at[:, t], pc.PAIR)
    for k in (1, 3, 2):
        home_out(k).start()
    back.wait_recv()
    return sums, home_out, i_rep


def pick_rows(key):
    keys = jnp.concatenate([key] * 8, axis=1)
    return (keys == iota((key.shape[0], ROWS), 1).astype(F32)).astype(F32).astype(BF)


def phase_c(R, pc, w, sums, home_out, i_rep):
    f, t, z, c, o = pc.f, pc.t, pc.z, pc.c, pc.o
    att = AttentionSums(R, pc, w)
    i_n = w.ids(1)
    i_sp, i_sc, i_sz = w.ids(1), w.ids(3), w.ids(3) - 1
    own = pl.ds(pl.multiple_of(t * 512, 512), 512)
    GH, GN = R.GH, R.EOO.reshape(512, WIDE)
    RG, RE = R.RG.reshape(ROWS, WIDE), R.RE.reshape(ROWS, WIDE)
    GBR = R.GC
    share = R.SHARE[0:1]
    vec = R.VEC[...]
    head = iota((24, HALF), 0)
    head = jnp.where(lax.rem(head, 8) < 2, 2 * lax.div(head, 8) + lax.rem(head, 8), -1)
    pick_head = (head == lax.div(iota((24, HALF), 1), 64)).astype(F32).astype(BF)

    def residual(i, carry):
        rows = pl.ds(pl.multiple_of(i * 256, 256), 256)
        gm = mm(R.ACT[rows, pl.ds(0, ROWS)], RG[...]) + R.GH[rows]
        mine = jnp.where(lax.div(i, 2) == t, 1.0, 0.0)
        h, f2 = R.HIDN[rows], R.STAT[rows, 1:2]
        g = gm * vec[1:2]
        inner = jnp.mean(g * h, axis=1, keepdims=True)
        gh = R.CT[rows].astype(F32) + f2 * (g - h * (f2 * f2 * inner))
        R.G2[0:1] += mine * jnp.sum(gm * h * f2, axis=0, keepdims=True)
        GH[rows] = gh
        low = gh.astype(BF)
        GBR[rows] = low
        ga = mm(low, R.WA[:, :, 3].reshape(WIDE, HALF)).astype(BF)
        for p in range(3):
            R.ATX[p, rows] = ga[:, 128 * p : 128 * p + 128]
        prod = ga.astype(F32) * joined(R.ATO, rows).astype(F32)
        top = prod.astype(BF)
        rest = (prod - top.astype(F32)).astype(BF)
        dd = mm(pick_head, top, 1, 1) + mm(pick_head, rest, 1, 1)
        for p in range(3):
            R.DD[p, :, rows] = dd[8 * p : 8 * p + 8]

        @pl.when(i == 2)
        def _():
            sums.two(1)
            sums.one(3)

        return carry

    R.G2[...] = jnp.zeros((8, WIDE), F32)
    lax.fori_loop(0, 4, residual, 0)
    part = jnp.where(iota((16, WIDE), 0) == 1, R.G2[0:1], 0.0)
    sums6 = jnp.concatenate([0.5 * R.PS[0:1], jnp.zeros((1, WIDE - 128), F32)], axis=1)
    keep = (iota((16, WIDE), 0) >= 2) & (iota((16, WIDE), 0) < 6)
    R.SB[...] = (
        jnp.where(keep, R.SB[...] + R.RGR[...], 0.0)
        + part
        + jnp.where(iota((16, WIDE), 0) == 6, sums6, 0.0)
    )

    def place(n, grad):
        for j in range(3):
            block = grad[:, 128 * j : 128 * j + 128].astype(BF).reshape(4, 4, 48, 128)
            R.AG[n, :, :, pl.ds(48 * j, 48)] = block

    place(0, mm(GBR[...], joined(R.ATO, pl.ds(0, ROWS)), 0, 0))

    def outputs_pair():
        return w.copy(i_rep, R.RE.at[:, t], R.RE.at[:, t], pc.PAIR)

    def outputs_home():
        for k in (1, 2, 3):
            home_out(k).wait()
        outputs_pair().start()


    agenda = {
        (0, 1): both(lambda: sums.two(2), lambda: sums.three(0)),
        (0, 3): lambda: sums.three(1),
        (1, 2): lambda: sums.two(3),
        (1, 3): lambda: att.one(0),
        (2, 0): lambda: sums.three(2),
        (2, 1): outputs_home,
        (2, 2): lambda: sums.three(3),
        (2, 3): lambda: att.two(0),
    }
    prefix = R.pre[0]

    def pair_of_heads(p, carry):
        key_t = R.KS[p].astype(F32).T.astype(BF)
        R.DK[...] = jnp.zeros((ROWS, 128), F32)
        R.DV[...] = jnp.zeros((ROWS, 128), F32)
        even = iota((256, 128), 1) < 64
        for qb in range(4):
            cols = pl.ds(qb * 256, 256)
            outs = []
            for i in range(2):
                side = even if i == 0 else ~even
                q = jnp.where(side, R.QS[p, cols].astype(F32), 0.0).astype(BF)
                do = jnp.where(side, R.ATX[p, cols].astype(F32), 0.0).astype(BF)
                lt, dd = R.LT[p, i : i + 1, cols], R.DD[p, i : i + 1, cols]
                dq = jnp.zeros((128, 256), F32)
                for kb in range(max(2, qb + 1)):
                    keys = pl.ds(kb * 256, 256)
                    s = mm(R.KS[p, keys], q, 1, 1)
                    if kb == qb or qb < 2:
                        ok = visible(kb * 256, 256, qb * 256, 256, prefix)
                        s = jnp.where(ok, s, masked_score)
                    prob = jnp.exp(s - lt)
                    ds = prob * (mm(R.VS[p, keys], do, 1, 1) - dd)
                    ds = ds.astype(BF)
                    R.DV[keys] += mm(prob.astype(BF), do)
                    R.DK[keys] += mm(ds, q)
                    dq = dq + mm(key_t[:, kb * 256 : kb * 256 + 256], ds)
                outs.append(dq)
            merged = jnp.where(iota((128, 256), 0) < 64, outs[0], outs[1])
            R.QS[p, cols] = (merged * 0.125).T.astype(BF)
            hook(agenda, p, qb)
        R.KS[p] = R.DK[...].astype(BF)
        R.VS[p] = R.DV[...].astype(BF)
        three = jnp.concatenate([R.QS[p], R.KS[p], R.VS[p]], axis=1)
        place(p + 1, mm(R.NM[...], three, 0, 0))

        @pl.when(p == 1)
        def _():
            att.one(1)

        @pl.when(p > 0)
        def _():
            att.one(p + 1)

        return carry

    lax.fori_loop(0, 3, pair_of_heads, 0)
    GP = (R.QS, R.KS, R.VS)

    XS, XN, BO = (r.reshape(512, WIDE) for r in (R.CS, R.XG, R.PE))

    R.G2[...] = jnp.zeros((8, WIDE), F32)

    def normed_grad(i, carry):
        mine = pl.ds(pl.multiple_of(i * 256, 256), 256)

        def half(start):
            rows = pl.ds(pl.multiple_of(start * 512 + i * 256, 256), 256)
            acc = jnp.zeros((256, WIDE), F32)
            for s in range(3):
                acc = acc + mm(joined(GP[s], rows), R.WA[:, :, s].reshape(WIDE, HALF), 1, 1)
            x = R.TK[rows].astype(F32) * R.STAT[rows, 0:1]
            R.G2[0:1] += jnp.sum(acc * x, axis=0, keepdims=True)
            return acc

        XS[mine] = half(o).astype(BF)
        GN[mine] = half(t)
        return carry

    w.flush()
    lax.fori_loop(0, 2, normed_grad, 0)
    xn = w.go(i_n, XS, XN, pc.PAIR)
    R.SB[0:1] = R.G2[0:1]
    sp = w.go(i_sp, R.SB, R.SP, pc.PAIR)
    att.two(1)
    att.three(0)
    outputs_pair().wait()

    def block_rows(i, carry):
        rows = pl.ds(pl.multiple_of(i * 256, 256), 256)
        full = pl.ds(pl.multiple_of(t * 512 + i * 256, 256), 256)
        eo = mm(R.ACT[full, pl.ds(0, ROWS)], RE[...])
        BO[rows] = (R.HIDN[full] + R.STAT[full, 2:3] * eo).astype(BF)
        return carry

    lax.fori_loop(0, 2, block_rows, 0)
    out_b = pltpu.make_async_copy(BO, R.block_out, R.ls.at[1])
    out_b.start()
    att.two(2)
    att.three(1)
    sp.wait_recv()
    R.SC[c] = R.SB[...] + R.SP[...]
    sc = [
        w.go(i_sc, R.SC.at[c], R.SC.at[c], pc.X),
        w.go(i_sc + 1, R.SC.at[c], R.SC.at[c], pc.Y),
        w.go(i_sc + 2, R.SC.at[c], R.SC.at[c], pc.DIAG),
    ]
    xn.wait_recv()

    def input_grad(i, carry):
        rows = pl.ds(pl.multiple_of(i * 128, 128), 128)
        full = pl.ds(pl.multiple_of(t * 512 + i * 128, 128), 128)
        gn = GN[rows] + XN[rows].astype(F32)
        x, f1 = R.TK[full].astype(F32), R.STAT[full, 0:1]
        g = gn * R.VEC[0:1]
        inner = jnp.mean(g * x, axis=1, keepdims=True)
        GH[full] = GH[full] + f1 * (g - x * (f1 * f1 * inner))
        return carry

    lax.fori_loop(0, 4, input_grad, 0)
    out_t = pltpu.make_async_copy(GH.at[own], R.tokens_grad, R.ls.at[0])
    out_t.start()
    att.two(3)
    att.three(2)
    for m in sc:
        m.wait_recv()
    R.SZ[z] = R.SC[0] + R.SC[1] + R.SC[2] + R.SC[3]
    sz = [w.go(i_sz + k, R.SZ.at[z], R.SZ.at[z], pc.Z(k)) for k in (1, 2, 3)]
    att.three(3)
    out_t.wait()
    out_b.wait()
    written = sums.last()
    for n in range(3):
        att.last(n)
    for m in sz:
        m.wait_recv()
    total = R.SZ[0] + R.SZ[1] + R.SZ[2] + R.SZ[3]
    probs = total[6:7, 0:128]
    R.balance[...] = (4.0 / (16 * ROWS)) * jnp.sum(share * probs, axis=1, keepdims=True)
    column = (iota((WIDE, 128), 0) == 48 * f + iota((WIDE, 128), 1)).astype(F32).astype(BF)
    mine = jnp.zeros((16, 128), F32)
    for _ in range(3):
        top = total.astype(BF)
        mine = mine + mm(top, column)
        total = total - top.astype(F32)
    R.gains_grad[...] = mine[0:2, 0:48]
    R.router_grad[...] = mine[2:6, 0:48]
    att.last(3)
    for m in written:
        m.wait()
    w.flush()


OUTS = {
    "block_out": ((512, WIDE), BF),
    "tokens_grad": ((512, WIDE), F32),
    "gains_grad": ((2, 48), F32),
    "qkv_grad": ((3, 48, HALF), F32),
    "out_grad": ((48, HALF), F32),
    "router_grad": ((4, 48), F32),
    "up_grad": ((4, 48, HID), F32),
    "down_grad": ((4, 48, HID), F32),
    "balance": ((1, 1), F32),
}
SCRATCH = {
    "STAT": ((ROWS, 128), F32),
    "ATO": ((3, ROWS, 128), BF),
    "ATX": ((3, ROWS, 128), BF),
    "PG": ((4, 128, WIDE), BF),
    "CQ": ((4, 128, WIDE), BF),
    "PE": ((4, 128, WIDE), BF),
    "GMB": ((2, 128, WIDE), F32),
    "EOO": ((4, 128, WIDE), F32),
    "GMO": ((4, 128, WIDE), F32),
    "GH": ((ROWS, WIDE), F32),
    "ACT": ((ROWS, HID), BF),
    "GB": ((ROWS, HID), BF),
    "TK": ((ROWS, WIDE), BF),
    "CT": ((ROWS, WIDE), BF),
    "WA": ((4, 4, 4, 48, HALF), BF),
    "WO": ((4, 4, 48, HALF), BF),
    "UE": ((4, 4, 48, HID), BF),
    "DE": ((4, 4, 48, HID), BF),
    "KC": ((ROWS, 128), F32),
    "CR": ((4, 2, 128, WIDE), BF),
    "DR": ((4, 2, 128, WIDE), BF),
    "VEC": ((16, WIDE), F32),
    "RW": ((WIDE, 128), BF),
    "SHARE": ((8, 128), F32),
    "NM": ((ROWS, WIDE), BF),
    "QS": ((3, ROWS, 128), BF),
    "KS": ((3, ROWS, 128), BF),
    "VS": ((3, ROWS, 128), BF),
    "LT": ((3, 8, ROWS), F32),
    "HIDN": ((ROWS, WIDE), F32),
    "PR": ((ROWS, 128), F32),
    "PS": ((8, 128), F32),
    "SM": ((16, 16, 128), BF),
    "CS": ((4, 128, WIDE), BF),
    "GC": ((ROWS, WIDE), BF),
    "XE": ((4, 128, WIDE), BF),
    "XG": ((4, 128, WIDE), BF),
    "RG": ((4, 2, 128, WIDE), BF),
    "RE": ((4, 2, 128, WIDE), BF),
    "RGR": ((16, WIDE), F32),
    "RU": ((2, 4, 48, HID), BF),
    "RD": ((2, 4, 48, HID), BF),
    "RU2": ((4, 48, HID), BF),
    "RD2": ((4, 48, HID), BF),
    "ZU": ((4, 48, HID), BF),
    "ZD": ((4, 48, HID), BF),
    "DD": ((3, 8, ROWS), F32),
    "DK": ((ROWS, 128), F32),
    "DV": ((ROWS, 128), F32),
    "AG": ((4, 4, 4, 144, 128), BF),
    "RA": ((4, 2, 2, 144, 128), BF),
    "RB": ((4, 2, 2, 144, 128), BF),
    "RA2": ((4, 2, 144, 128), BF),
    "RB2": ((4, 2, 144, 128), BF),
    "ZA": ((4, 4, 144, 128), BF),
    "G2": ((8, WIDE), F32),
    "SB": ((16, WIDE), F32),
    "SP": ((16, WIDE), F32),
    "SC": ((4, 16, WIDE), F32),
    "SZ": ((4, 16, WIDE), F32),
}
INS = ("tok", "cot", "pre", "idr", "gains", "qkv", "out", "router", "up", "down")
IN_HBM = ("tok", "cot", "up", "down")
OUT_HBM = ("block_out", "tokens_grad", "up_grad", "down_grad")
SEMAPHORES = 192


def fused(args):
    names = INS + tuple(OUTS) + tuple(SCRATCH) + ("ss", "rs", "ls")

    def body(*refs):
        R = types.SimpleNamespace(**dict(zip(names, refs)))
        pc = Place()
        w = Wire(R.ss, R.rs)
        phase_c(R, pc, w, *phase_b(R, pc, w, *phase_a(R, pc, w)))

    vm = pl.BlockSpec(memory_space=pltpu.VMEM)
    hbm = pl.BlockSpec(memory_space=pl.ANY)
    sm = pl.BlockSpec(memory_space=pltpu.SMEM)
    dma = pltpu.SemaphoreType.DMA
    return pl.pallas_call(
        body,
        out_shape=[jax.ShapeDtypeStruct(s, d) for s, d in OUTS.values()],
        in_specs=[sm if n == "pre" else hbm if n in IN_HBM else vm for n in INS],
        out_specs=[hbm if n in OUT_HBM else vm for n in OUTS],
        scratch_shapes=[pltpu.VMEM(s, d) for s, d in SCRATCH.values()]
        + [dma((SEMAPHORES,)), dma((SEMAPHORES,)), dma((4,))],
        compiler_params=pltpu.CompilerParams(
            collective_id=1, has_side_effects=True, vmem_limit_bytes=63 << 20
        ),
        name="block",
    )(*args)


def copy_out(arrays):
    n = len(arrays)

    def body(*refs):
        src, dst, held, sem = refs[:n], refs[n : 2 * n], refs[2 * n : 3 * n], refs[3 * n]
        come = [pltpu.make_async_copy(src[i], held[i], sem.at[0, i]) for i in range(n)]
        go = [pltpu.make_async_copy(held[i], dst[i], sem.at[1, i]) for i in range(n)]
        for m in come:
            m.start()
        for i in range(n):
            come[i].wait()
            go[i].start()
        for m in go:
            m.wait()

    hbm = pl.BlockSpec(memory_space=pl.ANY)
    return pl.pallas_call(
        body,
        out_shape=[jax.ShapeDtypeStruct(a.shape, a.dtype) for a in arrays],
        in_specs=[hbm] * n,
        out_specs=[hbm] * n,
        scratch_shapes=[pltpu.VMEM(a.shape, a.dtype) for a in arrays]
        + [pltpu.SemaphoreType.DMA((2, n))],
        name="outputs",
    )(*arrays)


def prepare(
    tokens, cotangent, prefix_len, expert_ids, norm_gains, qkv_weight, out_weight, router_weight, up_weight, down_weight
):
    ids = expert_ids.reshape(1, ROWS)
    return (tokens, cotangent, prefix_len, ids, norm_gains, qkv_weight, out_weight, router_weight, up_weight, down_weight)


def fast_device(*args):
    outs = copy_out(fused(prepare(*args)))
    return tuple(outs[:8]) + (outs[8].reshape(()),)


HEAD = 64
EXPERTS = 4
SEQ = 1024
CAP = 256


highest = lax.Precision.HIGHEST


def softmax_rows(scores):
    row_max = jnp.max(scores, axis=-1, keepdims=True)
    shifted = jnp.exp(scores - row_max)
    return shifted / jnp.sum(shifted, axis=-1, keepdims=True)


def slot_index(group_ids):
    onehot = (group_ids[:, None] == jnp.arange(EXPERTS, dtype=jnp.int32)[None, :]).astype(jnp.int32)
    rows = group_ids.shape[0]
    earlier = lax.broadcasted_iota(jnp.int32, (rows, rows), 1) <= lax.broadcasted_iota(
        jnp.int32, (rows, rows), 0
    )
    running = jnp.dot(
        earlier.astype(jnp.bfloat16),
        onehot.astype(jnp.bfloat16),
        preferred_element_type=jnp.float32,
    ).astype(jnp.int32)
    placed = jnp.sum(running * onehot, axis=1) - 1
    return jnp.where(placed < CAP, group_ids * CAP + placed, EXPERTS * CAP)


def rms_factor(values):
    return lax.rsqrt(jnp.mean(values * values, axis=-1, keepdims=True) + norm_eps)


def norm_back(grad_out, inputs, factor, gain):
    scaled = grad_out * gain
    row_inner = jnp.mean(scaled * inputs, axis=-1, keepdims=True)
    grad_in = factor * (scaled - inputs * factor * factor * row_inner)
    grad_gain = jnp.sum(grad_out * inputs * factor, axis=0)
    return (grad_in, grad_gain)


def gelu_slope(values):
    cumulative = 0.5 * (1.0 + lax.erf(values / math.sqrt(2.0)))
    density = jnp.exp(-0.5 * values * values) / math.sqrt(2.0 * math.pi)
    return cumulative + values * density


def block_scores(query_block, key_seq, offset, prefix, score_scale):
    scores = (
        jnp.einsum("qhd,khd->hqk", query_block, key_seq, preferred_element_type=jnp.float32)
        * score_scale
    )
    shape_pair = (query_block.shape[0], key_seq.shape[0])
    row_pos = offset + lax.broadcasted_iota(jnp.int32, shape_pair, 0)
    col_pos = lax.broadcasted_iota(jnp.int32, shape_pair, 1)
    allowed = (col_pos <= row_pos) | (col_pos < prefix)
    return jnp.where(allowed[None], scores, masked_score)


def attend(project, prefix_len, score_scale):
    group_rows = project.shape[0]
    full_width = project.shape[2]
    heads_here = full_width // HEAD
    block_rows = min(512, SEQ)
    shaped = project.reshape(group_rows, 3, heads_here, HEAD)
    query_all = shaped[:, 0]
    key_all = shaped[:, 1]
    value_all = shaped[:, 2]

    def one_block(number):
        row_start = number * block_rows
        seq_number = row_start // SEQ
        seq_start = seq_number * SEQ
        query_block = lax.dynamic_slice_in_dim(query_all, row_start, block_rows, 0)
        scores = block_scores(
            query_block, key_all, row_start - seq_start, prefix_len[seq_number], score_scale
        )
        row_max = jnp.max(scores, axis=-1, keepdims=True)
        shifted = jnp.exp(scores - row_max)
        row_total = jnp.sum(shifted, axis=-1, keepdims=True)
        prob_low = (shifted / row_total).astype(jnp.bfloat16)
        result = jnp.einsum("hqk,khd->qhd", prob_low, value_all, preferred_element_type=jnp.float32)
        return (
            result.reshape(block_rows, full_width).astype(jnp.bfloat16),
            (row_max + jnp.log(row_total))[..., 0],
        )

    outputs, log_total = lax.map(one_block, jnp.arange(group_rows // block_rows, dtype=jnp.int32))
    return (outputs.reshape(group_rows, full_width), log_total)


def attend_back(project, grad_att, log_total, prefix_len, score_scale):
    group_rows = project.shape[0]
    full_width = project.shape[2]
    heads_here = full_width // HEAD
    block_rows = min(512, SEQ)
    shaped = project.reshape(group_rows, 3, heads_here, HEAD)
    query_all = shaped[:, 0]
    key_all = shaped[:, 1]
    value_all = shaped[:, 2]
    grad_shaped = grad_att.reshape(group_rows, heads_here, HEAD)

    def one_block(carried, number):
        grad_keys, grad_values = carried
        row_start = number * block_rows
        seq_number = row_start // SEQ
        seq_start = seq_number * SEQ
        query_block = lax.dynamic_slice_in_dim(query_all, row_start, block_rows, 0)
        grad_block = lax.dynamic_slice_in_dim(grad_shaped, row_start, block_rows, 0)
        scores = block_scores(
            query_block, key_all, row_start - seq_start, prefix_len[seq_number], score_scale
        )
        prob_block = jnp.exp(scores - log_total[number][..., None])
        prob_low = prob_block.astype(jnp.bfloat16)
        grad_prob = jnp.einsum(
            "qhd,khd->hqk", grad_block, value_all, preferred_element_type=jnp.float32
        )
        value_part = jnp.einsum(
            "hqk,qhd->khd", prob_low, grad_block, preferred_element_type=jnp.float32
        )
        row_inner = jnp.sum(prob_block * grad_prob, axis=-1, keepdims=True)
        grad_scores = (prob_block * (grad_prob - row_inner)).astype(jnp.bfloat16)
        query_grad = (
            jnp.einsum("hqk,khd->qhd", grad_scores, key_all, preferred_element_type=jnp.float32)
            * score_scale
        )
        key_part = (
            jnp.einsum("hqk,qhd->khd", grad_scores, query_block, preferred_element_type=jnp.float32)
            * score_scale
        )
        old_keys = grad_keys
        grad_keys = old_keys + key_part
        old_values = grad_values
        grad_values = old_values + value_part
        return ((grad_keys, grad_values), query_grad)

    zero_rows = jnp.zeros((group_rows, heads_here, HEAD), jnp.float32)
    final, grad_query = lax.scan(
        one_block, (zero_rows, zero_rows), jnp.arange(group_rows // block_rows, dtype=jnp.int32)
    )
    grad_keys, grad_values = final
    stacked = jnp.stack(
        [
            grad_query.reshape(group_rows, full_width),
            grad_keys.reshape(group_rows, full_width),
            grad_values.reshape(group_rows, full_width),
        ],
        axis=1,
    )
    return stacked.astype(jnp.bfloat16)


def low_scatter(grad):
    return lax.psum_scatter(
        grad.astype(jnp.bfloat16), "fsdp", scatter_dimension=1, tiled=True
    ).astype(jnp.float32)


def per_device(
    tokens,
    cotangent,
    prefix_len,
    expert_ids,
    norm_gains,
    qkv_weight,
    out_weight,
    router_weight,
    up_weight,
    down_weight,
):
    tensor_size = lax.axis_size("tensor")
    fsdp_size = lax.axis_size("fsdp")
    own_rows = tokens.shape[0]
    group_rows = own_rows * tensor_size
    all_tokens = group_rows * fsdp_size
    own_start = lax.axis_index("tensor") * own_rows
    score_scale = 1.0 / math.sqrt(HEAD)
    gains_full, qkv_full, out_stack = (
        lax.all_gather(norm_gains, "fsdp", axis=1, tiled=True),
        lax.all_gather(qkv_weight, "fsdp", axis=1, tiled=True),
        lax.all_gather(out_weight[None], "fsdp", axis=1, tiled=True),
    )
    out_full = out_stack[0]
    router_full, up_full, down_full = (
        lax.all_gather(router_weight, "fsdp", axis=1, tiled=True),
        lax.all_gather(up_weight, "fsdp", axis=1, tiled=True),
        lax.all_gather(down_weight, "fsdp", axis=1, tiled=True),
    )
    inputs = lax.all_gather(tokens, "tensor", axis=0, tiled=True)
    input_float = inputs.astype(jnp.float32)
    factor_one = rms_factor(input_float)
    gain_one = gains_full[0].astype(jnp.float32)
    normed_one = (input_float * factor_one * gain_one).astype(jnp.bfloat16)
    project = jnp.einsum(
        "td,sdw->tsw", normed_one, qkv_full, preferred_element_type=jnp.float32
    ).astype(jnp.bfloat16)
    attended, log_total = attend(project, prefix_len, score_scale)
    branch = lax.psum_scatter(
        lax.dot_general(
            attended, out_full, (((1,), (1,)), ((), ())), preferred_element_type=jnp.float32
        ),
        "tensor",
        scatter_dimension=0,
        tiled=True,
    )
    hidden_own = tokens.astype(jnp.float32) + branch
    hidden_group = lax.all_gather(hidden_own, "tensor", axis=0, tiled=True)
    factor_two = rms_factor(hidden_group)
    gain_two = gains_full[1].astype(jnp.float32)
    moe_input = (hidden_group * factor_two * gain_two).astype(jnp.bfloat16)
    logits = lax.dot_general(
        moe_input, router_full, (((1,), (1,)), ((), ())), preferred_element_type=jnp.float32
    )
    group_ids = expert_ids[:, 0]
    onehot = (group_ids[:, None] == jnp.arange(EXPERTS, dtype=jnp.int32)[None, :]).astype(
        jnp.float32
    )
    gate_value = jax.nn.sigmoid(jnp.sum(logits * onehot, axis=-1))
    router_prob = softmax_rows(logits)
    counts, prob_sums = lax.psum((jnp.sum(onehot, axis=0), jnp.sum(router_prob, axis=0)), "fsdp")
    route_share = counts / all_tokens
    balance_loss = EXPERTS * jnp.sum(route_share * prob_sums) / all_tokens
    slot_rows = slot_index(group_ids)
    model_width = moe_input.shape[1]
    dispatched = (
        jnp.zeros((EXPERTS * CAP, model_width), jnp.bfloat16)
        .at[slot_rows]
        .set(moe_input, mode="drop")
        .reshape(EXPERTS, CAP, model_width)
    )
    before = jnp.einsum("ecd,edf->ecf", dispatched, up_full, preferred_element_type=jnp.float32)
    activated = jax.nn.gelu(before, approximate=False).astype(jnp.bfloat16)
    expert_out = jnp.einsum(
        "ecf,edf->ecd", activated, down_full, preferred_element_type=jnp.float32
    ).reshape(EXPERTS * CAP, model_width)
    combined_part = jnp.concatenate([expert_out, jnp.zeros((1, model_width), jnp.float32)], axis=0)[
        slot_rows
    ]
    combined = lax.psum_scatter(combined_part, "tensor", scatter_dimension=0, tiled=True)
    gate_own = lax.dynamic_slice_in_dim(gate_value, own_start, own_rows, 0)
    block_out = (hidden_own + gate_own[:, None] * combined).astype(jnp.bfloat16)
    gains_back, qkv_back, out_again, router_back, up_back, down_back = (
        lax.all_gather(norm_gains, "fsdp", axis=1, tiled=True),
        lax.all_gather(qkv_weight, "fsdp", axis=1, tiled=True),
        lax.all_gather(out_weight[None], "fsdp", axis=1, tiled=True),
        lax.all_gather(router_weight, "fsdp", axis=1, tiled=True),
        lax.all_gather(up_weight, "fsdp", axis=1, tiled=True),
        lax.all_gather(down_weight, "fsdp", axis=1, tiled=True),
    )
    out_back = out_again[0]
    cot_group = lax.all_gather(cotangent, "tensor", axis=0, tiled=True).astype(jnp.float32)
    grad_combined = (gate_value[:, None] * cot_group).astype(jnp.bfloat16)
    gate_grad_own = jnp.sum(cotangent.astype(jnp.float32) * combined, axis=-1)
    gate_grad_placed = lax.dynamic_update_slice_in_dim(
        jnp.zeros((group_rows,), jnp.float32), gate_grad_own, own_start, 0
    )
    grad_slots = (
        jnp.zeros((EXPERTS * CAP, model_width), jnp.bfloat16)
        .at[slot_rows]
        .set(grad_combined, mode="drop")
        .reshape(EXPERTS, CAP, model_width)
    )
    grad_activated = jnp.einsum(
        "ecd,edf->ecf", grad_slots, down_back, preferred_element_type=jnp.float32
    )
    down_grad = jnp.einsum(
        "ecd,ecf->edf", grad_slots, activated, preferred_element_type=jnp.float32
    )
    grad_before = (grad_activated * gelu_slope(before)).astype(jnp.bfloat16)
    up_grad = jnp.einsum(
        "ecd,ecf->edf", dispatched, grad_before, preferred_element_type=jnp.float32
    )
    grad_dispatched = jnp.einsum(
        "ecf,edf->ecd", grad_before, up_back, preferred_element_type=jnp.float32
    ).reshape(EXPERTS * CAP, model_width)
    grad_input_part = jnp.concatenate(
        [grad_dispatched, jnp.zeros((1, model_width), jnp.float32)], axis=0
    )[slot_rows]
    grad_moe, gate_grad = lax.psum((grad_input_part, gate_grad_placed), "tensor")
    gate_slope = gate_value * (1.0 - gate_value)
    mixed_share = jnp.sum(router_prob * route_share[None, :], axis=-1, keepdims=True)
    logit_grad = onehot * (gate_grad * gate_slope)[
        :, None
    ] + balance_weight * EXPERTS / all_tokens * router_prob * (route_share[None, :] - mixed_share)
    grad_norm_two = grad_moe + jnp.dot(
        logit_grad, router_back.astype(jnp.float32), precision=highest
    )
    router_grad = jnp.dot(logit_grad.T, moe_input.astype(jnp.float32), precision=highest)
    grad_hidden, gain_two_grad = norm_back(
        grad_norm_two, hidden_group, factor_two, gains_back[1].astype(jnp.float32)
    )
    grad_hidden = grad_hidden + cot_group
    grad_branch = grad_hidden.astype(jnp.bfloat16)
    grad_att = jnp.dot(grad_branch, out_back, preferred_element_type=jnp.float32).astype(
        jnp.bfloat16
    )
    out_grad = lax.dot_general(
        grad_branch, attended, (((0,), (0,)), ((), ())), preferred_element_type=jnp.float32
    )
    grad_project = attend_back(project, grad_att, log_total, prefix_len, score_scale)
    qkv_grad = jnp.einsum(
        "td,tsw->sdw", normed_one, grad_project, preferred_element_type=jnp.float32
    )
    grad_normed_part = jnp.einsum(
        "tsw,sdw->td", grad_project, qkv_back, preferred_element_type=jnp.float32
    )
    grad_normed = lax.psum(grad_normed_part, "tensor")
    grad_tokens, gain_one_grad = norm_back(
        grad_normed, input_float, factor_one, gains_back[0].astype(jnp.float32)
    )
    grad_tokens = grad_tokens + grad_hidden
    tokens_grad = lax.dynamic_slice_in_dim(grad_tokens, own_start, own_rows, 0)
    gains_own, qkv_own, out_own, router_own, up_own, down_own = (
        lax.psum_scatter(
            jnp.stack([gain_one_grad, gain_two_grad], axis=0),
            "fsdp",
            scatter_dimension=1,
            tiled=True,
        ),
        low_scatter(qkv_grad),
        low_scatter(out_grad[None]),
        lax.psum_scatter(router_grad, "fsdp", scatter_dimension=1, tiled=True),
        low_scatter(up_grad),
        low_scatter(down_grad),
    )
    return (
        block_out,
        tokens_grad,
        gains_own,
        qkv_own,
        out_own[0],
        router_own,
        up_own,
        down_own,
        balance_loss,
    )


def solution(mesh):
    placed = (
        P(("fsdp", "tensor"), None),
        P(("fsdp", "tensor"), None),
        P("fsdp"),
        P("fsdp", None),
        P(None, "fsdp"),
        P(None, "fsdp", "tensor"),
        P("fsdp", "tensor"),
        P(None, "fsdp"),
        P(None, "fsdp", "tensor"),
        P(None, "fsdp", "tensor"),
    )
    fits = mesh.shape["fsdp"] == 16 and mesh.shape["tensor"] == 2
    return jax.shard_map(
        fast_device if fits else per_device,
        mesh=mesh,
        in_specs=placed,
        out_specs=(
            P(("fsdp", "tensor"), None),
            P(("fsdp", "tensor"), None),
            P(None, "fsdp"),
            P(None, "fsdp", "tensor"),
            P("fsdp", "tensor"),
            P(None, "fsdp"),
            P(None, "fsdp", "tensor"),
            P(None, "fsdp", "tensor"),
            P(),
        ),
        check_vma=False,
    )
```

```python
import math
import types

import jax
import jax.numpy as jnp
from jax import lax
from jax.experimental import pallas as pl
from jax.experimental.pallas import tpu as pltpu
from jax.sharding import PartitionSpec as P

MESH = pl.DeviceIdType.MESH
BF = jnp.bfloat16
F32 = jnp.float32
ROWS = 1024
WIDE = 768
HALF = 384
HID = 1536
norm_eps = 1e-05
balance_weight = 0.01
masked_score = -1e30


def mm(a, b, ca=1, cb=0):
    return lax.dot_general(a, b, (((ca,), (cb,)), ((), ())), preferred_element_type=F32)


def iota(shape, axis):
    return lax.broadcasted_iota(jnp.int32, shape, axis)


def blocks(count, size, body, unroll=1):
    def step(i, carry):
        body(pl.ds(pl.multiple_of(i * size, size), size))
        return carry

    lax.fori_loop(0, count // size, step, 0, unroll=unroll)


class Place:
    def __init__(self):
        f, t = lax.axis_index("fsdp"), lax.axis_index("tensor")
        self.f, self.t, self.o = f, t, 1 - t
        self.z, self.c = lax.div(f, 4), lax.rem(f, 4)
        c = self.c
        self.cx = c + 1 - 2 * lax.rem(c, 2)
        self.cy = c + 2 - 4 * lax.div(c, 2)
        self.cd = 3 - c
        base = 4 * self.z
        self.X = {"fsdp": base + self.cx, "tensor": t}
        self.Y = {"fsdp": base + self.cy, "tensor": t}
        self.DIAG = {"fsdp": base + self.cd, "tensor": t}
        self.PAIR = {"fsdp": f, "tensor": 1 - t}

    def zto(self, k):
        return lax.rem(self.z + k, 4)

    def zfrom(self, k):
        return lax.rem(self.z + 4 - k, 4)

    def plane(self, z):
        return {"fsdp": 4 * z + self.c, "tensor": self.t}

    def Z(self, k):
        return {"fsdp": 4 * self.zto(k) + self.c, "tensor": self.t}


class Wire:
    def __init__(self, send, recv):
        self.send, self.recv, self.n, self.open = send, recv, 0, []

    def ids(self, n):
        self.n += n
        return self.n - n

    def copy(self, i, src, dst, dev):
        return pltpu.make_async_remote_copy(
            src_ref=src,
            dst_ref=dst,
            send_sem=self.send.at[i],
            recv_sem=self.recv.at[i],
            device_id=dev,
            device_id_type=MESH,
        )

    def go(self, i, src, dst, dev):
        c = self.copy(i, src, dst, dev)
        c.start()
        self.open.append(c)
        return c

    def flush(self):
        for c in self.open:
            c.wait_send()
        self.open = []


def joined(ref, rows):
    return jnp.concatenate([ref[p, rows] for p in range(3)], axis=1)


def enter(pc):
    barrier = pltpu.get_barrier_semaphore()
    for dev in (pc.PAIR, pc.X, pc.Y, pc.DIAG, pc.Z(1), pc.Z(2), pc.Z(3)):
        pl.semaphore_signal(barrier, inc=1, device_id=dev, device_id_type=MESH)
    pl.semaphore_wait(barrier, 7)


def order(i):
    return i + lax.div(i, 2) * (5 - 2 * i)


def visible(krow0, kn, qcol0, qn, prefix):
    kpos = krow0 + iota((kn, qn), 0)
    qpos = qcol0 + iota((kn, qn), 1)
    ok = kpos <= qpos
    if krow0 < 512 and qcol0 < 512:
        ok = ok | (kpos < prefix)
    return ok


SEEN = (
    ((0, 512, True),),
    ((0, 512, True),),
    ((0, 512, False), (512, 256, True)),
    ((0, 512, False), (512, 256, False), (768, 256, True)),
)


def hook(table, p, qb):
    for (pp, qq), step in table.items():
        if qq == qb:
            pl.when(p == pp)(step)


def both(*steps):
    def run():
        for step in steps:
            step()

    return run


def phase_a(R, pc, w):
    f, t, z, c = pc.f, pc.t, pc.z, pc.c
    idr = R.idr[...]
    ohr = (iota((16, ROWS), 0) - 8 == idr).astype(F32)
    cnt = jnp.sum(ohr, axis=1, keepdims=True)
    hi = jnp.floor(cnt * (1.0 / 256.0))
    lane16 = iota((16, 128), 1)
    six = jnp.concatenate(
        [R.gains[...].astype(F32), R.router[...].astype(F32), jnp.zeros((10, 48), F32)], axis=0
    )
    small = jnp.concatenate([six, jnp.zeros((16, 80), F32)], axis=1)
    R.SM[f] = jnp.where(
        lane16 == 48,
        cnt - 256.0 * hi,
        jnp.where(lane16 == 49, hi, small),
    ).astype(BF)
    R.WA[z, c, pl.ds(0, 3)] = R.qkv[...]
    R.WA[z, c, 3] = R.out[...]
    enter(pc)
    own = pl.ds(pl.multiple_of(t * 512, 512), 512)
    i_tok, i_cot, i_wo, i_att = w.ids(1), w.ids(1), w.ids(1), w.ids(3)
    i_up, i_dn, i_sz, i_s = w.ids(3) - 1, w.ids(3) - 1, w.ids(3) - 1, w.ids(3)
    i_x, i_y, i_fx, i_fy = (w.ids(4) for _ in range(4))
    i_mz = w.ids(18) - 1
    i_m = [w.ids(3) for _ in range(6)]
    i_cz, i_dz, i_cp, i_dp = w.ids(3) - 1, w.ids(3) - 1, w.ids(4), w.ids(4)

    SM = R.SM.reshape(4, 4, 16, 128)
    zs = [w.go(i_sz + k, SM.at[z, c], SM.at[z, c], pc.Z(k)) for k in (1, 2, 3)]

    def up(d):
        block = R.WA.at[z - d + 1, c]
        return w.copy(i_up + d, block, block, pc.plane(z + 1))

    def down(d):
        block = R.WA.at[z + d - 1, c]
        return w.copy(i_dn + d, block, block, pc.plane(z - 1))

    def spread(zz):
        block = R.WA.at[zz, c]
        return w.copy(i_x + zz, block, block, pc.X), w.copy(i_y + zz, block, block, pc.Y)

    def forward(zz):
        a = R.WA.at[zz, pc.cx, pl.ds(0, 2)]
        b = R.WA.at[zz, pc.cy, pl.ds(2, 2)]
        return w.copy(i_fx + zz, a, a, pc.Y), w.copy(i_fy + zz, b, b, pc.X)

    def start_all(copies):
        for m in copies:
            m.start()

    def pass_on(zz):
        for m in spread(zz):
            m.wait_recv()
        start_all(forward(zz))

    def stage(d):
        @pl.when(z >= d)
        def _():
            w.copy(i_up + d, R.WA.at[z, c], R.WA.at[z, c], pc.plane(z - 1)).wait_recv()
            start_all(spread(z - d))
            if d < 3:
                pl.when(z < 3)(lambda: up(d + 1).start())

        @pl.when(z + d <= 3)
        def _():
            w.copy(i_dn + d, R.WA.at[z, c], R.WA.at[z, c], pc.plane(z + 1)).wait_recv()
            start_all(spread(z + d))
            if d < 3:
                pl.when(z > 0)(lambda: down(d + 1).start())

    def pass_on_stage(d):
        pl.when(z >= d)(lambda: pass_on(z - d))
        pl.when(z + d <= 3)(lambda: pass_on(z + d))

    pl.when(z < 3)(lambda: up(1).start())
    pl.when(z > 0)(lambda: down(1).start())
    start_all(spread(z))
    cot_x = w.go(i_cot, R.cot, R.CT.at[own], pc.PAIR)
    tok_x = w.go(i_tok, R.tok, R.TK.at[own], pc.PAIR)
    local = [
        pltpu.make_async_copy(R.tok, R.TK.at[own], R.ls.at[0]),
        pltpu.make_async_copy(R.cot, R.CT.at[own], R.ls.at[1]),
        pltpu.make_async_copy(R.up.at[z], R.UE.at[z, c], R.ls.at[2]),
        pltpu.make_async_copy(R.down.at[z], R.DE.at[z, c], R.ls.at[3]),
    ]
    for m in local:
        m.start()
    before_or_at = (iota((ROWS, ROWS), 0) <= iota((ROWS, ROWS), 1)).astype(F32).astype(BF)
    running = mm(ohr.astype(BF), before_or_at)
    placed = jnp.sum(running * ohr, axis=0, keepdims=True) - 1.0
    key = jnp.where(placed < 256.0, idr.astype(F32) * 256.0 + placed, -1.0)
    R.KC[...] = jnp.broadcast_to(key, (128, ROWS)).T
    R.PR[...] = jnp.broadcast_to(idr.astype(F32), (128, ROWS)).T
    r = iota((512, ROWS), 0)
    want = lax.div(r, 128) * 256 + lax.rem(r, 128) + 128 * t
    R.ACT[0:512, 0:ROWS] = (key.astype(jnp.int32) == want).astype(F32).astype(BF)

    stage(1)
    pass_on(z)
    for m in local:
        m.wait()
    cot_x.wait_recv()

    def cot_rows(e, carry):
        R.CQ[e] = mm(R.ACT[pl.ds(pl.multiple_of(e * 128, 128), 128), pl.ds(0, ROWS)], R.CT[...]).astype(BF)
        return carry

    lax.fori_loop(0, 4, cot_rows, 0)
    R.CR[z, t] = R.CQ[z]
    w.copy(i_cp, R.CR.at[z, t], R.CR.at[z, t], pc.PAIR).start()
    stage(2)
    for m in zs:
        m.wait_recv()
    mine = SM.at[:, c]
    sx, sy = w.go(i_s, mine, mine, pc.X), w.go(i_s + 1, mine, mine, pc.Y)
    pass_on_stage(1)

    def chunk(j):
        return pl.ds(pl.multiple_of(j * 512, 128), 512)

    def from_plane(j):
        out = []
        for k in (1, 3, 2):
            to, cols, i = pc.zto(k), chunk(j), i_mz + 6 * j + k
            out.append(w.copy(i, R.up.at[to, :, cols], R.UE.at[z, c, :, cols], pc.Z(k)))
            out.append(w.copy(i + 3, R.down.at[to, :, cols], R.DE.at[z, c, :, cols], pc.Z(k)))
        return out

    def moe_spread(j):
        u, d = R.UE.at[:, c, :, chunk(j)], R.DE.at[:, c, :, chunk(j)]
        return [
            w.copy(i_m[0] + j, u, u, pc.X),
            w.copy(i_m[1] + j, d, d, pc.Y),
            w.copy(i_m[2] + j, u, u, pc.Y),
            w.copy(i_m[3] + j, d, d, pc.X),
        ]

    def moe_forward(j):
        u, d = R.UE.at[:, pc.cx, :, chunk(j)], R.DE.at[:, pc.cy, :, chunk(j)]
        return [w.copy(i_m[4] + j, u, u, pc.Y), w.copy(i_m[5] + j, d, d, pc.X)]

    def start_spread(j):
        for m in from_plane(j):
            m.wait()
        for m in moe_spread(j):
            m.start()

    def start_forward(j):
        a = moe_spread(j)
        a[0].wait()
        a[1].wait()
        for m in moe_forward(j):
            m.start()

    def weights_here(j):
        for m in moe_spread(j)[2:] + moe_forward(j):
            m.wait()

    def start_plane(j):
        for m in from_plane(j):
            m.start()

    def start_cot():
        for m in cz:
            m.start()

    cz = [w.copy(i_cz + k, R.CQ.at[pc.zto(k)], R.CR.at[z, t], pc.Z(k)) for k in (1, 3, 2)]
    start_plane(0)
    stage(3)
    sx.wait_recv()
    theirs = SM.at[:, pc.cx]
    sf = w.go(i_s + 2, theirs, theirs, pc.Y)
    pass_on_stage(2)
    pass_on_stage(3)
    start_plane(1)
    agenda = {
        (0, 3): lambda: start_spread(1),
        (1, 1): lambda: start_forward(0),
        (1, 3): start_cot,
        (2, 1): lambda: start_spread(2),
        (2, 3): lambda: start_forward(1),
    }

    tok_x.wait_recv()

    def factors(rows):
        x = R.TK[rows].astype(F32)
        R.STAT[rows, 0:1] = lax.rsqrt(jnp.mean(x * x, axis=1, keepdims=True) + norm_eps)

    blocks(ROWS, 128, factors)
    sy.wait_recv()
    sf.wait_recv()
    parts = [R.SM[g].astype(F32)[:, 0:48] for g in range(16)]
    vecs = jnp.concatenate(parts, axis=1)
    R.VEC[...] = vecs
    R.RW[...] = jnp.concatenate([vecs, jnp.zeros((112, WIDE), F32)], axis=0).T.astype(BF)
    total = jnp.zeros((16, 128), F32)
    for g in range(16):
        total = total + R.SM[g].astype(F32)
    counts = jnp.sum(
        jnp.where(lane16 == 48, total, jnp.where(lane16 == 49, 256.0 * total, 0.0)),
        axis=1,
        keepdims=True,
    )
    share = jnp.sum(
        jnp.where(iota((16, 128), 0) - 8 == lane16 - 2, counts, 0.0), axis=0, keepdims=True
    ) * (1.0 / (16 * ROWS))
    R.SHARE[...] = jnp.broadcast_to(share, (8, 128))

    def norm_one(rows):
        x = R.TK[rows].astype(F32)
        R.NM[rows] = (x * R.STAT[rows, 0:1] * R.VEC[0:1]).astype(BF)

    blocks(ROWS, 128, norm_one)
    for zz in range(4):
        for m in spread(zz):
            m.wait_send()
        for m in forward(zz):
            m.wait()
    for d in (1, 2, 3):
        pl.when((z < 3) & (z >= d - 1))(lambda: up(d).wait_send())
        pl.when((z > 0) & (z + d - 1 <= 3))(lambda: down(d).wait_send())
    wo = w.go(i_wo, R.WA.at[:, :, 3], R.WO, pc.PAIR)

    start_spread(0)
    start_plane(2)

    def project(rows):
        x = R.NM[rows]
        for s, ref in enumerate((R.QS, R.KS, R.VS)):
            y = mm(x, R.WA[:, :, s].reshape(WIDE, HALF))
            if s == 0:
                y = y.astype(BF).astype(F32) * 0.125
            for p in range(3):
                ref[p, rows] = y[:, 128 * p : 128 * p + 128].astype(BF)

    blocks(ROWS, 256, project)
    prefix = R.pre[0]

    def pair_of_heads(p, carry):
        value_t = R.VS[p].astype(F32).T.astype(BF)
        even = iota((256, 128), 1) < 64
        for qb in range(4):
            cols = pl.ds(qb * 256, 256)
            outs = []
            for i in range(2):
                q = R.QS[p, cols]
                q = jnp.where(even if i == 0 else ~even, q.astype(F32), 0.0).astype(BF)
                pieces = []
                for k0, kn, masked in SEEN[qb]:
                    s = mm(R.KS[p, pl.ds(k0, kn)], q, 1, 1)
                    if masked:
                        s = jnp.where(visible(k0, kn, qb * 256, 256, prefix), s, masked_score)
                    pieces.append(s)
                top = pieces[0].max(axis=0, keepdims=True)
                for s in pieces[1:]:
                    top = jnp.maximum(top, s.max(axis=0, keepdims=True))
                total_e = jnp.zeros((1, 256), F32)
                out = jnp.zeros((128, 256), F32)
                for (k0, kn, _), s in zip(SEEN[qb], pieces):
                    e = jnp.exp(s - top)
                    total_e = total_e + e.sum(axis=0, keepdims=True)
                    out = out + mm(value_t[:, k0 : k0 + kn], e.astype(BF))
                R.LT[p, i : i + 1, cols] = top + jnp.log(total_e)
                outs.append(out / total_e)
            merged = jnp.where(iota((128, 256), 0) < 64, outs[0], outs[1])
            R.ATO[p, cols] = merged.T.astype(BF)
            if qb == 3:
                w.copy(i_att + p, R.ATO.at[p], R.ATX.at[p], pc.PAIR).start()
            hook(agenda, p, qb)
        return carry

    lax.fori_loop(0, 3, pair_of_heads, 0)
    wo.wait_recv()
    for p in range(3):
        w.copy(i_att + p, R.ATO.at[p], R.ATX.at[p], pc.PAIR).wait()
    lane = iota((256, 128), 1)
    real = (lane >= 2) & (lane < 6)
    R.PS[...] = jnp.zeros((8, 128), F32)

    def out_block(rows):
        b = mm(joined(R.ATO, rows), R.WA[:, :, 3].reshape(WIDE, HALF), 1, 1)
        b = b + mm(joined(R.ATX, rows), R.WO[...].reshape(WIDE, HALF), 1, 1)
        h = R.TK[rows].astype(F32) + b
        R.HIDN[rows] = h
        f2 = lax.rsqrt(jnp.mean(h * h, axis=1, keepdims=True) + norm_eps)
        R.STAT[rows, 1:2] = f2
        moe = (h * f2 * R.VEC[1:2]).astype(BF)
        R.GC[rows] = moe
        logits = mm(moe, R.RW[...])
        mine = jnp.where((lane - 2).astype(F32) == R.PR[rows], logits, 0.0)
        picked = jnp.sum(jnp.where(real, mine, 0.0), axis=1, keepdims=True)
        R.STAT[rows, 2:3] = jax.nn.sigmoid(picked)
        lg = jnp.where(real, logits, masked_score)
        e = jnp.exp(lg - jnp.max(lg, axis=1, keepdims=True))
        e = jnp.where(real, e, 0.0)
        pr = e / jnp.sum(e, axis=1, keepdims=True)
        R.PR[rows] = pr
        R.PS[0:1] = R.PS[0:1] + jnp.sum(pr, axis=0, keepdims=True)

    blocks(ROWS, 256, out_block, 2)

    def moe_rows(i, carry):
        k = order(lax.rem(i + 1, 4))
        e = pc.zto(k)
        R.CS[e] = mm(R.ACT[pl.ds(pl.multiple_of(e * 128, 128), 128), pl.ds(0, ROWS)], R.GC[...]).astype(BF)

        @pl.when(i < 3)
        def _():
            w.copy(i_dz + k, R.CS.at[e], R.DR.at[z, t], pc.Z(k)).start()

        return carry

    lax.fori_loop(0, 4, moe_rows, 0)
    R.DR[z, t] = R.CS[z]
    w.copy(i_dp, R.DR.at[z, t], R.DR.at[z, t], pc.PAIR).start()
    start_forward(2)
    w.flush()
    return i_dz, i_dp, i_cz, i_cp, weights_here


def gelu_parts(v):
    cdf = 0.5 * (1.0 + lax.erf(v * (1.0 / math.sqrt(2.0))))
    slope = cdf + v * (jnp.exp(-0.5 * v * v) * (1.0 / math.sqrt(2.0 * math.pi)))
    return v * cdf, slope


class ExpertSums:
    def __init__(self, R, pc, w):
        self.R, self.pc, self.w = R, pc, w
        self.i1, self.i2, self.i3 = w.ids(16), w.ids(8), w.ids(24) - 1

    def cols(self, g):
        return pl.ds(pl.multiple_of(384 * g, 128), 384)

    def step_one(self, g):
        R, pc, w = self.R, self.pc, self.w
        cols, i = self.cols(g), self.i1 + 4 * g
        return [
            w.copy(i, R.UE.at[:, pc.cx, :, cols], R.RU.at[0, :, :, cols], pc.X),
            w.copy(i + 1, R.UE.at[:, pc.cd, :, cols], R.RU.at[1, :, :, cols], pc.X),
            w.copy(i + 2, R.DE.at[:, pc.cy, :, cols], R.RD.at[0, :, :, cols], pc.Y),
            w.copy(i + 3, R.DE.at[:, pc.cd, :, cols], R.RD.at[1, :, :, cols], pc.Y),
        ]

    def step_two(self, g):
        R, pc, w = self.R, self.pc, self.w
        cols, i = self.cols(g), self.i2 + 2 * g
        return [
            w.copy(i, R.UE.at[:, pc.cy, :, cols], R.RU2.at[:, :, cols], pc.Y),
            w.copy(i + 1, R.DE.at[:, pc.cx, :, cols], R.RD2.at[:, :, cols], pc.X),
        ]

    def step_three(self, g):
        R, pc, w = self.R, self.pc, self.w
        cols, i, out = self.cols(g), self.i3 + 6 * g, []
        for k in (1, 2, 3):
            to, z = pc.zto(k), pc.z
            out.append(w.copy(i + k, R.UE.at[to, pc.c, :, cols], R.ZU.at[z, :, cols], pc.Z(k)))
            out.append(w.copy(i + 3 + k, R.DE.at[to, pc.c, :, cols], R.ZD.at[z, :, cols], pc.Z(k)))
        return out

    def one(self, g):
        for m in self.step_one(g):
            m.start()

    def two(self, g):
        R, pc, cols = self.R, self.pc, self.cols(g)
        for m in self.step_one(g):
            m.wait()

        def add(zz, carry):
            R.UE[zz, pc.cy, :, cols] = R.UE[zz, pc.cy, :, cols] + R.RU[1, zz, :, cols]
            R.DE[zz, pc.cx, :, cols] = R.DE[zz, pc.cx, :, cols] + R.RD[1, zz, :, cols]
            R.UE[zz, pc.c, :, cols] = R.UE[zz, pc.c, :, cols] + R.RU[0, zz, :, cols]
            R.DE[zz, pc.c, :, cols] = R.DE[zz, pc.c, :, cols] + R.RD[0, zz, :, cols]
            return carry

        lax.fori_loop(0, 4, add, 0)
        for m in self.step_two(g):
            m.start()

    def three(self, g):
        R, pc, cols = self.R, self.pc, self.cols(g)
        for m in self.step_two(g):
            m.wait()

        def add(zz, carry):
            R.UE[zz, pc.c, :, cols] = R.UE[zz, pc.c, :, cols] + R.RU2[zz, :, cols]
            R.DE[zz, pc.c, :, cols] = R.DE[zz, pc.c, :, cols] + R.RD2[zz, :, cols]
            return carry

        lax.fori_loop(0, 4, add, 0)
        for m in self.step_three(g):
            m.start()

    def last(self):
        R, pc = self.R, self.pc
        R.ZU[pc.z] = R.UE[pc.z, pc.c]
        R.ZD[pc.z] = R.DE[pc.z, pc.c]
        out = []
        for g in range(4):
            for m in self.step_three(g):
                m.wait()
        for g in (0, 1):
            cols = pl.ds(768 * g, 768)
            for j, (got, to) in enumerate(((R.ZU, R.up_grad), (R.ZD, R.down_grad))):
                held = R.HIDN.at[pl.ds(192 * (2 * g + j), 192)].reshape(4, 48, 768)
                held[...] = got[:, :, cols].astype(F32)
                m = pltpu.make_async_copy(held, to.at[:, :, cols], R.ls.at[2 * g + j])
                m.start()
                out.append(m)
        return out


class AttentionSums:
    def __init__(self, R, pc, w):
        self.R, self.pc, self.w = R, pc, w
        self.i1, self.i2, self.i3 = w.ids(16), w.ids(8), w.ids(12) - 1
        self.low, self.high = pl.ds(0, 2), pl.ds(2, 2)

    def step_one(self, n):
        R, pc, w, i = self.R, self.pc, self.w, self.i1 + 4 * n
        return [
            w.copy(i, R.AG.at[n, self.low, pc.cx], R.RA.at[n, 0], pc.X),
            w.copy(i + 1, R.AG.at[n, self.low, pc.cd], R.RA.at[n, 1], pc.X),
            w.copy(i + 2, R.AG.at[n, self.high, pc.cy], R.RB.at[n, 0], pc.Y),
            w.copy(i + 3, R.AG.at[n, self.high, pc.cd], R.RB.at[n, 1], pc.Y),
        ]

    def step_two(self, n):
        R, pc, w, i = self.R, self.pc, self.w, self.i2 + 2 * n
        return [
            w.copy(i, R.AG.at[n, self.low, pc.cy], R.RA2.at[n], pc.Y),
            w.copy(i + 1, R.AG.at[n, self.high, pc.cx], R.RB2.at[n], pc.X),
        ]

    def step_three(self, n):
        R, pc, w, i = self.R, self.pc, self.w, self.i3 + 3 * n
        return [
            w.copy(i + k, R.AG.at[n, pc.zto(k), pc.c], R.ZA.at[n, pc.z], pc.Z(k))
            for k in (1, 2, 3)
        ]

    def one(self, n):
        for m in self.step_one(n):
            m.start()

    def two(self, n):
        R, pc = self.R, self.pc
        for m in self.step_one(n):
            m.wait()
        for j in range(2):
            R.AG[n, j, pc.cy] = R.AG[n, j, pc.cy] + R.RA[n, 1, j]
            R.AG[n, 2 + j, pc.cx] = R.AG[n, 2 + j, pc.cx] + R.RB[n, 1, j]
            R.AG[n, j, pc.c] = R.AG[n, j, pc.c] + R.RA[n, 0, j]
            R.AG[n, 2 + j, pc.c] = R.AG[n, 2 + j, pc.c] + R.RB[n, 0, j]
        for m in self.step_two(n):
            m.start()

    def three(self, n):
        R, pc = self.R, self.pc
        for m in self.step_two(n):
            m.wait()
        for j in range(2):
            R.AG[n, j, pc.c] = R.AG[n, j, pc.c] + R.RA2[n, j]
            R.AG[n, 2 + j, pc.c] = R.AG[n, 2 + j, pc.c] + R.RB2[n, j]
        for m in self.step_three(n):
            m.start()

    def last(self, n):
        R, pc = self.R, self.pc
        R.ZA[n, pc.z] = R.AG[n, pc.z, pc.c]
        for m in self.step_three(n):
            m.wait()
        total = R.ZA[n, 0].astype(F32)
        for zz in range(1, 4):
            total = total + R.ZA[n, zz].astype(F32)
        for j in range(3):
            block = total[48 * j : 48 * j + 48]
            if n == 0:
                R.out_grad[:, 128 * j : 128 * j + 128] = block
            else:
                R.qkv_grad[j, :, 128 * (n - 1) : 128 * n] = block


def phase_b(R, pc, w, i_dz, i_dp, i_cz, i_cp, weights_here):
    f, t, z, c, o = pc.f, pc.t, pc.z, pc.c, pc.o
    i_xe, i_xg = w.ids(4), w.ids(4)
    i_rg, i_re, i_rgp, i_rep = w.ids(3) - 1, w.ids(3) - 1, w.ids(1), w.ids(1)
    lane = iota((256, 128), 1)
    row = jnp.sum(
        jnp.where(iota((16, WIDE), 0) == 2 + z, R.VEC[...], 0.0), axis=0, keepdims=True
    )
    R.RGR[...] = jnp.zeros((16, WIDE), F32)

    def to_plane(s):
        return {"fsdp": 4 * s + c, "tensor": t}

    def rows_in(k):
        return w.copy(i_dz + k, R.CS.at[pc.zto(k)], R.DR.at[z, t], pc.Z(k))

    def cot_in(k):
        return w.copy(i_cz + k, R.CQ.at[pc.zto(k)], R.CR.at[z, t], pc.Z(k))

    def rows_pair(k):
        s = pc.zfrom(k)
        return (
            w.copy(i_dp + k, R.DR.at[s, t], R.DR.at[s, t], pc.PAIR),
            w.copy(i_cp + k, R.CR.at[s, t], R.CR.at[s, t], pc.PAIR),
        )

    def pair_sums(k):
        s = pc.zfrom(k)
        return (
            w.copy(i_xg + k, R.PG.at[s], R.XG.at[s], pc.PAIR),
            w.copy(i_xe + k, R.PE.at[s], R.XE.at[s], pc.PAIR),
        )

    def home(k):
        s = pc.zfrom(k)
        return w.copy(i_rg + k, R.XG.at[s], R.RG.at[z, t], to_plane(s))

    def home_out(k):
        s = pc.zfrom(k)
        return w.copy(i_re + k, R.XE.at[s], R.RE.at[z, t], to_plane(s))

    def finish(k):
        s = pc.zfrom(k)
        for m in pair_sums(k):
            m.wait()
        eo = R.EOO[s] + R.XE[s].astype(F32)
        gate = R.STAT[pl.ds(pl.multiple_of(s * 256 + t * 128, 128), 128), 3:4]
        gate_grad = jnp.sum(R.CR[s, t].astype(F32) * eo, axis=1, keepdims=True)
        gs = gate_grad * gate * (1.0 - gate)
        R.RGR[0:1] += jnp.sum(gs * R.DR[s, t].astype(F32), axis=0, keepdims=True)
        R.XG[s] = (R.GMO[s] + R.XG[s].astype(F32) + gs * row).astype(BF)
        R.XE[s] = eo.astype(BF)

    def source(i, carry):
        k = order(i)
        s = pc.zfrom(k)
        rows = pl.ds(pl.multiple_of(s * 256, 256), 256)

        for m in rows_pair(k):
            m.wait()
        x = R.DR[s].reshape(256, WIDE)
        logits = mm(x, R.RW[...])
        gate = jax.nn.sigmoid(
            jnp.sum(jnp.where(lane == 2 + z, logits, 0.0), axis=1, keepdims=True)
        )
        R.STAT[rows, 3:4] = gate
        R.GC[rows] = (gate * R.CR[s].reshape(256, WIDE).astype(F32)).astype(BF)

        def hidden_units(j, carry):
            @pl.when(i == 0)
            def _():
                weights_here(j)

            cols = pl.ds(pl.multiple_of(j * 512, 128), 512)
            up = R.UE[:, :, :, cols].reshape(WIDE, 512)
            down = R.DE[:, :, :, cols].reshape(WIDE, 512)
            act, slope = gelu_parts(mm(R.DR[s].reshape(256, WIDE), up))
            act = act.astype(BF)
            gb = (mm(R.GC[rows], down) * slope).astype(BF)
            R.ACT[rows, cols] = act
            R.GB[rows, cols] = gb
            return carry

        lax.fori_loop(0, 3, hidden_units, 0)
        @pl.when(i < 3)
        def _():
            after = order(i + 1)
            cot_in(after).wait()
            rows_pair(after)[1].start()
            rows_in(after).wait()
            rows_pair(after)[0].start()

        up, down = R.UE[...].reshape(WIDE, HID), R.DE[...].reshape(WIDE, HID)
        R.GMB[...] = mm(R.GB[rows], up, 1, 1).reshape(2, 128, WIDE)
        R.PG[s] = R.GMB[o].astype(BF)
        pair_sums(k)[0].start()
        R.GMO[s] = R.GMB[t]
        R.GMB[...] = mm(R.ACT[rows], down, 1, 1).reshape(2, 128, WIDE)
        R.PE[s] = R.GMB[o].astype(BF)
        pair_sums(k)[1].start()
        R.EOO[s] = R.GMB[t]

        @pl.when(i > 0)
        def _():
            last = order(i - 1)
            finish(last)

            @pl.when(i > 1)
            def _():
                home(last).start()

        return carry

    lax.fori_loop(0, 4, source, 0)
    finish(2)
    home(2).start()
    R.RG[z, t] = R.XG[z]
    R.RE[z, t] = R.XE[z]
    R.RGR[...] = jnp.where(iota((16, WIDE), 0) == 2 + z, R.RGR[0:1], 0.0)
    sums = ExpertSums(R, pc, w)
    DR = R.DR.reshape(ROWS, WIDE)

    def weight_grads(i, carry):
        cols = pl.ds(pl.multiple_of(i * 384, 128), 384)
        R.UE[:, :, :, cols] = mm(DR[...], R.GB[:, cols], 0, 0).astype(BF).reshape(4, 4, 48, 384)
        R.DE[:, :, :, cols] = mm(R.GC[...], R.ACT[:, cols], 0, 0).astype(BF).reshape(4, 4, 48, 384)


        @pl.when(i < 2)
        def _():
            for m in sums.step_one(i):
                m.start()

        return carry

    lax.fori_loop(0, 4, weight_grads, 0)
    share, vec = R.SHARE[0:1], R.VEC[...]
    R.SB[...] = jnp.zeros((16, WIDE), F32)

    def prepared(i, carry):
        rows = pl.ds(pl.multiple_of(i * 256, 256), 256)
        R.ACT[rows, pl.ds(0, ROWS)] = pick_rows(R.KC[rows])
        pr = R.PR[rows]
        mixed = jnp.sum(pr * share, axis=1, keepdims=True)
        aux = (balance_weight * 4.0 / (16 * ROWS)) * pr * (share - mixed)
        aux = aux[:, 0:16].astype(BF)
        R.GH[rows] = mm(aux, vec.astype(BF))
        mine = jnp.where(lax.div(i, 2) == t, 1.0, 0.0)
        moe = (R.HIDN[rows] * R.STAT[rows, 1:2] * vec[1:2]).astype(BF)
        R.SB[...] += mine * mm(aux, moe, 0, 0)
        return carry

    lax.fori_loop(0, 4, prepared, 0, unroll=2)
    sums.two(0)
    sums.one(2)
    for k in (1, 3, 2):
        home(k).wait()
    back = w.go(i_rgp, R.RG.at[:, t], R.RG.at[:, t], pc.PAIR)
    for k in (1, 3, 2):
        home_out(k).start()
    back.wait_recv()
    return sums, home_out, i_rep


def pick_rows(key):
    keys = jnp.concatenate([key] * 8, axis=1)
    return (keys == iota((key.shape[0], ROWS), 1).astype(F32)).astype(F32).astype(BF)


def phase_c(R, pc, w, sums, home_out, i_rep):
    f, t, z, c, o = pc.f, pc.t, pc.z, pc.c, pc.o
    att = AttentionSums(R, pc, w)
    i_n = w.ids(1)
    i_sp, i_sc, i_sz = w.ids(1), w.ids(3), w.ids(3) - 1
    own = pl.ds(pl.multiple_of(t * 512, 512), 512)
    GH, GN = R.GH, R.EOO.reshape(512, WIDE)
    RG, RE = R.RG.reshape(ROWS, WIDE), R.RE.reshape(ROWS, WIDE)
    GBR = R.GC
    share = R.SHARE[0:1]
    vec = R.VEC[...]
    head = iota((24, HALF), 0)
    head = jnp.where(lax.rem(head, 8) < 2, 2 * lax.div(head, 8) + lax.rem(head, 8), -1)
    pick_head = (head == lax.div(iota((24, HALF), 1), 64)).astype(F32).astype(BF)

    def residual(i, carry):
        rows = pl.ds(pl.multiple_of(i * 256, 256), 256)
        gm = mm(R.ACT[rows, pl.ds(0, ROWS)], RG[...]) + R.GH[rows]
        mine = jnp.where(lax.div(i, 2) == t, 1.0, 0.0)
        h, f2 = R.HIDN[rows], R.STAT[rows, 1:2]
        g = gm * vec[1:2]
        inner = jnp.mean(g * h, axis=1, keepdims=True)
        gh = R.CT[rows].astype(F32) + f2 * (g - h * (f2 * f2 * inner))
        R.G2[0:1] += mine * jnp.sum(gm * h * f2, axis=0, keepdims=True)
        GH[rows] = gh
        low = gh.astype(BF)
        GBR[rows] = low
        ga = mm(low, R.WA[:, :, 3].reshape(WIDE, HALF)).astype(BF)
        for p in range(3):
            R.ATX[p, rows] = ga[:, 128 * p : 128 * p + 128]
        prod = ga.astype(F32) * joined(R.ATO, rows).astype(F32)
        top = prod.astype(BF)
        rest = (prod - top.astype(F32)).astype(BF)
        dd = mm(pick_head, top, 1, 1) + mm(pick_head, rest, 1, 1)
        for p in range(3):
            R.DD[p, :, rows] = dd[8 * p : 8 * p + 8]

        @pl.when(i == 2)
        def _():
            sums.two(1)
            sums.one(3)

        return carry

    R.G2[...] = jnp.zeros((8, WIDE), F32)
    lax.fori_loop(0, 4, residual, 0, unroll=2)
    part = jnp.where(iota((16, WIDE), 0) == 1, R.G2[0:1], 0.0)
    sums6 = jnp.concatenate([0.5 * R.PS[0:1], jnp.zeros((1, WIDE - 128), F32)], axis=1)
    keep = (iota((16, WIDE), 0) >= 2) & (iota((16, WIDE), 0) < 6)
    R.SB[...] = (
        jnp.where(keep, R.SB[...] + R.RGR[...], 0.0)
        + part
        + jnp.where(iota((16, WIDE), 0) == 6, sums6, 0.0)
    )

    def place(n, grad):
        for j in range(3):
            block = grad[:, 128 * j : 128 * j + 128].astype(BF).reshape(4, 4, 48, 128)
            R.AG[n, :, :, pl.ds(48 * j, 48)] = block

    place(0, mm(GBR[...], joined(R.ATO, pl.ds(0, ROWS)), 0, 0))

    def outputs_pair():
        return w.copy(i_rep, R.RE.at[:, t], R.RE.at[:, t], pc.PAIR)

    def outputs_home():
        for k in (1, 2, 3):
            home_out(k).wait()
        outputs_pair().start()


    agenda = {
        (0, 1): both(lambda: sums.two(2), lambda: sums.three(0)),
        (0, 3): lambda: sums.three(1),
        (1, 2): lambda: sums.two(3),
        (1, 3): lambda: att.one(0),
        (2, 0): lambda: sums.three(2),
        (2, 1): outputs_home,
        (2, 2): lambda: sums.three(3),
        (2, 3): lambda: att.two(0),
    }
    prefix = R.pre[0]

    def pair_of_heads(p, carry):
        key_t = R.KS[p].astype(F32).T.astype(BF)
        R.DK[...] = jnp.zeros((ROWS, 128), F32)
        R.DV[...] = jnp.zeros((ROWS, 128), F32)
        even = iota((256, 128), 1) < 64
        for qb in range(4):
            cols = pl.ds(qb * 256, 256)
            outs = []
            for i in range(2):
                side = even if i == 0 else ~even
                q = jnp.where(side, R.QS[p, cols].astype(F32), 0.0).astype(BF)
                do = jnp.where(side, R.ATX[p, cols].astype(F32), 0.0).astype(BF)
                lt, dd = R.LT[p, i : i + 1, cols], R.DD[p, i : i + 1, cols]
                dq = jnp.zeros((128, 256), F32)
                for kb in range(max(2, qb + 1)):
                    keys = pl.ds(kb * 256, 256)
                    s = mm(R.KS[p, keys], q, 1, 1)
                    if kb == qb or qb < 2:
                        ok = visible(kb * 256, 256, qb * 256, 256, prefix)
                        s = jnp.where(ok, s, masked_score)
                    prob = jnp.exp(s - lt)
                    ds = prob * (mm(R.VS[p, keys], do, 1, 1) - dd)
                    ds = ds.astype(BF)
                    R.DV[keys] += mm(prob.astype(BF), do)
                    R.DK[keys] += mm(ds, q)
                    dq = dq + mm(key_t[:, kb * 256 : kb * 256 + 256], ds)
                outs.append(dq)
            merged = jnp.where(iota((128, 256), 0) < 64, outs[0], outs[1])
            R.QS[p, cols] = (merged * 0.125).T.astype(BF)
            hook(agenda, p, qb)
        R.KS[p] = R.DK[...].astype(BF)
        R.VS[p] = R.DV[...].astype(BF)
        three = jnp.concatenate([R.QS[p], R.KS[p], R.VS[p]], axis=1)
        place(p + 1, mm(R.NM[...], three, 0, 0))

        @pl.when(p == 1)
        def _():
            att.one(1)

        @pl.when(p > 0)
        def _():
            att.one(p + 1)

        return carry

    lax.fori_loop(0, 3, pair_of_heads, 0)
    GP = (R.QS, R.KS, R.VS)

    XS, XN, BO = (r.reshape(512, WIDE) for r in (R.CS, R.XG, R.PE))

    R.G2[...] = jnp.zeros((8, WIDE), F32)

    def normed_grad(i, carry):
        mine = pl.ds(pl.multiple_of(i * 256, 256), 256)

        def half(start):
            rows = pl.ds(pl.multiple_of(start * 512 + i * 256, 256), 256)
            acc = jnp.zeros((256, WIDE), F32)
            for s in range(3):
                acc = acc + mm(joined(GP[s], rows), R.WA[:, :, s].reshape(WIDE, HALF), 1, 1)
            x = R.TK[rows].astype(F32) * R.STAT[rows, 0:1]
            R.G2[0:1] += jnp.sum(acc * x, axis=0, keepdims=True)
            return acc

        XS[mine] = half(o).astype(BF)
        GN[mine] = half(t)
        return carry

    w.flush()
    lax.fori_loop(0, 2, normed_grad, 0)
    xn = w.go(i_n, XS, XN, pc.PAIR)
    R.SB[0:1] = R.G2[0:1]
    sp = w.go(i_sp, R.SB, R.SP, pc.PAIR)
    att.two(1)
    att.three(0)
    outputs_pair().wait()

    def block_rows(i, carry):
        rows = pl.ds(pl.multiple_of(i * 256, 256), 256)
        full = pl.ds(pl.multiple_of(t * 512 + i * 256, 256), 256)
        eo = mm(R.ACT[full, pl.ds(0, ROWS)], RE[...])
        BO[rows] = (R.HIDN[full] + R.STAT[full, 2:3] * eo).astype(BF)
        return carry

    lax.fori_loop(0, 2, block_rows, 0)
    out_b = pltpu.make_async_copy(BO, R.block_out, R.ls.at[1])
    out_b.start()
    att.two(2)
    att.three(1)
    sp.wait_recv()
    R.SC[c] = R.SB[...] + R.SP[...]
    sc = [
        w.go(i_sc, R.SC.at[c], R.SC.at[c], pc.X),
        w.go(i_sc + 1, R.SC.at[c], R.SC.at[c], pc.Y),
        w.go(i_sc + 2, R.SC.at[c], R.SC.at[c], pc.DIAG),
    ]
    xn.wait_recv()

    def input_grad(i, carry):
        rows = pl.ds(pl.multiple_of(i * 128, 128), 128)
        full = pl.ds(pl.multiple_of(t * 512 + i * 128, 128), 128)
        gn = GN[rows] + XN[rows].astype(F32)
        x, f1 = R.TK[full].astype(F32), R.STAT[full, 0:1]
        g = gn * R.VEC[0:1]
        inner = jnp.mean(g * x, axis=1, keepdims=True)
        GH[full] = GH[full] + f1 * (g - x * (f1 * f1 * inner))
        return carry

    lax.fori_loop(0, 4, input_grad, 0)
    out_t = pltpu.make_async_copy(GH.at[own], R.tokens_grad, R.ls.at[0])
    out_t.start()
    att.two(3)
    att.three(2)
    for m in sc:
        m.wait_recv()
    R.SZ[z] = R.SC[0] + R.SC[1] + R.SC[2] + R.SC[3]
    sz = [w.go(i_sz + k, R.SZ.at[z], R.SZ.at[z], pc.Z(k)) for k in (1, 2, 3)]
    att.three(3)
    out_t.wait()
    out_b.wait()
    written = sums.last()
    for n in range(3):
        att.last(n)
    for m in sz:
        m.wait_recv()
    total = R.SZ[0] + R.SZ[1] + R.SZ[2] + R.SZ[3]
    probs = total[6:7, 0:128]
    R.balance[...] = (4.0 / (16 * ROWS)) * jnp.sum(share * probs, axis=1, keepdims=True)
    column = (iota((WIDE, 128), 0) == 48 * f + iota((WIDE, 128), 1)).astype(F32).astype(BF)
    mine = jnp.zeros((16, 128), F32)
    for _ in range(3):
        top = total.astype(BF)
        mine = mine + mm(top, column)
        total = total - top.astype(F32)
    R.gains_grad[...] = mine[0:2, 0:48]
    R.router_grad[...] = mine[2:6, 0:48]
    att.last(3)
    for m in written:
        m.wait()
    w.flush()


OUTS = {
    "block_out": ((512, WIDE), BF),
    "tokens_grad": ((512, WIDE), F32),
    "gains_grad": ((2, 48), F32),
    "qkv_grad": ((3, 48, HALF), F32),
    "out_grad": ((48, HALF), F32),
    "router_grad": ((4, 48), F32),
    "up_grad": ((4, 48, HID), F32),
    "down_grad": ((4, 48, HID), F32),
    "balance": ((1, 1), F32),
}
SCRATCH = {
    "STAT": ((ROWS, 128), F32),
    "ATO": ((3, ROWS, 128), BF),
    "ATX": ((3, ROWS, 128), BF),
    "PG": ((4, 128, WIDE), BF),
    "CQ": ((4, 128, WIDE), BF),
    "PE": ((4, 128, WIDE), BF),
    "GMB": ((2, 128, WIDE), F32),
    "EOO": ((4, 128, WIDE), F32),
    "GMO": ((4, 128, WIDE), F32),
    "GH": ((ROWS, WIDE), F32),
    "ACT": ((ROWS, HID), BF),
    "GB": ((ROWS, HID), BF),
    "TK": ((ROWS, WIDE), BF),
    "CT": ((ROWS, WIDE), BF),
    "WA": ((4, 4, 4, 48, HALF), BF),
    "WO": ((4, 4, 48, HALF), BF),
    "UE": ((4, 4, 48, HID), BF),
    "DE": ((4, 4, 48, HID), BF),
    "KC": ((ROWS, 128), F32),
    "CR": ((4, 2, 128, WIDE), BF),
    "DR": ((4, 2, 128, WIDE), BF),
    "VEC": ((16, WIDE), F32),
    "RW": ((WIDE, 128), BF),
    "SHARE": ((8, 128), F32),
    "NM": ((ROWS, WIDE), BF),
    "QS": ((3, ROWS, 128), BF),
    "KS": ((3, ROWS, 128), BF),
    "VS": ((3, ROWS, 128), BF),
    "LT": ((3, 8, ROWS), F32),
    "HIDN": ((ROWS, WIDE), F32),
    "PR": ((ROWS, 128), F32),
    "PS": ((8, 128), F32),
    "SM": ((16, 16, 128), BF),
    "CS": ((4, 128, WIDE), BF),
    "GC": ((ROWS, WIDE), BF),
    "XE": ((4, 128, WIDE), BF),
    "XG": ((4, 128, WIDE), BF),
    "RG": ((4, 2, 128, WIDE), BF),
    "RE": ((4, 2, 128, WIDE), BF),
    "RGR": ((16, WIDE), F32),
    "RU": ((2, 4, 48, HID), BF),
    "RD": ((2, 4, 48, HID), BF),
    "RU2": ((4, 48, HID), BF),
    "RD2": ((4, 48, HID), BF),
    "ZU": ((4, 48, HID), BF),
    "ZD": ((4, 48, HID), BF),
    "DD": ((3, 8, ROWS), F32),
    "DK": ((ROWS, 128), F32),
    "DV": ((ROWS, 128), F32),
    "AG": ((4, 4, 4, 144, 128), BF),
    "RA": ((4, 2, 2, 144, 128), BF),
    "RB": ((4, 2, 2, 144, 128), BF),
    "RA2": ((4, 2, 144, 128), BF),
    "RB2": ((4, 2, 144, 128), BF),
    "ZA": ((4, 4, 144, 128), BF),
    "G2": ((8, WIDE), F32),
    "SB": ((16, WIDE), F32),
    "SP": ((16, WIDE), F32),
    "SC": ((4, 16, WIDE), F32),
    "SZ": ((4, 16, WIDE), F32),
}
INS = ("tok", "cot", "pre", "idr", "gains", "qkv", "out", "router", "up", "down")
IN_HBM = ("tok", "cot", "up", "down")
OUT_HBM = ("block_out", "tokens_grad", "up_grad", "down_grad")
SEMAPHORES = 192


def fused(args):
    names = INS + tuple(OUTS) + tuple(SCRATCH) + ("ss", "rs", "ls")

    def body(*refs):
        R = types.SimpleNamespace(**dict(zip(names, refs)))
        pc = Place()
        w = Wire(R.ss, R.rs)
        phase_c(R, pc, w, *phase_b(R, pc, w, *phase_a(R, pc, w)))

    vm = pl.BlockSpec(memory_space=pltpu.VMEM)
    hbm = pl.BlockSpec(memory_space=pl.ANY)
    sm = pl.BlockSpec(memory_space=pltpu.SMEM)
    dma = pltpu.SemaphoreType.DMA
    return pl.pallas_call(
        body,
        out_shape=[jax.ShapeDtypeStruct(s, d) for s, d in OUTS.values()],
        in_specs=[sm if n == "pre" else hbm if n in IN_HBM else vm for n in INS],
        out_specs=[hbm if n in OUT_HBM else vm for n in OUTS],
        scratch_shapes=[pltpu.VMEM(s, d) for s, d in SCRATCH.values()]
        + [dma((SEMAPHORES,)), dma((SEMAPHORES,)), dma((4,))],
        compiler_params=pltpu.CompilerParams(
            collective_id=1, has_side_effects=True, vmem_limit_bytes=63 << 20
        ),
        name="block",
    )(*args)


def copy_out(arrays):
    n = len(arrays)

    def body(*refs):
        src, dst, held, sem = refs[:n], refs[n : 2 * n], refs[2 * n : 3 * n], refs[3 * n]
        come = [pltpu.make_async_copy(src[i], held[i], sem.at[0, i]) for i in range(n)]
        go = [pltpu.make_async_copy(held[i], dst[i], sem.at[1, i]) for i in range(n)]
        for m in come:
            m.start()
        for i in range(n):
            come[i].wait()
            go[i].start()
        for m in go:
            m.wait()

    hbm = pl.BlockSpec(memory_space=pl.ANY)
    return pl.pallas_call(
        body,
        out_shape=[jax.ShapeDtypeStruct(a.shape, a.dtype) for a in arrays],
        in_specs=[hbm] * n,
        out_specs=[hbm] * n,
        scratch_shapes=[pltpu.VMEM(a.shape, a.dtype) for a in arrays]
        + [pltpu.SemaphoreType.DMA((2, n))],
        name="outputs",
    )(*arrays)


def prepare(
    tokens, cotangent, prefix_len, expert_ids, norm_gains, qkv_weight, out_weight, router_weight, up_weight, down_weight
):
    ids = expert_ids.reshape(1, ROWS)
    return (tokens, cotangent, prefix_len, ids, norm_gains, qkv_weight, out_weight, router_weight, up_weight, down_weight)


def fast_device(*args):
    outs = copy_out(fused(prepare(*args)))
    return tuple(outs[:8]) + (outs[8].reshape(()),)


HEAD = 64
EXPERTS = 4
SEQ = 1024
CAP = 256


highest = lax.Precision.HIGHEST


def softmax_rows(scores):
    row_max = jnp.max(scores, axis=-1, keepdims=True)
    shifted = jnp.exp(scores - row_max)
    return shifted / jnp.sum(shifted, axis=-1, keepdims=True)


def slot_index(group_ids):
    onehot = (group_ids[:, None] == jnp.arange(EXPERTS, dtype=jnp.int32)[None, :]).astype(jnp.int32)
    rows = group_ids.shape[0]
    earlier = lax.broadcasted_iota(jnp.int32, (rows, rows), 1) <= lax.broadcasted_iota(
        jnp.int32, (rows, rows), 0
    )
    running = jnp.dot(
        earlier.astype(jnp.bfloat16),
        onehot.astype(jnp.bfloat16),
        preferred_element_type=jnp.float32,
    ).astype(jnp.int32)
    placed = jnp.sum(running * onehot, axis=1) - 1
    return jnp.where(placed < CAP, group_ids * CAP + placed, EXPERTS * CAP)


def rms_factor(values):
    return lax.rsqrt(jnp.mean(values * values, axis=-1, keepdims=True) + norm_eps)


def norm_back(grad_out, inputs, factor, gain):
    scaled = grad_out * gain
    row_inner = jnp.mean(scaled * inputs, axis=-1, keepdims=True)
    grad_in = factor * (scaled - inputs * factor * factor * row_inner)
    grad_gain = jnp.sum(grad_out * inputs * factor, axis=0)
    return (grad_in, grad_gain)


def gelu_slope(values):
    cumulative = 0.5 * (1.0 + lax.erf(values / math.sqrt(2.0)))
    density = jnp.exp(-0.5 * values * values) / math.sqrt(2.0 * math.pi)
    return cumulative + values * density


def block_scores(query_block, key_seq, offset, prefix, score_scale):
    scores = (
        jnp.einsum("qhd,khd->hqk", query_block, key_seq, preferred_element_type=jnp.float32)
        * score_scale
    )
    shape_pair = (query_block.shape[0], key_seq.shape[0])
    row_pos = offset + lax.broadcasted_iota(jnp.int32, shape_pair, 0)
    col_pos = lax.broadcasted_iota(jnp.int32, shape_pair, 1)
    allowed = (col_pos <= row_pos) | (col_pos < prefix)
    return jnp.where(allowed[None], scores, masked_score)


def attend(project, prefix_len, score_scale):
    group_rows = project.shape[0]
    full_width = project.shape[2]
    heads_here = full_width // HEAD
    block_rows = min(512, SEQ)
    shaped = project.reshape(group_rows, 3, heads_here, HEAD)
    query_all = shaped[:, 0]
    key_all = shaped[:, 1]
    value_all = shaped[:, 2]

    def one_block(number):
        row_start = number * block_rows
        seq_number = row_start // SEQ
        seq_start = seq_number * SEQ
        query_block = lax.dynamic_slice_in_dim(query_all, row_start, block_rows, 0)
        scores = block_scores(
            query_block, key_all, row_start - seq_start, prefix_len[seq_number], score_scale
        )
        row_max = jnp.max(scores, axis=-1, keepdims=True)
        shifted = jnp.exp(scores - row_max)
        row_total = jnp.sum(shifted, axis=-1, keepdims=True)
        prob_low = (shifted / row_total).astype(jnp.bfloat16)
        result = jnp.einsum("hqk,khd->qhd", prob_low, value_all, preferred_element_type=jnp.float32)
        return (
            result.reshape(block_rows, full_width).astype(jnp.bfloat16),
            (row_max + jnp.log(row_total))[..., 0],
        )

    outputs, log_total = lax.map(one_block, jnp.arange(group_rows // block_rows, dtype=jnp.int32))
    return (outputs.reshape(group_rows, full_width), log_total)


def attend_back(project, grad_att, log_total, prefix_len, score_scale):
    group_rows = project.shape[0]
    full_width = project.shape[2]
    heads_here = full_width // HEAD
    block_rows = min(512, SEQ)
    shaped = project.reshape(group_rows, 3, heads_here, HEAD)
    query_all = shaped[:, 0]
    key_all = shaped[:, 1]
    value_all = shaped[:, 2]
    grad_shaped = grad_att.reshape(group_rows, heads_here, HEAD)

    def one_block(carried, number):
        grad_keys, grad_values = carried
        row_start = number * block_rows
        seq_number = row_start // SEQ
        seq_start = seq_number * SEQ
        query_block = lax.dynamic_slice_in_dim(query_all, row_start, block_rows, 0)
        grad_block = lax.dynamic_slice_in_dim(grad_shaped, row_start, block_rows, 0)
        scores = block_scores(
            query_block, key_all, row_start - seq_start, prefix_len[seq_number], score_scale
        )
        prob_block = jnp.exp(scores - log_total[number][..., None])
        prob_low = prob_block.astype(jnp.bfloat16)
        grad_prob = jnp.einsum(
            "qhd,khd->hqk", grad_block, value_all, preferred_element_type=jnp.float32
        )
        value_part = jnp.einsum(
            "hqk,qhd->khd", prob_low, grad_block, preferred_element_type=jnp.float32
        )
        row_inner = jnp.sum(prob_block * grad_prob, axis=-1, keepdims=True)
        grad_scores = (prob_block * (grad_prob - row_inner)).astype(jnp.bfloat16)
        query_grad = (
            jnp.einsum("hqk,khd->qhd", grad_scores, key_all, preferred_element_type=jnp.float32)
            * score_scale
        )
        key_part = (
            jnp.einsum("hqk,qhd->khd", grad_scores, query_block, preferred_element_type=jnp.float32)
            * score_scale
        )
        old_keys = grad_keys
        grad_keys = old_keys + key_part
        old_values = grad_values
        grad_values = old_values + value_part
        return ((grad_keys, grad_values), query_grad)

    zero_rows = jnp.zeros((group_rows, heads_here, HEAD), jnp.float32)
    final, grad_query = lax.scan(
        one_block, (zero_rows, zero_rows), jnp.arange(group_rows // block_rows, dtype=jnp.int32)
    )
    grad_keys, grad_values = final
    stacked = jnp.stack(
        [
            grad_query.reshape(group_rows, full_width),
            grad_keys.reshape(group_rows, full_width),
            grad_values.reshape(group_rows, full_width),
        ],
        axis=1,
    )
    return stacked.astype(jnp.bfloat16)


def low_scatter(grad):
    return lax.psum_scatter(
        grad.astype(jnp.bfloat16), "fsdp", scatter_dimension=1, tiled=True
    ).astype(jnp.float32)


def per_device(
    tokens,
    cotangent,
    prefix_len,
    expert_ids,
    norm_gains,
    qkv_weight,
    out_weight,
    router_weight,
    up_weight,
    down_weight,
):
    tensor_size = lax.axis_size("tensor")
    fsdp_size = lax.axis_size("fsdp")
    own_rows = tokens.shape[0]
    group_rows = own_rows * tensor_size
    all_tokens = group_rows * fsdp_size
    own_start = lax.axis_index("tensor") * own_rows
    score_scale = 1.0 / math.sqrt(HEAD)
    gains_full, qkv_full, out_stack = (
        lax.all_gather(norm_gains, "fsdp", axis=1, tiled=True),
        lax.all_gather(qkv_weight, "fsdp", axis=1, tiled=True),
        lax.all_gather(out_weight[None], "fsdp", axis=1, tiled=True),
    )
    out_full = out_stack[0]
    router_full, up_full, down_full = (
        lax.all_gather(router_weight, "fsdp", axis=1, tiled=True),
        lax.all_gather(up_weight, "fsdp", axis=1, tiled=True),
        lax.all_gather(down_weight, "fsdp", axis=1, tiled=True),
    )
    inputs = lax.all_gather(tokens, "tensor", axis=0, tiled=True)
    input_float = inputs.astype(jnp.float32)
    factor_one = rms_factor(input_float)
    gain_one = gains_full[0].astype(jnp.float32)
    normed_one = (input_float * factor_one * gain_one).astype(jnp.bfloat16)
    project = jnp.einsum(
        "td,sdw->tsw", normed_one, qkv_full, preferred_element_type=jnp.float32
    ).astype(jnp.bfloat16)
    attended, log_total = attend(project, prefix_len, score_scale)
    branch = lax.psum_scatter(
        lax.dot_general(
            attended, out_full, (((1,), (1,)), ((), ())), preferred_element_type=jnp.float32
        ),
        "tensor",
        scatter_dimension=0,
        tiled=True,
    )
    hidden_own = tokens.astype(jnp.float32) + branch
    hidden_group = lax.all_gather(hidden_own, "tensor", axis=0, tiled=True)
    factor_two = rms_factor(hidden_group)
    gain_two = gains_full[1].astype(jnp.float32)
    moe_input = (hidden_group * factor_two * gain_two).astype(jnp.bfloat16)
    logits = lax.dot_general(
        moe_input, router_full, (((1,), (1,)), ((), ())), preferred_element_type=jnp.float32
    )
    group_ids = expert_ids[:, 0]
    onehot = (group_ids[:, None] == jnp.arange(EXPERTS, dtype=jnp.int32)[None, :]).astype(
        jnp.float32
    )
    gate_value = jax.nn.sigmoid(jnp.sum(logits * onehot, axis=-1))
    router_prob = softmax_rows(logits)
    counts, prob_sums = lax.psum((jnp.sum(onehot, axis=0), jnp.sum(router_prob, axis=0)), "fsdp")
    route_share = counts / all_tokens
    balance_loss = EXPERTS * jnp.sum(route_share * prob_sums) / all_tokens
    slot_rows = slot_index(group_ids)
    model_width = moe_input.shape[1]
    dispatched = (
        jnp.zeros((EXPERTS * CAP, model_width), jnp.bfloat16)
        .at[slot_rows]
        .set(moe_input, mode="drop")
        .reshape(EXPERTS, CAP, model_width)
    )
    before = jnp.einsum("ecd,edf->ecf", dispatched, up_full, preferred_element_type=jnp.float32)
    activated = jax.nn.gelu(before, approximate=False).astype(jnp.bfloat16)
    expert_out = jnp.einsum(
        "ecf,edf->ecd", activated, down_full, preferred_element_type=jnp.float32
    ).reshape(EXPERTS * CAP, model_width)
    combined_part = jnp.concatenate([expert_out, jnp.zeros((1, model_width), jnp.float32)], axis=0)[
        slot_rows
    ]
    combined = lax.psum_scatter(combined_part, "tensor", scatter_dimension=0, tiled=True)
    gate_own = lax.dynamic_slice_in_dim(gate_value, own_start, own_rows, 0)
    block_out = (hidden_own + gate_own[:, None] * combined).astype(jnp.bfloat16)
    gains_back, qkv_back, out_again, router_back, up_back, down_back = (
        lax.all_gather(norm_gains, "fsdp", axis=1, tiled=True),
        lax.all_gather(qkv_weight, "fsdp", axis=1, tiled=True),
        lax.all_gather(out_weight[None], "fsdp", axis=1, tiled=True),
        lax.all_gather(router_weight, "fsdp", axis=1, tiled=True),
        lax.all_gather(up_weight, "fsdp", axis=1, tiled=True),
        lax.all_gather(down_weight, "fsdp", axis=1, tiled=True),
    )
    out_back = out_again[0]
    cot_group = lax.all_gather(cotangent, "tensor", axis=0, tiled=True).astype(jnp.float32)
    grad_combined = (gate_value[:, None] * cot_group).astype(jnp.bfloat16)
    gate_grad_own = jnp.sum(cotangent.astype(jnp.float32) * combined, axis=-1)
    gate_grad_placed = lax.dynamic_update_slice_in_dim(
        jnp.zeros((group_rows,), jnp.float32), gate_grad_own, own_start, 0
    )
    grad_slots = (
        jnp.zeros((EXPERTS * CAP, model_width), jnp.bfloat16)
        .at[slot_rows]
        .set(grad_combined, mode="drop")
        .reshape(EXPERTS, CAP, model_width)
    )
    grad_activated = jnp.einsum(
        "ecd,edf->ecf", grad_slots, down_back, preferred_element_type=jnp.float32
    )
    down_grad = jnp.einsum(
        "ecd,ecf->edf", grad_slots, activated, preferred_element_type=jnp.float32
    )
    grad_before = (grad_activated * gelu_slope(before)).astype(jnp.bfloat16)
    up_grad = jnp.einsum(
        "ecd,ecf->edf", dispatched, grad_before, preferred_element_type=jnp.float32
    )
    grad_dispatched = jnp.einsum(
        "ecf,edf->ecd", grad_before, up_back, preferred_element_type=jnp.float32
    ).reshape(EXPERTS * CAP, model_width)
    grad_input_part = jnp.concatenate(
        [grad_dispatched, jnp.zeros((1, model_width), jnp.float32)], axis=0
    )[slot_rows]
    grad_moe, gate_grad = lax.psum((grad_input_part, gate_grad_placed), "tensor")
    gate_slope = gate_value * (1.0 - gate_value)
    mixed_share = jnp.sum(router_prob * route_share[None, :], axis=-1, keepdims=True)
    logit_grad = onehot * (gate_grad * gate_slope)[
        :, None
    ] + balance_weight * EXPERTS / all_tokens * router_prob * (route_share[None, :] - mixed_share)
    grad_norm_two = grad_moe + jnp.dot(
        logit_grad, router_back.astype(jnp.float32), precision=highest
    )
    router_grad = jnp.dot(logit_grad.T, moe_input.astype(jnp.float32), precision=highest)
    grad_hidden, gain_two_grad = norm_back(
        grad_norm_two, hidden_group, factor_two, gains_back[1].astype(jnp.float32)
    )
    grad_hidden = grad_hidden + cot_group
    grad_branch = grad_hidden.astype(jnp.bfloat16)
    grad_att = jnp.dot(grad_branch, out_back, preferred_element_type=jnp.float32).astype(
        jnp.bfloat16
    )
    out_grad = lax.dot_general(
        grad_branch, attended, (((0,), (0,)), ((), ())), preferred_element_type=jnp.float32
    )
    grad_project = attend_back(project, grad_att, log_total, prefix_len, score_scale)
    qkv_grad = jnp.einsum(
        "td,tsw->sdw", normed_one, grad_project, preferred_element_type=jnp.float32
    )
    grad_normed_part = jnp.einsum(
        "tsw,sdw->td", grad_project, qkv_back, preferred_element_type=jnp.float32
    )
    grad_normed = lax.psum(grad_normed_part, "tensor")
    grad_tokens, gain_one_grad = norm_back(
        grad_normed, input_float, factor_one, gains_back[0].astype(jnp.float32)
    )
    grad_tokens = grad_tokens + grad_hidden
    tokens_grad = lax.dynamic_slice_in_dim(grad_tokens, own_start, own_rows, 0)
    gains_own, qkv_own, out_own, router_own, up_own, down_own = (
        lax.psum_scatter(
            jnp.stack([gain_one_grad, gain_two_grad], axis=0),
            "fsdp",
            scatter_dimension=1,
            tiled=True,
        ),
        low_scatter(qkv_grad),
        low_scatter(out_grad[None]),
        lax.psum_scatter(router_grad, "fsdp", scatter_dimension=1, tiled=True),
        low_scatter(up_grad),
        low_scatter(down_grad),
    )
    return (
        block_out,
        tokens_grad,
        gains_own,
        qkv_own,
        out_own[0],
        router_own,
        up_own,
        down_own,
        balance_loss,
    )


def solution(mesh):
    placed = (
        P(("fsdp", "tensor"), None),
        P(("fsdp", "tensor"), None),
        P("fsdp"),
        P("fsdp", None),
        P(None, "fsdp"),
        P(None, "fsdp", "tensor"),
        P("fsdp", "tensor"),
        P(None, "fsdp"),
        P(None, "fsdp", "tensor"),
        P(None, "fsdp", "tensor"),
    )
    fits = mesh.shape["fsdp"] == 16 and mesh.shape["tensor"] == 2
    return jax.shard_map(
        fast_device if fits else per_device,
        mesh=mesh,
        in_specs=placed,
        out_specs=(
            P(("fsdp", "tensor"), None),
            P(("fsdp", "tensor"), None),
            P(None, "fsdp"),
            P(None, "fsdp", "tensor"),
            P("fsdp", "tensor"),
            P(None, "fsdp"),
            P(None, "fsdp", "tensor"),
            P(None, "fsdp", "tensor"),
            P(),
        ),
        check_vma=False,
    )
```
